32 devices in a mesh: seq: 8 (over z, x), head: 4 (over y, core).
Axes of the slice: x: 2, y: 2, z: 4, core: 2. Of those that a mesh axis runs over, the one named last changes fastest.
Arguments:
- queries: bfloat16 [4096, 4096], P(('seq', 'head')), may hold values from -6 to 6
- keys: bfloat16 [4096, 4096], P(('seq', 'head')), may hold values from -6 to 6
- values: bfloat16 [4096, 4096], P(('seq', 'head')), may hold values from -128 to 128
- out_grad: bfloat16 [4096, 4096], P(('seq', 'head')), may hold values from -16 to 16
- doc_lengths: int32 [8], replicated, may hold values from 1 to 2048, 4096 in all
Outputs:
- attn_out: bfloat16 [4096, 4096], P(('seq', 'head'))
- grad_queries: bfloat16 [4096, 4096], P(('seq', 'head'))
- grad_keys: bfloat16 [4096, 4096], P(('seq', 'head'))
- grad_values: bfloat16 [4096, 4096], P(('seq', 'head'))
The draws below stay inside these ranges and needn't reach their ends.
Inputs may be any that keep to these rules, and one draw needn't show every extreme that they name: `doc_lengths`: the lengths sum to 4096; the longest is exactly 2048.
All inputs are finite; a program needn't handle non-finite values.
Results may differ from the reference program's by a relative error of at most 0.011.
Values may be sent and summed in bfloat16 or wider, within the bound.
No kernel may reach another device: no remote copies, remote signals or barrier semaphores. Data moves between devices by JAX's collectives and lax.ppermute only.
A program may use at most 128 MiB of HBM per device.

```python
import math
import jax
import jax.numpy as jnp
import numpy as np
from jax import lax

H = 32
DH = 128
GROUP = 512
NDOC = 8
TOKENS = 4096
DOC_MOST = 2048
N_SEQ = 8


def draw_values(key, part):
    key_base, key_cols, key_rows = jax.random.split(key, 3)
    sample = jnp.clip(jax.random.normal(key_base, (TOKENS, H * DH), jnp.float32), -4.0, 4.0)
    log_top = math.log(10.0)
    col_scale = jnp.exp(jax.random.uniform(key_cols, (1, H * DH), jnp.float32, 0.0, log_top))
    row_scale = jnp.exp(jax.random.uniform(key_rows, (TOKENS, 1), jnp.float32, 0.0, log_top))
    return (sample * col_scale * row_scale / 8.0).astype(jnp.bfloat16)


def block_scale(own_key, extent, cuts, smallest, high):
    factor_of, own = 1.0, jax.random.fold_in(own_key, 6)
    for dim, blocks in cuts:
        heights = jnp.exp(jax.random.uniform(jax.random.fold_in(own, dim), (blocks,), jnp.float32, smallest / len(cuts), high / len(cuts)))
        factor_of = factor_of * jnp.repeat(heights, extent[dim] // blocks).reshape([-1 if axis == dim else 1 for axis in range(len(extent))])
    return factor_of


def length_profile(amount, total, bound, skew):
    portions = [(1 << 20) // math.isqrt(standing ** skew) + 1 for standing in range(2, amount + 1)]
    surplus, holding = total - bound - (amount - 1), [1] * (amount - 1)
    while surplus > 0:
        candidates = [i for i in range(amount - 1) if holding[i] < bound]
        mass, remaining = sum([portions[i] for i in candidates]), surplus
        for i in candidates:
            more = min(bound - holding[i], max(1, remaining * portions[i] // mass), surplus)
            holding[i] = holding[i] + more
            surplus = surplus - more
    return np.array([bound] + holding)


def uneven(key, amount, total, bound, skew):
    if amount == 2:
        one = jax.random.randint(key, (), max(1, total - bound), min(bound, total - 1) + 1)
        return jnp.stack([one, total - one])
    sizes = jnp.asarray(length_profile(amount, total, bound, skew), jnp.int32)
    couples = (amount - 1) // 2
    giver, receiver = sizes[1:1 + 2 * couples:2], sizes[2:2 + 2 * couples:2]
    margin = jnp.minimum(giver - 1, bound - receiver)
    moved = jax.random.randint(jax.random.fold_in(key, 1), (couples,), 0, 1 << 20) % (margin + 1)
    sizes = sizes.at[1:1 + 2 * couples:2].set(giver - moved).at[2:2 + 2 * couples:2].set(receiver + moved)
    return sizes[jax.random.permutation(jax.random.fold_in(key, 2), amount)]


def noise(rng, extent, deviation, limit, pieces=(), kind=jnp.bfloat16):
    drawn = jax.random.normal(rng, extent, jnp.float32) * deviation
    if len(pieces) > 0:
        drawn = block_scale(rng, extent, pieces, -0.22, 0.18) * drawn
    return jnp.clip(drawn, min=-limit, max=limit).astype(kind)


def setup_inputs(seed: int = 0) -> dict:
    seeds = jax.random.split(jax.random.key(seed), 6)
    queries = noise(seeds[0], (TOKENS, H * DH), 1.0, 6.0, ((0, 32),))
    keys = noise(seeds[1], (TOKENS, H * DH), 1.0, 6.0, ((0, 32),))
    values = draw_values(jax.random.fold_in(seeds[5], 71), 0)
    out_grad = noise(seeds[3], (TOKENS, H * DH), 4.0, 16.0, ((0, 32),))
    doc_lengths = uneven(seeds[4], NDOC, TOKENS, DOC_MOST, 1).astype(jnp.int32)
    return {"queries": queries, "keys": keys, "values": values, "out_grad": out_grad, "doc_lengths": doc_lengths}


def feature(array):
    wide = array.astype(jnp.float32)
    return jnp.where(wide > 0, wide + 1.0, jnp.exp(jnp.minimum(wide, 0.0)))

def slope(array):
    wide = array.astype(jnp.float32)
    return jnp.where(wide > 0, 1.0, jnp.exp(jnp.minimum(wide, 0.0)))

def doc_index(doc_ends, where):
    return lax.optimization_barrier(jnp.sum((where[..., None] >= doc_ends).astype(jnp.int32), axis=-1))

def reference(queries, keys, values, out_grad, doc_lengths):
    doc_ends = jnp.cumsum(doc_lengths).astype(jnp.int32)
    within = jnp.arange(GROUP, dtype=jnp.int32)
    causal = within[:, None] >= within[None, :]

    def blocked(array):
        return array.reshape(N_SEQ, GROUP, H, DH)
    query_all = blocked(queries)
    key_all = blocked(keys)
    value_all = blocked(values)
    grad_all = blocked(out_grad)
    block_ids = jnp.arange(N_SEQ, dtype=jnp.int32)

    def layout(block_index):
        block_start = block_index * GROUP
        doc_of = doc_index(doc_ends, block_start + within)
        doc_first = doc_of[0]
        doc_last = doc_of[GROUP - 1]
        before = doc_index(doc_ends, block_start - 1)
        doc_after = doc_index(doc_ends, block_start + GROUP)
        visible = causal & (doc_of[:, None] == doc_of[None, :])
        head_rows = (doc_of == doc_first).astype(jnp.float32)[:, None, None]
        tail_rows = (doc_of == doc_last).astype(jnp.float32)[:, None, None]
        return (doc_first, doc_last, before, doc_after, visible, head_rows, tail_rows)

    def forward_part(query_blk, key_blk, value_blk, incoming, visible, head_rows):
        feat_query = feature(query_blk).astype(jnp.bfloat16)
        feat_key = feature(key_blk).astype(jnp.bfloat16)
        scores = jnp.einsum('thd,shd->hts', feat_query.astype(jnp.float32), feat_key.astype(jnp.float32))
        scores = jnp.where(visible[None], scores, 0.0).astype(jnp.bfloat16)
        carried_term = jnp.einsum('thd,hde->the', feat_query.astype(jnp.float32), incoming.astype(jnp.float32)) * head_rows
        attended = carried_term + jnp.einsum('hts,she->the', scores.astype(jnp.float32), value_blk.astype(jnp.float32))
        inv_rms = lax.rsqrt(lax.optimization_barrier(jnp.mean(attended * attended, axis=-1, keepdims=True)) + 1e-05)
        normed = attended * inv_rms
        return (feat_query, feat_key, scores, inv_rms, normed)

    def forward_step(state, members):
        block_index, query_blk, key_blk, value_blk = members
        doc_first, doc_last, before, doc_after, visible, head_rows, tail_rows = layout(block_index)
        incoming = jnp.where(doc_first == before, state, 0.0).astype(jnp.bfloat16)
        feat_query, feat_key, scores, inv_rms, normed = forward_part(query_blk, key_blk, value_blk, incoming, visible, head_rows)
        tail_state = jnp.einsum('shd,she->hde', feat_key.astype(jnp.float32) * tail_rows, value_blk.astype(jnp.float32))
        new_state = jnp.where(doc_last == before, state, 0.0) + tail_state
        return (new_state, (incoming, normed.astype(jnp.bfloat16)))
    zero_state = jnp.zeros((H, DH, DH), jnp.float32)
    _, (incomings, outputs) = lax.scan(forward_step, zero_state, (block_ids, query_all, key_all, value_all))

    def backward_step(state, members):
        block_index, query_blk, key_blk, value_blk, grad_blk, incoming = members
        doc_first, doc_last, before, doc_after, visible, head_rows, tail_rows = layout(block_index)
        feat_query, feat_key, scores, inv_rms, normed = forward_part(query_blk, key_blk, value_blk, incoming, visible, head_rows)
        grad_out = grad_blk.astype(jnp.float32)
        grad_att = ((grad_out - normed * lax.optimization_barrier(jnp.mean(grad_out * normed, axis=-1, keepdims=True))) * inv_rms).astype(jnp.bfloat16)
        outgoing = jnp.where(doc_last == doc_after, state, 0.0).astype(jnp.bfloat16)
        fq32 = feat_query.astype(jnp.float32)
        fk32 = feat_key.astype(jnp.float32)
        value32 = value_blk.astype(jnp.float32)
        ga32 = grad_att.astype(jnp.float32)
        grad_scores = jnp.einsum('the,she->hts', ga32, value32)
        grad_scores = jnp.where(visible[None], grad_scores, 0.0).astype(jnp.bfloat16).astype(jnp.float32)
        grad_fq = jnp.einsum('hts,shd->thd', grad_scores, fk32) + jnp.einsum('the,hde->thd', ga32, incoming.astype(jnp.float32)) * head_rows
        grad_fk = jnp.einsum('hts,thd->shd', grad_scores, fq32) + jnp.einsum('she,hde->shd', value32, outgoing.astype(jnp.float32)) * tail_rows
        grad_fv = jnp.einsum('hts,the->she', scores.astype(jnp.float32), ga32) + jnp.einsum('shd,hde->she', fk32, outgoing.astype(jnp.float32)) * tail_rows
        head_sum = jnp.einsum('thd,the->hde', fq32 * head_rows, ga32)
        new_state = jnp.where(doc_first == doc_after, state, 0.0) + head_sum
        grad_query = (grad_fq * slope(query_blk)).astype(jnp.bfloat16)
        grad_key = (grad_fk * slope(key_blk)).astype(jnp.bfloat16)
        return (new_state, (grad_query, grad_key, grad_fv.astype(jnp.bfloat16)))
    _, (grad_query_all, grad_key_all, grad_value_all) = lax.scan(backward_step, zero_state, (block_ids, query_all, key_all, value_all, grad_all, incomings), reverse=True)
    width = H * DH
    return (outputs.reshape(TOKENS, width), grad_query_all.reshape(TOKENS, width), grad_key_all.reshape(TOKENS, width), grad_value_all.reshape(TOKENS, width))
```

```python
import functools

import jax
import jax.numpy as jnp
from jax import lax
from jax.experimental import pallas as pl
from jax.experimental.pallas import tpu as pltpu
from jax.sharding import Mesh, PartitionSpec as P

DH = 128
F32 = jnp.float32
BF16 = jnp.bfloat16
NN = (((1,), (0,)), ((), ()))
NT = (((1,), (1,)), ((), ()))
TN = (((0,), (0,)), ((), ()))
LAYER = ("x", "head")


def mul(a, b, dims):
    return lax.dot_general(a, b, dims, preferred_element_type=F32)


def feature(wide):
    return jnp.where(wide > 0, wide + 1.0, jnp.exp(jnp.minimum(wide, 0.0)))


def slope(wide):
    return jnp.where(wide > 0, 1.0, jnp.exp(jnp.minimum(wide, 0.0)))


def doc_ends(lens):
    ends, total = [], 0
    for j in range(lens.shape[0]):
        total = total + lens[j]
        ends.append(total)
    return ends


def doc_at(ends, where):
    found = 0
    for end in ends:
        found = found + jnp.where(where >= end, 1, 0)
    return found


def rows_of(ends, first, count):
    at = first + lax.broadcasted_iota(jnp.int32, (count, 1), 0)
    return doc_at(ends, at)


def columns_of(ends, first, count):
    at = first + lax.broadcasted_iota(jnp.int32, (1, count), 1)
    return doc_at(ends, at)


def visible(ends, first, count):
    later = lax.broadcasted_iota(jnp.int32, (count, count), 0)
    earlier = lax.broadcasted_iota(jnp.int32, (count, count), 1)
    return (later >= earlier) & (
        rows_of(ends, first, count) == columns_of(ends, first, count)
    )


def head_mask(ends, first, count):
    return rows_of(ends, first, count) == doc_at(ends, first)


def tail_mask(ends, first, count):
    return rows_of(ends, first, count) == doc_at(ends, first + count - 1)


def cols(h):
    return slice(h * DH, (h + 1) * DH)


def tail_kernel(lens, place, k, v, out):
    count = k.shape[0]
    tail = tail_mask(doc_ends(lens), place[0] * count, count)
    for h in range(out.shape[0]):
        fk = jnp.where(tail, feature(k[:, cols(h)].astype(F32)), 0.0).astype(BF16)
        out[h] = mul(fk, v[:, cols(h)], TN).astype(BF16)


def local_kernel(lens, place, q, k, v, scores, part):
    count = q.shape[0]
    seen = visible(doc_ends(lens), place[0] * count, count)
    for h in range(scores.shape[0]):
        fq = feature(q[:, cols(h)].astype(F32)).astype(BF16)
        fk = feature(k[:, cols(h)].astype(F32)).astype(BF16)
        s = jnp.where(seen, mul(fq, fk, NT), 0.0).astype(BF16)
        scores[h] = s
        part[:, cols(h)] = mul(s, v[:, cols(h)], NN)


def norm_kernel(lens, place, q, g, part, incoming, out, grad_att, state):
    count = q.shape[0]
    head = head_mask(doc_ends(lens), place[0] * count, count)
    for h in range(state.shape[0]):
        fq = jnp.where(head, feature(q[:, cols(h)].astype(F32)), 0.0).astype(BF16)
        att = part[:, cols(h)] + mul(fq, incoming[h], NN)
        inv = lax.rsqrt(jnp.mean(att * att, axis=-1, keepdims=True) + 1e-05)
        normed = att * inv
        out[:, cols(h)] = normed.astype(BF16)
        go = g[:, cols(h)].astype(F32)
        ga = (go - normed * jnp.mean(go * normed, axis=-1, keepdims=True)) * inv
        ga = ga.astype(BF16)
        grad_att[:, cols(h)] = ga
        state[h] = mul(fq, ga, TN).astype(BF16)


def inner_kernel(lens, place, q, k, v, grad_att, incoming, scores, gq, gk, gv):
    count = q.shape[0]
    ends = doc_ends(lens)
    first = place[0] * count
    seen = visible(ends, first, count)
    head = head_mask(ends, first, count)
    for h in range(scores.shape[0]):
        wide = q[:, cols(h)].astype(F32)
        fq = feature(wide).astype(BF16)
        fk = feature(k[:, cols(h)].astype(F32)).astype(BF16)
        ga = grad_att[:, cols(h)]
        gs = jnp.where(seen, mul(ga, v[:, cols(h)], NT), 0.0).astype(BF16)
        total = mul(gs, fk, NN) + jnp.where(head, mul(ga, incoming[h], NT), 0.0)
        gq[:, cols(h)] = (total * slope(wide)).astype(BF16)
        gk[:, cols(h)] = mul(gs, fq, TN)
        gv[:, cols(h)] = mul(scores[h], ga, TN)


def last_kernel(lens, place, k, v, gk_part, gv_part, outgoing, gk, gv):
    count = k.shape[0]
    tail = tail_mask(doc_ends(lens), place[0] * count, count)
    for h in range(outgoing.shape[0]):
        wide = k[:, cols(h)].astype(F32)
        fk = jnp.where(tail, feature(wide), 0.0).astype(BF16)
        vt = jnp.where(tail, v[:, cols(h)].astype(F32), 0.0).astype(BF16)
        gk[:, cols(h)] = (
            (gk_part[:, cols(h)] + mul(vt, outgoing[h], NT)) * slope(wide)
        ).astype(BF16)
        gv[:, cols(h)] = (gv_part[:, cols(h)] + mul(fk, outgoing[h], NN)).astype(BF16)


def same(a, b):
    return jnp.where(a == b, 1.0, 0.0).astype(F32)


def total_kernel(forward, count, lens, place, held, total):
    members = held.shape[0]
    ends = doc_ends(lens)
    layer = place[1] * (members * count)
    carry = None
    for step in range(members):
        i = step if forward else members - 1 - step
        mine = held[i, 0].astype(F32)
        edge = layer + ((i + 1) * count - 1 if forward else i * count)
        here = doc_at(ends, edge)
        if carry is not None:
            mine = mine + carry * same(here, previous)
        carry, previous = mine, here
    total[0] = carry.astype(BF16)


def prefix_kernel(forward, count, lens, place, held, *rest):
    others, out = rest[:-1], rest[-1]
    members = held.shape[0]
    span = members * count
    ends = doc_ends(lens)
    layer = place[1] * span
    sign = -1 if forward else 1
    previous = doc_at(ends, layer - 1 if forward else layer + span)
    carry = None
    for s, other in enumerate(others):
        far = layer + sign * s * span
        there = doc_at(ends, far - 1 if forward else far + span)
        term = other[0].astype(F32) * same(there, previous)
        carry = term if carry is None else carry + term
    for step in range(members):
        i = step if forward else members - 1 - step
        near, far = layer + i * count, layer + (i + 1) * count - 1
        if not forward:
            near, far = far, near
        if carry is None:
            out[i, 0] = jnp.zeros(out.shape[2:], BF16)
        else:
            out[i, 0] = (carry * same(doc_at(ends, near), previous)).astype(BF16)
        if step < members - 1:
            here = doc_at(ends, far)
            mine = held[i, 0].astype(F32)
            if carry is not None:
                mine = mine + carry * same(here, previous)
            carry, previous = mine, here


SMEM = pl.BlockSpec(memory_space=pltpu.SMEM)
PARAMS = pltpu.CompilerParams(
    dimension_semantics=("arbitrary",), vmem_limit_bytes=48 * 1024 * 1024
)


def local(queries, keys, values, out_grad, doc_lengths):
    count, width = queries.shape
    heads = width // DH
    layers = lax.axis_size("z")
    members = lax.axis_size("x") * lax.axis_size("head")
    owned = heads // members
    place = jnp.stack(
        [lax.axis_index(("z", "x", "head")), lax.axis_index("z")]
    ).astype(jnp.int32)
    block_heads = 4
    steps = heads // block_heads
    tokens = pl.BlockSpec((count, block_heads * DH), lambda i: (0, i))
    states = pl.BlockSpec((block_heads, DH, DH), lambda i: (i, 0, 0))
    tiles = pl.BlockSpec((block_heads, count, count), lambda i: (i, 0, 0))
    token_bf = jax.ShapeDtypeStruct((count, width), BF16)
    token_f32 = jax.ShapeDtypeStruct((count, width), F32)
    state_bf = jax.ShapeDtypeStruct((heads, DH, DH), BF16)
    tile_bf = jax.ShapeDtypeStruct((heads, count, count), BF16)

    def run(kernel, ins, outs, shapes, args, products, name):
        return pl.pallas_call(
            kernel,
            grid=(steps,),
            in_specs=[SMEM, SMEM] + ins,
            out_specs=outs,
            out_shape=shapes,
            compiler_params=PARAMS,
            cost_estimate=pl.CostEstimate(
                flops=2 * products * heads * count * DH * DH,
                bytes_accessed=2 * (len(ins) + len(outs)) * count * width,
                transcendentals=count * width,
            ),
            name=name,
        )(doc_lengths, place, *args)

    def combine(kernel, args, many, forward, name):
        group = pl.BlockSpec((members, 1, DH, DH), lambda i: (0, i, 0, 0))
        single = pl.BlockSpec((1, DH, DH), lambda i: (i, 0, 0))
        return pl.pallas_call(
            functools.partial(kernel, forward, count),
            grid=(owned,),
            in_specs=[SMEM, SMEM, group] + [single] * (len(args) - 1),
            out_specs=group if many else single,
            out_shape=jax.ShapeDtypeStruct(
                ((members,) if many else ()) + (owned, DH, DH), BF16
            ),
            compiler_params=PARAMS,
            cost_estimate=pl.CostEstimate(
                flops=4 * heads * DH * DH,
                bytes_accessed=4 * heads * DH * DH,
                transcendentals=0,
            ),
            name=name,
        )(doc_lengths, place, *args)

    def scan(state, forward, name):
        held = lax.all_to_all(state, LAYER, split_axis=0, concat_axis=0, tiled=True)
        held = held.reshape(members, owned, DH, DH)
        others = []
        if layers > 1:
            total = combine(total_kernel, (held,), False, forward, name + "_total")
            for s in range(1, min(layers - 1, -(-layers // 2)) + 1):
                pairs = [(i, i + s) if forward else (i + s, i) for i in range(layers - s)]
                others.append(lax.ppermute(total, "z", pairs))
        sums = combine(prefix_kernel, (held, *others), True, forward, name + "_prefix")
        return lax.all_to_all(
            sums.reshape(heads, DH, DH), LAYER, split_axis=0, concat_axis=0, tiled=True
        )

    (tail,) = run(tail_kernel, [tokens] * 2, [states], [state_bf], (keys, values), 1, "tail")
    incoming = scan(tail, True, "carried")
    scores, part = run(
        local_kernel,
        [tokens] * 3,
        [tiles, tokens],
        [tile_bf, token_f32],
        (queries, keys, values),
        2,
        "within",
    )
    attn_out, grad_att, head_state = run(
        norm_kernel,
        [tokens, tokens, tokens, states],
        [tokens, tokens, states],
        [token_bf, token_bf, state_bf],
        (queries, out_grad, part, incoming),
        2,
        "normed",
    )
    outgoing = scan(head_state, False, "future")
    grad_queries, gk_part, gv_part = run(
        inner_kernel,
        [tokens] * 4 + [states, tiles],
        [tokens] * 3,
        [token_bf, token_f32, token_f32],
        (queries, keys, values, grad_att, incoming, scores),
        5,
        "grads_within",
    )
    grad_keys, grad_values = run(
        last_kernel,
        [tokens] * 4 + [states],
        [tokens] * 2,
        [token_bf, token_bf],
        (keys, values, gk_part, gv_part, outgoing),
        2,
        "grads_last",
    )
    return attn_out, grad_queries, grad_keys, grad_values


def solution(mesh):
    n_seq, n_head = mesh.shape["seq"], mesh.shape["head"]
    inner = 2 if n_seq % 2 == 0 else 1
    fine = Mesh(mesh.devices.reshape(n_seq // inner, inner, n_head), ("z", "x", "head"))
    rows = P(("z", "x", "head"), None)
    return jax.shard_map(
        local,
        mesh=fine,
        in_specs=(rows, rows, rows, rows, P()),
        out_specs=(rows, rows, rows, rows),
        check_vma=False,
    )
```

```python
import functools

import jax
import jax.numpy as jnp
from jax import lax
from jax.experimental import pallas as pl
from jax.experimental.pallas import tpu as pltpu
from jax.sharding import Mesh, PartitionSpec as P

DH = 128
F32 = jnp.float32
BF16 = jnp.bfloat16
NN = (((1,), (0,)), ((), ()))
NT = (((1,), (1,)), ((), ()))
TN = (((0,), (0,)), ((), ()))
LAYER = ("x", "head")


def mul(a, b, dims):
    return lax.dot_general(a, b, dims, preferred_element_type=F32)


def feature(wide):
    return jnp.where(wide > 0, wide + 1.0, jnp.exp(jnp.minimum(wide, 0.0)))


def slope(wide):
    return jnp.where(wide > 0, 1.0, jnp.exp(jnp.minimum(wide, 0.0)))


def doc_ends(info):
    ends, total = [], 0
    for j in range(2, info.shape[0]):
        total = total + info[j]
        ends.append(total)
    return ends


def doc_at(ends, where):
    found = 0
    for end in ends:
        found = found + jnp.where(where >= end, 1, 0)
    return found


def rows_of(ends, first, count):
    at = first + lax.broadcasted_iota(jnp.int32, (count, 1), 0)
    return doc_at(ends, at)


def columns_of(ends, first, count):
    at = first + lax.broadcasted_iota(jnp.int32, (1, count), 1)
    return doc_at(ends, at)


def visible(ends, first, count):
    later = lax.broadcasted_iota(jnp.int32, (count, count), 0)
    earlier = lax.broadcasted_iota(jnp.int32, (count, count), 1)
    return (later >= earlier) & (
        rows_of(ends, first, count) == columns_of(ends, first, count)
    )


def head_mask(ends, first, count):
    return rows_of(ends, first, count) == doc_at(ends, first)


def tail_mask(ends, first, count):
    return rows_of(ends, first, count) == doc_at(ends, first + count - 1)


def cols(h):
    return slice(h * DH, (h + 1) * DH)


def bunches(heads, size=4):
    return [range(h, min(h + size, heads)) for h in range(0, heads, size)]


def halves(wide):
    high = wide.astype(BF16)
    return jnp.concatenate([high, (wide - high.astype(F32)).astype(BF16)], axis=1)


def row_mean(wide, weights):
    return mul(halves(wide), weights, NN)


def tail_kernel(info, k, v, out):
    count = k.shape[0]
    tail = tail_mask(doc_ends(info), info[0] * count, count)
    for hs in bunches(out.shape[0]):
        fks = [
            jnp.where(tail, feature(k[:, cols(h)].astype(F32)), 0.0).astype(BF16) for h in hs
        ]
        sums = [mul(fk, v[:, cols(h)], TN).astype(BF16) for h, fk in zip(hs, fks)]
        for h, value in zip(hs, sums):
            out[h] = value


def local_kernel(info, q, k, v, scores, part, head_fq, turned):
    count = q.shape[0]
    ends = doc_ends(info)
    first = info[0] * count
    seen = visible(ends, first, count)
    head = head_mask(ends, first, count)
    for hs in bunches(scores.shape[0]):
        wides = [feature(q[:, cols(h)].astype(F32)) for h in hs]
        fks = [feature(k[:, cols(h)].astype(F32)).astype(BF16) for h in hs]
        kept = [
            jnp.where(seen, mul(wide.astype(BF16), fk, NT), 0.0).astype(BF16)
            for wide, fk in zip(wides, fks)
        ]
        parts = [mul(s, v[:, cols(h)], NN) for h, s in zip(hs, kept)]
        heads = [jnp.where(head, wide, 0.0) for wide in wides]
        for h, s, p, f in zip(hs, kept, parts, heads):
            scores[h] = s
            part[:, cols(h)] = p
            head_fq[:, cols(h)] = f.astype(BF16)
            turned[h] = f.T.astype(BF16)


def norm_kernel(info, head_fq, turned, g, part, incoming, out, grad_att, state):
    weights = jnp.full((2 * DH, DH), 1.0 / DH, BF16)
    for hs in bunches(state.shape[0]):
        atts = [part[:, cols(h)] + mul(head_fq[:, cols(h)], incoming[h], NN) for h in hs]
        invs = [lax.rsqrt(row_mean(att * att, weights) + 1e-05) for att in atts]
        norms = [att * inv for att, inv in zip(atts, invs)]
        gos = [g[:, cols(h)].astype(F32) for h in hs]
        means = [row_mean(go * normed, weights) for go, normed in zip(gos, norms)]
        gas = [
            ((go - normed * m) * inv).astype(BF16)
            for go, normed, m, inv in zip(gos, norms, means, invs)
        ]
        sums = [mul(turned[h], ga, NN).astype(BF16) for h, ga in zip(hs, gas)]
        for h, normed, ga, value in zip(hs, norms, gas, sums):
            out[:, cols(h)] = normed.astype(BF16)
            grad_att[:, cols(h)] = ga
            state[h] = value


def inner_kernel(info, q, k, v, grad_att, incoming, scores, gq, gk, gv):
    count = q.shape[0]
    ends = doc_ends(info)
    first = info[0] * count
    seen = visible(ends, first, count)
    head = head_mask(ends, first, count)
    for hs in bunches(scores.shape[0]):
        wides = [q[:, cols(h)].astype(F32) for h in hs]
        fqs = [feature(wide).astype(BF16) for wide in wides]
        fks = [feature(k[:, cols(h)].astype(F32)).astype(BF16) for h in hs]
        gas = [grad_att[:, cols(h)] for h in hs]
        gss = [
            jnp.where(seen, mul(ga, v[:, cols(h)], NT), 0.0).astype(BF16)
            for h, ga in zip(hs, gas)
        ]
        totals = [
            mul(gs, fk, NN) + jnp.where(head, mul(ga, incoming[h], NT), 0.0)
            for h, gs, fk, ga in zip(hs, gss, fks, gas)
        ]
        gks = [mul(gs, fq, TN) for gs, fq in zip(gss, fqs)]
        gvs = [mul(scores[h], ga, TN) for h, ga in zip(hs, gas)]
        for h, total, wide, a, b in zip(hs, totals, wides, gks, gvs):
            gq[:, cols(h)] = (total * slope(wide)).astype(BF16)
            gk[:, cols(h)] = a
            gv[:, cols(h)] = b


def last_kernel(info, k, v, gk_part, gv_part, outgoing, gk, gv):
    count = k.shape[0]
    tail = tail_mask(doc_ends(info), info[0] * count, count)
    for hs in bunches(outgoing.shape[0]):
        wides = [k[:, cols(h)].astype(F32) for h in hs]
        fks = [jnp.where(tail, feature(wide), 0.0).astype(BF16) for wide in wides]
        vts = [jnp.where(tail, v[:, cols(h)].astype(F32), 0.0).astype(BF16) for h in hs]
        gks = [gk_part[:, cols(h)] + mul(vt, outgoing[h], NT) for h, vt in zip(hs, vts)]
        gvs = [gv_part[:, cols(h)] + mul(fk, outgoing[h], NN) for h, fk in zip(hs, fks)]
        for h, a, wide, b in zip(hs, gks, wides, gvs):
            gk[:, cols(h)] = (a * slope(wide)).astype(BF16)
            gv[:, cols(h)] = b.astype(BF16)


def same(a, b):
    return jnp.where(a == b, 1.0, 0.0).astype(F32)


def total_kernel(forward, count, info, held, total):
    members = held.shape[0]
    ends = doc_ends(info)
    layer = info[1] * (members * count)
    carry = None
    for step in range(members):
        i = step if forward else members - 1 - step
        mine = held[i].astype(F32)
        edge = layer + ((i + 1) * count - 1 if forward else i * count)
        here = doc_at(ends, edge)
        if carry is not None:
            mine = mine + carry * same(here, previous)
        carry, previous = mine, here
    total[...] = carry.astype(BF16)


def prefix_kernel(forward, count, info, held, *rest):
    others, out = rest[:-1], rest[-1]
    members = held.shape[0]
    span = members * count
    ends = doc_ends(info)
    layer = info[1] * span
    sign = -1 if forward else 1
    previous = doc_at(ends, layer - 1 if forward else layer + span)
    carry = None
    for s, other in enumerate(others):
        far = layer + sign * s * span
        there = doc_at(ends, far - 1 if forward else far + span)
        term = other[...].astype(F32) * same(there, previous)
        carry = term if carry is None else carry + term
    for step in range(members):
        i = step if forward else members - 1 - step
        near, far = layer + i * count, layer + (i + 1) * count - 1
        if not forward:
            near, far = far, near
        if carry is None:
            out[i] = jnp.zeros(out.shape[1:], BF16)
        else:
            out[i] = (carry * same(doc_at(ends, near), previous)).astype(BF16)
        if step < members - 1:
            here = doc_at(ends, far)
            mine = held[i].astype(F32)
            if carry is not None:
                mine = mine + carry * same(here, previous)
            carry, previous = mine, here


SMEM = pl.BlockSpec(memory_space=pltpu.SMEM)
PARAMS = pltpu.CompilerParams(dimension_semantics=("arbitrary",))


def local(queries, keys, values, out_grad, doc_lengths):
    count, width = queries.shape
    heads = width // DH
    layers = lax.axis_size("z")
    members = lax.axis_size("x") * lax.axis_size("head")
    owned = heads // members
    place = jnp.stack([lax.axis_index(("z", "x", "head")), lax.axis_index("z")])
    info = jnp.concatenate([place.astype(jnp.int32), doc_lengths])
    block_heads = 8 if heads % 8 == 0 else 1
    steps = heads // block_heads
    tokens = pl.BlockSpec((count, block_heads * DH), lambda i: (0, i))
    states = pl.BlockSpec((block_heads, DH, DH), lambda i: (i, 0, 0))
    tiles = pl.BlockSpec((block_heads, count, count), lambda i: (i, 0, 0))
    token_bf = jax.ShapeDtypeStruct((count, width), BF16)
    token_f32 = jax.ShapeDtypeStruct((count, width), F32)
    state_bf = jax.ShapeDtypeStruct((heads, DH, DH), BF16)
    tile_bf = jax.ShapeDtypeStruct((heads, count, count), BF16)

    def run(kernel, ins, outs, shapes, args, products, name):
        return pl.pallas_call(
            kernel,
            grid=(steps,),
            in_specs=[SMEM] + ins,
            out_specs=outs,
            out_shape=shapes,
            compiler_params=PARAMS,
            cost_estimate=pl.CostEstimate(
                flops=2 * products * heads * count * DH * DH,
                bytes_accessed=2 * (len(ins) + len(outs)) * count * width,
                transcendentals=count * width,
            ),
            name=name,
        )(info, *args)

    def combine(kernel, args, many, forward, name):
        group = pl.BlockSpec((members, None, DH, DH), lambda i: (0, i, 0, 0))
        single = pl.BlockSpec((None, DH, DH), lambda i: (i, 0, 0))
        return pl.pallas_call(
            functools.partial(kernel, forward, count),
            grid=(owned,),
            in_specs=[SMEM, group] + [single] * (len(args) - 1),
            out_specs=group if many else single,
            out_shape=jax.ShapeDtypeStruct(
                ((members,) if many else ()) + (owned, DH, DH), BF16
            ),
            compiler_params=PARAMS,
            cost_estimate=pl.CostEstimate(
                flops=4 * heads * DH * DH,
                bytes_accessed=4 * heads * DH * DH,
                transcendentals=0,
            ),
            name=name,
        )(info, *args)

    def scan(state, forward, name):
        held = lax.all_to_all(state, LAYER, split_axis=0, concat_axis=0, tiled=True)
        held = held.reshape(members, owned, DH, DH)
        others = []
        if layers > 1:
            total = combine(total_kernel, (held,), False, forward, name + "_total")
            for s in range(1, min(layers - 1, -(-layers // 2)) + 1):
                pairs = [(i, i + s) if forward else (i + s, i) for i in range(layers - s)]
                others.append(lax.ppermute(total, "z", pairs))
        sums = combine(prefix_kernel, (held, *others), True, forward, name + "_prefix")
        return lax.all_to_all(
            sums.reshape(heads, DH, DH), LAYER, split_axis=0, concat_axis=0, tiled=True
        )

    (tail,) = run(tail_kernel, [tokens] * 2, [states], [state_bf], (keys, values), 1, "tail")
    incoming = scan(tail, True, "carried")
    turned_bf = jax.ShapeDtypeStruct((heads, DH, count), BF16)
    turns = pl.BlockSpec((block_heads, DH, count), lambda i: (i, 0, 0))
    scores, part, head_fq, turned = run(
        local_kernel,
        [tokens] * 3,
        [tiles, tokens, tokens, turns],
        [tile_bf, token_f32, token_bf, turned_bf],
        (queries, keys, values),
        2,
        "within",
    )
    attn_out, grad_att, head_state = run(
        norm_kernel,
        [tokens, turns, tokens, tokens, states],
        [tokens, tokens, states],
        [token_bf, token_bf, state_bf],
        (head_fq, turned, out_grad, part, incoming),
        2,
        "normed",
    )
    outgoing = scan(head_state, False, "future")
    grad_queries, gk_part, gv_part = run(
        inner_kernel,
        [tokens] * 4 + [states, tiles],
        [tokens] * 3,
        [token_bf, token_f32, token_f32],
        (queries, keys, values, grad_att, incoming, scores),
        5,
        "grads_within",
    )
    grad_keys, grad_values = run(
        last_kernel,
        [tokens] * 4 + [states],
        [tokens] * 2,
        [token_bf, token_bf],
        (keys, values, gk_part, gv_part, outgoing),
        2,
        "grads_last",
    )
    return attn_out, grad_queries, grad_keys, grad_values


def solution(mesh):
    n_seq, n_head = mesh.shape["seq"], mesh.shape["head"]
    inner = next(n for n in (4, 2, 1) if n_seq % n == 0)
    fine = Mesh(mesh.devices.reshape(n_seq // inner, inner, n_head), ("z", "x", "head"))
    rows = P(("z", "x", "head"), None)
    return jax.shard_map(
        local,
        mesh=fine,
        in_specs=(rows, rows, rows, rows, P()),
        out_specs=(rows, rows, rows, rows),
        check_vma=False,
    )
```

```python
import functools

import jax
import jax.numpy as jnp
from jax import lax
from jax.experimental import pallas as pl
from jax.experimental.pallas import tpu as pltpu
from jax.sharding import Mesh, PartitionSpec as P

DH = 128
F32 = jnp.float32
BF16 = jnp.bfloat16
NN = (((1,), (0,)), ((), ()))
NT = (((1,), (1,)), ((), ()))
TN = (((0,), (0,)), ((), ()))
LAYER = ("x", "head")


def mul(a, b, dims):
    return lax.dot_general(a, b, dims, preferred_element_type=F32)


def feature(wide):
    return jnp.where(wide > 0, wide + 1.0, jnp.exp(jnp.minimum(wide, 0.0)))


def slope(wide):
    return jnp.where(wide > 0, 1.0, jnp.exp(jnp.minimum(wide, 0.0)))


def doc_ends(lens):
    ends, total = [], 0
    for j in range(lens.shape[0]):
        total = total + lens[j]
        ends.append(total)
    return ends


def doc_at(ends, where):
    found = 0
    for end in ends:
        found = found + jnp.where(where >= end, 1, 0)
    return found


def rows_of(ends, first, count):
    at = first + lax.broadcasted_iota(jnp.int32, (count, 1), 0)
    return doc_at(ends, at)


def columns_of(ends, first, count):
    at = first + lax.broadcasted_iota(jnp.int32, (1, count), 1)
    return doc_at(ends, at)


def visible(ends, first, count):
    later = lax.broadcasted_iota(jnp.int32, (count, count), 0)
    earlier = lax.broadcasted_iota(jnp.int32, (count, count), 1)
    return (later >= earlier) & (
        rows_of(ends, first, count) == columns_of(ends, first, count)
    )


def head_mask(ends, first, count):
    return rows_of(ends, first, count) == doc_at(ends, first)


def tail_mask(ends, first, count):
    return rows_of(ends, first, count) == doc_at(ends, first + count - 1)


def cols(h):
    return slice(h * DH, (h + 1) * DH)


def bunches(heads, size=4):
    return [range(h, min(h + size, heads)) for h in range(0, heads, size)]


def row_mean(wide, weights):
    return mul(wide.astype(BF16), weights, NN)


def tail_kernel(lens, place, k, v, out):
    count = k.shape[0]
    tail = tail_mask(doc_ends(lens), place[0] * count, count)
    for hs in bunches(out.shape[0]):
        fks = [
            jnp.where(tail, feature(k[:, cols(h)].astype(F32)), 0.0).astype(BF16) for h in hs
        ]
        sums = [mul(fk, v[:, cols(h)], TN).astype(BF16) for h, fk in zip(hs, fks)]
        for h, value in zip(hs, sums):
            out[h] = value


def local_kernel(lens, place, q, k, v, scores, part, head_fq, turned):
    count = q.shape[0]
    ends = doc_ends(lens)
    first = place[0] * count
    seen = visible(ends, first, count)
    head = head_mask(ends, first, count)
    for hs in bunches(scores.shape[0]):
        wides = [feature(q[:, cols(h)].astype(F32)) for h in hs]
        fks = [feature(k[:, cols(h)].astype(F32)).astype(BF16) for h in hs]
        kept = [
            jnp.where(seen, mul(wide.astype(BF16), fk, NT), 0.0).astype(BF16)
            for wide, fk in zip(wides, fks)
        ]
        parts = [mul(s, v[:, cols(h)], NN) for h, s in zip(hs, kept)]
        heads = [jnp.where(head, wide, 0.0) for wide in wides]
        for h, s, p, f in zip(hs, kept, parts, heads):
            scores[h] = s
            part[:, cols(h)] = p
            head_fq[:, cols(h)] = f.astype(BF16)
            turned[h] = f.T.astype(BF16)


def norm_kernel(lens, place, head_fq, turned, g, part, incoming, out, grad_att, state):
    weights = jnp.full((DH, DH), 1.0 / DH, BF16)
    for hs in bunches(state.shape[0]):
        atts = [part[:, cols(h)] + mul(head_fq[:, cols(h)], incoming[h], NN) for h in hs]
        invs = [lax.rsqrt(row_mean(att * att, weights) + 1e-05) for att in atts]
        norms = [att * inv for att, inv in zip(atts, invs)]
        gos = [g[:, cols(h)].astype(F32) for h in hs]
        means = [row_mean(go * normed, weights) for go, normed in zip(gos, norms)]
        gas = [
            ((go - normed * m) * inv).astype(BF16)
            for go, normed, m, inv in zip(gos, norms, means, invs)
        ]
        sums = [mul(turned[h], ga, NN).astype(BF16) for h, ga in zip(hs, gas)]
        for h, normed, ga, value in zip(hs, norms, gas, sums):
            out[:, cols(h)] = normed.astype(BF16)
            grad_att[:, cols(h)] = ga
            state[h] = value


def inner_kernel(lens, place, q, k, v, grad_att, incoming, scores, gq, gk, gv):
    count = q.shape[0]
    ends = doc_ends(lens)
    first = place[0] * count
    seen = visible(ends, first, count)
    head = head_mask(ends, first, count)
    for hs in bunches(scores.shape[0]):
        wides = [q[:, cols(h)].astype(F32) for h in hs]
        fqs = [feature(wide).astype(BF16) for wide in wides]
        fks = [feature(k[:, cols(h)].astype(F32)).astype(BF16) for h in hs]
        gas = [grad_att[:, cols(h)] for h in hs]
        gss = [
            jnp.where(seen, mul(ga, v[:, cols(h)], NT), 0.0).astype(BF16)
            for h, ga in zip(hs, gas)
        ]
        totals = [
            mul(gs, fk, NN) + jnp.where(head, mul(ga, incoming[h], NT), 0.0)
            for h, gs, fk, ga in zip(hs, gss, fks, gas)
        ]
        gks = [mul(gs, fq, TN) for gs, fq in zip(gss, fqs)]
        gvs = [mul(scores[h], ga, TN) for h, ga in zip(hs, gas)]
        for h, total, wide, a, b in zip(hs, totals, wides, gks, gvs):
            gq[:, cols(h)] = (total * slope(wide)).astype(BF16)
            gk[:, cols(h)] = a
            gv[:, cols(h)] = b


def last_kernel(lens, place, k, v, gk_part, gv_part, outgoing, gk, gv):
    count = k.shape[0]
    tail = tail_mask(doc_ends(lens), place[0] * count, count)
    for hs in bunches(outgoing.shape[0]):
        wides = [k[:, cols(h)].astype(F32) for h in hs]
        fks = [jnp.where(tail, feature(wide), 0.0).astype(BF16) for wide in wides]
        vts = [jnp.where(tail, v[:, cols(h)].astype(F32), 0.0).astype(BF16) for h in hs]
        gks = [gk_part[:, cols(h)] + mul(vt, outgoing[h], NT) for h, vt in zip(hs, vts)]
        gvs = [gv_part[:, cols(h)] + mul(fk, outgoing[h], NN) for h, fk in zip(hs, fks)]
        for h, a, wide, b in zip(hs, gks, wides, gvs):
            gk[:, cols(h)] = (a * slope(wide)).astype(BF16)
            gv[:, cols(h)] = b.astype(BF16)


def same(a, b):
    return jnp.where(a == b, 1.0, 0.0).astype(F32)


def total_kernel(forward, count, lens, place, held, total):
    members = held.shape[0]
    ends = doc_ends(lens)
    layer = place[1] * (members * count)
    carry = None
    for step in range(members):
        i = step if forward else members - 1 - step
        mine = held[i].astype(F32)
        edge = layer + ((i + 1) * count - 1 if forward else i * count)
        here = doc_at(ends, edge)
        if carry is not None:
            mine = mine + carry * same(here, previous)
        carry, previous = mine, here
    total[...] = carry.astype(BF16)


def prefix_kernel(forward, count, lens, place, held, *rest):
    others, out = rest[:-1], rest[-1]
    members = held.shape[0]
    span = members * count
    ends = doc_ends(lens)
    layer = place[1] * span
    sign = -1 if forward else 1
    previous = doc_at(ends, layer - 1 if forward else layer + span)
    carry = None
    for s, other in enumerate(others):
        far = layer + sign * s * span
        there = doc_at(ends, far - 1 if forward else far + span)
        term = other[...].astype(F32) * same(there, previous)
        carry = term if carry is None else carry + term
    for step in range(members):
        i = step if forward else members - 1 - step
        near, far = layer + i * count, layer + (i + 1) * count - 1
        if not forward:
            near, far = far, near
        if carry is None:
            out[i] = jnp.zeros(out.shape[1:], BF16)
        else:
            out[i] = (carry * same(doc_at(ends, near), previous)).astype(BF16)
        if step < members - 1:
            here = doc_at(ends, far)
            mine = held[i].astype(F32)
            if carry is not None:
                mine = mine + carry * same(here, previous)
            carry, previous = mine, here


SMEM = pl.BlockSpec(memory_space=pltpu.SMEM)
SMALL = pltpu.CompilerParams(
    dimension_semantics=("arbitrary",), vmem_limit_bytes=16 * 1024 * 1024
)
LARGE = pltpu.CompilerParams(
    dimension_semantics=("arbitrary",), vmem_limit_bytes=60 * 1024 * 1024
)


def local(queries, keys, values, out_grad, doc_lengths):
    count, width = queries.shape
    heads = width // DH
    layers = lax.axis_size("z")
    members = lax.axis_size("x") * lax.axis_size("head")
    owned = heads // members
    place = jnp.stack(
        [lax.axis_index(("z", "x", "head")), lax.axis_index("z")]
    ).astype(jnp.int32)
    block_heads = 8 if heads % 8 == 0 else 1
    steps = heads // block_heads
    tokens = pl.BlockSpec((count, block_heads * DH), lambda i: (0, i))
    states = pl.BlockSpec((block_heads, DH, DH), lambda i: (i, 0, 0))
    tiles = pl.BlockSpec((block_heads, count, count), lambda i: (i, 0, 0))
    token_bf = jax.ShapeDtypeStruct((count, width), BF16)
    token_f32 = jax.ShapeDtypeStruct((count, width), F32)
    state_bf = jax.ShapeDtypeStruct((heads, DH, DH), BF16)
    tile_bf = jax.ShapeDtypeStruct((heads, count, count), BF16)

    def run(kernel, ins, outs, shapes, args, products, name, params=SMALL):
        return pl.pallas_call(
            kernel,
            grid=(steps,),
            in_specs=[SMEM, SMEM] + ins,
            out_specs=outs,
            out_shape=shapes,
            compiler_params=params,
            cost_estimate=pl.CostEstimate(
                flops=2 * products * heads * count * DH * DH,
                bytes_accessed=2 * (len(ins) + len(outs)) * count * width,
                transcendentals=count * width,
            ),
            name=name,
        )(doc_lengths, place, *args)

    def combine(kernel, args, many, forward, name):
        group = pl.BlockSpec((members, None, DH, DH), lambda i: (0, i, 0, 0))
        single = pl.BlockSpec((None, DH, DH), lambda i: (i, 0, 0))
        return pl.pallas_call(
            functools.partial(kernel, forward, count),
            grid=(owned,),
            in_specs=[SMEM, SMEM, group] + [single] * (len(args) - 1),
            out_specs=group if many else single,
            out_shape=jax.ShapeDtypeStruct(
                ((members,) if many else ()) + (owned, DH, DH), BF16
            ),
            compiler_params=SMALL,
            cost_estimate=pl.CostEstimate(
                flops=4 * heads * DH * DH,
                bytes_accessed=4 * heads * DH * DH,
                transcendentals=0,
            ),
            name=name,
        )(doc_lengths, place, *args)

    def scan(state, forward, name):
        held = lax.all_to_all(state, LAYER, split_axis=0, concat_axis=0, tiled=True)
        held = held.reshape(members, owned, DH, DH)
        others = []
        if layers > 1:
            total = combine(total_kernel, (held,), False, forward, name + "_total")
            for s in range(1, min(layers - 1, -(-layers // 2)) + 1):
                pairs = [(i, i + s) if forward else (i + s, i) for i in range(layers - s)]
                others.append(lax.ppermute(total, "z", pairs))
        sums = combine(prefix_kernel, (held, *others), True, forward, name + "_prefix")
        return lax.all_to_all(
            sums.reshape(heads, DH, DH), LAYER, split_axis=0, concat_axis=0, tiled=True
        )

    (tail,) = run(tail_kernel, [tokens] * 2, [states], [state_bf], (keys, values), 1, "tail", LARGE)
    incoming = scan(tail, True, "carried")
    turned_bf = jax.ShapeDtypeStruct((heads, DH, count), BF16)
    turns = pl.BlockSpec((block_heads, DH, count), lambda i: (i, 0, 0))
    scores, part, head_fq, turned = run(
        local_kernel,
        [tokens] * 3,
        [tiles, tokens, tokens, turns],
        [tile_bf, token_f32, token_bf, turned_bf],
        (queries, keys, values),
        2,
        "within",
    )
    attn_out, grad_att, head_state = run(
        norm_kernel,
        [tokens, turns, tokens, tokens, states],
        [tokens, tokens, states],
        [token_bf, token_bf, state_bf],
        (head_fq, turned, out_grad, part, incoming),
        2,
        "normed",
    )
    outgoing = scan(head_state, False, "future")
    grad_queries, gk_part, gv_part = run(
        inner_kernel,
        [tokens] * 4 + [states, tiles],
        [tokens] * 3,
        [token_bf, token_f32, token_f32],
        (queries, keys, values, grad_att, incoming, scores),
        5,
        "grads_within",
    )
    grad_keys, grad_values = run(
        last_kernel,
        [tokens] * 4 + [states],
        [tokens] * 2,
        [token_bf, token_bf],
        (keys, values, gk_part, gv_part, outgoing),
        2,
        "grads_last",
    )
    return attn_out, grad_queries, grad_keys, grad_values


def solution(mesh):
    n_seq, n_head = mesh.shape["seq"], mesh.shape["head"]
    inner = next(n for n in (2, 1) if n_seq % n == 0)
    fine = Mesh(mesh.devices.reshape(n_seq // inner, inner, n_head), ("z", "x", "head"))
    rows = P(("z", "x", "head"), None)
    return jax.shard_map(
        local,
        mesh=fine,
        in_specs=(rows, rows, rows, rows, P()),
        out_specs=(rows, rows, rows, rows),
        check_vma=False,
    )
```

```python
import functools

import jax
import jax.numpy as jnp
from jax import lax
from jax.experimental import pallas as pl
from jax.experimental.pallas import tpu as pltpu
from jax.sharding import Mesh, PartitionSpec as P

DH = 128
F32 = jnp.float32
BF16 = jnp.bfloat16
NN = (((1,), (0,)), ((), ()))
NT = (((1,), (1,)), ((), ()))
TN = (((0,), (0,)), ((), ()))
LAYER = ("x", "head")


def mul(a, b, dims):
    return lax.dot_general(a, b, dims, preferred_element_type=F32)


def feature(wide):
    return jnp.where(wide > 0, wide + 1.0, jnp.exp(jnp.minimum(wide, 0.0)))


def slope(wide):
    return jnp.where(wide > 0, 1.0, jnp.exp(jnp.minimum(wide, 0.0)))


def doc_ends(lens):
    ends, total = [], 0
    for j in range(lens.shape[0]):
        total = total + lens[j]
        ends.append(total)
    return ends


def doc_at(ends, where):
    found = 0
    for end in ends:
        found = found + jnp.where(where >= end, 1, 0)
    return found


def rows_of(ends, first, count):
    at = first + lax.broadcasted_iota(jnp.int32, (count, 1), 0)
    return doc_at(ends, at)


def columns_of(ends, first, count):
    at = first + lax.broadcasted_iota(jnp.int32, (1, count), 1)
    return doc_at(ends, at)


def visible(ends, first, count):
    later = lax.broadcasted_iota(jnp.int32, (count, count), 0)
    earlier = lax.broadcasted_iota(jnp.int32, (count, count), 1)
    return (later >= earlier) & (
        rows_of(ends, first, count) == columns_of(ends, first, count)
    )


def head_mask(ends, first, count):
    return rows_of(ends, first, count) == doc_at(ends, first)


def tail_mask(ends, first, count):
    return rows_of(ends, first, count) == doc_at(ends, first + count - 1)


def cols(h):
    return slice(h * DH, (h + 1) * DH)


def bunches(heads, size=8):
    return [range(h, min(h + size, heads)) for h in range(0, heads, size)]


def halves(wide):
    high = wide.astype(BF16)
    return jnp.concatenate([high, (wide - high.astype(F32)).astype(BF16)], axis=1)


def tail_kernel(lens, place, k, v, out):
    count = k.shape[0]
    tail = tail_mask(doc_ends(lens), place[0] * count, count)
    for hs in bunches(out.shape[0]):
        fks = [
            jnp.where(tail, feature(k[:, cols(h)].astype(F32)), 0.0).astype(BF16) for h in hs
        ]
        sums = [mul(fk, v[:, cols(h)], TN).astype(BF16) for h, fk in zip(hs, fks)]
        for h, value in zip(hs, sums):
            out[h] = value


def local_kernel(lens, place, q, k, v, scores, part, head_fq, turned):
    count = q.shape[0]
    ends = doc_ends(lens)
    first = place[0] * count
    seen = visible(ends, first, count)
    head = head_mask(ends, first, count)
    for hs in bunches(scores.shape[0]):
        wides = [feature(q[:, cols(h)].astype(F32)) for h in hs]
        fks = [feature(k[:, cols(h)].astype(F32)).astype(BF16) for h in hs]
        kept = [
            jnp.where(seen, mul(wide.astype(BF16), fk, NT), 0.0).astype(BF16)
            for wide, fk in zip(wides, fks)
        ]
        parts = [mul(s, v[:, cols(h)], NN) for h, s in zip(hs, kept)]
        heads = [jnp.where(head, wide, 0.0) for wide in wides]
        for h, s, p, f in zip(hs, kept, parts, heads):
            scores[h] = s
            part[:, cols(h)] = p
            head_fq[:, cols(h)] = f.astype(BF16)
            turned[h] = f.T.astype(BF16)


def norm_kernel(lens, place, head_fq, turned, g, part, incoming, out, grad_att, state):
    count = g.shape[0]
    weights = jnp.full((2 * DH, DH), 1.0 / DH, BF16)
    for hs in bunches(state.shape[0]):
        atts = [part[:, cols(h)] + mul(head_fq[:, cols(h)], incoming[h], NN) for h in hs]
        gos = [g[:, cols(h)].astype(F32) for h in hs]
        means = [
            mul(jnp.concatenate([halves(att * att), halves(go * att)], axis=0), weights, NN)
            for att, go in zip(atts, gos)
        ]
        invs = [lax.rsqrt(m[:count] + 1e-05) for m in means]
        norms = [att * inv for att, inv in zip(atts, invs)]
        gas = [
            ((go - normed * (m[count:] * inv)) * inv).astype(BF16)
            for go, normed, m, inv in zip(gos, norms, means, invs)
        ]
        sums = [mul(turned[h], ga, NN).astype(BF16) for h, ga in zip(hs, gas)]
        for h, normed, ga, value in zip(hs, norms, gas, sums):
            out[:, cols(h)] = normed.astype(BF16)
            grad_att[:, cols(h)] = ga
            state[h] = value


def inner_kernel(lens, place, q, k, v, grad_att, incoming, scores, gq, gk, gv):
    count = q.shape[0]
    ends = doc_ends(lens)
    first = place[0] * count
    seen = visible(ends, first, count)
    head = head_mask(ends, first, count)
    for hs in bunches(scores.shape[0]):
        wides = [q[:, cols(h)].astype(F32) for h in hs]
        fqs = [feature(wide).astype(BF16) for wide in wides]
        fks = [feature(k[:, cols(h)].astype(F32)).astype(BF16) for h in hs]
        gas = [grad_att[:, cols(h)] for h in hs]
        gss = [
            jnp.where(seen, mul(ga, v[:, cols(h)], NT), 0.0).astype(BF16)
            for h, ga in zip(hs, gas)
        ]
        totals = [
            mul(gs, fk, NN) + jnp.where(head, mul(ga, incoming[h], NT), 0.0)
            for h, gs, fk, ga in zip(hs, gss, fks, gas)
        ]
        gks = [mul(gs, fq, TN) for gs, fq in zip(gss, fqs)]
        gvs = [mul(scores[h], ga, TN) for h, ga in zip(hs, gas)]
        for h, total, wide, a, b in zip(hs, totals, wides, gks, gvs):
            gq[:, cols(h)] = (total * slope(wide)).astype(BF16)
            gk[:, cols(h)] = a
            gv[:, cols(h)] = b


def last_kernel(lens, place, k, v, gk_part, gv_part, outgoing, gk, gv):
    count = k.shape[0]
    tail = tail_mask(doc_ends(lens), place[0] * count, count)
    for hs in bunches(outgoing.shape[0]):
        wides = [k[:, cols(h)].astype(F32) for h in hs]
        fks = [jnp.where(tail, feature(wide), 0.0).astype(BF16) for wide in wides]
        vts = [jnp.where(tail, v[:, cols(h)].astype(F32), 0.0).astype(BF16) for h in hs]
        gks = [gk_part[:, cols(h)] + mul(vt, outgoing[h], NT) for h, vt in zip(hs, vts)]
        gvs = [gv_part[:, cols(h)] + mul(fk, outgoing[h], NN) for h, fk in zip(hs, fks)]
        for h, a, wide, b in zip(hs, gks, wides, gvs):
            gk[:, cols(h)] = (a * slope(wide)).astype(BF16)
            gv[:, cols(h)] = b.astype(BF16)


def same(a, b):
    return jnp.where(a == b, 1.0, 0.0).astype(F32)


def total_kernel(forward, count, lens, place, held, total):
    members = held.shape[0]
    ends = doc_ends(lens)
    layer = place[1] * (members * count)
    carry = None
    for step in range(members):
        i = step if forward else members - 1 - step
        mine = held[i].astype(F32)
        edge = layer + ((i + 1) * count - 1 if forward else i * count)
        here = doc_at(ends, edge)
        if carry is not None:
            mine = mine + carry * same(here, previous)
        carry, previous = mine, here
    total[...] = carry.astype(BF16)


def prefix_kernel(forward, count, lens, place, held, *rest):
    others, out = rest[:-1], rest[-1]
    members = held.shape[0]
    span = members * count
    ends = doc_ends(lens)
    layer = place[1] * span
    sign = -1 if forward else 1
    previous = doc_at(ends, layer - 1 if forward else layer + span)
    carry = None
    for s, other in enumerate(others):
        far = layer + sign * s * span
        there = doc_at(ends, far - 1 if forward else far + span)
        term = other[...].astype(F32) * same(there, previous)
        carry = term if carry is None else carry + term
    for step in range(members):
        i = step if forward else members - 1 - step
        near, far = layer + i * count, layer + (i + 1) * count - 1
        if not forward:
            near, far = far, near
        if carry is None:
            out[i] = jnp.zeros(out.shape[1:], BF16)
        else:
            out[i] = (carry * same(doc_at(ends, near), previous)).astype(BF16)
        if step < members - 1:
            here = doc_at(ends, far)
            mine = held[i].astype(F32)
            if carry is not None:
                mine = mine + carry * same(here, previous)
            carry, previous = mine, here


SMEM = pl.BlockSpec(memory_space=pltpu.SMEM)
SMALL = pltpu.CompilerParams(
    dimension_semantics=("arbitrary",), vmem_limit_bytes=24 * 1024 * 1024
)
LARGE = pltpu.CompilerParams(
    dimension_semantics=("arbitrary",), vmem_limit_bytes=60 * 1024 * 1024
)


def local(queries, keys, values, out_grad, doc_lengths):
    count, width = queries.shape
    heads = width // DH
    layers = lax.axis_size("z")
    members = lax.axis_size("x") * lax.axis_size("head")
    owned = heads // members
    place = jnp.stack(
        [lax.axis_index(("z", "x", "head")), lax.axis_index("z")]
    ).astype(jnp.int32)
    block_heads = 8 if heads % 8 == 0 else 1
    steps = heads // block_heads
    tokens = pl.BlockSpec((count, block_heads * DH), lambda i: (0, i))
    states = pl.BlockSpec((block_heads, DH, DH), lambda i: (i, 0, 0))
    tiles = pl.BlockSpec((block_heads, count, count), lambda i: (i, 0, 0))
    token_bf = pltpu.HBM((count, width), BF16)
    token_f32 = pltpu.HBM((count, width), F32)
    state_bf = jax.ShapeDtypeStruct((heads, DH, DH), BF16)
    tile_bf = pltpu.HBM((heads, count, count), BF16)

    def run(kernel, ins, outs, shapes, args, products, name, params=SMALL):
        args = [
            arg if spec is states else pltpu.with_memory_space_constraint(arg, pltpu.HBM)
            for spec, arg in zip(ins, args)
        ]
        return pl.pallas_call(
            kernel,
            grid=(steps,),
            in_specs=[SMEM, SMEM] + ins,
            out_specs=outs,
            out_shape=shapes,
            compiler_params=params,
            cost_estimate=pl.CostEstimate(
                flops=2 * products * heads * count * DH * DH,
                bytes_accessed=2 * (len(ins) + len(outs)) * count * width,
                transcendentals=count * width,
            ),
            name=name,
        )(doc_lengths, place, *args)

    def combine(kernel, args, many, forward, name):
        group = pl.BlockSpec((members, None, DH, DH), lambda i: (0, i, 0, 0))
        single = pl.BlockSpec((None, DH, DH), lambda i: (i, 0, 0))
        return pl.pallas_call(
            functools.partial(kernel, forward, count),
            grid=(owned,),
            in_specs=[SMEM, SMEM, group] + [single] * (len(args) - 1),
            out_specs=group if many else single,
            out_shape=(
                pltpu.HBM((members, owned, DH, DH), BF16)
                if many
                else jax.ShapeDtypeStruct((owned, DH, DH), BF16)
            ),
            compiler_params=SMALL,
            cost_estimate=pl.CostEstimate(
                flops=4 * heads * DH * DH,
                bytes_accessed=4 * heads * DH * DH,
                transcendentals=0,
            ),
            name=name,
        )(doc_lengths, place, *args)

    def scan(state, forward, name):
        held = lax.all_to_all(state, LAYER, split_axis=0, concat_axis=0, tiled=True)
        held = held.reshape(members, owned, DH, DH)
        others = []
        if layers > 1:
            total = combine(total_kernel, (held,), False, forward, name + "_total")
            for s in range(1, min(layers - 1, -(-layers // 2)) + 1):
                pairs = [(i, i + s) if forward else (i + s, i) for i in range(layers - s)]
                others.append(lax.ppermute(total, "z", pairs))
        sums = combine(prefix_kernel, (held, *others), True, forward, name + "_prefix")
        return lax.all_to_all(
            sums.reshape(heads, DH, DH), LAYER, split_axis=0, concat_axis=0, tiled=True
        )

    (tail,) = run(tail_kernel, [tokens] * 2, [states], [state_bf], (keys, values), 1, "tail", LARGE)
    incoming = scan(tail, True, "carried")
    turned_bf = pltpu.HBM((heads, DH, count), BF16)
    turns = pl.BlockSpec((block_heads, DH, count), lambda i: (i, 0, 0))
    scores, part, head_fq, turned = run(
        local_kernel,
        [tokens] * 3,
        [tiles, tokens, tokens, turns],
        [tile_bf, token_f32, token_bf, turned_bf],
        (queries, keys, values),
        2,
        "within",
    )
    attn_out, grad_att, head_state = run(
        norm_kernel,
        [tokens, turns, tokens, tokens, states],
        [tokens, tokens, states],
        [token_bf, token_bf, state_bf],
        (head_fq, turned, out_grad, part, incoming),
        2,
        "normed",
    )
    outgoing = scan(head_state, False, "future")
    grad_queries, gk_part, gv_part = run(
        inner_kernel,
        [tokens] * 4 + [states, tiles],
        [tokens] * 3,
        [token_bf, token_f32, token_f32],
        (queries, keys, values, grad_att, incoming, scores),
        5,
        "grads_within",
    )
    grad_keys, grad_values = run(
        last_kernel,
        [tokens] * 4 + [states],
        [tokens] * 2,
        [token_bf, token_bf],
        (keys, values, gk_part, gv_part, outgoing),
        2,
        "grads_last",
    )
    return attn_out, grad_queries, grad_keys, grad_values


def solution(mesh):
    n_seq, n_head = mesh.shape["seq"], mesh.shape["head"]
    inner = next(n for n in (2, 1) if n_seq % n == 0)
    fine = Mesh(mesh.devices.reshape(n_seq // inner, inner, n_head), ("z", "x", "head"))
    rows = P(("z", "x", "head"), None)
    return jax.shard_map(
        local,
        mesh=fine,
        in_specs=(rows, rows, rows, rows, P()),
        out_specs=(rows, rows, rows, rows),
        check_vma=False,
    )
```

```python
import functools

import jax
import jax.numpy as jnp
from jax import lax
from jax.experimental import pallas as pl
from jax.experimental.pallas import tpu as pltpu
from jax.sharding import Mesh, PartitionSpec as P

DH = 128
F32 = jnp.float32
BF16 = jnp.bfloat16
NN = (((1,), (0,)), ((), ()))
NT = (((1,), (1,)), ((), ()))
TN = (((0,), (0,)), ((), ()))
LAYER = ("x", "head")


def mul(a, b, dims):
    return lax.dot_general(a, b, dims, preferred_element_type=F32)


def feature(wide):
    return jnp.where(wide > 0, wide + 1.0, jnp.exp(jnp.minimum(wide, 0.0)))


def slope(wide):
    return jnp.where(wide > 0, 1.0, jnp.exp(jnp.minimum(wide, 0.0)))


def doc_ends(lens):
    ends, total = [], 0
    for j in range(lens.shape[0]):
        total = total + lens[j]
        ends.append(total)
    return ends


def doc_at(ends, where):
    found = 0
    for end in ends:
        found = found + jnp.where(where >= end, 1, 0)
    return found


def rows_of(ends, first, count):
    at = first + lax.broadcasted_iota(jnp.int32, (count, 1), 0)
    return doc_at(ends, at)


def columns_of(ends, first, count):
    at = first + lax.broadcasted_iota(jnp.int32, (1, count), 1)
    return doc_at(ends, at)


def visible(ends, first, count):
    later = lax.broadcasted_iota(jnp.int32, (count, count), 0)
    earlier = lax.broadcasted_iota(jnp.int32, (count, count), 1)
    return (later >= earlier) & (
        rows_of(ends, first, count) == columns_of(ends, first, count)
    )


def head_mask(ends, first, count):
    return rows_of(ends, first, count) == doc_at(ends, first)


def tail_mask(ends, first, count):
    return rows_of(ends, first, count) == doc_at(ends, first + count - 1)


def cols(h):
    return slice(h * DH, (h + 1) * DH)


def bunches(heads, size=8):
    return [range(h, min(h + size, heads)) for h in range(0, heads, size)]


def halves(wide):
    high = wide.astype(BF16)
    return jnp.concatenate([high, (wide - high.astype(F32)).astype(BF16)], axis=1)


def slot(place, n, owned):
    return pl.ds(((place[2] ^ n) >> 1) * owned, owned)


def tail_kernel(ns, lens, place, k, v, *rest):
    outs, kept = rest[:-1], rest[-1]
    count = k.shape[0]
    heads = k.shape[1] // DH
    step = pl.program_id(0)
    tail = tail_mask(doc_ends(lens), place[0] * count, count)
    for hs in bunches(heads):
        fks = [
            jnp.where(tail, feature(k[:, cols(h)].astype(F32)), 0.0).astype(BF16) for h in hs
        ]
        sums = [mul(fk, v[:, cols(h)], TN).astype(BF16) for h, fk in zip(hs, fks)]
        for h, value in zip(hs, sums):
            kept[step * heads + h] = value

    @pl.when(step == pl.num_programs(0) - 1)
    def _():
        for n, out in zip(ns, outs):
            out[...] = kept[slot(place, n, out.shape[0])]


def local_kernel(lens, place, q, k, v, scores, part, head_fq, turned):
    count = q.shape[0]
    ends = doc_ends(lens)
    first = place[0] * count
    seen = visible(ends, first, count)
    head = head_mask(ends, first, count)
    for hs in bunches(scores.shape[0]):
        wides = [feature(q[:, cols(h)].astype(F32)) for h in hs]
        fks = [feature(k[:, cols(h)].astype(F32)).astype(BF16) for h in hs]
        kept = [
            jnp.where(seen, mul(wide.astype(BF16), fk, NT), 0.0).astype(BF16)
            for wide, fk in zip(wides, fks)
        ]
        parts = [mul(s, v[:, cols(h)], NN) for h, s in zip(hs, kept)]
        heads = [jnp.where(head, wide, 0.0) for wide in wides]
        for h, s, p, f in zip(hs, kept, parts, heads):
            scores[h] = s
            part[:, cols(h)] = p
            head_fq[:, cols(h)] = f.astype(BF16)
            turned[h] = f.T.astype(BF16)


def norm_kernel(ns, filled, lens, place, head_fq, turned, g, part, *rest):
    size = len(ns)
    incoming, rest = rest[:size], rest[size + filled :]
    out, grad_att, outs, (came, kept) = rest[0], rest[1], rest[2:-2], rest[-2:]
    count = g.shape[0]
    heads = turned.shape[0]
    step = pl.program_id(0)

    @pl.when(step == 0)
    def _():
        for n, state in zip(ns, incoming):
            came[slot(place, n, state.shape[0])] = state[...]

    weights = jnp.full((2 * DH, DH), 1.0 / DH, BF16)
    for hs in bunches(heads):
        atts = [
            part[:, cols(h)] + mul(head_fq[:, cols(h)], came[step * heads + h], NN) for h in hs
        ]
        gos = [g[:, cols(h)].astype(F32) for h in hs]
        means = [
            mul(jnp.concatenate([halves(att * att), halves(go * att)], axis=0), weights, NN)
            for att, go in zip(atts, gos)
        ]
        invs = [lax.rsqrt(m[:count] + 1e-05) for m in means]
        norms = [att * inv for att, inv in zip(atts, invs)]
        gas = [
            ((go - normed * (m[count:] * inv)) * inv).astype(BF16)
            for go, normed, m, inv in zip(gos, norms, means, invs)
        ]
        sums = [mul(turned[h], ga, NN).astype(BF16) for h, ga in zip(hs, gas)]
        for h, normed, ga, value in zip(hs, norms, gas, sums):
            out[:, cols(h)] = normed.astype(BF16)
            grad_att[:, cols(h)] = ga
            kept[step * heads + h] = value

    @pl.when(step == pl.num_programs(0) - 1)
    def _():
        for n, state in zip(ns, outs):
            state[...] = kept[slot(place, n, state.shape[0])]


def inner_kernel(lens, place, q, k, v, grad_att, scores, *rest):
    states, (gq, gk, gv, came) = rest[:-4], rest[-4:]
    count = q.shape[0]
    heads = scores.shape[0]
    step = pl.program_id(0)

    @pl.when(step == 0)
    def _():
        for n, state in enumerate(states):
            owned = state.shape[0]
            owner = place[2] ^ n
            turn = (owner & 1) * (len(states) // 2) + (owner >> 1)
            came[pl.ds(turn * owned, owned)] = state[...]

    ends = doc_ends(lens)
    first = place[0] * count
    seen = visible(ends, first, count)
    head = head_mask(ends, first, count)
    for hs in bunches(scores.shape[0]):
        wides = [q[:, cols(h)].astype(F32) for h in hs]
        fqs = [feature(wide).astype(BF16) for wide in wides]
        fks = [feature(k[:, cols(h)].astype(F32)).astype(BF16) for h in hs]
        gas = [grad_att[:, cols(h)] for h in hs]
        gss = [
            jnp.where(seen, mul(ga, v[:, cols(h)], NT), 0.0).astype(BF16)
            for h, ga in zip(hs, gas)
        ]
        totals = [
            mul(gs, fk, NN) + jnp.where(head, mul(ga, came[step * heads + h], NT), 0.0)
            for h, gs, fk, ga in zip(hs, gss, fks, gas)
        ]
        gks = [mul(gs, fq, TN) for gs, fq in zip(gss, fqs)]
        gvs = [mul(scores[h], ga, TN) for h, ga in zip(hs, gas)]
        for h, total, wide, a, b in zip(hs, totals, wides, gks, gvs):
            gq[:, cols(h)] = (total * slope(wide)).astype(BF16)
            gk[:, cols(h)] = a
            gv[:, cols(h)] = b


def last_kernel(ns, filled, lens, place, k, v, gk_part, gv_part, *rest):
    size = len(ns)
    outgoing, (gk, gv, came) = rest[:size], rest[size + filled :]
    count = k.shape[0]
    heads = k.shape[1] // DH
    step = pl.program_id(0)

    @pl.when(step == 0)
    def _():
        for n, state in zip(ns, outgoing):
            came[slot(place, n, state.shape[0])] = state[...]

    tail = tail_mask(doc_ends(lens), place[0] * count, count)
    for hs in bunches(heads):
        wides = [k[:, cols(h)].astype(F32) for h in hs]
        fks = [jnp.where(tail, feature(wide), 0.0).astype(BF16) for wide in wides]
        vts = [jnp.where(tail, v[:, cols(h)].astype(F32), 0.0).astype(BF16) for h in hs]
        gks = [gk_part[:, cols(h)] + mul(vt, came[step * heads + h], NT) for h, vt in zip(hs, vts)]
        gvs = [gv_part[:, cols(h)] + mul(fk, came[step * heads + h], NN) for h, fk in zip(hs, fks)]
        for h, a, wide, b in zip(hs, gks, wides, gvs):
            gk[:, cols(h)] = (a * slope(wide)).astype(BF16)
            gv[:, cols(h)] = b.astype(BF16)


def same(a, b):
    return jnp.where(a == b, 1.0, 0.0).astype(F32)


def total_kernel(forward, count, lens, place, *rest):
    states, total, held = rest[:-2], rest[-2], rest[-1]
    members = len(states)
    for n, state in enumerate(states):
        held[place[2] ^ n] = state[...]
    ends = doc_ends(lens)
    layer = place[1] * (members * count)
    carry = None
    for step in range(members):
        i = step if forward else members - 1 - step
        mine = held[i].astype(F32)
        edge = layer + ((i + 1) * count - 1 if forward else i * count)
        here = doc_at(ends, edge)
        if carry is not None:
            mine = mine + carry * same(here, previous)
        carry, previous = mine, here
    total[...] = carry.astype(BF16)


def prefix_kernel(forward, count, members, lens, place, *rest):
    states, outs, (held, sums) = rest[:members], rest[-members - 2 : -2], rest[-2:]
    others = rest[members : -members - 2]
    for n, state in enumerate(states):
        held[place[2] ^ n] = state[...]
    span = members * count
    ends = doc_ends(lens)
    layer = place[1] * span
    sign = -1 if forward else 1
    previous = doc_at(ends, layer - 1 if forward else layer + span)
    carry = None
    for s, other in enumerate(others):
        far = layer + sign * s * span
        there = doc_at(ends, far - 1 if forward else far + span)
        term = other[...].astype(F32) * same(there, previous)
        carry = term if carry is None else carry + term
    for step in range(members):
        i = step if forward else members - 1 - step
        near, far = layer + i * count, layer + (i + 1) * count - 1
        if not forward:
            near, far = far, near
        if carry is None:
            sums[i] = jnp.zeros(sums.shape[1:], BF16)
        else:
            sums[i] = (carry * same(doc_at(ends, near), previous)).astype(BF16)
        if step < members - 1:
            here = doc_at(ends, far)
            mine = held[i].astype(F32)
            if carry is not None:
                mine = mine + carry * same(here, previous)
            carry, previous = mine, here
    for n, out in enumerate(outs):
        out[...] = sums[place[2] ^ n]


SMALL = pltpu.CompilerParams(
    dimension_semantics=("arbitrary",), vmem_limit_bytes=24 * 1024 * 1024
)
LARGE = pltpu.CompilerParams(
    dimension_semantics=("arbitrary",), vmem_limit_bytes=60 * 1024 * 1024
)


def local(queries, keys, values, out_grad, doc_lengths):
    count, width = queries.shape
    heads = width // DH
    layers = lax.axis_size("z")
    members = lax.axis_size("x") * lax.axis_size("head")
    owned = heads // members
    half = heads // 2
    reach = range(1, min(layers - 1, -(-layers // 2)) + 1)
    place = jnp.stack(
        [lax.axis_index(("z", "x", "head")), lax.axis_index("z"), lax.axis_index(LAYER)]
    ).astype(jnp.int32)
    same_core = [n for n in reversed(range(members)) if n % 2 == 0]
    other_core = [n for n in reversed(range(members)) if n % 2 == 1]
    step_heads = max(n for n in (8, 4, 2, 1) if half % n == 0)
    steps = half // step_heads

    def held_in_hbm(arg):
        return pltpu.with_memory_space_constraint(arg, pltpu.HBM)

    def at(parity):
        if parity is None:
            return lambda i, lens, place: i
        return lambda i, lens, place: ((place[2] & 1) ^ parity) * steps + i

    def tokens(parity):
        block = at(parity)
        return pl.BlockSpec((count, step_heads * DH), lambda *a: (0, block(*a)))

    def tiles(parity, rows, columns):
        block = at(parity)
        return pl.BlockSpec((step_heads, rows, columns), lambda *a: (block(*a), 0, 0))

    whole = pl.BlockSpec((owned, DH, DH), lambda *a: (0, 0, 0))
    untouched = pl.BlockSpec(memory_space=pl.ANY)
    token_bf = pltpu.HBM((count, width), BF16)
    token_f32 = pltpu.HBM((count, width), F32)
    tile_bf = pltpu.HBM((heads, count, count), BF16)
    turned_bf = pltpu.HBM((heads, DH, count), BF16)
    owned_bf = jax.ShapeDtypeStruct((owned, DH, DH), BF16)

    def run(kernel, grid, ins, outs, shapes, scratch, args, cost, name, params=SMALL, aliases={}):
        args = [
            arg if arg.shape == (owned, DH, DH) else held_in_hbm(arg) for arg in args
        ]
        flops, moved, exps = cost
        return pl.pallas_call(
            kernel,
            grid_spec=pltpu.PrefetchScalarGridSpec(
                num_scalar_prefetch=2,
                grid=(grid,),
                in_specs=ins,
                out_specs=outs,
                scratch_shapes=scratch,
            ),
            out_shape=shapes,
            input_output_aliases=aliases,
            compiler_params=params,
            cost_estimate=pl.CostEstimate(
                flops=flops, bytes_accessed=moved, transcendentals=exps
            ),
            name=name,
        )(doc_lengths, place, *args)

    product = 2 * half * count * DH * DH
    array = half * count * DH * 2
    half_states = pltpu.VMEM((half, DH, DH), BF16)
    all_states = pltpu.VMEM((heads, DH, DH), BF16)

    def exchange(states):
        pairs = {n: [(i, i ^ n) for i in range(members)] for n in states}
        return {
            n: state if n == 0 else lax.ppermute(state, LAYER, pairs[n])
            for n, state in states.items()
        }

    def scan(states, forward, name):
        block = 2 if owned % 2 == 0 else 1
        single = pl.BlockSpec((block, DH, DH), lambda i, *a: (i, 0, 0))
        buffer = pltpu.VMEM((members, block, DH, DH), BF16)
        came = exchange(states)
        came = [came[n] for n in range(members)]
        cost = (4 * heads * DH * DH, 4 * heads * DH * DH, 0)
        others = []
        if layers > 1:
            (total,) = run(
                functools.partial(total_kernel, forward, count),
                owned // block,
                [single] * members,
                [single],
                [owned_bf],
                [buffer],
                came,
                cost,
                name + "_total",
            )
            for s in reach:
                pairs = [(i, i + s) if forward else (i + s, i) for i in range(layers - s)]
                others.append(lax.ppermute(total, "z", pairs))
        sums = run(
            functools.partial(prefix_kernel, forward, count, members),
            owned // block,
            [single] * (members + len(others)),
            [single] * members,
            [owned_bf] * members,
            [buffer, buffer],
            came + others,
            cost,
            name + "_prefix",
        )
        return exchange({n: sums[n] for n in same_core + other_core})

    groups = ((0, same_core), (1, other_core))
    tail = {}
    for parity, ns in groups:
        outs = run(
            functools.partial(tail_kernel, ns),
            steps,
            [tokens(parity)] * 2,
            [whole] * len(ns),
            [owned_bf] * len(ns),
            [half_states],
            (keys, values),
            (product, 3 * array, half * count * DH),
            f"tail_{parity}",
            LARGE,
        )
        tail.update(zip(ns, outs))
    incoming = scan(tail, True, "carried")
    scores, part, head_fq, turned = run(
        local_kernel,
        2 * steps,
        [tokens(None)] * 3,
        [tiles(None, count, count), tokens(None), tokens(None), tiles(None, DH, count)],
        [tile_bf, token_f32, token_bf, turned_bf],
        [],
        (queries, keys, values),
        (4 * product, 16 * array, 4 * half * count * DH),
        "within",
    )
    head_state, made = {}, ()
    for parity, ns in groups:
        outs = run(
            functools.partial(norm_kernel, ns, len(made)),
            steps,
            [tokens(parity), tiles(parity, DH, count), tokens(parity), tokens(parity)]
            + [whole] * len(ns)
            + [untouched] * len(made),
            [tokens(parity)] * 2 + [whole] * len(ns),
            [token_bf] * 2 + [owned_bf] * len(ns),
            [half_states, half_states],
            (head_fq, turned, out_grad, part, *[incoming[n] for n in ns], *made),
            (4 * product, 9 * array, half * count * DH),
            f"normed_{parity}",
            aliases={6 + len(ns) + j: j for j in range(len(made))},
        )
        made = tuple(outs[:2])
        head_state.update(zip(ns, outs[2:]))
    attn_out, grad_att = made
    outgoing = scan(head_state, False, "future")
    grad_queries, gk_part, gv_part = run(
        inner_kernel,
        2 * steps,
        [tokens(None)] * 4 + [tiles(None, count, count)] + [whole] * members,
        [tokens(None)] * 3,
        [token_bf, token_f32, token_f32],
        [all_states],
        (queries, keys, values, grad_att, scores, *[incoming[n] for n in range(members)]),
        (10 * product, 22 * array, 4 * half * count * DH),
        "grads_within",
    )
    made = ()
    for parity, ns in groups:
        made = tuple(
            run(
                functools.partial(last_kernel, ns, len(made)),
                steps,
                [tokens(parity)] * 4 + [whole] * len(ns) + [untouched] * len(made),
                [tokens(parity)] * 2,
                [token_bf] * 2,
                [half_states],
                (keys, values, gk_part, gv_part, *[outgoing[n] for n in ns], *made),
                (2 * product, 9 * array, half * count * DH),
                f"grads_last_{parity}",
                aliases={6 + len(ns) + j: j for j in range(len(made))},
            )
        )
    return attn_out, grad_queries, *made


def solution(mesh):
    n_seq, n_head = mesh.shape["seq"], mesh.shape["head"]
    inner = 2 if n_seq % 2 == 0 else 1
    fine = Mesh(mesh.devices.reshape(n_seq // inner, inner, n_head), ("z", "x", "head"))
    rows = P(("z", "x", "head"), None)
    return jax.shard_map(
        local,
        mesh=fine,
        in_specs=(rows, rows, rows, rows, P()),
        out_specs=(rows, rows, rows, rows),
        check_vma=False,
    )
```

```python
import functools

import jax
import jax.numpy as jnp
from jax import lax
from jax.experimental import pallas as pl
from jax.experimental.pallas import tpu as pltpu
from jax.sharding import Mesh, PartitionSpec as P

DH = 128
F32 = jnp.float32
BF16 = jnp.bfloat16
NN = (((1,), (0,)), ((), ()))
NT = (((1,), (1,)), ((), ()))
LAYER = ("x", "head")


def mul(a, b, dims):
    return lax.dot_general(a, b, dims, preferred_element_type=F32)


def feature(wide):
    return jnp.where(wide > 0, wide + 1.0, jnp.exp(jnp.minimum(wide, 0.0)))


def slope(wide):
    return jnp.where(wide > 0, 1.0, jnp.exp(jnp.minimum(wide, 0.0)))


def doc_ends(lens):
    ends, total = [], 0
    for j in range(lens.shape[0]):
        total = total + lens[j]
        ends.append(total)
    return ends


def doc_at(ends, where):
    found = 0
    for end in ends:
        found = found + jnp.where(where >= end, 1, 0)
    return found


def rows_of(ends, first, count):
    at = first + lax.broadcasted_iota(jnp.int32, (count, 1), 0)
    return doc_at(ends, at)


def columns_of(ends, first, count):
    at = first + lax.broadcasted_iota(jnp.int32, (1, count), 1)
    return doc_at(ends, at)


def visible(ends, first, count):
    row = lax.broadcasted_iota(jnp.int32, (count, count), 0)
    column = lax.broadcasted_iota(jnp.int32, (count, count), 1)
    together = rows_of(ends, first, count) == columns_of(ends, first, count)
    return (row >= column) & together, (row <= column) & together


def identity(count):
    row = lax.broadcasted_iota(jnp.int32, (count, count), 0)
    column = lax.broadcasted_iota(jnp.int32, (count, count), 1)
    return jnp.where(row == column, 1.0, 0.0).astype(BF16)


def turn(array, eye):
    return mul(eye, array, NT).astype(BF16)


def head_mask(ends, first, count):
    return rows_of(ends, first, count) == doc_at(ends, first)


def tail_mask(ends, first, count):
    return rows_of(ends, first, count) == doc_at(ends, first + count - 1)


def cols(h):
    return slice(h * DH, (h + 1) * DH)


def bunches(heads, size=8):
    return [range(h, min(h + size, heads)) for h in range(0, heads, size)]


def halves(wide):
    high = wide.astype(BF16)
    return jnp.concatenate([high, (wide - high.astype(F32)).astype(BF16)], axis=1)


def slot(place, n, owned):
    return pl.ds(((place[2] ^ n) >> 1) * owned, owned)


def tail_kernel(ns, lens, place, k, v, *rest):
    outs, kept = rest[:-1], rest[-1]
    count = k.shape[0]
    heads = k.shape[1] // DH
    step = pl.program_id(0)
    tail = tail_mask(doc_ends(lens), place[0] * count, count)
    eye = identity(DH)
    for hs in bunches(heads):
        fks = [
            jnp.where(tail, feature(k[:, cols(h)].astype(F32)), 0.0).astype(BF16) for h in hs
        ]
        turned = [turn(fk, eye) for fk in fks]
        sums = [mul(fk, v[:, cols(h)], NN).astype(BF16) for h, fk in zip(hs, turned)]
        for h, value in zip(hs, sums):
            kept[step * heads + h] = value

    @pl.when(step == pl.num_programs(0) - 1)
    def _():
        for n, out in zip(ns, outs):
            out[...] = kept[slot(place, n, out.shape[0])]


def local_kernel(lens, place, q, k, v, scores, part, head_fq, turned):
    count = q.shape[0]
    ends = doc_ends(lens)
    first = place[0] * count
    seen, seeing = visible(ends, first, count)
    head = head_mask(ends, first, count)
    eye = identity(DH)
    for hs in bunches(scores.shape[0]):
        wides = [feature(q[:, cols(h)].astype(F32)) for h in hs]
        fqs = [wide.astype(BF16) for wide in wides]
        fks = [feature(k[:, cols(h)].astype(F32)).astype(BF16) for h in hs]
        kept = [
            jnp.where(seen, mul(fq, fk, NT), 0.0).astype(BF16) for fq, fk in zip(fqs, fks)
        ]
        flipped = [
            jnp.where(seeing, mul(fk, fq, NT), 0.0).astype(BF16) for fq, fk in zip(fqs, fks)
        ]
        parts = [mul(s, v[:, cols(h)], NN) for h, s in zip(hs, kept)]
        heads = [jnp.where(head, wide, 0.0).astype(BF16) for wide in wides]
        turns = [turn(f, eye) for f in heads]
        for h, s, p, f, t in zip(hs, flipped, parts, heads, turns):
            scores[h] = s
            part[:, cols(h)] = p
            head_fq[:, cols(h)] = f
            turned[h] = t


def norm_kernel(ns, filled, lens, place, head_fq, turned, g, part, *rest):
    size = len(ns)
    incoming, rest = rest[:size], rest[size + filled :]
    out, grad_att, outs, (came, kept) = rest[0], rest[1], rest[2:-2], rest[-2:]
    count = g.shape[0]
    heads = turned.shape[0]
    step = pl.program_id(0)

    @pl.when(step == 0)
    def _():
        for n, state in zip(ns, incoming):
            came[slot(place, n, state.shape[0])] = state[...]

    weights = jnp.full((2 * DH, DH), 1.0 / DH, BF16)
    for hs in bunches(heads):
        atts = [
            part[:, cols(h)] + mul(head_fq[:, cols(h)], came[step * heads + h], NN) for h in hs
        ]
        gos = [g[:, cols(h)].astype(F32) for h in hs]
        means = [
            mul(jnp.concatenate([halves(att * att), halves(go * att)], axis=0), weights, NN)
            for att, go in zip(atts, gos)
        ]
        invs = [lax.rsqrt(m[:count] + 1e-05) for m in means]
        norms = [att * inv for att, inv in zip(atts, invs)]
        gas = [
            ((go - normed * (m[count:] * inv)) * inv).astype(BF16)
            for go, normed, m, inv in zip(gos, norms, means, invs)
        ]
        sums = [mul(turned[h], ga, NN).astype(BF16) for h, ga in zip(hs, gas)]
        for h, normed, ga, value in zip(hs, norms, gas, sums):
            out[:, cols(h)] = normed.astype(BF16)
            grad_att[:, cols(h)] = ga
            kept[step * heads + h] = value

    @pl.when(step == pl.num_programs(0) - 1)
    def _():
        for n, state in zip(ns, outs):
            state[...] = kept[slot(place, n, state.shape[0])]


def inner_kernel(lens, place, q, k, v, grad_att, scores, *rest):
    states, (gq, gk, gv, came) = rest[:-4], rest[-4:]
    count = q.shape[0]
    heads = scores.shape[0]
    step = pl.program_id(0)

    @pl.when(step == 0)
    def _():
        for n, state in enumerate(states):
            owned = state.shape[0]
            owner = place[2] ^ n
            turn = (owner & 1) * (len(states) // 2) + (owner >> 1)
            came[pl.ds(turn * owned, owned)] = state[...]

    ends = doc_ends(lens)
    first = place[0] * count
    seen, seeing = visible(ends, first, count)
    head = head_mask(ends, first, count)
    for hs in bunches(scores.shape[0]):
        wides = [q[:, cols(h)].astype(F32) for h in hs]
        fqs = [feature(wide).astype(BF16) for wide in wides]
        fks = [feature(k[:, cols(h)].astype(F32)).astype(BF16) for h in hs]
        gas = [grad_att[:, cols(h)] for h in hs]
        gss = [
            jnp.where(seen, mul(ga, v[:, cols(h)], NT), 0.0).astype(BF16)
            for h, ga in zip(hs, gas)
        ]
        totals = [
            mul(gs, fk, NN) + jnp.where(head, mul(ga, came[step * heads + h], NT), 0.0)
            for h, gs, fk, ga in zip(hs, gss, fks, gas)
        ]
        flipped = [
            jnp.where(seeing, mul(v[:, cols(h)], ga, NT), 0.0).astype(BF16)
            for h, ga in zip(hs, gas)
        ]
        gks = [mul(gs, fq, NN) for gs, fq in zip(flipped, fqs)]
        gvs = [mul(scores[h], ga, NN) for h, ga in zip(hs, gas)]
        for h, total, wide, a, b in zip(hs, totals, wides, gks, gvs):
            gq[:, cols(h)] = (total * slope(wide)).astype(BF16)
            gk[:, cols(h)] = a
            gv[:, cols(h)] = b


def last_kernel(ns, filled, lens, place, k, v, gk_part, gv_part, *rest):
    size = len(ns)
    outgoing, (gk, gv, came) = rest[:size], rest[size + filled :]
    count = k.shape[0]
    heads = k.shape[1] // DH
    step = pl.program_id(0)

    @pl.when(step == 0)
    def _():
        for n, state in zip(ns, outgoing):
            came[slot(place, n, state.shape[0])] = state[...]

    tail = tail_mask(doc_ends(lens), place[0] * count, count)
    for hs in bunches(heads):
        wides = [k[:, cols(h)].astype(F32) for h in hs]
        fks = [jnp.where(tail, feature(wide), 0.0).astype(BF16) for wide in wides]
        vts = [jnp.where(tail, v[:, cols(h)].astype(F32), 0.0).astype(BF16) for h in hs]
        gks = [gk_part[:, cols(h)] + mul(vt, came[step * heads + h], NT) for h, vt in zip(hs, vts)]
        gvs = [gv_part[:, cols(h)] + mul(fk, came[step * heads + h], NN) for h, fk in zip(hs, fks)]
        for h, a, wide, b in zip(hs, gks, wides, gvs):
            gk[:, cols(h)] = (a * slope(wide)).astype(BF16)
            gv[:, cols(h)] = b.astype(BF16)


def same(a, b):
    return jnp.where(a == b, 1.0, 0.0).astype(F32)


def total_kernel(forward, count, lens, place, *rest):
    states, total, held = rest[:-2], rest[-2], rest[-1]
    members = len(states)
    for n, state in enumerate(states):
        held[place[2] ^ n] = state[...]
    ends = doc_ends(lens)
    layer = place[1] * (members * count)
    carry = None
    for step in range(members):
        i = step if forward else members - 1 - step
        mine = held[i].astype(F32)
        edge = layer + ((i + 1) * count - 1 if forward else i * count)
        here = doc_at(ends, edge)
        if carry is not None:
            mine = mine + carry * same(here, previous)
        carry, previous = mine, here
    total[...] = carry.astype(BF16)


def prefix_kernel(forward, count, members, lens, place, *rest):
    states, outs, (held, sums) = rest[:members], rest[-members - 2 : -2], rest[-2:]
    others = rest[members + 1 : -members - 2]
    for n, state in enumerate(states):
        held[place[2] ^ n] = state[...]
    span = members * count
    ends = doc_ends(lens)
    layer = place[1] * span
    sign = -1 if forward else 1
    previous = doc_at(ends, layer - 1 if forward else layer + span)
    carry = None
    for s, other in enumerate(others):
        far = layer + sign * s * span
        there = doc_at(ends, far - 1 if forward else far + span)
        term = other[...].astype(F32) * same(there, previous)
        carry = term if carry is None else carry + term
    for step in range(members):
        i = step if forward else members - 1 - step
        near, far = layer + i * count, layer + (i + 1) * count - 1
        if not forward:
            near, far = far, near
        if carry is None:
            sums[i] = jnp.zeros(sums.shape[1:], BF16)
        else:
            sums[i] = (carry * same(doc_at(ends, near), previous)).astype(BF16)
        if step < members - 1:
            here = doc_at(ends, far)
            mine = held[i].astype(F32)
            if carry is not None:
                mine = mine + carry * same(here, previous)
            carry, previous = mine, here
    for n, out in enumerate(outs):
        out[...] = sums[place[2] ^ n]


SMALL = pltpu.CompilerParams(
    dimension_semantics=("arbitrary",), vmem_limit_bytes=24 * 1024 * 1024
)

def local(queries, keys, values, out_grad, doc_lengths):
    count, width = queries.shape
    heads = width // DH
    layers = lax.axis_size("z")
    members = lax.axis_size("x") * lax.axis_size("head")
    owned = heads // members
    half = heads // 2
    reach = range(1, min(layers - 1, -(-layers // 2)) + 1)
    place = jnp.stack(
        [lax.axis_index(("z", "x", "head")), lax.axis_index("z"), lax.axis_index(LAYER)]
    ).astype(jnp.int32)
    same_core = [n for n in reversed(range(members)) if n % 2 == 0]
    other_core = [n for n in reversed(range(members)) if n % 2 == 1]
    step_heads = max(n for n in (8, 4, 2, 1) if half % n == 0)
    steps = half // step_heads

    def held_in_hbm(arg):
        return pltpu.with_memory_space_constraint(arg, pltpu.HBM)

    def at(parity):
        if parity is None:
            return lambda i, lens, place: i
        return lambda i, lens, place: ((place[2] & 1) ^ parity) * steps + i

    def tokens(parity):
        block = at(parity)
        return pl.BlockSpec((count, step_heads * DH), lambda *a: (0, block(*a)))

    def tiles(parity, rows, columns):
        block = at(parity)
        return pl.BlockSpec((step_heads, rows, columns), lambda *a: (block(*a), 0, 0))

    whole = pl.BlockSpec((owned, DH, DH), lambda *a: (0, 0, 0))
    untouched = pl.BlockSpec(memory_space=pl.ANY)
    token_bf = pltpu.HBM((count, width), BF16)
    token_f32 = pltpu.HBM((count, width), F32)
    tile_bf = pltpu.HBM((heads, count, count), BF16)
    turned_bf = pltpu.HBM((heads, DH, count), BF16)
    owned_bf = jax.ShapeDtypeStruct((owned, DH, DH), BF16)

    def run(kernel, grid, ins, outs, shapes, scratch, args, cost, name, params=SMALL, aliases={}):
        args = [
            arg if arg.shape == (owned, DH, DH) else held_in_hbm(arg) for arg in args
        ]
        flops, moved, exps = cost
        return pl.pallas_call(
            kernel,
            grid_spec=pltpu.PrefetchScalarGridSpec(
                num_scalar_prefetch=2,
                grid=(grid,),
                in_specs=ins,
                out_specs=outs,
                scratch_shapes=scratch,
            ),
            out_shape=shapes,
            input_output_aliases=aliases,
            compiler_params=params,
            cost_estimate=pl.CostEstimate(
                flops=flops, bytes_accessed=moved, transcendentals=exps
            ),
            name=name,
        )(doc_lengths, place, *args)

    product = 2 * half * count * DH * DH
    array = half * count * DH * 2
    half_states = pltpu.VMEM((half, DH, DH), BF16)
    all_states = pltpu.VMEM((heads, DH, DH), BF16)

    def exchange(states):
        pairs = {n: [(i, i ^ n) for i in range(members)] for n in states}
        return {
            n: state if n == 0 else lax.ppermute(state, LAYER, pairs[n])
            for n, state in states.items()
        }

    def gather(states, forward, name):
        came = exchange(states)
        came = [came[n] for n in range(members)]
        others = []
        if layers > 1:
            (total,) = run(
                functools.partial(total_kernel, forward, count),
                owned // block,
                [single] * members,
                [single],
                [owned_bf],
                [buffer],
                came,
                combining,
                name + "_total",
            )
            for s in reach:
                pairs = [(i, i + s) if forward else (i + s, i) for i in range(layers - s)]
                others.append(lax.ppermute(total, "z", pairs))
        return came, others

    def spread(came, others, after, forward, name):
        sums = run(
            functools.partial(prefix_kernel, forward, count, members),
            owned // block,
            [single] * members + [untouched] + [single] * len(others),
            [single] * members,
            [owned_bf] * members,
            [buffer, buffer],
            [*came, after, *others],
            combining,
            name + "_prefix",
        )
        return exchange({n: sums[n] for n in other_core + same_core})

    block = 2 if owned % 2 == 0 else 1
    single = pl.BlockSpec((block, DH, DH), lambda i, *a: (i, 0, 0))
    buffer = pltpu.VMEM((members, block, DH, DH), BF16)
    combining = (4 * heads * DH * DH, 4 * heads * DH * DH, 0)
    groups = ((1, other_core), (0, same_core))
    tail = {}
    for parity, ns in groups:
        outs = run(
            functools.partial(tail_kernel, ns),
            steps,
            [tokens(parity)] * 2,
            [whole] * len(ns),
            [owned_bf] * len(ns),
            [half_states],
            (keys, values),
            (product, 3 * array, half * count * DH),
            f"tail_{parity}",
        )
        tail.update(zip(ns, outs))
    came, others = gather(tail, True, "carried")
    scores, part, head_fq, turned = run(
        local_kernel,
        2 * steps,
        [tokens(None)] * 3,
        [tiles(None, count, count), tokens(None), tokens(None), tiles(None, DH, count)],
        [tile_bf, token_f32, token_bf, turned_bf],
        [],
        (queries, keys, values),
        (4 * product, 16 * array, 4 * half * count * DH),
        "within",
    )
    incoming = spread(came, others, part, True, "carried")
    head_state, made = {}, ()
    for parity, ns in groups:
        outs = run(
            functools.partial(norm_kernel, ns, len(made)),
            steps,
            [tokens(parity), tiles(parity, DH, count), tokens(parity), tokens(parity)]
            + [whole] * len(ns)
            + [untouched] * len(made),
            [tokens(parity)] * 2 + [whole] * len(ns),
            [token_bf] * 2 + [owned_bf] * len(ns),
            [half_states, half_states],
            (head_fq, turned, out_grad, part, *[incoming[n] for n in ns], *made),
            (4 * product, 9 * array, half * count * DH),
            f"normed_{parity}",
            aliases={6 + len(ns) + j: j for j in range(len(made))},
        )
        made = tuple(outs[:2])
        head_state.update(zip(ns, outs[2:]))
    attn_out, grad_att = made
    came, others = gather(head_state, False, "future")
    grad_queries, gk_part, gv_part = run(
        inner_kernel,
        2 * steps,
        [tokens(None)] * 4 + [tiles(None, count, count)] + [whole] * members,
        [tokens(None)] * 3,
        [token_bf, token_f32, token_f32],
        [all_states],
        (queries, keys, values, grad_att, scores, *[incoming[n] for n in range(members)]),
        (10 * product, 22 * array, 4 * half * count * DH),
        "grads_within",
    )
    outgoing = spread(came, others, gk_part, False, "future")
    made = ()
    for parity, ns in groups:
        made = tuple(
            run(
                functools.partial(last_kernel, ns, len(made)),
                steps,
                [tokens(parity)] * 4 + [whole] * len(ns) + [untouched] * len(made),
                [tokens(parity)] * 2,
                [token_bf] * 2,
                [half_states],
                (keys, values, gk_part, gv_part, *[outgoing[n] for n in ns], *made),
                (2 * product, 9 * array, half * count * DH),
                f"grads_last_{parity}",
                aliases={6 + len(ns) + j: j for j in range(len(made))},
            )
        )
    return attn_out, grad_queries, *made


def solution(mesh):
    n_seq, n_head = mesh.shape["seq"], mesh.shape["head"]
    inner = 2 if n_seq % 2 == 0 else 1
    fine = Mesh(mesh.devices.reshape(n_seq // inner, inner, n_head), ("z", "x", "head"))
    rows = P(("z", "x", "head"), None)
    return jax.shard_map(
        local,
        mesh=fine,
        in_specs=(rows, rows, rows, rows, P()),
        out_specs=(rows, rows, rows, rows),
        check_vma=False,
    )
```

```python
import functools

import jax
import jax.numpy as jnp
from jax import lax
from jax.experimental import pallas as pl
from jax.experimental.pallas import tpu as pltpu
from jax.sharding import Mesh, PartitionSpec as P

DH = 128
F32 = jnp.float32
BF16 = jnp.bfloat16
NN = (((1,), (0,)), ((), ()))
NT = (((1,), (1,)), ((), ()))
LAYER = ("x", "head")


def mul(a, b, dims):
    return lax.dot_general(a, b, dims, preferred_element_type=F32)


def feature(wide):
    return jnp.where(wide > 0, wide + 1.0, jnp.exp(jnp.minimum(wide, 0.0)))


def slope(wide):
    return jnp.where(wide > 0, 1.0, jnp.exp(jnp.minimum(wide, 0.0)))


def doc_ends(lens):
    ends, total = [], 0
    for j in range(lens.shape[0]):
        total = total + lens[j]
        ends.append(total)
    return ends


def doc_at(ends, where):
    found = 0
    for end in ends:
        found = found + jnp.where(where >= end, 1, 0)
    return found


def rows_of(ends, first, count):
    at = first + lax.broadcasted_iota(jnp.int32, (count, 1), 0)
    return doc_at(ends, at)


def columns_of(ends, first, count):
    at = first + lax.broadcasted_iota(jnp.int32, (1, count), 1)
    return doc_at(ends, at)


def visible(ends, first, count):
    row = lax.broadcasted_iota(jnp.int32, (count, count), 0)
    column = lax.broadcasted_iota(jnp.int32, (count, count), 1)
    together = rows_of(ends, first, count) == columns_of(ends, first, count)
    return (row >= column) & together, (row <= column) & together


def identity(count):
    row = lax.broadcasted_iota(jnp.int32, (count, count), 0)
    column = lax.broadcasted_iota(jnp.int32, (count, count), 1)
    return jnp.where(row == column, 1.0, 0.0).astype(BF16)


def turn(array, eye):
    return mul(eye, array, NT).astype(BF16)


def head_mask(ends, first, count):
    return rows_of(ends, first, count) == doc_at(ends, first)


def tail_mask(ends, first, count):
    return rows_of(ends, first, count) == doc_at(ends, first + count - 1)


def cols(h):
    return slice(h * DH, (h + 1) * DH)


def bunches(heads, size=8):
    return [range(h, min(h + size, heads)) for h in range(0, heads, size)]


def halves(wide):
    high = wide.astype(BF16)
    return jnp.concatenate([high, (wide - high.astype(F32)).astype(BF16)], axis=1)


def tail_kernel(lens, place, k, v, out):
    count = k.shape[0]
    tail = tail_mask(doc_ends(lens), place[0] * count, count)
    eye = identity(DH)
    for hs in bunches(out.shape[0]):
        fks = [
            jnp.where(tail, feature(k[:, cols(h)].astype(F32)), 0.0).astype(BF16) for h in hs
        ]
        turned = [turn(fk, eye) for fk in fks]
        sums = [mul(fk, v[:, cols(h)], NN).astype(BF16) for h, fk in zip(hs, turned)]
        for h, value in zip(hs, sums):
            out[h] = value


def local_kernel(lens, place, q, k, v, scores, part, head_fq, turned):
    count = q.shape[0]
    ends = doc_ends(lens)
    first = place[0] * count
    seen, seeing = visible(ends, first, count)
    head = head_mask(ends, first, count)
    eye = identity(DH)
    for hs in bunches(scores.shape[0]):
        wides = [feature(q[:, cols(h)].astype(F32)) for h in hs]
        fqs = [wide.astype(BF16) for wide in wides]
        fks = [feature(k[:, cols(h)].astype(F32)).astype(BF16) for h in hs]
        kept = [
            jnp.where(seen, mul(fq, fk, NT), 0.0).astype(BF16) for fq, fk in zip(fqs, fks)
        ]
        flipped = [
            jnp.where(seeing, mul(fk, fq, NT), 0.0).astype(BF16) for fq, fk in zip(fqs, fks)
        ]
        parts = [mul(s, v[:, cols(h)], NN) for h, s in zip(hs, kept)]
        heads = [jnp.where(head, wide, 0.0).astype(BF16) for wide in wides]
        turns = [turn(f, eye) for f in heads]
        for h, s, p, f, t in zip(hs, flipped, parts, heads, turns):
            scores[h] = s
            part[:, cols(h)] = p
            head_fq[:, cols(h)] = f
            turned[h] = t


def norm_kernel(lens, place, head_fq, turned, g, part, incoming, *rest):
    out, grad_att, state = rest[-3:]
    count = g.shape[0]
    weights = jnp.full((2 * DH, DH), 1.0 / DH, BF16)
    for hs in bunches(state.shape[0]):
        atts = [part[:, cols(h)] + mul(head_fq[:, cols(h)], incoming[h], NN) for h in hs]
        gos = [g[:, cols(h)].astype(F32) for h in hs]
        means = [
            mul(jnp.concatenate([halves(att * att), halves(go * att)], axis=0), weights, NN)
            for att, go in zip(atts, gos)
        ]
        invs = [lax.rsqrt(m[:count] + 1e-05) for m in means]
        norms = [att * inv for att, inv in zip(atts, invs)]
        gas = [
            ((go - normed * (m[count:] * inv)) * inv).astype(BF16)
            for go, normed, m, inv in zip(gos, norms, means, invs)
        ]
        sums = [mul(turned[h], ga, NN).astype(BF16) for h, ga in zip(hs, gas)]
        for h, normed, ga, value in zip(hs, norms, gas, sums):
            out[:, cols(h)] = normed.astype(BF16)
            grad_att[:, cols(h)] = ga
            state[h] = value


def inner_kernel(lens, place, q, k, v, grad_att, scores, mine, other, gq, gk, gv, came):
    count = q.shape[0]
    heads = scores.shape[0]
    step = pl.program_id(0)

    @pl.when(step == 0)
    def _():
        half = mine.shape[0]
        core = place[2] & 1
        came[pl.ds(core * half, half)] = mine[...]
        came[pl.ds((1 - core) * half, half)] = other[...]

    ends = doc_ends(lens)
    first = place[0] * count
    seen, seeing = visible(ends, first, count)
    head = head_mask(ends, first, count)
    for hs in bunches(scores.shape[0]):
        wides = [q[:, cols(h)].astype(F32) for h in hs]
        fqs = [feature(wide).astype(BF16) for wide in wides]
        fks = [feature(k[:, cols(h)].astype(F32)).astype(BF16) for h in hs]
        gas = [grad_att[:, cols(h)] for h in hs]
        gss = [
            jnp.where(seen, mul(ga, v[:, cols(h)], NT), 0.0).astype(BF16)
            for h, ga in zip(hs, gas)
        ]
        totals = [
            mul(gs, fk, NN) + jnp.where(head, mul(ga, came[step * heads + h], NT), 0.0)
            for h, gs, fk, ga in zip(hs, gss, fks, gas)
        ]
        flipped = [
            jnp.where(seeing, mul(v[:, cols(h)], ga, NT), 0.0).astype(BF16)
            for h, ga in zip(hs, gas)
        ]
        gks = [mul(gs, fq, NN) for gs, fq in zip(flipped, fqs)]
        gvs = [mul(scores[h], ga, NN) for h, ga in zip(hs, gas)]
        for h, total, wide, a, b in zip(hs, totals, wides, gks, gvs):
            gq[:, cols(h)] = (total * slope(wide)).astype(BF16)
            gk[:, cols(h)] = a
            gv[:, cols(h)] = b


def last_kernel(lens, place, k, v, gk_part, gv_part, outgoing, *rest):
    gk, gv = rest[-2:]
    count = k.shape[0]
    tail = tail_mask(doc_ends(lens), place[0] * count, count)
    for hs in bunches(outgoing.shape[0]):
        wides = [k[:, cols(h)].astype(F32) for h in hs]
        fks = [jnp.where(tail, feature(wide), 0.0).astype(BF16) for wide in wides]
        vts = [jnp.where(tail, v[:, cols(h)].astype(F32), 0.0).astype(BF16) for h in hs]
        gks = [gk_part[:, cols(h)] + mul(vt, outgoing[h], NT) for h, vt in zip(hs, vts)]
        gvs = [gv_part[:, cols(h)] + mul(fk, outgoing[h], NN) for h, fk in zip(hs, fks)]
        for h, a, wide, b in zip(hs, gks, wides, gvs):
            gk[:, cols(h)] = (a * slope(wide)).astype(BF16)
            gv[:, cols(h)] = b.astype(BF16)


def same(a, b):
    return jnp.where(a == b, 1.0, 0.0).astype(F32)


def chip_docs(lens, place, count):
    ends = doc_ends(lens)
    core = place[2] & 1
    start = (place[0] - core) * count
    marks = (start, start + count - 1, start + count, start + 2 * count - 1)
    return core, [doc_at(ends, mark) for mark in marks]


def merge_kernel(forward, count, lens, place, mine, other, *outs):
    core, (early_b, early_e, late_b, late_e) = chip_docs(lens, place, count)
    far = same(early_e, late_e) if forward else same(early_b, late_b)
    i_am_far = (core == 0) if forward else (core == 1)
    mine_by = jnp.where(i_am_far, far, 1.0)
    other_by = jnp.where(i_am_far, 1.0, far)
    chip = place[2] >> 1
    for n, out in enumerate(outs):
        at = chip ^ n
        out[...] = (mine[at].astype(F32) * mine_by + other[at].astype(F32) * other_by).astype(
            BF16
        )


def form_kernel(forward, count, lens, place, *rest):
    came, (mine, other, own_in, mate_in) = rest[:-4], rest[-4:]
    core, (early_b, early_e, late_b, late_e) = chip_docs(lens, place, count)
    if forward:
        by_came, by_near, i_am_near = same(late_b, early_b), same(late_b, early_e), core == 1
    else:
        by_came, by_near, i_am_near = same(early_e, late_e), same(early_e, late_b), core == 0
    chip = place[2] >> 1
    for n, state in enumerate(came):
        at = chip ^ n
        total = state[...].astype(F32)
        near = jnp.where(i_am_near, other[at].astype(F32), mine[at].astype(F32))
        both = total * by_came + near * by_near
        own_in[at] = jnp.where(i_am_near, both, total).astype(BF16)
        mate_in[at] = jnp.where(i_am_near, total, both).astype(BF16)


def total_kernel(forward, unit, lens, place, *rest):
    states, total, held = rest[:-2], rest[-2], rest[-1]
    members = len(states)
    chip = place[2] >> 1
    for n, state in enumerate(states):
        held[chip ^ n] = state[...]
    ends = doc_ends(lens)
    layer = place[1] * (members * unit)
    carry = None
    for step in range(members):
        i = step if forward else members - 1 - step
        mine = held[i].astype(F32)
        edge = layer + ((i + 1) * unit - 1 if forward else i * unit)
        here = doc_at(ends, edge)
        if carry is not None:
            mine = mine + carry * same(here, previous)
        carry, previous = mine, here
    total[...] = carry.astype(BF16)


def prefix_kernel(forward, unit, members, lens, place, *rest):
    states, outs, (held, sums) = rest[:members], rest[-members - 2 : -2], rest[-2:]
    others = rest[members + 1 : -members - 2]
    chip = place[2] >> 1
    for n, state in enumerate(states):
        held[chip ^ n] = state[...]
    span = members * unit
    ends = doc_ends(lens)
    layer = place[1] * span
    sign = -1 if forward else 1
    previous = doc_at(ends, layer - 1 if forward else layer + span)
    carry = None
    for s, other in enumerate(others):
        far = layer + sign * s * span
        there = doc_at(ends, far - 1 if forward else far + span)
        term = other[...].astype(F32) * same(there, previous)
        carry = term if carry is None else carry + term
    for step in range(members):
        i = step if forward else members - 1 - step
        near, far = layer + i * unit, layer + (i + 1) * unit - 1
        if not forward:
            near, far = far, near
        if carry is None:
            sums[i] = jnp.zeros(sums.shape[1:], BF16)
        else:
            sums[i] = (carry * same(doc_at(ends, near), previous)).astype(BF16)
        if step < members - 1:
            here = doc_at(ends, far)
            mine = held[i].astype(F32)
            if carry is not None:
                mine = mine + carry * same(here, previous)
            carry, previous = mine, here
    for n, out in enumerate(outs):
        out[...] = sums[chip ^ n]


SMALL = pltpu.CompilerParams(
    dimension_semantics=("arbitrary",), vmem_limit_bytes=24 * 1024 * 1024
)

def local(queries, keys, values, out_grad, doc_lengths):
    count, width = queries.shape
    heads = width // DH
    layers = lax.axis_size("z")
    members = lax.axis_size("x") * lax.axis_size("head")
    owned = heads // members
    half = heads // 2
    reach = range(1, min(layers - 1, -(-layers // 2)) + 1)
    place = jnp.stack(
        [lax.axis_index(("z", "x", "head")), lax.axis_index("z"), lax.axis_index(LAYER)]
    ).astype(jnp.int32)
    chips = members // 2
    step_heads = max(n for n in (8, 4, 2, 1) if half % n == 0)
    steps = half // step_heads

    def held_in_hbm(arg):
        return pltpu.with_memory_space_constraint(arg, pltpu.HBM)

    def at(parity):
        if parity is None:
            return lambda i, lens, place: i
        return lambda i, lens, place: ((place[2] & 1) ^ parity) * steps + i

    def tokens(parity):
        block = at(parity)
        return pl.BlockSpec((count, step_heads * DH), lambda *a: (0, block(*a)))

    def tiles(parity, rows, columns):
        block = at(parity)
        return pl.BlockSpec((step_heads, rows, columns), lambda *a: (block(*a), 0, 0))

    whole = pl.BlockSpec((half, DH, DH), lambda *a: (0, 0, 0))
    halved = pl.BlockSpec((step_heads, DH, DH), lambda i, *a: (i, 0, 0))
    untouched = pl.BlockSpec(memory_space=pl.ANY)
    token_bf = pltpu.HBM((count, width), BF16)
    token_f32 = pltpu.HBM((count, width), F32)
    tile_bf = pltpu.HBM((heads, count, count), BF16)
    turned_bf = pltpu.HBM((heads, DH, count), BF16)
    owned_bf = jax.ShapeDtypeStruct((owned, DH, DH), BF16)
    half_bf = jax.ShapeDtypeStruct((half, DH, DH), BF16)
    chips_bf = jax.ShapeDtypeStruct((chips, owned, DH, DH), BF16)

    def run(kernel, grid, ins, outs, shapes, scratch, args, cost, name, params=SMALL, aliases={}):
        args = [
            arg if arg.shape[-2:] == (DH, DH) and arg.size <= half * DH * DH else held_in_hbm(arg)
            for arg in args
        ]
        flops, moved, exps = cost
        return pl.pallas_call(
            kernel,
            grid_spec=pltpu.PrefetchScalarGridSpec(
                num_scalar_prefetch=2,
                grid=(grid,),
                in_specs=ins,
                out_specs=outs,
                scratch_shapes=scratch,
            ),
            out_shape=shapes,
            input_output_aliases=aliases,
            compiler_params=params,
            cost_estimate=pl.CostEstimate(
                flops=flops, bytes_accessed=moved, transcendentals=exps
            ),
            name=name,
        )(doc_lengths, place, *args)

    product = 2 * half * count * DH * DH
    array = half * count * DH * 2
    all_states = pltpu.VMEM((heads, DH, DH), BF16)
    block = 2 if owned % 2 == 0 else 1
    single = pl.BlockSpec((block, DH, DH), lambda i, *a: (i, 0, 0))
    grouped = pl.BlockSpec((chips, block, DH, DH), lambda i, *a: (0, i, 0, 0))
    buffer = pltpu.VMEM((chips, block, DH, DH), BF16)
    combining = (4 * half * DH * DH, 4 * half * DH * DH, 0)
    moves = owned // block

    def swap(state):
        return lax.ppermute(state, LAYER, [(i, i ^ 1) for i in range(members)])

    def exchange(states):
        pairs = [[(i, i ^ (2 * n)) for i in range(members)] for n in range(chips)]
        return [
            state if n == 0 else lax.ppermute(state, LAYER, pairs[n])
            for n, state in enumerate(states)
        ]

    def gather(mine, theirs, forward, name):
        mine = mine.reshape(chips, owned, DH, DH)
        other = swap(theirs).reshape(chips, owned, DH, DH)
        merged = run(
            functools.partial(merge_kernel, forward, count),
            moves,
            [grouped] * 2,
            [single] * chips,
            [owned_bf] * chips,
            [],
            (mine, other),
            combining,
            name + "_chip",
        )
        came = exchange(merged)
        others = []
        if layers > 1:
            (total,) = run(
                functools.partial(total_kernel, forward, 2 * count),
                moves,
                [single] * chips,
                [single],
                [owned_bf],
                [buffer],
                came,
                combining,
                name + "_total",
            )
            for s in reach:
                pairs = [(i, i + s) if forward else (i + s, i) for i in range(layers - s)]
                others.append(lax.ppermute(total, "z", pairs))
        return mine, other, came, others

    def spread(mine, other, came, others, after, forward, name):
        sums = run(
            functools.partial(prefix_kernel, forward, 2 * count, chips),
            moves,
            [single] * chips + [untouched] + [single] * len(others),
            [single] * chips,
            [owned_bf] * chips,
            [buffer, buffer],
            [*came, after, *others],
            combining,
            name + "_prefix",
        )
        own_in, mate_in = run(
            functools.partial(form_kernel, forward, count),
            moves,
            [single] * chips + [grouped] * 2,
            [grouped] * 2,
            [chips_bf] * 2,
            [],
            [*exchange(sums), mine, other],
            combining,
            name + "_device",
        )
        return own_in.reshape(half, DH, DH), swap(mate_in.reshape(half, DH, DH))

    tail = [None, None]
    for parity in (1, 0):
        (tail[parity],) = run(
            tail_kernel,
            steps,
            [tokens(parity)] * 2,
            [halved],
            [half_bf],
            [],
            (keys, values),
            (product, 3 * array, half * count * DH),
            f"tail_{parity}",
        )
    scan = gather(*tail, True, "carried")
    scores, part, head_fq, turned = run(
        local_kernel,
        2 * steps,
        [tokens(None)] * 3,
        [tiles(None, count, count), tokens(None), tokens(None), tiles(None, DH, count)],
        [tile_bf, token_f32, token_bf, turned_bf],
        [],
        (queries, keys, values),
        (4 * product, 16 * array, 4 * half * count * DH),
        "within",
    )
    incoming = spread(*scan, part, True, "carried")
    head_state, made = [None, None], ()
    for parity in (0, 1):
        *made_now, head_state[parity] = run(
            norm_kernel,
            steps,
            [tokens(parity), tiles(parity, DH, count), tokens(parity), tokens(parity), halved]
            + [untouched] * len(made),
            [tokens(parity)] * 2 + [halved],
            [token_bf] * 2 + [half_bf],
            [],
            (head_fq, turned, out_grad, part, incoming[parity], *made),
            (4 * product, 9 * array, half * count * DH),
            f"normed_{parity}",
            aliases={7 + j: j for j in range(len(made))},
        )
        made = tuple(made_now)
    attn_out, grad_att = made
    scan = gather(*head_state, False, "future")
    grad_queries, gk_part, gv_part = run(
        inner_kernel,
        2 * steps,
        [tokens(None)] * 4 + [tiles(None, count, count)] + [whole] * 2,
        [tokens(None)] * 3,
        [token_bf, token_f32, token_f32],
        [all_states],
        (queries, keys, values, grad_att, scores, *incoming),
        (10 * product, 22 * array, 4 * half * count * DH),
        "grads_within",
    )
    outgoing = spread(*scan, gk_part, False, "future")
    made = ()
    for parity in (0, 1):
        made = tuple(
            run(
                last_kernel,
                steps,
                [tokens(parity)] * 4 + [halved] + [untouched] * len(made),
                [tokens(parity)] * 2,
                [token_bf] * 2,
                [],
                (keys, values, gk_part, gv_part, outgoing[parity], *made),
                (2 * product, 9 * array, half * count * DH),
                f"grads_last_{parity}",
                aliases={7 + j: j for j in range(len(made))},
            )
        )
    return attn_out, grad_queries, *made


def solution(mesh):
    n_seq, n_head = mesh.shape["seq"], mesh.shape["head"]
    inner = 2 if n_seq % 2 == 0 else 1
    fine = Mesh(mesh.devices.reshape(n_seq // inner, inner, n_head), ("z", "x", "head"))
    rows = P(("z", "x", "head"), None)
    return jax.shard_map(
        local,
        mesh=fine,
        in_specs=(rows, rows, rows, rows, P()),
        out_specs=(rows, rows, rows, rows),
        check_vma=False,
    )
```

```python
import functools

import jax
import jax.numpy as jnp
from jax import lax
from jax.experimental import pallas as pl
from jax.experimental.pallas import tpu as pltpu
from jax.sharding import Mesh, PartitionSpec as P

DH = 128
F32 = jnp.float32
BF16 = jnp.bfloat16
NN = (((1,), (0,)), ((), ()))
NT = (((1,), (1,)), ((), ()))
LAYER = ("x", "head")


def mul(a, b, dims):
    return lax.dot_general(a, b, dims, preferred_element_type=F32)


def feature(wide):
    return jnp.where(wide > 0, wide + 1.0, jnp.exp(jnp.minimum(wide, 0.0)))


def slope(wide):
    return jnp.where(wide > 0, 1.0, jnp.exp(jnp.minimum(wide, 0.0)))


def doc_ends(lens):
    ends, total = [], 0
    for j in range(lens.shape[0]):
        total = total + lens[j]
        ends.append(total)
    return ends


def doc_at(ends, where):
    found = 0
    for end in ends:
        found = found + jnp.where(where >= end, 1, 0)
    return found


def rows_of(ends, first, count):
    at = first + lax.broadcasted_iota(jnp.int32, (count, 1), 0)
    return doc_at(ends, at)


def columns_of(ends, first, count):
    at = first + lax.broadcasted_iota(jnp.int32, (1, count), 1)
    return doc_at(ends, at)


def visible(ends, first, count):
    row = lax.broadcasted_iota(jnp.int32, (count, count), 0)
    column = lax.broadcasted_iota(jnp.int32, (count, count), 1)
    together = rows_of(ends, first, count) == columns_of(ends, first, count)
    return (row >= column) & together, (row <= column) & together


def identity(count):
    row = lax.broadcasted_iota(jnp.int32, (count, count), 0)
    column = lax.broadcasted_iota(jnp.int32, (count, count), 1)
    return jnp.where(row == column, 1.0, 0.0).astype(BF16)


def turn(array, eye):
    return mul(eye, array, NT).astype(BF16)


def head_mask(ends, first, count):
    return rows_of(ends, first, count) == doc_at(ends, first)


def tail_mask(ends, first, count):
    return rows_of(ends, first, count) == doc_at(ends, first + count - 1)


def cols(h):
    return slice(h * DH, (h + 1) * DH)


def bunches(heads, size=8):
    return [range(h, min(h + size, heads)) for h in range(0, heads, size)]


def halves(wide):
    high = wide.astype(BF16)
    return jnp.concatenate([high, (wide - high.astype(F32)).astype(BF16)], axis=1)


def tail_kernel(lens, place, k, v, out):
    count = k.shape[0]
    tail = tail_mask(doc_ends(lens), place[0] * count, count)
    eye = identity(DH)
    for hs in bunches(out.shape[0]):
        fks = [
            jnp.where(tail, feature(k[:, cols(h)].astype(F32)), 0.0).astype(BF16) for h in hs
        ]
        turned = [turn(fk, eye) for fk in fks]
        sums = [mul(fk, v[:, cols(h)], NN).astype(BF16) for h, fk in zip(hs, turned)]
        for h, value in zip(hs, sums):
            out[h] = value


def local_kernel(lens, place, q, k, v, scores, part, head_fq, turned):
    count = q.shape[0]
    ends = doc_ends(lens)
    first = place[0] * count
    seen, seeing = visible(ends, first, count)
    head = head_mask(ends, first, count)
    eye = identity(DH)
    for hs in bunches(scores.shape[0]):
        wides = [feature(q[:, cols(h)].astype(F32)) for h in hs]
        fqs = [wide.astype(BF16) for wide in wides]
        fks = [feature(k[:, cols(h)].astype(F32)).astype(BF16) for h in hs]
        kept = [
            jnp.where(seen, mul(fq, fk, NT), 0.0).astype(BF16) for fq, fk in zip(fqs, fks)
        ]
        flipped = [
            jnp.where(seeing, mul(fk, fq, NT), 0.0).astype(BF16) for fq, fk in zip(fqs, fks)
        ]
        parts = [mul(s, v[:, cols(h)], NN) for h, s in zip(hs, kept)]
        heads = [jnp.where(head, wide, 0.0).astype(BF16) for wide in wides]
        turns = [turn(f, eye) for f in heads]
        for h, s, p, f, t in zip(hs, flipped, parts, heads, turns):
            scores[h] = s
            part[:, cols(h)] = p
            head_fq[:, cols(h)] = f
            turned[h] = t


def norm_kernel(lens, place, head_fq, turned, g, part, incoming, *rest):
    out, grad_att, state = rest[-3:]
    count = g.shape[0]
    weights = jnp.full((2 * DH, DH), 1.0 / DH, BF16)
    for hs in bunches(state.shape[0]):
        atts = [part[:, cols(h)] + mul(head_fq[:, cols(h)], incoming[h], NN) for h in hs]
        gos = [g[:, cols(h)].astype(F32) for h in hs]
        means = [
            mul(jnp.concatenate([halves(att * att), halves(go * att)], axis=0), weights, NN)
            for att, go in zip(atts, gos)
        ]
        invs = [lax.rsqrt(m[:count] + 1e-05) for m in means]
        norms = [att * inv for att, inv in zip(atts, invs)]
        gas = [
            ((go - normed * (m[count:] * inv)) * inv).astype(BF16)
            for go, normed, m, inv in zip(gos, norms, means, invs)
        ]
        sums = [mul(turned[h], ga, NN).astype(BF16) for h, ga in zip(hs, gas)]
        for h, normed, ga, value in zip(hs, norms, gas, sums):
            out[:, cols(h)] = normed.astype(BF16)
            grad_att[:, cols(h)] = ga
            state[h] = value


def inner_kernel(lens, place, q, k, v, grad_att, scores, mine, other, gq, gk, gv, came):
    count = q.shape[0]
    heads = scores.shape[0]
    step = pl.program_id(0)

    @pl.when(step == 0)
    def _():
        half = mine.shape[0]
        core = place[2] & 1
        came[pl.ds(core * half, half)] = mine[...]
        came[pl.ds((1 - core) * half, half)] = other[...]

    ends = doc_ends(lens)
    first = place[0] * count
    seen, seeing = visible(ends, first, count)
    head = head_mask(ends, first, count)
    for hs in bunches(scores.shape[0]):
        wides = [q[:, cols(h)].astype(F32) for h in hs]
        fqs = [feature(wide).astype(BF16) for wide in wides]
        fks = [feature(k[:, cols(h)].astype(F32)).astype(BF16) for h in hs]
        gas = [grad_att[:, cols(h)] for h in hs]
        gss = [
            jnp.where(seen, mul(ga, v[:, cols(h)], NT), 0.0).astype(BF16)
            for h, ga in zip(hs, gas)
        ]
        totals = [
            mul(gs, fk, NN) + jnp.where(head, mul(ga, came[step * heads + h], NT), 0.0)
            for h, gs, fk, ga in zip(hs, gss, fks, gas)
        ]
        flipped = [
            jnp.where(seeing, mul(v[:, cols(h)], ga, NT), 0.0).astype(BF16)
            for h, ga in zip(hs, gas)
        ]
        gks = [mul(gs, fq, NN) for gs, fq in zip(flipped, fqs)]
        gvs = [mul(scores[h], ga, NN) for h, ga in zip(hs, gas)]
        for h, total, wide, a, b in zip(hs, totals, wides, gks, gvs):
            gq[:, cols(h)] = (total * slope(wide)).astype(BF16)
            gk[:, cols(h)] = a
            gv[:, cols(h)] = b


def last_kernel(lens, place, k, v, gk_part, gv_part, outgoing, *rest):
    gk, gv = rest[-2:]
    count = k.shape[0]
    tail = tail_mask(doc_ends(lens), place[0] * count, count)
    for hs in bunches(outgoing.shape[0]):
        wides = [k[:, cols(h)].astype(F32) for h in hs]
        fks = [jnp.where(tail, feature(wide), 0.0).astype(BF16) for wide in wides]
        vts = [jnp.where(tail, v[:, cols(h)].astype(F32), 0.0).astype(BF16) for h in hs]
        gks = [gk_part[:, cols(h)] + mul(vt, outgoing[h], NT) for h, vt in zip(hs, vts)]
        gvs = [gv_part[:, cols(h)] + mul(fk, outgoing[h], NN) for h, fk in zip(hs, fks)]
        for h, a, wide, b in zip(hs, gks, wides, gvs):
            gk[:, cols(h)] = (a * slope(wide)).astype(BF16)
            gv[:, cols(h)] = b.astype(BF16)


def same(a, b):
    return jnp.where(a == b, 1.0, 0.0).astype(F32)


def chip_docs(lens, place, count):
    ends = doc_ends(lens)
    core = place[2] & 1
    start = (place[0] - core) * count
    marks = (start, start + count - 1, start + count, start + 2 * count - 1)
    return core, [doc_at(ends, mark) for mark in marks]


def merge_kernel(forward, count, lens, place, mine, other, *outs):
    core, (early_b, early_e, late_b, late_e) = chip_docs(lens, place, count)
    far = same(early_e, late_e) if forward else same(early_b, late_b)
    i_am_far = (core == 0) if forward else (core == 1)
    mine_by = jnp.where(i_am_far, far, 1.0)
    other_by = jnp.where(i_am_far, 1.0, far)
    chip = place[2] >> 1
    for n, out in enumerate(outs):
        at = chip ^ n
        out[...] = (mine[at].astype(F32) * mine_by + other[at].astype(F32) * other_by).astype(
            BF16
        )


def form_kernel(forward, count, lens, place, *rest):
    came, (mine, other, own_in, mate_in) = rest[:-4], rest[-4:]
    core, (early_b, early_e, late_b, late_e) = chip_docs(lens, place, count)
    if forward:
        by_came, by_near, i_am_near = same(late_b, early_b), same(late_b, early_e), core == 1
    else:
        by_came, by_near, i_am_near = same(early_e, late_e), same(early_e, late_b), core == 0
    chip = place[2] >> 1
    for n, state in enumerate(came):
        at = chip ^ n
        total = state[...].astype(F32)
        near = jnp.where(i_am_near, other[at].astype(F32), mine[at].astype(F32))
        both = total * by_came + near * by_near
        own_in[at] = jnp.where(i_am_near, both, total).astype(BF16)
        mate_in[at] = jnp.where(i_am_near, total, both).astype(BF16)


def total_kernel(forward, unit, lens, place, *rest):
    states, total, held = rest[:-2], rest[-2], rest[-1]
    members = len(states)
    chip = place[2] >> 1
    for n, state in enumerate(states):
        held[chip ^ n] = state[...]
    ends = doc_ends(lens)
    layer = place[1] * (members * unit)
    carry = None
    for step in range(members):
        i = step if forward else members - 1 - step
        mine = held[i].astype(F32)
        edge = layer + ((i + 1) * unit - 1 if forward else i * unit)
        here = doc_at(ends, edge)
        if carry is not None:
            mine = mine + carry * same(here, previous)
        carry, previous = mine, here
    total[...] = carry.astype(BF16)


def prefix_kernel(forward, unit, members, lens, place, *rest):
    states, outs, (held, sums) = rest[:members], rest[-members - 2 : -2], rest[-2:]
    others = rest[members + 1 : -members - 2]
    chip = place[2] >> 1
    for n, state in enumerate(states):
        held[chip ^ n] = state[...]
    span = members * unit
    ends = doc_ends(lens)
    layer = place[1] * span
    sign = -1 if forward else 1
    previous = doc_at(ends, layer - 1 if forward else layer + span)
    carry = None
    for s, other in enumerate(others):
        far = layer + sign * s * span
        there = doc_at(ends, far - 1 if forward else far + span)
        term = other[...].astype(F32) * same(there, previous)
        carry = term if carry is None else carry + term
    for step in range(members):
        i = step if forward else members - 1 - step
        near, far = layer + i * unit, layer + (i + 1) * unit - 1
        if not forward:
            near, far = far, near
        if carry is None:
            sums[i] = jnp.zeros(sums.shape[1:], BF16)
        else:
            sums[i] = (carry * same(doc_at(ends, near), previous)).astype(BF16)
        if step < members - 1:
            here = doc_at(ends, far)
            mine = held[i].astype(F32)
            if carry is not None:
                mine = mine + carry * same(here, previous)
            carry, previous = mine, here
    for n, out in enumerate(outs):
        out[...] = sums[chip ^ n]


SMALL = pltpu.CompilerParams(
    dimension_semantics=("arbitrary",), vmem_limit_bytes=16 * 1024 * 1024
)

def local(queries, keys, values, out_grad, doc_lengths):
    count, width = queries.shape
    heads = width // DH
    layers = lax.axis_size("z")
    members = lax.axis_size("x") * lax.axis_size("head")
    owned = heads // members
    half = heads // 2
    reach = range(1, min(layers - 1, -(-layers // 2)) + 1)
    place = jnp.stack(
        [lax.axis_index(("z", "x", "head")), lax.axis_index("z"), lax.axis_index(LAYER)]
    ).astype(jnp.int32)
    chips = members // 2
    step_heads = max(n for n in (8, 4, 2, 1) if half % n == 0)
    steps = half // step_heads

    def held_in_hbm(arg):
        return pltpu.with_memory_space_constraint(arg, pltpu.HBM)

    def at(parity):
        if parity is None:
            return lambda i, lens, place: i
        return lambda i, lens, place: ((place[2] & 1) ^ parity) * steps + i

    def tokens(parity):
        block = at(parity)
        return pl.BlockSpec((count, step_heads * DH), lambda *a: (0, block(*a)))

    def tiles(parity, rows, columns):
        block = at(parity)
        return pl.BlockSpec((step_heads, rows, columns), lambda *a: (block(*a), 0, 0))

    whole = pl.BlockSpec((half, DH, DH), lambda *a: (0, 0, 0))
    halved = pl.BlockSpec((step_heads, DH, DH), lambda i, *a: (i, 0, 0))
    untouched = pl.BlockSpec(memory_space=pl.ANY)
    token_bf = pltpu.HBM((count, width), BF16)
    inner_bf = jax.ShapeDtypeStruct((count, width), BF16)
    token_f32 = jax.ShapeDtypeStruct((count, width), F32)
    tile_bf = jax.ShapeDtypeStruct((heads, count, count), BF16)
    turned_bf = jax.ShapeDtypeStruct((heads, DH, count), BF16)
    owned_bf = jax.ShapeDtypeStruct((owned, DH, DH), BF16)
    half_bf = jax.ShapeDtypeStruct((half, DH, DH), BF16)
    chips_bf = jax.ShapeDtypeStruct((chips, owned, DH, DH), BF16)

    def run(kernel, grid, ins, outs, shapes, scratch, args, cost, name, params=SMALL, aliases={}):
        flops, moved, exps = cost
        return pl.pallas_call(
            kernel,
            grid_spec=pltpu.PrefetchScalarGridSpec(
                num_scalar_prefetch=2,
                grid=(grid,),
                in_specs=ins,
                out_specs=outs,
                scratch_shapes=scratch,
            ),
            out_shape=shapes,
            input_output_aliases=aliases,
            compiler_params=params,
            cost_estimate=pl.CostEstimate(
                flops=flops, bytes_accessed=moved, transcendentals=exps
            ),
            name=name,
        )(doc_lengths, place, *args)

    product = 2 * half * count * DH * DH
    array = half * count * DH * 2
    all_states = pltpu.VMEM((heads, DH, DH), BF16)
    block = 2 if owned % 2 == 0 else 1
    single = pl.BlockSpec((block, DH, DH), lambda i, *a: (i, 0, 0))
    grouped = pl.BlockSpec((chips, block, DH, DH), lambda i, *a: (0, i, 0, 0))
    buffer = pltpu.VMEM((chips, block, DH, DH), BF16)
    combining = (4 * half * DH * DH, 4 * half * DH * DH, 0)
    moves = owned // block

    def swap(state):
        return lax.ppermute(state, LAYER, [(i, i ^ 1) for i in range(members)])

    def exchange(states):
        pairs = [[(i, i ^ (2 * n)) for i in range(members)] for n in range(chips)]
        return [
            state if n == 0 else lax.ppermute(state, LAYER, pairs[n])
            for n, state in enumerate(states)
        ]

    def gather(mine, theirs, forward, name):
        mine = mine.reshape(chips, owned, DH, DH)
        other = swap(theirs).reshape(chips, owned, DH, DH)
        merged = run(
            functools.partial(merge_kernel, forward, count),
            moves,
            [grouped] * 2,
            [single] * chips,
            [owned_bf] * chips,
            [],
            (mine, other),
            combining,
            name + "_chip",
        )
        came = exchange(merged)
        others = []
        if layers > 1:
            (total,) = run(
                functools.partial(total_kernel, forward, 2 * count),
                moves,
                [single] * chips,
                [single],
                [owned_bf],
                [buffer],
                came,
                combining,
                name + "_total",
            )
            for s in reach:
                pairs = [(i, i + s) if forward else (i + s, i) for i in range(layers - s)]
                others.append(lax.ppermute(total, "z", pairs))
        return mine, other, came, others

    def spread(mine, other, came, others, after, forward, name):
        sums = run(
            functools.partial(prefix_kernel, forward, 2 * count, chips),
            moves,
            [single] * chips + [untouched] + [single] * len(others),
            [single] * chips,
            [owned_bf] * chips,
            [buffer, buffer],
            [*came, after, *others],
            combining,
            name + "_prefix",
        )
        own_in, mate_in = run(
            functools.partial(form_kernel, forward, count),
            moves,
            [single] * chips + [grouped] * 2,
            [grouped] * 2,
            [chips_bf] * 2,
            [],
            [*exchange(sums), mine, other],
            combining,
            name + "_device",
        )
        return own_in.reshape(half, DH, DH), swap(mate_in.reshape(half, DH, DH))

    tail = [None, None]
    for parity in (1, 0):
        (tail[parity],) = run(
            tail_kernel,
            steps,
            [tokens(parity)] * 2,
            [halved],
            [half_bf],
            [],
            (held_in_hbm(keys), held_in_hbm(values)),
            (product, 3 * array, half * count * DH),
            f"tail_{parity}",
        )
    scan = gather(*tail, True, "carried")
    scores, part, head_fq, turned = run(
        local_kernel,
        2 * steps,
        [tokens(None)] * 3,
        [tiles(None, count, count), tokens(None), tokens(None), tiles(None, DH, count)],
        [tile_bf, token_f32, inner_bf, turned_bf],
        [],
        (queries, keys, values),
        (4 * product, 16 * array, 4 * half * count * DH),
        "within",
    )
    incoming = spread(*scan, part, True, "carried")
    head_state, made = [None, None], ()
    for parity in (0, 1):
        *made_now, head_state[parity] = run(
            norm_kernel,
            steps,
            [tokens(parity), tiles(parity, DH, count), tokens(parity), tokens(parity), halved]
            + [untouched] * len(made),
            [tokens(parity)] * 2 + [halved],
            [token_bf, inner_bf, half_bf],
            [],
            (head_fq, turned, out_grad, part, incoming[parity], *made),
            (4 * product, 9 * array, half * count * DH),
            f"normed_{parity}",
            aliases={7 + j: j for j in range(len(made))},
        )
        made = tuple(made_now)
    attn_out, grad_att = made
    scan = gather(*head_state, False, "future")
    grad_queries, gk_part, gv_part = run(
        inner_kernel,
        2 * steps,
        [tokens(None)] * 4 + [tiles(None, count, count)] + [whole] * 2,
        [tokens(None)] * 3,
        [token_bf, token_f32, token_f32],
        [all_states],
        (queries, keys, values, grad_att, scores, *incoming),
        (10 * product, 22 * array, 4 * half * count * DH),
        "grads_within",
    )
    outgoing = spread(*scan, gk_part, False, "future")
    made = ()
    for parity in (0, 1):
        made = tuple(
            run(
                last_kernel,
                steps,
                [tokens(parity)] * 4 + [halved] + [untouched] * len(made),
                [tokens(parity)] * 2,
                [token_bf] * 2,
                [],
                (keys, values, gk_part, gv_part, outgoing[parity], *made),
                (2 * product, 9 * array, half * count * DH),
                f"grads_last_{parity}",
                aliases={7 + j: j for j in range(len(made))},
            )
        )
    return attn_out, grad_queries, *made


def solution(mesh):
    n_seq, n_head = mesh.shape["seq"], mesh.shape["head"]
    inner = 2 if n_seq % 2 == 0 else 1
    fine = Mesh(mesh.devices.reshape(n_seq // inner, inner, n_head), ("z", "x", "head"))
    rows = P(("z", "x", "head"), None)
    return jax.shard_map(
        local,
        mesh=fine,
        in_specs=(rows, rows, rows, rows, P()),
        out_specs=(rows, rows, rows, rows),
        check_vma=False,
    )
```

```python
import functools

import jax
import jax.numpy as jnp
from jax import lax
from jax.experimental import pallas as pl
from jax.experimental.pallas import tpu as pltpu
from jax.sharding import Mesh, PartitionSpec as P

DH = 128
F32 = jnp.float32
BF16 = jnp.bfloat16
NN = (((1,), (0,)), ((), ()))
NT = (((1,), (1,)), ((), ()))
LAYER = ("x", "head")


def mul(a, b, dims):
    return lax.dot_general(a, b, dims, preferred_element_type=F32)


def feature(wide):
    return jnp.where(wide > 0, wide + 1.0, jnp.exp(jnp.minimum(wide, 0.0)))


def slope(wide):
    return jnp.where(wide > 0, 1.0, jnp.exp(jnp.minimum(wide, 0.0)))


def doc_ends(lens):
    ends, total = [], 0
    for j in range(lens.shape[0]):
        total = total + lens[j]
        ends.append(total)
    return ends


def doc_at(ends, where):
    found = 0
    for end in ends:
        found = found + jnp.where(where >= end, 1, 0)
    return found


def rows_of(ends, first, count):
    at = first + lax.broadcasted_iota(jnp.int32, (count, 1), 0)
    return doc_at(ends, at)


def columns_of(ends, first, count):
    at = first + lax.broadcasted_iota(jnp.int32, (1, count), 1)
    return doc_at(ends, at)


def visible(ends, first, count):
    row = lax.broadcasted_iota(jnp.int32, (count, count), 0)
    column = lax.broadcasted_iota(jnp.int32, (count, count), 1)
    together = rows_of(ends, first, count) == columns_of(ends, first, count)
    return (row >= column) & together, (row <= column) & together


def identity(count):
    row = lax.broadcasted_iota(jnp.int32, (count, count), 0)
    column = lax.broadcasted_iota(jnp.int32, (count, count), 1)
    return jnp.where(row == column, 1.0, 0.0).astype(BF16)


def turn(array, eye):
    return mul(eye, array, NT).astype(BF16)


def head_mask(ends, first, count):
    return rows_of(ends, first, count) == doc_at(ends, first)


def tail_mask(ends, first, count):
    return rows_of(ends, first, count) == doc_at(ends, first + count - 1)


def cols(h):
    return slice(h * DH, (h + 1) * DH)


def bunches(heads, size=8):
    return [range(h, min(h + size, heads)) for h in range(0, heads, size)]


def halves(wide):
    high = wide.astype(BF16)
    return jnp.concatenate([high, (wide - high.astype(F32)).astype(BF16)], axis=1)


def tail_kernel(lens, place, k, v, *rest):
    if len(rest) > 1:
        q, g, out, three, last = rest
        three[0], three[1], three[2] = q[...], k[...], v[...]
        last[...] = g[...]
    else:
        (out,) = rest
    count = k.shape[0]
    tail = tail_mask(doc_ends(lens), place[0] * count, count)
    eye = identity(DH)
    for hs in bunches(out.shape[0]):
        fks = [
            jnp.where(tail, feature(k[:, cols(h)].astype(F32)), 0.0).astype(BF16) for h in hs
        ]
        turned = [turn(fk, eye) for fk in fks]
        sums = [mul(fk, v[:, cols(h)], NN).astype(BF16) for h, fk in zip(hs, turned)]
        for h, value in zip(hs, sums):
            out[h] = value


def pair_docs(lens, place, count):
    ends = doc_ends(lens)
    core = place[2] & 1
    own, mate = place[0] * count, (place[0] + 1 - 2 * core) * count

    def along(axis):
        shape = (2 * count, 1) if axis == 0 else (1, 2 * count)
        at = lax.broadcasted_iota(jnp.int32, shape, axis)
        return jnp.where(at < count, own + at, mate + at - count)

    rows, columns = along(0), along(1)
    row_docs, column_docs = doc_at(ends, rows), doc_at(ends, columns)
    seen = (rows >= columns) & (row_docs == column_docs)
    first = (place[0] - core) * count
    late = columns >= first + count
    return (
        seen,
        row_docs == doc_at(ends, first),
        column_docs == doc_at(ends, first),
        late & (column_docs == doc_at(ends, first + count)),
    )


def fill_kernel(lens, place, array, held, after, out):
    out[...] = array[...]


def chip_kernel(lens, place, q, k, v, mate, part, head_fq, turned):
    count = q.shape[0]
    seen, head, _, _ = pair_docs(lens, place, count)
    eye = identity(DH)

    def both(mine, slot, h):
        return jnp.concatenate([mine[:, cols(h)], mate[slot, :, cols(h)]], axis=0)

    for hs in bunches(turned.shape[0], 4):
        wides = [feature(both(q, 0, h).astype(F32)) for h in hs]
        fks = [feature(both(k, 1, h).astype(F32)).astype(BF16) for h in hs]
        kept = [
            jnp.where(seen, mul(wide.astype(BF16), fk, NT), 0.0).astype(BF16)
            for wide, fk in zip(wides, fks)
        ]
        parts = [mul(s, both(v, 2, h), NN) for h, s in zip(hs, kept)]
        heads = [jnp.where(head, wide, 0.0).astype(BF16) for wide in wides]
        turns = [turn(wide.astype(BF16), eye) for wide in wides]
        for h, p, f, t in zip(hs, parts, heads, turns):
            part[:, cols(h)] = p
            head_fq[:, cols(h)] = f
            turned[h] = t


def norm_kernel(lens, place, head_fq, turned, g, mate_g, part, *rest):
    kept = rest[-1]
    chips = (len(rest) - 7) // 2
    incoming, (out, mate_out, ga_out, mate_ga, came, lates) = (
        rest[:chips],
        rest[chips : chips + 6],
    )
    states = rest[chips + 6 : -1]
    count = g.shape[0]
    _, _, head, late = pair_docs(lens, place, count)
    heads = turned.shape[0]
    step = pl.program_id(0)
    chip = place[2] >> 1

    @pl.when(step == 0)
    def _():
        for n, state in enumerate(incoming):
            owned = state.shape[0]
            came[pl.ds((chip ^ n) * owned, owned)] = state[...]

    weights = jnp.full((2 * DH, DH), 1.0 / DH, BF16)
    for hs in bunches(heads, 4):
        atts = [
            part[:, cols(h)] + mul(head_fq[:, cols(h)], came[step * heads + h], NN) for h in hs
        ]
        gos = [
            jnp.concatenate([g[:, cols(h)], mate_g[:, cols(h)]], axis=0).astype(F32) for h in hs
        ]
        means = [
            mul(jnp.concatenate([halves(att * att), halves(go * att)], axis=0), weights, NN)
            for att, go in zip(atts, gos)
        ]
        invs = [lax.rsqrt(m[: 2 * count] + 1e-05) for m in means]
        norms = [att * inv for att, inv in zip(atts, invs)]
        gas = [
            ((go - normed * (m[2 * count :] * inv)) * inv).astype(BF16)
            for go, normed, m, inv in zip(gos, norms, means, invs)
        ]
        sums = []
        for h, ga in zip(hs, gas):
            wide = turned[h].astype(F32)
            two = jnp.concatenate([jnp.where(head, wide, 0.0), jnp.where(late, wide, 0.0)], axis=0)
            sums.append(mul(two.astype(BF16), ga, NN).astype(BF16))
        for h, normed, ga, value in zip(hs, norms, gas, sums):
            normed = normed.astype(BF16)
            out[:, cols(h)], mate_out[:, cols(h)] = normed[:count], normed[count:]
            ga_out[:, cols(h)], mate_ga[:, cols(h)] = ga[:count], ga[count:]
            kept[step * heads + h] = value[:DH]
            lates[h] = value[DH:]

    @pl.when(step == pl.num_programs(0) - 1)
    def _():
        for n, state in enumerate(states):
            owned = state.shape[0]
            state[...] = kept[pl.ds((chip ^ n) * owned, owned)]


def inner_kernel(lens, place, q, k, v, mine_ga, other_ga, *rest):
    passed, earlier, (gq, gk, gv, came) = rest[:2], rest[2:4], rest[5:]
    count = q.shape[0]
    heads = q.shape[1] // DH
    step = pl.program_id(0)
    own = step < pl.num_programs(0) // 2

    @pl.when(step == 0)
    def _():
        half = came.shape[0] // 2
        core, (early_b, early_e, late_b, late_e) = chip_docs(lens, place, count)
        by_chip = jnp.where(core == 0, 1.0, same(late_b, early_b))
        by_mate = jnp.where(core == 0, 0.0, same(late_b, early_e))
        for j in range(2):
            came[pl.ds(j * half, half)] = (
                passed[j][...].astype(F32) * by_chip + earlier[j][...].astype(F32) * by_mate
            ).astype(BF16)

    ends = doc_ends(lens)
    first = place[0] * count
    seen, seeing = visible(ends, first, count)
    head = head_mask(ends, first, count)
    for hs in bunches(heads):
        wides = [q[:, cols(h)].astype(F32) for h in hs]
        fqs = [feature(wide).astype(BF16) for wide in wides]
        fks = [feature(k[:, cols(h)].astype(F32)).astype(BF16) for h in hs]
        gas = [jnp.where(own, mine_ga[:, cols(h)], other_ga[:, cols(h)]) for h in hs]
        gss = [
            jnp.where(seen, mul(ga, v[:, cols(h)], NT), 0.0).astype(BF16)
            for h, ga in zip(hs, gas)
        ]
        totals = [
            mul(gs, fk, NN) + jnp.where(head, mul(ga, came[step * heads + h], NT), 0.0)
            for h, gs, fk, ga in zip(hs, gss, fks, gas)
        ]
        flipped = [
            jnp.where(seeing, mul(v[:, cols(h)], ga, NT), 0.0).astype(BF16)
            for h, ga in zip(hs, gas)
        ]
        scores = [
            jnp.where(seeing, mul(fk, fq, NT), 0.0).astype(BF16) for fq, fk in zip(fqs, fks)
        ]
        gks = [mul(gs, fq, NN) for gs, fq in zip(flipped, fqs)]
        gvs = [mul(s, ga, NN) for s, ga in zip(scores, gas)]
        for h, total, wide, a, b in zip(hs, totals, wides, gks, gvs):
            gq[:, cols(h)] = (total * slope(wide)).astype(BF16)
            gk[:, cols(h)] = a
            gv[:, cols(h)] = b


def last_kernel(chips, lens, place, k, v, gk_part, gv_part, late, *rest):
    gk, gv, came = rest[-3:]
    outgoing = rest[:chips]
    count = k.shape[0]
    heads = k.shape[1] // DH
    step = pl.program_id(0)

    @pl.when(step == 0)
    def _():
        core, (early_b, early_e, late_b, late_e) = chip_docs(lens, place, count)
        chip = place[2] >> 1
        by_far = jnp.where(core == 0, same(early_e, late_e), 1.0)
        by_late = jnp.where(core == 0, same(early_e, late_b), 0.0)
        for n, state in enumerate(outgoing):
            owned = state.shape[0]
            at = pl.ds((chip ^ n) * owned, owned)
            came[at] = (
                state[...].astype(F32) * by_far + late[at].astype(F32) * by_late
            ).astype(BF16)

    tail = tail_mask(doc_ends(lens), place[0] * count, count)
    for hs in bunches(heads):
        wides = [k[:, cols(h)].astype(F32) for h in hs]
        fks = [jnp.where(tail, feature(wide), 0.0).astype(BF16) for wide in wides]
        vts = [jnp.where(tail, v[:, cols(h)].astype(F32), 0.0).astype(BF16) for h in hs]
        states = [came[step * heads + h] for h in hs]
        gks = [gk_part[:, cols(h)] + mul(vt, o, NT) for h, vt, o in zip(hs, vts, states)]
        gvs = [gv_part[:, cols(h)] + mul(fk, o, NN) for h, fk, o in zip(hs, fks, states)]
        for h, a, wide, b in zip(hs, gks, wides, gvs):
            gk[:, cols(h)] = (a * slope(wide)).astype(BF16)
            gv[:, cols(h)] = b.astype(BF16)


def same(a, b):
    return jnp.where(a == b, 1.0, 0.0).astype(F32)


def chip_docs(lens, place, count):
    ends = doc_ends(lens)
    core = place[2] & 1
    start = (place[0] - core) * count
    marks = (start, start + count - 1, start + count, start + 2 * count - 1)
    return core, [doc_at(ends, mark) for mark in marks]


def merge_kernel(count, chips, lens, place, mine, other, *rest):
    outs = rest[-chips - 2 : -2]
    core, (early_b, early_e, late_b, late_e) = chip_docs(lens, place, count)
    far = same(early_e, late_e)
    mine_by = jnp.where(core == 0, far, 1.0)
    other_by = jnp.where(core == 0, 1.0, far)
    chip = place[2] >> 1
    for n, out in enumerate(outs):
        at = chip ^ n
        out[...] = (mine[at].astype(F32) * mine_by + other[at].astype(F32) * other_by).astype(
            BF16
        )


def total_kernel(forward, unit, members, passed, lens, place, *rest):
    states, total, held = rest[:members], rest[members + passed], rest[-1]
    chip = place[2] >> 1
    for n, state in enumerate(states):
        held[chip ^ n] = state[...]
    ends = doc_ends(lens)
    layer = place[1] * (members * unit)
    carry = None
    for step in range(members):
        i = step if forward else members - 1 - step
        mine = held[i].astype(F32)
        edge = layer + ((i + 1) * unit - 1 if forward else i * unit)
        here = doc_at(ends, edge)
        if carry is not None:
            mine = mine + carry * same(here, previous)
        carry, previous = mine, here
    total[...] = carry.astype(BF16)


def prefix_kernel(forward, unit, members, unread, lens, place, *rest):
    states, outs, (held, sums) = rest[:members], rest[-members - 2 : -2], rest[-2:]
    others = rest[members + unread : -members - 2]
    chip = place[2] >> 1
    for n, state in enumerate(states):
        held[chip ^ n] = state[...]
    span = members * unit
    ends = doc_ends(lens)
    layer = place[1] * span
    sign = -1 if forward else 1
    previous = doc_at(ends, layer - 1 if forward else layer + span)
    carry = None
    for s, other in enumerate(others):
        far = layer + sign * s * span
        there = doc_at(ends, far - 1 if forward else far + span)
        term = other[...].astype(F32) * same(there, previous)
        carry = term if carry is None else carry + term
    for step in range(members):
        i = step if forward else members - 1 - step
        near, far = layer + i * unit, layer + (i + 1) * unit - 1
        if not forward:
            near, far = far, near
        if carry is None:
            sums[i] = jnp.zeros(sums.shape[1:], BF16)
        else:
            sums[i] = (carry * same(doc_at(ends, near), previous)).astype(BF16)
        if step < members - 1:
            here = doc_at(ends, far)
            mine = held[i].astype(F32)
            if carry is not None:
                mine = mine + carry * same(here, previous)
            carry, previous = mine, here
    for n, out in enumerate(outs):
        out[...] = sums[chip ^ n]


SMALL = pltpu.CompilerParams(
    dimension_semantics=("arbitrary",), vmem_limit_bytes=16 * 1024 * 1024
)

def local(queries, keys, values, out_grad, doc_lengths):
    count, width = queries.shape
    heads = width // DH
    layers = lax.axis_size("z")
    members = lax.axis_size("x") * lax.axis_size("head")
    owned = heads // members
    half = heads // 2
    reach = range(1, min(layers - 1, -(-layers // 2)) + 1)
    place = jnp.stack(
        [lax.axis_index(("z", "x", "head")), lax.axis_index("z"), lax.axis_index(LAYER)]
    ).astype(jnp.int32)
    chips = members // 2
    step_heads = max(n for n in (8, 4, 2, 1) if half % n == 0)
    steps = half // step_heads

    def held_in_hbm(arg):
        return pltpu.with_memory_space_constraint(arg, pltpu.HBM)

    def at(parity):
        if parity is None:
            return lambda i, lens, place: i
        return lambda i, lens, place: ((place[2] & 1) ^ parity) * steps + i

    def tokens(parity):
        block = at(parity)
        return pl.BlockSpec((count, step_heads * DH), lambda *a: (0, block(*a)))

    whole = pl.BlockSpec((half, DH, DH), lambda *a: (0, 0, 0))
    halved = pl.BlockSpec((step_heads, DH, DH), lambda i, *a: (i, 0, 0))
    untouched = pl.BlockSpec(memory_space=pl.ANY)
    token_bf = pltpu.HBM((count, width), BF16)
    token_f32 = jax.ShapeDtypeStruct((count, width), F32)
    owned_bf = jax.ShapeDtypeStruct((owned, DH, DH), BF16)
    half_bf = jax.ShapeDtypeStruct((half, DH, DH), BF16)

    def run(kernel, grid, ins, outs, shapes, scratch, args, cost, name, params=SMALL, aliases={}):
        flops, moved, exps = cost
        return pl.pallas_call(
            kernel,
            grid_spec=pltpu.PrefetchScalarGridSpec(
                num_scalar_prefetch=2,
                grid=(grid,),
                in_specs=ins,
                out_specs=outs,
                scratch_shapes=scratch,
            ),
            out_shape=shapes,
            input_output_aliases=aliases,
            compiler_params=params,
            cost_estimate=pl.CostEstimate(
                flops=flops, bytes_accessed=moved, transcendentals=exps
            ),
            name=name,
        )(doc_lengths, place, *args)

    product = 2 * half * count * DH * DH
    array = half * count * DH * 2
    all_states = pltpu.VMEM((heads, DH, DH), BF16)
    block = 2 if owned % 2 == 0 else 1
    single = pl.BlockSpec((block, DH, DH), lambda i, *a: (i, 0, 0))
    grouped = pl.BlockSpec((chips, block, DH, DH), lambda i, *a: (0, i, 0, 0))
    buffer = pltpu.VMEM((chips, block, DH, DH), BF16)
    combining = (4 * half * DH * DH, 4 * half * DH * DH, 0)
    moves = owned // block

    def swap(state):
        return lax.ppermute(state, LAYER, [(i, i ^ 1) for i in range(members)])

    def exchange(states):
        pairs = [[(i, i ^ (2 * n)) for i in range(members)] for n in range(chips)]
        return [
            state if n == 0 else lax.ppermute(state, LAYER, pairs[n])
            for n, state in enumerate(states)
        ]

    def reach_out(merged, along, forward, name):
        came = exchange(merged)
        total, *along = run(
            functools.partial(total_kernel, forward, 2 * count, chips, len(along)),
            moves,
            [single] * chips + [untouched] * len(along),
            [single] + [untouched] * len(along),
            [owned_bf] + [jax.ShapeDtypeStruct(array.shape, array.dtype) for array in along],
            [buffer],
            [*came, *along],
            combining,
            name + "_total",
            aliases={2 + chips + j: 1 + j for j in range(len(along))},
        )
        others = []
        for s in reach:
            pairs = [(i, i + s) if forward else (i + s, i) for i in range(layers - s)]
            others.append(lax.ppermute(total, "z", pairs))
        return came, others, total, along

    def spread(came, others, after, forward, name):
        sums = run(
            functools.partial(prefix_kernel, forward, 2 * count, chips, len(after)),
            moves,
            [single] * chips + [untouched] * len(after) + [single] * len(others),
            [single] * chips,
            [owned_bf] * chips,
            [buffer, buffer],
            [*came, *after, *others],
            combining,
            name + "_prefix",
        )
        return exchange(sums)

    narrow = (count, half * DH)
    lane = pl.BlockSpec((count, step_heads * DH), lambda i, *a: (0, i))
    pinned = [held_in_hbm(array) for array in (queries, keys, values, out_grad)]
    tail_work = (product, 3 * array, half * count * DH)
    copies = [
        jax.ShapeDtypeStruct((3, *narrow), BF16),
        jax.ShapeDtypeStruct(narrow, BF16),
    ]
    mate_tail, mate_three, mate_g = run(
        tail_kernel,
        steps,
        [tokens(1)] * 4,
        [halved, pl.BlockSpec((3, count, step_heads * DH), lambda i, *a: (0, 0, i)), lane],
        [half_bf, *copies],
        [],
        (pinned[1], pinned[2], pinned[0], pinned[3]),
        tail_work,
        "tail_mate",
    )
    (own_tail,) = run(
        tail_kernel,
        steps,
        [tokens(0)] * 2,
        [halved],
        [half_bf],
        [],
        pinned[1:3],
        tail_work,
        "tail_own",
    )
    mine = own_tail.reshape(chips, owned, DH, DH)
    other = swap(mate_tail).reshape(chips, owned, DH, DH)
    *merged, mate_three, mate_g = run(
        functools.partial(merge_kernel, count, chips),
        moves,
        [grouped] * 2 + [untouched] * 2,
        [single] * chips + [untouched] * 2,
        [owned_bf] * chips + copies,
        [],
        (mine, other, mate_three, mate_g),
        combining,
        "carried_chip",
        aliases={4: chips, 5: chips + 1},
    )
    came, others, _, _ = reach_out(merged, (), True, "carried")

    mate_three, mate_g = swap(mate_three), swap(mate_g)
    few = 4 if half % 4 == 0 else 1
    parts = half // few

    def own_few(i, lens, place):
        return 0, (place[2] & 1) * parts + i

    own_tokens = pl.BlockSpec((count, few * DH), own_few)
    pair_tokens = pl.BlockSpec((2 * count, few * DH), lambda i, *a: (0, i))
    lane_few = pl.BlockSpec((count, few * DH), lambda i, *a: (0, i))
    turns = pl.BlockSpec((few, DH, 2 * count), lambda i, *a: (i, 0, 0))
    part, head_fq, turned = run(
        chip_kernel,
        parts,
        [own_tokens] * 3 + [pl.BlockSpec((3, count, few * DH), lambda i, *a: (0, 0, i))],
        [pair_tokens, pair_tokens, turns],
        [
            jax.ShapeDtypeStruct((2 * count, half * DH), F32),
            jax.ShapeDtypeStruct((2 * count, half * DH), BF16),
            jax.ShapeDtypeStruct((half, DH, 2 * count), BF16),
        ],
        [],
        (queries, keys, values, mate_three),
        (10 * product, 14 * array, 4 * half * count * DH),
        "within_chip",
    )
    late_tail = swap(own_tail)
    chip_in = spread(came, others, (part, late_tail), True, "carried")
    few_states = pl.BlockSpec((few, DH, DH), lambda i, *a: (i, 0, 0))
    one_owner = pl.BlockSpec((owned, DH, DH), lambda *a: (0, 0, 0))
    half_states = pltpu.VMEM((half, DH, DH), BF16)
    narrow_bf = jax.ShapeDtypeStruct(narrow, BF16)
    attn_half, mate_out, mine_ga, mate_ga, mine_in, mine_late, *merged = run(
        norm_kernel,
        parts,
        [pair_tokens, turns, own_tokens, lane_few, pair_tokens] + [one_owner] * chips,
        [own_tokens] + [lane_few] * 3 + [whole, few_states] + [one_owner] * chips,
        [token_bf] + [narrow_bf] * 3 + [half_bf] * 2 + [owned_bf] * chips,
        [half_states],
        (head_fq, turned, out_grad, mate_g, part, *chip_in),
        (8 * product, 16 * array, 2 * half * count * DH),
        "normed",
    )
    came, others, total, (mate_out, mine_late) = reach_out(
        merged, (mate_out, mine_late), False, "future"
    )
    other_ga, other_in = swap(mate_ga), swap(mine_in)
    other_ga = swap(mate_ga)
    def both(i, lens, place):
        return ((place[2] & 1) ^ (i // steps)) * steps + i % steps

    spans = pl.BlockSpec((count, step_heads * DH), lambda *a: (0, both(*a)))
    lanes = pl.BlockSpec((count, step_heads * DH), lambda i, *a: (0, i % steps))
    grad_queries, gk_part, gv_part = run(
        inner_kernel,
        2 * steps,
        [spans] * 3 + [lanes] * 2 + [whole] * 4 + [untouched],
        [spans] * 3,
        [token_bf, token_f32, token_f32],
        [all_states],
        (
            queries,
            keys,
            values,
            mine_ga,
            other_ga,
            mine_in,
            other_in,
            other.reshape(half, DH, DH),
            late_tail,
            total,
        ),
        (16 * product, 22 * array, 4 * half * count * DH),
        "grads_within",
    )
    late = (mine_late, swap(mine_late))
    chip_out = spread(came, others, (gk_part,), False, "future")
    (attn_out,) = run(
        fill_kernel,
        steps,
        [lane, untouched, untouched],
        [tokens(1)],
        [token_bf],
        [],
        (swap(mate_out), held_in_hbm(attn_half), chip_out[0]),
        (0, 2 * array, 0),
        "attn_out",
        aliases={3: 0},
    )
    outgoing = (chip_out, [swap(state) for state in chip_out])
    made = ()
    for parity in (0, 1):
        after = (held_in_hbm(attn_out),) if parity == 0 else made
        made = tuple(
            run(
                functools.partial(last_kernel, chips),
                steps,
                [tokens(parity)] * 4
                + [whole]
                + [one_owner] * chips
                + [untouched] * len(after),
                [tokens(parity)] * 2,
                [token_bf] * 2,
                [half_states],
                (keys, values, gk_part, gv_part, late[parity], *outgoing[parity], *after),
                (2 * product, 9 * array, half * count * DH),
                f"grads_last_{parity}",
                aliases={7 + chips + j: j for j in range(2)} if parity else {},
            )
        )
    return attn_out, grad_queries, *made


def solution(mesh):
    n_seq, n_head = mesh.shape["seq"], mesh.shape["head"]
    inner = 2 if n_seq % 2 == 0 else 1
    fine = Mesh(mesh.devices.reshape(n_seq // inner, inner, n_head), ("z", "x", "head"))
    rows = P(("z", "x", "head"), None)
    return jax.shard_map(
        local,
        mesh=fine,
        in_specs=(rows, rows, rows, rows, P()),
        out_specs=(rows, rows, rows, rows),
        check_vma=False,
    )
```

```python
import functools

import jax
import jax.numpy as jnp
from jax import lax
from jax.experimental import pallas as pl
from jax.experimental.pallas import tpu as pltpu
from jax.sharding import Mesh, PartitionSpec as P

DH = 128
F32 = jnp.float32
BF16 = jnp.bfloat16
NN = (((1,), (0,)), ((), ()))
NT = (((1,), (1,)), ((), ()))
LAYER = ("x", "head")


def mul(a, b, dims):
    return lax.dot_general(a, b, dims, preferred_element_type=F32)


def feature(wide):
    return jnp.where(wide > 0, wide + 1.0, jnp.exp(jnp.minimum(wide, 0.0)))


def slope(wide):
    return jnp.where(wide > 0, 1.0, jnp.exp(jnp.minimum(wide, 0.0)))


def doc_ends(lens):
    ends, total = [], 0
    for j in range(lens.shape[0]):
        total = total + lens[j]
        ends.append(total)
    return ends


def doc_at(ends, where):
    found = 0
    for end in ends:
        found = found + jnp.where(where >= end, 1, 0)
    return found


def rows_of(ends, first, count):
    at = first + lax.broadcasted_iota(jnp.int32, (count, 1), 0)
    return doc_at(ends, at)


def columns_of(ends, first, count):
    at = first + lax.broadcasted_iota(jnp.int32, (1, count), 1)
    return doc_at(ends, at)


def visible(ends, first, count):
    row = lax.broadcasted_iota(jnp.int32, (count, count), 0)
    column = lax.broadcasted_iota(jnp.int32, (count, count), 1)
    together = rows_of(ends, first, count) == columns_of(ends, first, count)
    return (row >= column) & together, (row <= column) & together


def identity(count):
    row = lax.broadcasted_iota(jnp.int32, (count, count), 0)
    column = lax.broadcasted_iota(jnp.int32, (count, count), 1)
    return jnp.where(row == column, 1.0, 0.0).astype(BF16)


def turn(array, eye):
    return mul(eye, array, NT).astype(BF16)


def head_mask(ends, first, count):
    return rows_of(ends, first, count) == doc_at(ends, first)


def tail_mask(ends, first, count):
    return rows_of(ends, first, count) == doc_at(ends, first + count - 1)


def cols(h):
    return slice(h * DH, (h + 1) * DH)


def bunches(heads, size=8):
    return [range(h, min(h + size, heads)) for h in range(0, heads, size)]


def halves(wide):
    high = wide.astype(BF16)
    return jnp.concatenate([high, (wide - high.astype(F32)).astype(BF16)], axis=1)


def tail_kernel(lens, place, k, v, *rest):
    if len(rest) > 1:
        q, g, out, three, last = rest
        three[0], three[1], three[2] = q[...], k[...], v[...]
        last[...] = g[...]
    else:
        (out,) = rest
    count = k.shape[0]
    tail = tail_mask(doc_ends(lens), place[0] * count, count)
    eye = identity(DH)
    for hs in bunches(out.shape[0]):
        fks = [
            jnp.where(tail, feature(k[:, cols(h)].astype(F32)), 0.0).astype(BF16) for h in hs
        ]
        turned = [turn(fk, eye) for fk in fks]
        sums = [mul(fk, v[:, cols(h)], NN).astype(BF16) for h, fk in zip(hs, turned)]
        for h, value in zip(hs, sums):
            out[h] = value


def pair_docs(lens, place, count):
    ends = doc_ends(lens)
    core = place[2] & 1
    own, mate = place[0] * count, (place[0] + 1 - 2 * core) * count

    def along(axis):
        shape = (2 * count, 1) if axis == 0 else (1, 2 * count)
        at = lax.broadcasted_iota(jnp.int32, shape, axis)
        return jnp.where(at < count, own + at, mate + at - count)

    rows, columns = along(0), along(1)
    row_docs, column_docs = doc_at(ends, rows), doc_at(ends, columns)
    seen = (rows >= columns) & (row_docs == column_docs)
    first = (place[0] - core) * count
    late = columns >= first + count
    return (
        seen,
        row_docs == doc_at(ends, first),
        column_docs == doc_at(ends, first),
        late & (column_docs == doc_at(ends, first + count)),
    )


def chip_kernel(lens, place, q, k, v, mate, part, head_fq, turned):
    count = q.shape[0]
    seen, head, _, _ = pair_docs(lens, place, count)
    eye = identity(DH)

    def both(mine, slot, h):
        return jnp.concatenate([mine[:, cols(h)], mate[slot, :, cols(h)]], axis=0)

    for hs in bunches(turned.shape[0], 4):
        wides = [feature(both(q, 0, h).astype(F32)) for h in hs]
        fks = [feature(both(k, 1, h).astype(F32)).astype(BF16) for h in hs]
        kept = [
            jnp.where(seen, mul(wide.astype(BF16), fk, NT), 0.0).astype(BF16)
            for wide, fk in zip(wides, fks)
        ]
        parts = [mul(s, both(v, 2, h), NN) for h, s in zip(hs, kept)]
        heads = [jnp.where(head, wide, 0.0).astype(BF16) for wide in wides]
        turns = [turn(wide.astype(BF16), eye) for wide in wides]
        for h, p, f, t in zip(hs, parts, heads, turns):
            part[:, cols(h)] = p
            head_fq[:, cols(h)] = f
            turned[h] = t


def norm_kernel(lens, place, head_fq, turned, g, mate_g, part, *rest):
    kept = rest[-1]
    chips = (len(rest) - 7) // 2
    incoming, (out, mate_out, ga_out, mate_ga, came, lates) = (
        rest[:chips],
        rest[chips : chips + 6],
    )
    states = rest[chips + 6 : -1]
    count = g.shape[0]
    _, _, head, late = pair_docs(lens, place, count)
    heads = turned.shape[0]
    step = pl.program_id(0)
    chip = place[2] >> 1

    @pl.when(step == 0)
    def _():
        for n, state in enumerate(incoming):
            owned = state.shape[0]
            came[pl.ds((chip ^ n) * owned, owned)] = state[...]

    weights = jnp.full((2 * DH, DH), 1.0 / DH, BF16)
    for hs in bunches(heads, 4):
        atts = [
            part[:, cols(h)] + mul(head_fq[:, cols(h)], came[step * heads + h], NN) for h in hs
        ]
        gos = [
            jnp.concatenate([g[:, cols(h)], mate_g[:, cols(h)]], axis=0).astype(F32) for h in hs
        ]
        means = [
            mul(jnp.concatenate([halves(att * att), halves(go * att)], axis=0), weights, NN)
            for att, go in zip(atts, gos)
        ]
        invs = [lax.rsqrt(m[: 2 * count] + 1e-05) for m in means]
        norms = [att * inv for att, inv in zip(atts, invs)]
        gas = [
            ((go - normed * (m[2 * count :] * inv)) * inv).astype(BF16)
            for go, normed, m, inv in zip(gos, norms, means, invs)
        ]
        sums = []
        for h, ga in zip(hs, gas):
            wide = turned[h].astype(F32)
            two = jnp.concatenate([jnp.where(head, wide, 0.0), jnp.where(late, wide, 0.0)], axis=0)
            sums.append(mul(two.astype(BF16), ga, NN).astype(BF16))
        for h, normed, ga, value in zip(hs, norms, gas, sums):
            normed = normed.astype(BF16)
            out[:, cols(h)], mate_out[:, cols(h)] = normed[:count], normed[count:]
            ga_out[:, cols(h)], mate_ga[:, cols(h)] = ga[:count], ga[count:]
            kept[step * heads + h] = value[:DH]
            lates[h] = value[DH:]

    @pl.when(step == pl.num_programs(0) - 1)
    def _():
        for n, state in enumerate(states):
            owned = state.shape[0]
            state[...] = kept[pl.ds((chip ^ n) * owned, owned)]


def inner_kernel(lens, place, q, k, v, mine_ga, other_ga, *rest):
    passed, earlier, (gq, gk, gv, came) = rest[:2], rest[2:4], rest[5:]
    count = q.shape[0]
    heads = q.shape[1] // DH
    step = pl.program_id(0)
    own = step < pl.num_programs(0) // 2

    @pl.when(step == 0)
    def _():
        half = came.shape[0] // 2
        core, (early_b, early_e, late_b, late_e) = chip_docs(lens, place, count)
        by_chip = jnp.where(core == 0, 1.0, same(late_b, early_b))
        by_mate = jnp.where(core == 0, 0.0, same(late_b, early_e))
        for j in range(2):
            came[pl.ds(j * half, half)] = (
                passed[j][...].astype(F32) * by_chip + earlier[j][...].astype(F32) * by_mate
            ).astype(BF16)

    ends = doc_ends(lens)
    first = place[0] * count
    seen, seeing = visible(ends, first, count)
    head = head_mask(ends, first, count)
    for hs in bunches(heads):
        wides = [q[:, cols(h)].astype(F32) for h in hs]
        fqs = [feature(wide).astype(BF16) for wide in wides]
        fks = [feature(k[:, cols(h)].astype(F32)).astype(BF16) for h in hs]
        gas = [jnp.where(own, mine_ga[:, cols(h)], other_ga[:, cols(h)]) for h in hs]
        gss = [
            jnp.where(seen, mul(ga, v[:, cols(h)], NT), 0.0).astype(BF16)
            for h, ga in zip(hs, gas)
        ]
        totals = [
            mul(gs, fk, NN) + jnp.where(head, mul(ga, came[step * heads + h], NT), 0.0)
            for h, gs, fk, ga in zip(hs, gss, fks, gas)
        ]
        flipped = [
            jnp.where(seeing, mul(v[:, cols(h)], ga, NT), 0.0).astype(BF16)
            for h, ga in zip(hs, gas)
        ]
        scores = [
            jnp.where(seeing, mul(fk, fq, NT), 0.0).astype(BF16) for fq, fk in zip(fqs, fks)
        ]
        gks = [mul(gs, fq, NN) for gs, fq in zip(flipped, fqs)]
        gvs = [mul(s, ga, NN) for s, ga in zip(scores, gas)]
        for h, total, wide, a, b in zip(hs, totals, wides, gks, gvs):
            gq[:, cols(h)] = (total * slope(wide)).astype(BF16)
            gk[:, cols(h)] = a
            gv[:, cols(h)] = b


def last_kernel(chips, lens, place, k, v, gk_part, gv_part, late, *rest):
    came = rest[-1]
    outgoing, gk, gv = rest[:chips], rest[-3], rest[-2]
    if len(rest) > chips + 3:
        rest[-4][...] = rest[chips][...]
        gk, gv = rest[-3], rest[-2]
    count = k.shape[0]
    heads = k.shape[1] // DH
    step = pl.program_id(0)

    @pl.when(step == 0)
    def _():
        core, (early_b, early_e, late_b, late_e) = chip_docs(lens, place, count)
        chip = place[2] >> 1
        by_far = jnp.where(core == 0, same(early_e, late_e), 1.0)
        by_late = jnp.where(core == 0, same(early_e, late_b), 0.0)
        for n, state in enumerate(outgoing):
            owned = state.shape[0]
            at = pl.ds((chip ^ n) * owned, owned)
            came[at] = (
                state[...].astype(F32) * by_far + late[at].astype(F32) * by_late
            ).astype(BF16)

    tail = tail_mask(doc_ends(lens), place[0] * count, count)
    for hs in bunches(heads):
        wides = [k[:, cols(h)].astype(F32) for h in hs]
        fks = [jnp.where(tail, feature(wide), 0.0).astype(BF16) for wide in wides]
        vts = [jnp.where(tail, v[:, cols(h)].astype(F32), 0.0).astype(BF16) for h in hs]
        states = [came[step * heads + h] for h in hs]
        gks = [gk_part[:, cols(h)] + mul(vt, o, NT) for h, vt, o in zip(hs, vts, states)]
        gvs = [gv_part[:, cols(h)] + mul(fk, o, NN) for h, fk, o in zip(hs, fks, states)]
        for h, a, wide, b in zip(hs, gks, wides, gvs):
            gk[:, cols(h)] = (a * slope(wide)).astype(BF16)
            gv[:, cols(h)] = b.astype(BF16)


def same(a, b):
    return jnp.where(a == b, 1.0, 0.0).astype(F32)


def chip_docs(lens, place, count):
    ends = doc_ends(lens)
    core = place[2] & 1
    start = (place[0] - core) * count
    marks = (start, start + count - 1, start + count, start + 2 * count - 1)
    return core, [doc_at(ends, mark) for mark in marks]


def merge_kernel(count, lens, place, mine, other, *outs):
    core, (early_b, early_e, late_b, late_e) = chip_docs(lens, place, count)
    far = same(early_e, late_e)
    mine_by = jnp.where(core == 0, far, 1.0)
    other_by = jnp.where(core == 0, 1.0, far)
    chip = place[2] >> 1
    for n, out in enumerate(outs):
        at = chip ^ n
        out[...] = (mine[at].astype(F32) * mine_by + other[at].astype(F32) * other_by).astype(
            BF16
        )


def total_kernel(forward, unit, members, passed, lens, place, *rest):
    states, total, held = rest[:members], rest[members + passed], rest[-1]
    chip = place[2] >> 1
    for n, state in enumerate(states):
        held[chip ^ n] = state[...]
    ends = doc_ends(lens)
    layer = place[1] * (members * unit)
    carry = None
    for step in range(members):
        i = step if forward else members - 1 - step
        mine = held[i].astype(F32)
        edge = layer + ((i + 1) * unit - 1 if forward else i * unit)
        here = doc_at(ends, edge)
        if carry is not None:
            mine = mine + carry * same(here, previous)
        carry, previous = mine, here
    total[...] = carry.astype(BF16)


def prefix_kernel(forward, unit, members, unread, lens, place, *rest):
    states, outs, (held, sums) = rest[:members], rest[-members - 2 : -2], rest[-2:]
    others = rest[members + unread : -members - 2]
    chip = place[2] >> 1
    for n, state in enumerate(states):
        held[chip ^ n] = state[...]
    span = members * unit
    ends = doc_ends(lens)
    layer = place[1] * span
    sign = -1 if forward else 1
    previous = doc_at(ends, layer - 1 if forward else layer + span)
    carry = None
    for s, other in enumerate(others):
        far = layer + sign * s * span
        there = doc_at(ends, far - 1 if forward else far + span)
        term = other[...].astype(F32) * same(there, previous)
        carry = term if carry is None else carry + term
    for step in range(members):
        i = step if forward else members - 1 - step
        near, far = layer + i * unit, layer + (i + 1) * unit - 1
        if not forward:
            near, far = far, near
        if carry is None:
            sums[i] = jnp.zeros(sums.shape[1:], BF16)
        else:
            sums[i] = (carry * same(doc_at(ends, near), previous)).astype(BF16)
        if step < members - 1:
            here = doc_at(ends, far)
            mine = held[i].astype(F32)
            if carry is not None:
                mine = mine + carry * same(here, previous)
            carry, previous = mine, here
    for n, out in enumerate(outs):
        out[...] = sums[chip ^ n]


SMALL = pltpu.CompilerParams(
    dimension_semantics=("arbitrary",), vmem_limit_bytes=16 * 1024 * 1024
)

def local(queries, keys, values, out_grad, doc_lengths):
    count, width = queries.shape
    heads = width // DH
    layers = lax.axis_size("z")
    members = lax.axis_size("x") * lax.axis_size("head")
    owned = heads // members
    half = heads // 2
    reach = range(1, min(layers - 1, -(-layers // 2)) + 1)
    place = jnp.stack(
        [lax.axis_index(("z", "x", "head")), lax.axis_index("z"), lax.axis_index(LAYER)]
    ).astype(jnp.int32)
    chips = members // 2
    step_heads = max(n for n in (8, 4, 2, 1) if half % n == 0)
    steps = half // step_heads

    def held_in_hbm(arg):
        return pltpu.with_memory_space_constraint(arg, pltpu.HBM)

    def at(parity):
        if parity is None:
            return lambda i, lens, place: i
        return lambda i, lens, place: ((place[2] & 1) ^ parity) * steps + i

    def tokens(parity):
        block = at(parity)
        return pl.BlockSpec((count, step_heads * DH), lambda *a: (0, block(*a)))

    whole = pl.BlockSpec((half, DH, DH), lambda *a: (0, 0, 0))
    halved = pl.BlockSpec((step_heads, DH, DH), lambda i, *a: (i, 0, 0))
    untouched = pl.BlockSpec(memory_space=pl.ANY)
    token_bf = pltpu.HBM((count, width), BF16)
    token_f32 = jax.ShapeDtypeStruct((count, width), F32)
    owned_bf = jax.ShapeDtypeStruct((owned, DH, DH), BF16)
    half_bf = jax.ShapeDtypeStruct((half, DH, DH), BF16)

    def run(kernel, grid, ins, outs, shapes, scratch, args, cost, name, params=SMALL, aliases={}):
        flops, moved, exps = cost
        return pl.pallas_call(
            kernel,
            grid_spec=pltpu.PrefetchScalarGridSpec(
                num_scalar_prefetch=2,
                grid=(grid,),
                in_specs=ins,
                out_specs=outs,
                scratch_shapes=scratch,
            ),
            out_shape=shapes,
            input_output_aliases=aliases,
            compiler_params=params,
            cost_estimate=pl.CostEstimate(
                flops=flops, bytes_accessed=moved, transcendentals=exps
            ),
            name=name,
        )(doc_lengths, place, *args)

    product = 2 * half * count * DH * DH
    array = half * count * DH * 2
    all_states = pltpu.VMEM((heads, DH, DH), BF16)
    block = owned
    single = pl.BlockSpec((block, DH, DH), lambda i, *a: (i, 0, 0))
    grouped = pl.BlockSpec((chips, block, DH, DH), lambda i, *a: (0, i, 0, 0))
    buffer = pltpu.VMEM((chips, block, DH, DH), BF16)
    combining = (4 * half * DH * DH, 4 * half * DH * DH, 0)
    moves = owned // block

    def swap(state):
        return lax.ppermute(state, LAYER, [(i, i ^ 1) for i in range(members)])

    def exchange(states):
        pairs = [[(i, i ^ (2 * n)) for i in range(members)] for n in range(chips)]
        return [
            state if n == 0 else lax.ppermute(state, LAYER, pairs[n])
            for n, state in enumerate(states)
        ]

    def reach_out(merged, along, forward, name):
        came = exchange(merged)
        total, *along = run(
            functools.partial(total_kernel, forward, 2 * count, chips, len(along)),
            moves,
            [single] * chips + [untouched] * len(along),
            [single] + [untouched] * len(along),
            [owned_bf] + [jax.ShapeDtypeStruct(array.shape, array.dtype) for array in along],
            [buffer],
            [*came, *along],
            combining,
            name + "_total",
            aliases={2 + chips + j: 1 + j for j in range(len(along))},
        )
        others = []
        for s in reach:
            pairs = [(i, i + s) if forward else (i + s, i) for i in range(layers - s)]
            others.append(lax.ppermute(total, "z", pairs))
        return came, others, total, along

    def spread(came, others, after, forward, name):
        sums = run(
            functools.partial(prefix_kernel, forward, 2 * count, chips, len(after)),
            moves,
            [single] * chips + [untouched] * len(after) + [single] * len(others),
            [single] * chips,
            [owned_bf] * chips,
            [buffer, buffer],
            [*came, *after, *others],
            combining,
            name + "_prefix",
        )
        return exchange(sums)

    narrow = (count, half * DH)
    lane = pl.BlockSpec((count, step_heads * DH), lambda i, *a: (0, i))
    pinned = [held_in_hbm(array) for array in (queries, keys, values, out_grad)]
    tail_work = (product, 3 * array, half * count * DH)
    copies = [
        jax.ShapeDtypeStruct((3, *narrow), BF16),
        jax.ShapeDtypeStruct(narrow, BF16),
    ]
    mate_tail, mate_three, mate_g = run(
        tail_kernel,
        steps,
        [tokens(1)] * 4,
        [halved, pl.BlockSpec((3, count, step_heads * DH), lambda i, *a: (0, 0, i)), lane],
        [half_bf, *copies],
        [],
        (pinned[1], pinned[2], pinned[0], pinned[3]),
        tail_work,
        "tail_mate",
    )
    (own_tail,) = run(
        tail_kernel,
        steps,
        [tokens(0)] * 2,
        [halved],
        [half_bf],
        [],
        pinned[1:3],
        tail_work,
        "tail_own",
    )
    mine = own_tail.reshape(chips, owned, DH, DH)
    other = swap(mate_tail).reshape(chips, owned, DH, DH)
    merged = run(
        functools.partial(merge_kernel, count),
        moves,
        [grouped] * 2,
        [single] * chips,
        [owned_bf] * chips,
        [],
        (mine, other),
        combining,
        "carried_chip",
    )
    came, others, _, (mate_three, mate_g, own_tail) = reach_out(
        merged, (mate_three, mate_g, own_tail), True, "carried"
    )
    mate_three, mate_g = swap(mate_three), swap(mate_g)
    few = 4 if half % 4 == 0 else 1
    parts = half // few

    def own_few(i, lens, place):
        return 0, (place[2] & 1) * parts + i

    own_tokens = pl.BlockSpec((count, few * DH), own_few)
    pair_tokens = pl.BlockSpec((2 * count, few * DH), lambda i, *a: (0, i))
    lane_few = pl.BlockSpec((count, few * DH), lambda i, *a: (0, i))
    turns = pl.BlockSpec((few, DH, 2 * count), lambda i, *a: (i, 0, 0))
    part, head_fq, turned = run(
        chip_kernel,
        parts,
        [own_tokens] * 3 + [pl.BlockSpec((3, count, few * DH), lambda i, *a: (0, 0, i))],
        [pair_tokens, pair_tokens, turns],
        [
            jax.ShapeDtypeStruct((2 * count, half * DH), F32),
            jax.ShapeDtypeStruct((2 * count, half * DH), BF16),
            jax.ShapeDtypeStruct((half, DH, 2 * count), BF16),
        ],
        [],
        (queries, keys, values, mate_three),
        (10 * product, 14 * array, 4 * half * count * DH),
        "within_chip",
    )
    late_tail = swap(own_tail)
    chip_in = spread(came, others, (part, late_tail), True, "carried")
    few_states = pl.BlockSpec((few, DH, DH), lambda i, *a: (i, 0, 0))
    one_owner = pl.BlockSpec((owned, DH, DH), lambda *a: (0, 0, 0))
    half_states = pltpu.VMEM((half, DH, DH), BF16)
    narrow_bf = jax.ShapeDtypeStruct(narrow, BF16)
    attn_half, mate_out, mine_ga, mate_ga, mine_in, mine_late, *merged = run(
        norm_kernel,
        parts,
        [pair_tokens, turns, own_tokens, lane_few, pair_tokens] + [one_owner] * chips,
        [own_tokens] + [lane_few] * 3 + [whole, few_states] + [one_owner] * chips,
        [token_bf] + [narrow_bf] * 3 + [half_bf] * 2 + [owned_bf] * chips,
        [half_states],
        (head_fq, turned, out_grad, mate_g, part, *chip_in),
        (8 * product, 16 * array, 2 * half * count * DH),
        "normed",
    )
    came, others, total, (mate_out, mine_late) = reach_out(
        merged, (mate_out, mine_late), False, "future"
    )
    other_ga, other_in = swap(mate_ga), swap(mine_in)
    other_ga = swap(mate_ga)
    def both(i, lens, place):
        return ((place[2] & 1) ^ (i // steps)) * steps + i % steps

    spans = pl.BlockSpec((count, step_heads * DH), lambda *a: (0, both(*a)))
    lanes = pl.BlockSpec((count, step_heads * DH), lambda i, *a: (0, i % steps))
    grad_queries, gk_part, gv_part = run(
        inner_kernel,
        2 * steps,
        [spans] * 3 + [lanes] * 2 + [whole] * 4 + [untouched],
        [spans] * 3,
        [token_bf, token_f32, token_f32],
        [all_states],
        (
            queries,
            keys,
            values,
            mine_ga,
            other_ga,
            mine_in,
            other_in,
            other.reshape(half, DH, DH),
            late_tail,
            total,
        ),
        (16 * product, 22 * array, 4 * half * count * DH),
        "grads_within",
    )
    late = (mine_late, swap(mine_late))
    chip_out = spread(came, others, (gk_part,), False, "future")
    outgoing = (chip_out, [swap(state) for state in chip_out])
    def last(parity, extra_ins, extra_outs, shapes, args, aliases):
        return run(
            functools.partial(last_kernel, chips),
            steps,
            [tokens(parity)] * 4 + [whole] + [one_owner] * chips + extra_ins,
            extra_outs + [tokens(parity)] * 2,
            shapes,
            [half_states],
            (keys, values, gk_part, gv_part, late[parity], *outgoing[parity], *args),
            (2 * product, 9 * array, half * count * DH),
            f"grads_last_{parity}",
            aliases=aliases,
        )

    grad_keys, grad_values = last(0, [], [], [token_bf] * 2, (), {})
    attn_out, grad_keys, grad_values = last(
        1,
        [lane] + [untouched] * 3,
        [tokens(1)],
        [token_bf] * 3,
        (swap(mate_out), held_in_hbm(attn_half), grad_keys, grad_values),
        {8 + chips + j: j for j in range(3)},
    )
    return attn_out, grad_queries, grad_keys, grad_values


def solution(mesh):
    n_seq, n_head = mesh.shape["seq"], mesh.shape["head"]
    inner = 2 if n_seq % 2 == 0 else 1
    fine = Mesh(mesh.devices.reshape(n_seq // inner, inner, n_head), ("z", "x", "head"))
    rows = P(("z", "x", "head"), None)
    return jax.shard_map(
        local,
        mesh=fine,
        in_specs=(rows, rows, rows, rows, P()),
        out_specs=(rows, rows, rows, rows),
        check_vma=False,
    )
```

```python
import functools

import jax
import jax.numpy as jnp
from jax import lax
from jax.experimental import pallas as pl
from jax.experimental.pallas import tpu as pltpu
from jax.sharding import Mesh, PartitionSpec as P

DH = 128
F32 = jnp.float32
BF16 = jnp.bfloat16
NN = (((1,), (0,)), ((), ()))
NT = (((1,), (1,)), ((), ()))
LAYER = ("x", "head")


def mul(a, b, dims):
    return lax.dot_general(a, b, dims, preferred_element_type=F32)


def feature(wide):
    return jnp.where(wide > 0, wide + 1.0, jnp.exp(jnp.minimum(wide, 0.0)))


def slope(wide):
    return jnp.where(wide > 0, 1.0, jnp.exp(jnp.minimum(wide, 0.0)))


def doc_ends(lens):
    ends, total = [], 0
    for j in range(lens.shape[0]):
        total = total + lens[j]
        ends.append(total)
    return ends


def doc_at(ends, where):
    found = 0
    for end in ends:
        found = found + jnp.where(where >= end, 1, 0)
    return found


def rows_of(ends, first, count):
    at = first + lax.broadcasted_iota(jnp.int32, (count, 1), 0)
    return doc_at(ends, at)


def columns_of(ends, first, count):
    at = first + lax.broadcasted_iota(jnp.int32, (1, count), 1)
    return doc_at(ends, at)


def visible(ends, first, count):
    row = lax.broadcasted_iota(jnp.int32, (count, count), 0)
    column = lax.broadcasted_iota(jnp.int32, (count, count), 1)
    together = rows_of(ends, first, count) == columns_of(ends, first, count)
    return (row >= column) & together, (row <= column) & together


def identity(count):
    row = lax.broadcasted_iota(jnp.int32, (count, count), 0)
    column = lax.broadcasted_iota(jnp.int32, (count, count), 1)
    return jnp.where(row == column, 1.0, 0.0).astype(BF16)


def turn(array, eye):
    return mul(eye, array, NT).astype(BF16)


def head_mask(ends, first, count):
    return rows_of(ends, first, count) == doc_at(ends, first)


def tail_mask(ends, first, count):
    return rows_of(ends, first, count) == doc_at(ends, first + count - 1)


def cols(h):
    return slice(h * DH, (h + 1) * DH)


def bunches(heads, size=8):
    return [range(h, min(h + size, heads)) for h in range(0, heads, size)]


def halves(wide):
    high = wide.astype(BF16)
    return jnp.concatenate([high, (wide - high.astype(F32)).astype(BF16)], axis=1)


def tail_kernel(lens, place, k, v, *rest):
    if len(rest) > 1:
        q, g, out, three, last = rest
        three[0], three[1], three[2] = q[...], k[...], v[...]
        last[...] = g[...]
    else:
        (out,) = rest
    count = k.shape[0]
    tail = tail_mask(doc_ends(lens), place[0] * count, count)
    eye = identity(DH)
    for hs in bunches(out.shape[0]):
        fks = [
            jnp.where(tail, feature(k[:, cols(h)].astype(F32)), 0.0).astype(BF16) for h in hs
        ]
        turned = [turn(fk, eye) for fk in fks]
        sums = [mul(fk, v[:, cols(h)], NN).astype(BF16) for h, fk in zip(hs, turned)]
        for h, value in zip(hs, sums):
            out[h] = value


def pair_docs(lens, place, count):
    ends = doc_ends(lens)
    core = place[2] & 1
    own, mate = place[0] * count, (place[0] + 1 - 2 * core) * count

    def along(axis):
        shape = (2 * count, 1) if axis == 0 else (1, 2 * count)
        at = lax.broadcasted_iota(jnp.int32, shape, axis)
        return jnp.where(at < count, own + at, mate + at - count)

    rows, columns = along(0), along(1)
    row_docs, column_docs = doc_at(ends, rows), doc_at(ends, columns)
    seen = (rows >= columns) & (row_docs == column_docs)
    first = (place[0] - core) * count
    late = columns >= first + count
    return (
        seen,
        row_docs == doc_at(ends, first),
        column_docs == doc_at(ends, first),
        late & (column_docs == doc_at(ends, first + count)),
    )


def chip_kernel(lens, place, q, k, v, mate, part, head_fq, turned):
    count = q.shape[0]
    seen, head, _, _ = pair_docs(lens, place, count)
    eye = identity(DH)

    def both(mine, slot, h):
        return jnp.concatenate([mine[:, cols(h)], mate[slot, :, cols(h)]], axis=0)

    for hs in bunches(turned.shape[0], 4):
        wides = [feature(both(q, 0, h).astype(F32)) for h in hs]
        fks = [feature(both(k, 1, h).astype(F32)).astype(BF16) for h in hs]
        kept = [
            jnp.where(seen, mul(wide.astype(BF16), fk, NT), 0.0).astype(BF16)
            for wide, fk in zip(wides, fks)
        ]
        parts = [mul(s, both(v, 2, h), NN) for h, s in zip(hs, kept)]
        heads = [jnp.where(head, wide, 0.0).astype(BF16) for wide in wides]
        turns = [turn(wide.astype(BF16), eye) for wide in wides]
        for h, p, f, t in zip(hs, parts, heads, turns):
            part[:, cols(h)] = p
            head_fq[:, cols(h)] = f
            turned[h] = t


def norm_kernel(lens, place, head_fq, turned, g, mate_g, part, *rest):
    kept = rest[-1]
    chips = (len(rest) - 7) // 2
    incoming, (out, mate_out, ga_out, mate_ga, came, lates) = (
        rest[:chips],
        rest[chips : chips + 6],
    )
    states = rest[chips + 6 : -1]
    count = g.shape[0]
    _, _, head, late = pair_docs(lens, place, count)
    heads = turned.shape[0]
    step = pl.program_id(0)
    chip = place[2] >> 1

    @pl.when(step == 0)
    def _():
        for n, state in enumerate(incoming):
            owned = state.shape[0]
            came[pl.ds((chip ^ n) * owned, owned)] = state[...]

    weights = jnp.full((2 * DH, DH), 1.0 / DH, BF16)
    for hs in bunches(heads, 4):
        atts = [
            part[:, cols(h)] + mul(head_fq[:, cols(h)], came[step * heads + h], NN) for h in hs
        ]
        gos = [
            jnp.concatenate([g[:, cols(h)], mate_g[:, cols(h)]], axis=0).astype(F32) for h in hs
        ]
        means = [
            mul(jnp.concatenate([halves(att * att), halves(go * att)], axis=0), weights, NN)
            for att, go in zip(atts, gos)
        ]
        invs = [lax.rsqrt(m[: 2 * count] + 1e-05) for m in means]
        norms = [att * inv for att, inv in zip(atts, invs)]
        gas = [
            ((go - normed * (m[2 * count :] * inv)) * inv).astype(BF16)
            for go, normed, m, inv in zip(gos, norms, means, invs)
        ]
        sums = []
        for h, ga in zip(hs, gas):
            wide = turned[h].astype(F32)
            two = jnp.concatenate([jnp.where(head, wide, 0.0), jnp.where(late, wide, 0.0)], axis=0)
            sums.append(mul(two.astype(BF16), ga, NN).astype(BF16))
        for h, normed, ga, value in zip(hs, norms, gas, sums):
            normed = normed.astype(BF16)
            out[:, cols(h)], mate_out[:, cols(h)] = normed[:count], normed[count:]
            ga_out[:, cols(h)], mate_ga[:, cols(h)] = ga[:count], ga[count:]
            kept[step * heads + h] = value[:DH]
            lates[h] = value[DH:]

    @pl.when(step == pl.num_programs(0) - 1)
    def _():
        for n, state in enumerate(states):
            owned = state.shape[0]
            state[...] = kept[pl.ds((chip ^ n) * owned, owned)]


def inner_kernel(lens, place, q, k, v, mine_ga, other_ga, *rest):
    passed, earlier, (gq, gk, gv, came) = rest[:2], rest[2:4], rest[5:]
    count = q.shape[0]
    heads = q.shape[1] // DH
    step = pl.program_id(0)
    own = step < pl.num_programs(0) // 2

    @pl.when(step == 0)
    def _():
        half = came.shape[0] // 2
        core, (early_b, early_e, late_b, late_e) = chip_docs(lens, place, count)
        by_chip = jnp.where(core == 0, 1.0, same(late_b, early_b))
        by_mate = jnp.where(core == 0, 0.0, same(late_b, early_e))
        for j in range(2):
            came[pl.ds(j * half, half)] = (
                passed[j][...].astype(F32) * by_chip + earlier[j][...].astype(F32) * by_mate
            ).astype(BF16)

    ends = doc_ends(lens)
    first = place[0] * count
    seen, seeing = visible(ends, first, count)
    head = head_mask(ends, first, count)
    for hs in bunches(heads):
        wides = [q[:, cols(h)].astype(F32) for h in hs]
        fqs = [feature(wide).astype(BF16) for wide in wides]
        fks = [feature(k[:, cols(h)].astype(F32)).astype(BF16) for h in hs]
        gas = [jnp.where(own, mine_ga[:, cols(h)], other_ga[:, cols(h)]) for h in hs]
        gss = [
            jnp.where(seen, mul(ga, v[:, cols(h)], NT), 0.0).astype(BF16)
            for h, ga in zip(hs, gas)
        ]
        totals = [
            mul(gs, fk, NN) + jnp.where(head, mul(ga, came[step * heads + h], NT), 0.0)
            for h, gs, fk, ga in zip(hs, gss, fks, gas)
        ]
        flipped = [
            jnp.where(seeing, mul(v[:, cols(h)], ga, NT), 0.0).astype(BF16)
            for h, ga in zip(hs, gas)
        ]
        scores = [
            jnp.where(seeing, mul(fk, fq, NT), 0.0).astype(BF16) for fq, fk in zip(fqs, fks)
        ]
        gks = [mul(gs, fq, NN) for gs, fq in zip(flipped, fqs)]
        gvs = [mul(s, ga, NN) for s, ga in zip(scores, gas)]
        for h, total, wide, a, b in zip(hs, totals, wides, gks, gvs):
            gq[:, cols(h)] = (total * slope(wide)).astype(BF16)
            gk[:, cols(h)] = a
            gv[:, cols(h)] = b


def last_kernel(chips, lens, place, k, v, gk_part, gv_part, late, *rest):
    came = rest[-1]
    outgoing, gk, gv = rest[:chips], rest[-3], rest[-2]
    if len(rest) > chips + 3:
        rest[-4][...] = rest[chips][...]
        gk, gv = rest[-3], rest[-2]
    count = k.shape[0]
    heads = k.shape[1] // DH
    step = pl.program_id(0)

    @pl.when(step == 0)
    def _():
        core, (early_b, early_e, late_b, late_e) = chip_docs(lens, place, count)
        chip = place[2] >> 1
        by_far = jnp.where(core == 0, same(early_e, late_e), 1.0)
        by_late = jnp.where(core == 0, same(early_e, late_b), 0.0)
        for n, state in enumerate(outgoing):
            owned = state.shape[0]
            at = pl.ds((chip ^ n) * owned, owned)
            came[at] = (
                state[...].astype(F32) * by_far + late[at].astype(F32) * by_late
            ).astype(BF16)

    tail = tail_mask(doc_ends(lens), place[0] * count, count)
    for hs in bunches(heads):
        wides = [k[:, cols(h)].astype(F32) for h in hs]
        fks = [jnp.where(tail, feature(wide), 0.0).astype(BF16) for wide in wides]
        vts = [jnp.where(tail, v[:, cols(h)].astype(F32), 0.0).astype(BF16) for h in hs]
        states = [came[step * heads + h] for h in hs]
        gks = [gk_part[:, cols(h)] + mul(vt, o, NT) for h, vt, o in zip(hs, vts, states)]
        gvs = [gv_part[:, cols(h)] + mul(fk, o, NN) for h, fk, o in zip(hs, fks, states)]
        for h, a, wide, b in zip(hs, gks, wides, gvs):
            gk[:, cols(h)] = (a * slope(wide)).astype(BF16)
            gv[:, cols(h)] = b.astype(BF16)


def same(a, b):
    return jnp.where(a == b, 1.0, 0.0).astype(F32)


def chip_docs(lens, place, count):
    ends = doc_ends(lens)
    core = place[2] & 1
    start = (place[0] - core) * count
    marks = (start, start + count - 1, start + count, start + 2 * count - 1)
    return core, [doc_at(ends, mark) for mark in marks]


def merge_kernel(count, lens, place, mine, other, *outs):
    core, (early_b, early_e, late_b, late_e) = chip_docs(lens, place, count)
    far = same(early_e, late_e)
    mine_by = jnp.where(core == 0, far, 1.0)
    other_by = jnp.where(core == 0, 1.0, far)
    chip = place[2] >> 1
    for n, out in enumerate(outs):
        at = chip ^ n
        out[...] = (mine[at].astype(F32) * mine_by + other[at].astype(F32) * other_by).astype(
            BF16
        )


def total_kernel(forward, unit, members, passed, lens, place, *rest):
    states, total, held = rest[:members], rest[members + passed], rest[-1]
    chip = place[2] >> 1
    for n, state in enumerate(states):
        held[chip ^ n] = state[...]
    ends = doc_ends(lens)
    layer = place[1] * (members * unit)
    carry = None
    for step in range(members):
        i = step if forward else members - 1 - step
        mine = held[i].astype(F32)
        edge = layer + ((i + 1) * unit - 1 if forward else i * unit)
        here = doc_at(ends, edge)
        if carry is not None:
            mine = mine + carry * same(here, previous)
        carry, previous = mine, here
    total[...] = carry.astype(BF16)


def prefix_kernel(forward, unit, members, unread, lens, place, *rest):
    states, outs, (held, sums) = rest[:members], rest[-members - 2 : -2], rest[-2:]
    others = rest[members + unread : -members - 2]
    chip = place[2] >> 1
    for n, state in enumerate(states):
        held[chip ^ n] = state[...]
    span = members * unit
    ends = doc_ends(lens)
    layer = place[1] * span
    previous = doc_at(ends, layer - 1 if forward else layer + span)
    carry = None
    for other in others:
        for z in range(other.shape[0]):
            there = doc_at(ends, (z + 1) * span - 1 if forward else z * span)
            beyond = z < place[1] if forward else z > place[1]
            term = other[z].astype(F32) * jnp.where(beyond, same(there, previous), 0.0)
            carry = term if carry is None else carry + term
    for step in range(members):
        i = step if forward else members - 1 - step
        near, far = layer + i * unit, layer + (i + 1) * unit - 1
        if not forward:
            near, far = far, near
        if carry is None:
            sums[i] = jnp.zeros(sums.shape[1:], BF16)
        else:
            sums[i] = (carry * same(doc_at(ends, near), previous)).astype(BF16)
        if step < members - 1:
            here = doc_at(ends, far)
            mine = held[i].astype(F32)
            if carry is not None:
                mine = mine + carry * same(here, previous)
            carry, previous = mine, here
    for n, out in enumerate(outs):
        out[...] = sums[chip ^ n]


SMALL = pltpu.CompilerParams(
    dimension_semantics=("arbitrary",), vmem_limit_bytes=16 * 1024 * 1024
)

def local(queries, keys, values, out_grad, doc_lengths):
    count, width = queries.shape
    heads = width // DH
    layers = lax.axis_size("z")
    members = lax.axis_size("x") * lax.axis_size("head")
    owned = heads // members
    half = heads // 2
    place = jnp.stack(
        [lax.axis_index(("z", "x", "head")), lax.axis_index("z"), lax.axis_index(LAYER)]
    ).astype(jnp.int32)
    chips = members // 2
    step_heads = max(n for n in (8, 4, 2, 1) if half % n == 0)
    steps = half // step_heads

    def held_in_hbm(arg):
        return pltpu.with_memory_space_constraint(arg, pltpu.HBM)

    def at(parity):
        if parity is None:
            return lambda i, lens, place: i
        return lambda i, lens, place: ((place[2] & 1) ^ parity) * steps + i

    def tokens(parity):
        block = at(parity)
        return pl.BlockSpec((count, step_heads * DH), lambda *a: (0, block(*a)))

    whole = pl.BlockSpec((half, DH, DH), lambda *a: (0, 0, 0))
    halved = pl.BlockSpec((step_heads, DH, DH), lambda i, *a: (i, 0, 0))
    untouched = pl.BlockSpec(memory_space=pl.ANY)
    token_bf = pltpu.HBM((count, width), BF16)
    token_f32 = jax.ShapeDtypeStruct((count, width), F32)
    owned_bf = jax.ShapeDtypeStruct((owned, DH, DH), BF16)
    half_bf = jax.ShapeDtypeStruct((half, DH, DH), BF16)

    def run(kernel, grid, ins, outs, shapes, scratch, args, cost, name, params=SMALL, aliases={}):
        flops, moved, exps = cost
        return pl.pallas_call(
            kernel,
            grid_spec=pltpu.PrefetchScalarGridSpec(
                num_scalar_prefetch=2,
                grid=(grid,),
                in_specs=ins,
                out_specs=outs,
                scratch_shapes=scratch,
            ),
            out_shape=shapes,
            input_output_aliases=aliases,
            compiler_params=params,
            cost_estimate=pl.CostEstimate(
                flops=flops, bytes_accessed=moved, transcendentals=exps
            ),
            name=name,
        )(doc_lengths, place, *args)

    product = 2 * half * count * DH * DH
    array = half * count * DH * 2
    all_states = pltpu.VMEM((heads, DH, DH), BF16)
    block = owned
    single = pl.BlockSpec((block, DH, DH), lambda i, *a: (i, 0, 0))
    stacked = pl.BlockSpec((layers, block, DH, DH), lambda i, *a: (0, i, 0, 0))
    grouped = pl.BlockSpec((chips, block, DH, DH), lambda i, *a: (0, i, 0, 0))
    buffer = pltpu.VMEM((chips, block, DH, DH), BF16)
    combining = (4 * half * DH * DH, 4 * half * DH * DH, 0)
    moves = owned // block

    def swap(state):
        return lax.ppermute(state, LAYER, [(i, i ^ 1) for i in range(members)])

    def exchange(states):
        pairs = [[(i, i ^ (2 * n)) for i in range(members)] for n in range(chips)]
        return [
            state if n == 0 else lax.ppermute(state, LAYER, pairs[n])
            for n, state in enumerate(states)
        ]

    def reach_out(merged, along, forward, name):
        came = exchange(merged)
        total, *along = run(
            functools.partial(total_kernel, forward, 2 * count, chips, len(along)),
            moves,
            [single] * chips + [untouched] * len(along),
            [single] + [untouched] * len(along),
            [owned_bf] + [jax.ShapeDtypeStruct(array.shape, array.dtype) for array in along],
            [buffer],
            [*came, *along],
            combining,
            name + "_total",
            aliases={2 + chips + j: 1 + j for j in range(len(along))},
        )
        others = [held_in_hbm(lax.all_gather(total, "z"))] if layers > 1 else []
        return came, others, total, along

    def spread(came, others, after, forward, name):
        sums = run(
            functools.partial(prefix_kernel, forward, 2 * count, chips, len(after)),
            moves,
            [single] * chips + [untouched] * len(after) + [stacked] * len(others),
            [single] * chips,
            [owned_bf] * chips,
            [buffer, buffer],
            [*came, *after, *others],
            combining,
            name + "_prefix",
        )
        return exchange(sums)

    narrow = (count, half * DH)
    lane = pl.BlockSpec((count, step_heads * DH), lambda i, *a: (0, i))
    pinned = [held_in_hbm(array) for array in (queries, keys, values, out_grad)]
    tail_work = (product, 3 * array, half * count * DH)
    copies = [
        jax.ShapeDtypeStruct((3, *narrow), BF16),
        jax.ShapeDtypeStruct(narrow, BF16),
    ]
    mate_tail, mate_three, mate_g = run(
        tail_kernel,
        steps,
        [tokens(1)] * 4,
        [halved, pl.BlockSpec((3, count, step_heads * DH), lambda i, *a: (0, 0, i)), lane],
        [half_bf, *copies],
        [],
        (pinned[1], pinned[2], pinned[0], pinned[3]),
        tail_work,
        "tail_mate",
    )
    (own_tail,) = run(
        tail_kernel,
        steps,
        [tokens(0)] * 2,
        [halved],
        [half_bf],
        [],
        pinned[1:3],
        tail_work,
        "tail_own",
    )
    mine = own_tail.reshape(chips, owned, DH, DH)
    other = swap(mate_tail).reshape(chips, owned, DH, DH)
    merged = run(
        functools.partial(merge_kernel, count),
        moves,
        [grouped] * 2,
        [single] * chips,
        [owned_bf] * chips,
        [],
        (mine, other),
        combining,
        "carried_chip",
    )
    came, others, _, (mate_three, mate_g, own_tail) = reach_out(
        merged, (mate_three, mate_g, own_tail), True, "carried"
    )
    mate_three, mate_g = swap(mate_three), swap(mate_g)
    few = 4 if half % 4 == 0 else 1
    parts = half // few

    def own_few(i, lens, place):
        return 0, (place[2] & 1) * parts + i

    own_tokens = pl.BlockSpec((count, few * DH), own_few)
    pair_tokens = pl.BlockSpec((2 * count, few * DH), lambda i, *a: (0, i))
    lane_few = pl.BlockSpec((count, few * DH), lambda i, *a: (0, i))
    turns = pl.BlockSpec((few, DH, 2 * count), lambda i, *a: (i, 0, 0))
    part, head_fq, turned = run(
        chip_kernel,
        parts,
        [own_tokens] * 3 + [pl.BlockSpec((3, count, few * DH), lambda i, *a: (0, 0, i))],
        [pair_tokens, pair_tokens, turns],
        [
            jax.ShapeDtypeStruct((2 * count, half * DH), F32),
            jax.ShapeDtypeStruct((2 * count, half * DH), BF16),
            jax.ShapeDtypeStruct((half, DH, 2 * count), BF16),
        ],
        [],
        (queries, keys, values, mate_three),
        (10 * product, 14 * array, 4 * half * count * DH),
        "within_chip",
    )
    late_tail = swap(own_tail)
    chip_in = spread(came, others, (part, late_tail), True, "carried")
    few_states = pl.BlockSpec((few, DH, DH), lambda i, *a: (i, 0, 0))
    one_owner = pl.BlockSpec((owned, DH, DH), lambda *a: (0, 0, 0))
    half_states = pltpu.VMEM((half, DH, DH), BF16)
    narrow_bf = jax.ShapeDtypeStruct(narrow, BF16)
    attn_half, mate_out, mine_ga, mate_ga, mine_in, mine_late, *merged = run(
        norm_kernel,
        parts,
        [pair_tokens, turns, own_tokens, lane_few, pair_tokens] + [one_owner] * chips,
        [own_tokens] + [lane_few] * 3 + [whole, few_states] + [one_owner] * chips,
        [token_bf] + [narrow_bf] * 3 + [half_bf] * 2 + [owned_bf] * chips,
        [half_states],
        (head_fq, turned, out_grad, mate_g, part, *chip_in),
        (8 * product, 16 * array, 2 * half * count * DH),
        "normed",
    )
    came, others, total, (mate_out, mine_late) = reach_out(
        merged, (mate_out, mine_late), False, "future"
    )
    other_ga, other_in = swap(mate_ga), swap(mine_in)
    other_ga = swap(mate_ga)
    def both(i, lens, place):
        return ((place[2] & 1) ^ (i // steps)) * steps + i % steps

    spans = pl.BlockSpec((count, step_heads * DH), lambda *a: (0, both(*a)))
    lanes = pl.BlockSpec((count, step_heads * DH), lambda i, *a: (0, i % steps))
    grad_queries, gk_part, gv_part = run(
        inner_kernel,
        2 * steps,
        [spans] * 3 + [lanes] * 2 + [whole] * 4 + [untouched],
        [spans] * 3,
        [token_bf, token_f32, token_f32],
        [all_states],
        (
            queries,
            keys,
            values,
            mine_ga,
            other_ga,
            mine_in,
            other_in,
            other.reshape(half, DH, DH),
            late_tail,
            total,
        ),
        (16 * product, 22 * array, 4 * half * count * DH),
        "grads_within",
    )
    late = (mine_late, swap(mine_late))
    chip_out = spread(came, others, (gk_part,), False, "future")
    outgoing = (chip_out, [swap(state) for state in chip_out])
    def last(parity, extra_ins, extra_outs, shapes, args, aliases):
        return run(
            functools.partial(last_kernel, chips),
            steps,
            [tokens(parity)] * 4 + [whole] + [one_owner] * chips + extra_ins,
            extra_outs + [tokens(parity)] * 2,
            shapes,
            [half_states],
            (keys, values, gk_part, gv_part, late[parity], *outgoing[parity], *args),
            (2 * product, 9 * array, half * count * DH),
            f"grads_last_{parity}",
            aliases=aliases,
        )

    grad_keys, grad_values = last(0, [], [], [token_bf] * 2, (), {})
    attn_out, grad_keys, grad_values = last(
        1,
        [lane] + [untouched] * 3,
        [tokens(1)],
        [token_bf] * 3,
        (swap(mate_out), held_in_hbm(attn_half), grad_keys, grad_values),
        {8 + chips + j: j for j in range(3)},
    )
    return attn_out, grad_queries, grad_keys, grad_values


def solution(mesh):
    n_seq, n_head = mesh.shape["seq"], mesh.shape["head"]
    inner = 2 if n_seq % 2 == 0 else 1
    fine = Mesh(mesh.devices.reshape(n_seq // inner, inner, n_head), ("z", "x", "head"))
    rows = P(("z", "x", "head"), None)
    return jax.shard_map(
        local,
        mesh=fine,
        in_specs=(rows, rows, rows, rows, P()),
        out_specs=(rows, rows, rows, rows),
        check_vma=False,
    )
```

```python
import functools

import jax
import jax.numpy as jnp
from jax import lax
from jax.experimental import pallas as pl
from jax.experimental.pallas import tpu as pltpu
from jax.sharding import Mesh, PartitionSpec as P

DH = 128
F32 = jnp.float32
BF16 = jnp.bfloat16
NN = (((1,), (0,)), ((), ()))
NT = (((1,), (1,)), ((), ()))
LAYER = ("x", "head")


def mul(a, b, dims):
    return lax.dot_general(a, b, dims, preferred_element_type=F32)


def feature(wide):
    return jnp.where(wide > 0, wide + 1.0, jnp.exp(jnp.minimum(wide, 0.0)))


def slope(wide):
    return jnp.where(wide > 0, 1.0, jnp.exp(jnp.minimum(wide, 0.0)))


def doc_ends(lens):
    ends, total = [], 0
    for j in range(lens.shape[0]):
        total = total + lens[j]
        ends.append(total)
    return ends


def doc_at(ends, where):
    found = 0
    for end in ends:
        found = found + jnp.where(where >= end, 1, 0)
    return found


def rows_of(ends, first, count):
    at = first + lax.broadcasted_iota(jnp.int32, (count, 1), 0)
    return doc_at(ends, at)


def columns_of(ends, first, count):
    at = first + lax.broadcasted_iota(jnp.int32, (1, count), 1)
    return doc_at(ends, at)


def visible(ends, first, count):
    row = lax.broadcasted_iota(jnp.int32, (count, count), 0)
    column = lax.broadcasted_iota(jnp.int32, (count, count), 1)
    together = rows_of(ends, first, count) == columns_of(ends, first, count)
    return (row >= column) & together, (row <= column) & together


def identity(count):
    row = lax.broadcasted_iota(jnp.int32, (count, count), 0)
    column = lax.broadcasted_iota(jnp.int32, (count, count), 1)
    return jnp.where(row == column, 1.0, 0.0).astype(BF16)


def turn(array, eye):
    return mul(eye, array, NT).astype(BF16)


def head_mask(ends, first, count):
    return rows_of(ends, first, count) == doc_at(ends, first)


def tail_mask(ends, first, count):
    return rows_of(ends, first, count) == doc_at(ends, first + count - 1)


def cols(h):
    return slice(h * DH, (h + 1) * DH)


def bunches(heads, size=8):
    return [range(h, min(h + size, heads)) for h in range(0, heads, size)]


def halves(wide):
    high = wide.astype(BF16)
    return jnp.concatenate([high, (wide - high.astype(F32)).astype(BF16)], axis=1)


def tail_kernel(lens, place, k, v, *rest):
    if len(rest) > 1:
        q, g, out, three, last = rest
        three[0], three[1], three[2] = q[...], k[...], v[...]
        last[...] = g[...]
    else:
        (out,) = rest
    count = k.shape[0]
    tail = tail_mask(doc_ends(lens), place[0] * count, count)
    eye = identity(DH)
    for hs in bunches(out.shape[0]):
        fks = [
            jnp.where(tail, feature(k[:, cols(h)].astype(F32)), 0.0).astype(BF16) for h in hs
        ]
        turned = [turn(fk, eye) for fk in fks]
        sums = [mul(fk, v[:, cols(h)], NN).astype(BF16) for h, fk in zip(hs, turned)]
        for h, value in zip(hs, sums):
            out[h] = value


def pair_docs(lens, place, count):
    ends = doc_ends(lens)
    core = place[2] & 1
    own, mate = place[0] * count, (place[0] + 1 - 2 * core) * count

    def along(axis):
        shape = (2 * count, 1) if axis == 0 else (1, 2 * count)
        at = lax.broadcasted_iota(jnp.int32, shape, axis)
        return jnp.where(at < count, own + at, mate + at - count)

    rows, columns = along(0), along(1)
    row_docs, column_docs = doc_at(ends, rows), doc_at(ends, columns)
    seen = (rows >= columns) & (row_docs == column_docs)
    first = (place[0] - core) * count
    late = columns >= first + count
    return (
        seen,
        row_docs == doc_at(ends, first),
        column_docs == doc_at(ends, first),
        late & (column_docs == doc_at(ends, first + count)),
    )


def chip_kernel(lens, place, q, k, v, mate, part, head_fq, turned):
    count = q.shape[0]
    seen, head, _, _ = pair_docs(lens, place, count)
    eye = identity(DH)

    def both(mine, slot, h):
        return jnp.concatenate([mine[:, cols(h)], mate[slot, :, cols(h)]], axis=0)

    for hs in bunches(turned.shape[0], 4):
        wides = [feature(both(q, 0, h).astype(F32)) for h in hs]
        fks = [feature(both(k, 1, h).astype(F32)).astype(BF16) for h in hs]
        kept = [
            jnp.where(seen, mul(wide.astype(BF16), fk, NT), 0.0).astype(BF16)
            for wide, fk in zip(wides, fks)
        ]
        parts = [mul(s, both(v, 2, h), NN) for h, s in zip(hs, kept)]
        heads = [jnp.where(head, wide, 0.0).astype(BF16) for wide in wides]
        turns = [turn(wide.astype(BF16), eye) for wide in wides]
        for h, p, f, t in zip(hs, parts, heads, turns):
            part[:, cols(h)] = p
            head_fq[:, cols(h)] = f
            turned[h] = t


def norm_kernel(lens, place, head_fq, turned, g, mate_g, part, *rest):
    kept = rest[-1]
    chips = (len(rest) - 7) // 2
    incoming, (out, mate_out, ga_out, mate_ga, came, lates) = (
        rest[:chips],
        rest[chips : chips + 6],
    )
    states = rest[chips + 6 : -1]
    count = g.shape[0]
    _, _, head, late = pair_docs(lens, place, count)
    heads = turned.shape[0]
    step = pl.program_id(0)
    chip = place[2] >> 1

    @pl.when(step == 0)
    def _():
        for n, state in enumerate(incoming):
            owned = state.shape[0]
            came[pl.ds((chip ^ n) * owned, owned)] = state[...]

    weights = jnp.full((2 * DH, DH), 1.0 / DH, BF16)
    for hs in bunches(heads, 4):
        atts = [
            part[:, cols(h)] + mul(head_fq[:, cols(h)], came[step * heads + h], NN) for h in hs
        ]
        gos = [
            jnp.concatenate([g[:, cols(h)], mate_g[:, cols(h)]], axis=0).astype(F32) for h in hs
        ]
        means = [
            mul(jnp.concatenate([halves(att * att), halves(go * att)], axis=0), weights, NN)
            for att, go in zip(atts, gos)
        ]
        invs = [lax.rsqrt(m[: 2 * count] + 1e-05) for m in means]
        norms = [att * inv for att, inv in zip(atts, invs)]
        gas = [
            ((go - normed * (m[2 * count :] * inv)) * inv).astype(BF16)
            for go, normed, m, inv in zip(gos, norms, means, invs)
        ]
        sums = []
        for h, ga in zip(hs, gas):
            wide = turned[h].astype(F32)
            two = jnp.concatenate([jnp.where(head, wide, 0.0), jnp.where(late, wide, 0.0)], axis=0)
            sums.append(mul(two.astype(BF16), ga, NN).astype(BF16))
        for h, normed, ga, value in zip(hs, norms, gas, sums):
            normed = normed.astype(BF16)
            out[:, cols(h)], mate_out[:, cols(h)] = normed[:count], normed[count:]
            ga_out[:, cols(h)], mate_ga[:, cols(h)] = ga[:count], ga[count:]
            kept[step * heads + h] = value[:DH]
            lates[h] = value[DH:]

    @pl.when(step == pl.num_programs(0) - 1)
    def _():
        for n, state in enumerate(states):
            owned = state.shape[0]
            state[...] = kept[pl.ds((chip ^ n) * owned, owned)]


def inner_kernel(lens, place, q, k, v, mine_ga, other_ga, *rest):
    passed, earlier, (gq, gk, gv, came) = rest[:2], rest[2:4], rest[5:]
    count = q.shape[0]
    heads = q.shape[1] // DH
    step = pl.program_id(0)
    own = step < pl.num_programs(0) // 2

    @pl.when(step == 0)
    def _():
        half = came.shape[0] // 2
        core, (early_b, early_e, late_b, late_e) = chip_docs(lens, place, count)
        by_chip = jnp.where(core == 0, 1.0, same(late_b, early_b))
        by_mate = jnp.where(core == 0, 0.0, same(late_b, early_e))
        for j in range(2):
            came[pl.ds(j * half, half)] = (
                passed[j][...].astype(F32) * by_chip + earlier[j][...].astype(F32) * by_mate
            ).astype(BF16)

    ends = doc_ends(lens)
    first = place[0] * count
    seen, seeing = visible(ends, first, count)
    head = head_mask(ends, first, count)
    for hs in bunches(heads):
        wides = [q[:, cols(h)].astype(F32) for h in hs]
        fqs = [feature(wide).astype(BF16) for wide in wides]
        fks = [feature(k[:, cols(h)].astype(F32)).astype(BF16) for h in hs]
        gas = [jnp.where(own, mine_ga[:, cols(h)], other_ga[:, cols(h)]) for h in hs]
        gss = [
            jnp.where(seen, mul(ga, v[:, cols(h)], NT), 0.0).astype(BF16)
            for h, ga in zip(hs, gas)
        ]
        totals = [
            mul(gs, fk, NN) + jnp.where(head, mul(ga, came[step * heads + h], NT), 0.0)
            for h, gs, fk, ga in zip(hs, gss, fks, gas)
        ]
        flipped = [
            jnp.where(seeing, mul(v[:, cols(h)], ga, NT), 0.0).astype(BF16)
            for h, ga in zip(hs, gas)
        ]
        scores = [
            jnp.where(seeing, mul(fk, fq, NT), 0.0).astype(BF16) for fq, fk in zip(fqs, fks)
        ]
        gks = [mul(gs, fq, NN) for gs, fq in zip(flipped, fqs)]
        gvs = [mul(s, ga, NN) for s, ga in zip(scores, gas)]
        for h, total, wide, a, b in zip(hs, totals, wides, gks, gvs):
            gq[:, cols(h)] = (total * slope(wide)).astype(BF16)
            gk[:, cols(h)] = a
            gv[:, cols(h)] = b


def last_kernel(chips, lens, place, k, v, gk_part, gv_part, late, *rest):
    came = rest[-1]
    outgoing, gk, gv = rest[:chips], rest[-3], rest[-2]
    if len(rest) > chips + 3:
        rest[-4][...] = rest[chips][...]
        gk, gv = rest[-3], rest[-2]
    count = k.shape[0]
    heads = k.shape[1] // DH
    step = pl.program_id(0)

    @pl.when(step == 0)
    def _():
        core, (early_b, early_e, late_b, late_e) = chip_docs(lens, place, count)
        chip = place[2] >> 1
        by_far = jnp.where(core == 0, same(early_e, late_e), 1.0)
        by_late = jnp.where(core == 0, same(early_e, late_b), 0.0)
        for n, state in enumerate(outgoing):
            owned = state.shape[0]
            at = pl.ds((chip ^ n) * owned, owned)
            came[at] = (
                state[...].astype(F32) * by_far + late[at].astype(F32) * by_late
            ).astype(BF16)

    tail = tail_mask(doc_ends(lens), place[0] * count, count)
    for hs in bunches(heads):
        wides = [k[:, cols(h)].astype(F32) for h in hs]
        fks = [jnp.where(tail, feature(wide), 0.0).astype(BF16) for wide in wides]
        vts = [jnp.where(tail, v[:, cols(h)].astype(F32), 0.0).astype(BF16) for h in hs]
        states = [came[step * heads + h] for h in hs]
        gks = [gk_part[:, cols(h)] + mul(vt, o, NT) for h, vt, o in zip(hs, vts, states)]
        gvs = [gv_part[:, cols(h)] + mul(fk, o, NN) for h, fk, o in zip(hs, fks, states)]
        for h, a, wide, b in zip(hs, gks, wides, gvs):
            gk[:, cols(h)] = (a * slope(wide)).astype(BF16)
            gv[:, cols(h)] = b.astype(BF16)


def same(a, b):
    return jnp.where(a == b, 1.0, 0.0).astype(F32)


def chip_docs(lens, place, count):
    ends = doc_ends(lens)
    core = place[2] & 1
    start = (place[0] - core) * count
    marks = (start, start + count - 1, start + count, start + 2 * count - 1)
    return core, [doc_at(ends, mark) for mark in marks]


def merge_kernel(count, lens, place, mine, other, *outs):
    core, (early_b, early_e, late_b, late_e) = chip_docs(lens, place, count)
    far = same(early_e, late_e)
    mine_by = jnp.where(core == 0, far, 1.0)
    other_by = jnp.where(core == 0, 1.0, far)
    chip = place[2] >> 1
    for n, out in enumerate(outs):
        at = chip ^ n
        out[...] = (mine[at].astype(F32) * mine_by + other[at].astype(F32) * other_by).astype(
            BF16
        )


def total_kernel(forward, unit, members, passed, lens, place, *rest):
    states, total, held = rest[:members], rest[members + passed], rest[-1]
    chip = place[2] >> 1
    for n, state in enumerate(states):
        held[chip ^ n] = state[...]
    ends = doc_ends(lens)
    layer = place[1] * (members * unit)
    carry = None
    for step in range(members):
        i = step if forward else members - 1 - step
        mine = held[i].astype(F32)
        edge = layer + ((i + 1) * unit - 1 if forward else i * unit)
        here = doc_at(ends, edge)
        if carry is not None:
            mine = mine + carry * same(here, previous)
        carry, previous = mine, here
    total[...] = carry.astype(BF16)


def prefix_kernel(forward, unit, members, unread, lens, place, *rest):
    states, outs, (held, sums) = rest[:members], rest[-members - 2 : -2], rest[-2:]
    others = rest[members + unread : -members - 2]
    chip = place[2] >> 1
    for n, state in enumerate(states):
        held[chip ^ n] = state[...]
    span = members * unit
    ends = doc_ends(lens)
    layer = place[1] * span
    sign = -1 if forward else 1
    previous = doc_at(ends, layer - 1 if forward else layer + span)
    carry = None
    for s, other in enumerate(others):
        far = layer + sign * s * span
        there = doc_at(ends, far - 1 if forward else far + span)
        term = other[...].astype(F32) * same(there, previous)
        carry = term if carry is None else carry + term
    for step in range(members):
        i = step if forward else members - 1 - step
        near, far = layer + i * unit, layer + (i + 1) * unit - 1
        if not forward:
            near, far = far, near
        if carry is None:
            sums[i] = jnp.zeros(sums.shape[1:], BF16)
        else:
            sums[i] = (carry * same(doc_at(ends, near), previous)).astype(BF16)
        if step < members - 1:
            here = doc_at(ends, far)
            mine = held[i].astype(F32)
            if carry is not None:
                mine = mine + carry * same(here, previous)
            carry, previous = mine, here
    for n, out in enumerate(outs):
        out[...] = sums[chip ^ n]


SMALL = pltpu.CompilerParams(
    dimension_semantics=("arbitrary",), vmem_limit_bytes=16 * 1024 * 1024
)

def local(queries, keys, values, out_grad, doc_lengths):
    count, width = queries.shape
    heads = width // DH
    layers = lax.axis_size("z")
    members = lax.axis_size("x") * lax.axis_size("head")
    owned = heads // members
    half = heads // 2
    reach = range(1, min(layers - 1, -(-layers // 2)) + 1)
    place = jnp.stack(
        [lax.axis_index(("z", "x", "head")), lax.axis_index("z"), lax.axis_index(LAYER)]
    ).astype(jnp.int32)
    chips = members // 2
    step_heads = max(n for n in (8, 4, 2, 1) if half % n == 0)
    steps = half // step_heads

    def held_in_hbm(arg):
        return pltpu.with_memory_space_constraint(arg, pltpu.HBM)

    def at(parity):
        if parity is None:
            return lambda i, lens, place: i
        return lambda i, lens, place: ((place[2] & 1) ^ parity) * steps + i

    def tokens(parity):
        block = at(parity)
        return pl.BlockSpec((count, step_heads * DH), lambda *a: (0, block(*a)))

    whole = pl.BlockSpec(memory_space=pltpu.VMEM)
    halved = pl.BlockSpec((step_heads, DH, DH), lambda i, *a: (i, 0, 0))
    untouched = pl.BlockSpec(memory_space=pl.ANY)
    token_bf = pltpu.HBM((count, width), BF16)
    token_f32 = jax.ShapeDtypeStruct((count, width), F32)
    owned_bf = jax.ShapeDtypeStruct((owned, DH, DH), BF16)
    half_bf = jax.ShapeDtypeStruct((half, DH, DH), BF16)

    def run(kernel, grid, ins, outs, shapes, scratch, args, cost, name, aliases={}, lens=None):
        flops, moved, exps = cost
        return pl.pallas_call(
            kernel,
            grid_spec=pltpu.PrefetchScalarGridSpec(
                num_scalar_prefetch=2,
                grid=(grid,),
                in_specs=ins,
                out_specs=outs,
                scratch_shapes=scratch,
            ),
            out_shape=shapes,
            input_output_aliases=aliases,
            compiler_params=SMALL,
            cost_estimate=pl.CostEstimate(
                flops=flops, bytes_accessed=moved, transcendentals=exps
            ),
            name=name,
        )(doc_lengths if lens is None else lens, place, *args)

    product = 2 * half * count * DH * DH
    array = half * count * DH * 2
    all_states = pltpu.VMEM((heads, DH, DH), BF16)
    block = owned
    single = grouped = whole
    buffer = pltpu.VMEM((chips, block, DH, DH), BF16)
    combining = (4 * half * DH * DH, 4 * half * DH * DH, 0)
    moves = 1

    def swap(state):
        return lax.ppermute(state, LAYER, [(i, i ^ 1) for i in range(members)])

    def exchange(states):
        pairs = [[(i, i ^ (2 * n)) for i in range(members)] for n in range(chips)]
        return [
            state if n == 0 else lax.ppermute(state, LAYER, pairs[n])
            for n, state in enumerate(states)
        ]

    def reach_out(merged, along, forward, name):
        came = exchange(merged)
        total, *along = run(
            functools.partial(total_kernel, forward, 2 * count, chips, len(along)),
            moves,
            [single] * chips + [untouched] * len(along),
            [single] + [untouched] * len(along),
            [owned_bf] + [jax.ShapeDtypeStruct(array.shape, array.dtype) for array in along],
            [buffer],
            [*came, *along],
            combining,
            name + "_total",
            aliases={2 + chips + j: 1 + j for j in range(len(along))},
        )
        others = []
        for s in reversed(reach):
            pairs = [(i, i + s) if forward else (i + s, i) for i in range(layers - s)]
            others.insert(0, lax.ppermute(total, "z", pairs))
        return came, others, total, along

    def spread(came, others, after, forward, name):
        sums = run(
            functools.partial(prefix_kernel, forward, 2 * count, chips, len(after)),
            moves,
            [single] * chips + [untouched] * len(after) + [single] * len(others),
            [single] * chips,
            [owned_bf] * chips,
            [buffer, buffer],
            [*came, *after, *others],
            combining,
            name + "_prefix",
        )
        return exchange(sums)

    narrow = (count, half * DH)
    lane = pl.BlockSpec((count, step_heads * DH), lambda i, *a: (0, i))
    pinned = [held_in_hbm(array) for array in (queries, keys, values, out_grad)]
    tail_work = (product, 3 * array, half * count * DH)
    copies = [
        jax.ShapeDtypeStruct((3, *narrow), BF16),
        jax.ShapeDtypeStruct(narrow, BF16),
    ]
    mate_tail, mate_three, mate_g = run(
        tail_kernel,
        steps,
        [tokens(1)] * 4,
        [halved, pl.BlockSpec((3, count, step_heads * DH), lambda i, *a: (0, 0, i)), lane],
        [half_bf, *copies],
        [],
        (pinned[1], pinned[2], pinned[0], pinned[3]),
        tail_work,
        "tail_mate",
        lens=held_in_hbm(doc_lengths),
    )
    (own_tail,) = run(
        tail_kernel,
        steps,
        [tokens(0)] * 2,
        [halved],
        [half_bf],
        [],
        pinned[1:3],
        tail_work,
        "tail_own",
        lens=held_in_hbm(doc_lengths),
    )
    mine = own_tail.reshape(chips, owned, DH, DH)
    other = swap(mate_tail).reshape(chips, owned, DH, DH)
    merged = run(
        functools.partial(merge_kernel, count),
        moves,
        [grouped] * 2,
        [single] * chips,
        [owned_bf] * chips,
        [],
        (mine, other),
        combining,
        "carried_chip",
    )
    came, others, _, (mate_three, mate_g, own_tail) = reach_out(
        merged, (mate_three, mate_g, own_tail), True, "carried"
    )
    mate_three, mate_g = swap(mate_three), swap(mate_g)
    few = 4 if half % 4 == 0 else 1
    parts = half // few

    def own_few(i, lens, place):
        return 0, (place[2] & 1) * parts + i

    own_tokens = pl.BlockSpec((count, few * DH), own_few)
    pair_tokens = pl.BlockSpec((2 * count, few * DH), lambda i, *a: (0, i))
    lane_few = pl.BlockSpec((count, few * DH), lambda i, *a: (0, i))
    turns = pl.BlockSpec((few, DH, 2 * count), lambda i, *a: (i, 0, 0))
    part, head_fq, turned = run(
        chip_kernel,
        parts,
        [own_tokens] * 3 + [pl.BlockSpec((3, count, few * DH), lambda i, *a: (0, 0, i))],
        [pair_tokens, pair_tokens, turns],
        [
            jax.ShapeDtypeStruct((2 * count, half * DH), F32),
            jax.ShapeDtypeStruct((2 * count, half * DH), BF16),
            jax.ShapeDtypeStruct((half, DH, 2 * count), BF16),
        ],
        [],
        (queries, keys, values, mate_three),
        (10 * product, 14 * array, 4 * half * count * DH),
        "within_chip",
    )
    late_tail = swap(own_tail)
    chip_in = spread(came, others, (part, late_tail), True, "carried")
    few_states = pl.BlockSpec((few, DH, DH), lambda i, *a: (i, 0, 0))
    one_owner = whole
    half_states = pltpu.VMEM((half, DH, DH), BF16)
    narrow_bf = jax.ShapeDtypeStruct(narrow, BF16)
    attn_half, mate_out, mine_ga, mate_ga, mine_in, mine_late, *merged = run(
        norm_kernel,
        parts,
        [pair_tokens, turns, own_tokens, lane_few, pair_tokens] + [one_owner] * chips,
        [own_tokens] + [lane_few] * 3 + [whole, few_states] + [one_owner] * chips,
        [token_bf] + [narrow_bf] * 3 + [half_bf] * 2 + [owned_bf] * chips,
        [half_states],
        (head_fq, turned, out_grad, mate_g, part, *chip_in),
        (8 * product, 16 * array, 2 * half * count * DH),
        "normed",
    )
    came, others, total, (mate_out, mine_late) = reach_out(
        merged, (mate_out, mine_late), False, "future"
    )
    other_ga, other_in = swap(mate_ga), swap(mine_in)
    other_ga = swap(mate_ga)
    def both(i, lens, place):
        return ((place[2] & 1) ^ (i // steps)) * steps + i % steps

    spans = pl.BlockSpec((count, step_heads * DH), lambda *a: (0, both(*a)))
    lanes = pl.BlockSpec((count, step_heads * DH), lambda i, *a: (0, i % steps))
    grad_queries, gk_part, gv_part = run(
        inner_kernel,
        2 * steps,
        [spans] * 3 + [lanes] * 2 + [whole] * 4 + [untouched],
        [spans] * 3,
        [token_bf, token_f32, token_f32],
        [all_states],
        (
            queries,
            keys,
            values,
            mine_ga,
            other_ga,
            mine_in,
            other_in,
            other.reshape(half, DH, DH),
            late_tail,
            total,
        ),
        (16 * product, 22 * array, 4 * half * count * DH),
        "grads_within",
    )
    late = (mine_late, swap(mine_late))
    chip_out = spread(came, others, (gk_part,), False, "future")
    outgoing = (chip_out, [swap(state) for state in chip_out])
    def last(parity, extra_ins, extra_outs, shapes, args, aliases):
        return run(
            functools.partial(last_kernel, chips),
            steps,
            [tokens(parity)] * 4 + [whole] + [one_owner] * chips + extra_ins,
            extra_outs + [tokens(parity)] * 2,
            shapes,
            [half_states],
            (keys, values, gk_part, gv_part, late[parity], *outgoing[parity], *args),
            (2 * product, 9 * array, half * count * DH),
            f"grads_last_{parity}",
            aliases=aliases,
        )

    grad_keys, grad_values = last(0, [], [], [token_bf] * 2, (), {})
    attn_out, grad_keys, grad_values = last(
        1,
        [lane] + [untouched] * 3,
        [tokens(1)],
        [token_bf] * 3,
        (swap(mate_out), held_in_hbm(attn_half), grad_keys, grad_values),
        {8 + chips + j: j for j in range(3)},
    )
    return attn_out, grad_queries, grad_keys, grad_values


def solution(mesh):
    n_seq, n_head = mesh.shape["seq"], mesh.shape["head"]
    inner = 2 if n_seq % 2 == 0 else 1
    fine = Mesh(mesh.devices.reshape(n_seq // inner, inner, n_head), ("z", "x", "head"))
    rows = P(("z", "x", "head"), None)
    return jax.shard_map(
        local,
        mesh=fine,
        in_specs=(rows, rows, rows, rows, P()),
        out_specs=(rows, rows, rows, rows),
        check_vma=False,
    )
```

```python
import functools

import jax
import jax.numpy as jnp
from jax import lax
from jax.experimental import pallas as pl
from jax.experimental.pallas import tpu as pltpu
from jax.sharding import Mesh, PartitionSpec as P

DH = 128
F32 = jnp.float32
BF16 = jnp.bfloat16
NN = (((1,), (0,)), ((), ()))
NT = (((1,), (1,)), ((), ()))
LAYER = ("x", "head")


def mul(a, b, dims):
    return lax.dot_general(a, b, dims, preferred_element_type=F32)


def feature(wide):
    return jnp.where(wide > 0, wide + 1.0, jnp.exp(jnp.minimum(wide, 0.0)))


def slope(wide):
    return jnp.where(wide > 0, 1.0, jnp.exp(jnp.minimum(wide, 0.0)))


def doc_ends(lens):
    ends, total = [], 0
    for j in range(lens.shape[0]):
        total = total + lens[j]
        ends.append(total)
    return ends


def doc_at(ends, where):
    found = 0
    for end in ends:
        found = found + jnp.where(where >= end, 1, 0)
    return found


def rows_of(ends, first, count):
    at = first + lax.broadcasted_iota(jnp.int32, (count, 1), 0)
    return doc_at(ends, at)


def columns_of(ends, first, count):
    at = first + lax.broadcasted_iota(jnp.int32, (1, count), 1)
    return doc_at(ends, at)


def visible(ends, first, count):
    row = lax.broadcasted_iota(jnp.int32, (count, count), 0)
    column = lax.broadcasted_iota(jnp.int32, (count, count), 1)
    together = rows_of(ends, first, count) == columns_of(ends, first, count)
    return (row >= column) & together, (row <= column) & together


def identity(count):
    row = lax.broadcasted_iota(jnp.int32, (count, count), 0)
    column = lax.broadcasted_iota(jnp.int32, (count, count), 1)
    return jnp.where(row == column, 1.0, 0.0).astype(BF16)


def turn(array, eye):
    return mul(eye, array, NT).astype(BF16)


def head_mask(ends, first, count):
    return rows_of(ends, first, count) == doc_at(ends, first)


def tail_mask(ends, first, count):
    return rows_of(ends, first, count) == doc_at(ends, first + count - 1)


def cols(h):
    return slice(h * DH, (h + 1) * DH)


def bunches(heads, size=8):
    return [range(h, min(h + size, heads)) for h in range(0, heads, size)]


def halves(wide):
    high = wide.astype(BF16)
    return jnp.concatenate([high, (wide - high.astype(F32)).astype(BF16)], axis=1)


def tail_kernel(lens, place, k, v, *rest):
    if len(rest) > 1:
        q, g, out, three, last = rest
        three[0], three[1], three[2] = q[...], k[...], v[...]
        last[...] = g[...]
    else:
        (out,) = rest
    count = k.shape[0]
    tail = tail_mask(doc_ends(lens), place[0] * count, count)
    eye = identity(DH)
    for hs in bunches(out.shape[0]):
        fks = [
            jnp.where(tail, feature(k[:, cols(h)].astype(F32)), 0.0).astype(BF16) for h in hs
        ]
        turned = [turn(fk, eye) for fk in fks]
        sums = [mul(fk, v[:, cols(h)], NN).astype(BF16) for h, fk in zip(hs, turned)]
        for h, value in zip(hs, sums):
            out[h] = value


def pair_docs(lens, place, count):
    ends = doc_ends(lens)
    core = place[2] & 1
    own, mate = place[0] * count, (place[0] + 1 - 2 * core) * count

    def along(axis):
        shape = (2 * count, 1) if axis == 0 else (1, 2 * count)
        at = lax.broadcasted_iota(jnp.int32, shape, axis)
        return jnp.where(at < count, own + at, mate + at - count)

    rows, columns = along(0), along(1)
    row_docs, column_docs = doc_at(ends, rows), doc_at(ends, columns)
    seen = (rows >= columns) & (row_docs == column_docs)
    first = (place[0] - core) * count
    late = columns >= first + count
    return (
        seen,
        row_docs == doc_at(ends, first),
        column_docs == doc_at(ends, first),
        late & (column_docs == doc_at(ends, first + count)),
    )


def chip_kernel(lens, place, q, k, v, mate, part, head_fq, turned):
    count = q.shape[0]
    seen, head, _, _ = pair_docs(lens, place, count)
    eye = identity(DH)

    def both(mine, slot, h):
        return jnp.concatenate([mine[:, cols(h)], mate[slot, :, cols(h)]], axis=0)

    for hs in bunches(turned.shape[0], 4):
        wides = [feature(both(q, 0, h).astype(F32)) for h in hs]
        fks = [feature(both(k, 1, h).astype(F32)).astype(BF16) for h in hs]
        kept = [
            jnp.where(seen, mul(wide.astype(BF16), fk, NT), 0.0).astype(BF16)
            for wide, fk in zip(wides, fks)
        ]
        parts = [mul(s, both(v, 2, h), NN) for h, s in zip(hs, kept)]
        heads = [jnp.where(head, wide, 0.0).astype(BF16) for wide in wides]
        turns = [turn(wide.astype(BF16), eye) for wide in wides]
        for h, p, f, t in zip(hs, parts, heads, turns):
            part[:, cols(h)] = p
            head_fq[:, cols(h)] = f
            turned[h] = t


def norm_kernel(lens, place, head_fq, turned, g, mate_g, part, *rest):
    kept = rest[-1]
    chips = (len(rest) - 9) // 2
    incoming, (out, mate_out, ga_out, mate_ga, came, lates, sent_in, sent_late) = (
        rest[:chips],
        rest[chips : chips + 8],
    )
    states = rest[chips + 8 : -1]
    count = g.shape[0]
    _, _, head, late = pair_docs(lens, place, count)
    heads = turned.shape[0]
    step = pl.program_id(0)
    chip = place[2] >> 1

    @pl.when(step == 0)
    def _():
        for n, state in enumerate(incoming):
            owned = state.shape[0]
            came[pl.ds((chip ^ n) * owned, owned)] = state[...]
            sent_in[pl.ds((chip ^ n) * owned, owned)] = state[...]

    weights = jnp.full((2 * DH, DH), 1.0 / DH, BF16)
    for hs in bunches(heads, 4):
        atts = [
            part[:, cols(h)] + mul(head_fq[:, cols(h)], came[step * heads + h], NN) for h in hs
        ]
        gos = [
            jnp.concatenate([g[:, cols(h)], mate_g[:, cols(h)]], axis=0).astype(F32) for h in hs
        ]
        means = [
            mul(jnp.concatenate([halves(att * att), halves(go * att)], axis=0), weights, NN)
            for att, go in zip(atts, gos)
        ]
        invs = [lax.rsqrt(m[: 2 * count] + 1e-05) for m in means]
        norms = [att * inv for att, inv in zip(atts, invs)]
        gas = [
            ((go - normed * (m[2 * count :] * inv)) * inv).astype(BF16)
            for go, normed, m, inv in zip(gos, norms, means, invs)
        ]
        sums = []
        for h, ga in zip(hs, gas):
            wide = turned[h].astype(F32)
            two = jnp.concatenate([jnp.where(head, wide, 0.0), jnp.where(late, wide, 0.0)], axis=0)
            sums.append(mul(two.astype(BF16), ga, NN).astype(BF16))
        for h, normed, ga, value in zip(hs, norms, gas, sums):
            normed = normed.astype(BF16)
            out[:, cols(h)], mate_out[:, cols(h)] = normed[:count], normed[count:]
            ga_out[:, cols(h)], mate_ga[:, cols(h)] = ga[:count], ga[count:]
            kept[step * heads + h] = value[:DH]
            lates[h] = value[DH:]
            sent_late[h] = value[DH:]

    @pl.when(step == pl.num_programs(0) - 1)
    def _():
        for n, state in enumerate(states):
            owned = state.shape[0]
            state[...] = kept[pl.ds((chip ^ n) * owned, owned)]


def inner_kernel(lens, place, q, k, v, mine_ga, other_ga, *rest):
    passed, earlier, (gq, gk, gv, _, _, came) = rest[:2], rest[2:4], rest[7:]
    count = q.shape[0]
    heads = q.shape[1] // DH
    step = pl.program_id(0)
    own = step < pl.num_programs(0) // 2

    @pl.when(step == 0)
    def _():
        half = came.shape[0] // 2
        core, (early_b, early_e, late_b, late_e) = chip_docs(lens, place, count)
        by_chip = jnp.where(core == 0, 1.0, same(late_b, early_b))
        by_mate = jnp.where(core == 0, 0.0, same(late_b, early_e))
        for j in range(2):
            came[pl.ds(j * half, half)] = (
                passed[j][...].astype(F32) * by_chip + earlier[j][...].astype(F32) * by_mate
            ).astype(BF16)

    ends = doc_ends(lens)
    first = place[0] * count
    seen, seeing = visible(ends, first, count)
    head = head_mask(ends, first, count)
    for hs in bunches(heads):
        wides = [q[:, cols(h)].astype(F32) for h in hs]
        fqs = [feature(wide).astype(BF16) for wide in wides]
        fks = [feature(k[:, cols(h)].astype(F32)).astype(BF16) for h in hs]
        gas = [jnp.where(own, mine_ga[:, cols(h)], other_ga[:, cols(h)]) for h in hs]
        gss = [
            jnp.where(seen, mul(ga, v[:, cols(h)], NT), 0.0).astype(BF16)
            for h, ga in zip(hs, gas)
        ]
        totals = [
            mul(gs, fk, NN) + jnp.where(head, mul(ga, came[step * heads + h], NT), 0.0)
            for h, gs, fk, ga in zip(hs, gss, fks, gas)
        ]
        flipped = [
            jnp.where(seeing, mul(v[:, cols(h)], ga, NT), 0.0).astype(BF16)
            for h, ga in zip(hs, gas)
        ]
        scores = [
            jnp.where(seeing, mul(fk, fq, NT), 0.0).astype(BF16) for fq, fk in zip(fqs, fks)
        ]
        gks = [mul(gs, fq, NN) for gs, fq in zip(flipped, fqs)]
        gvs = [mul(s, ga, NN) for s, ga in zip(scores, gas)]
        for h, total, wide, a, b in zip(hs, totals, wides, gks, gvs):
            gq[:, cols(h)] = (total * slope(wide)).astype(BF16)
            gk[:, cols(h)] = a
            gv[:, cols(h)] = b


def last_kernel(chips, lens, place, k, v, gk_part, gv_part, late, *rest):
    came = rest[-1]
    outgoing, gk, gv = rest[:chips], rest[-3], rest[-2]
    if len(rest) > chips + 3:
        rest[-4][...] = rest[chips][...]
        gk, gv = rest[-3], rest[-2]
    count = k.shape[0]
    heads = k.shape[1] // DH
    step = pl.program_id(0)

    @pl.when(step == 0)
    def _():
        core, (early_b, early_e, late_b, late_e) = chip_docs(lens, place, count)
        chip = place[2] >> 1
        by_far = jnp.where(core == 0, same(early_e, late_e), 1.0)
        by_late = jnp.where(core == 0, same(early_e, late_b), 0.0)
        for n, state in enumerate(outgoing):
            owned = state.shape[0]
            at = pl.ds((chip ^ n) * owned, owned)
            came[at] = (
                state[...].astype(F32) * by_far + late[at].astype(F32) * by_late
            ).astype(BF16)

    tail = tail_mask(doc_ends(lens), place[0] * count, count)
    for hs in bunches(heads):
        wides = [k[:, cols(h)].astype(F32) for h in hs]
        fks = [jnp.where(tail, feature(wide), 0.0).astype(BF16) for wide in wides]
        vts = [jnp.where(tail, v[:, cols(h)].astype(F32), 0.0).astype(BF16) for h in hs]
        states = [came[step * heads + h] for h in hs]
        gks = [gk_part[:, cols(h)] + mul(vt, o, NT) for h, vt, o in zip(hs, vts, states)]
        gvs = [gv_part[:, cols(h)] + mul(fk, o, NN) for h, fk, o in zip(hs, fks, states)]
        for h, a, wide, b in zip(hs, gks, wides, gvs):
            gk[:, cols(h)] = (a * slope(wide)).astype(BF16)
            gv[:, cols(h)] = b.astype(BF16)


def same(a, b):
    return jnp.where(a == b, 1.0, 0.0).astype(F32)


def chip_docs(lens, place, count):
    ends = doc_ends(lens)
    core = place[2] & 1
    start = (place[0] - core) * count
    marks = (start, start + count - 1, start + count, start + 2 * count - 1)
    return core, [doc_at(ends, mark) for mark in marks]


def merge_kernel(count, lens, place, mine, other, _, *outs):
    outs = outs[:-1]
    core, (early_b, early_e, late_b, late_e) = chip_docs(lens, place, count)
    far = same(early_e, late_e)
    mine_by = jnp.where(core == 0, far, 1.0)
    other_by = jnp.where(core == 0, 1.0, far)
    chip = place[2] >> 1
    for n, out in enumerate(outs):
        at = chip ^ n
        out[...] = (mine[at].astype(F32) * mine_by + other[at].astype(F32) * other_by).astype(
            BF16
        )


def total_kernel(forward, unit, members, passed, lens, place, *rest):
    states, total, held = rest[:members], rest[members + passed], rest[-1]
    chip = place[2] >> 1
    for n, state in enumerate(states):
        held[chip ^ n] = state[...]
    ends = doc_ends(lens)
    layer = place[1] * (members * unit)
    carry = None
    for step in range(members):
        i = step if forward else members - 1 - step
        mine = held[i].astype(F32)
        edge = layer + ((i + 1) * unit - 1 if forward else i * unit)
        here = doc_at(ends, edge)
        if carry is not None:
            mine = mine + carry * same(here, previous)
        carry, previous = mine, here
    total[...] = carry.astype(BF16)


def prefix_kernel(forward, unit, members, unread, lens, place, *rest):
    states, outs, (held, sums) = rest[:members], rest[-members - 2 : -2], rest[-2:]
    others = rest[members + unread : -members - 2]
    chip = place[2] >> 1
    for n, state in enumerate(states):
        held[chip ^ n] = state[...]
    span = members * unit
    ends = doc_ends(lens)
    layer = place[1] * span
    sign = -1 if forward else 1
    previous = doc_at(ends, layer - 1 if forward else layer + span)
    carry = None
    for s, other in enumerate(others):
        far = layer + sign * s * span
        there = doc_at(ends, far - 1 if forward else far + span)
        term = other[...].astype(F32) * same(there, previous)
        carry = term if carry is None else carry + term
    for step in range(members):
        i = step if forward else members - 1 - step
        near, far = layer + i * unit, layer + (i + 1) * unit - 1
        if not forward:
            near, far = far, near
        if carry is None:
            sums[i] = jnp.zeros(sums.shape[1:], BF16)
        else:
            sums[i] = (carry * same(doc_at(ends, near), previous)).astype(BF16)
        if step < members - 1:
            here = doc_at(ends, far)
            mine = held[i].astype(F32)
            if carry is not None:
                mine = mine + carry * same(here, previous)
            carry, previous = mine, here
    for n, out in enumerate(outs):
        out[...] = sums[chip ^ n]


SMALL = pltpu.CompilerParams(
    dimension_semantics=("arbitrary",), vmem_limit_bytes=16 * 1024 * 1024
)

def local(queries, keys, values, out_grad, doc_lengths):
    count, width = queries.shape
    heads = width // DH
    layers = lax.axis_size("z")
    members = lax.axis_size("x") * lax.axis_size("head")
    owned = heads // members
    half = heads // 2
    reach = range(1, min(layers - 1, -(-layers // 2)) + 1)
    place = jnp.stack(
        [lax.axis_index(("z", "x", "head")), lax.axis_index("z"), lax.axis_index(LAYER)]
    ).astype(jnp.int32)
    chips = members // 2
    step_heads = max(n for n in (8, 4, 2, 1) if half % n == 0)
    steps = half // step_heads

    def held_in_hbm(arg):
        return pltpu.with_memory_space_constraint(arg, pltpu.HBM)

    def at(parity):
        if parity is None:
            return lambda i, lens, place: i
        return lambda i, lens, place: ((place[2] & 1) ^ parity) * steps + i

    def tokens(parity):
        block = at(parity)
        return pl.BlockSpec((count, step_heads * DH), lambda *a: (0, block(*a)))

    whole = pl.BlockSpec(memory_space=pltpu.VMEM)
    halved = pl.BlockSpec((step_heads, DH, DH), lambda i, *a: (i, 0, 0))
    untouched = pl.BlockSpec(memory_space=pl.ANY)
    token_bf = pltpu.HBM((count, width), BF16)
    token_f32 = jax.ShapeDtypeStruct((count, width), F32)
    owned_bf = jax.ShapeDtypeStruct((owned, DH, DH), BF16)
    half_bf = jax.ShapeDtypeStruct((half, DH, DH), BF16)

    def run(kernel, grid, ins, outs, shapes, scratch, args, cost, name, aliases={}, lens=None):
        flops, moved, exps = cost
        return pl.pallas_call(
            kernel,
            grid_spec=pltpu.PrefetchScalarGridSpec(
                num_scalar_prefetch=2,
                grid=(grid,),
                in_specs=ins,
                out_specs=outs,
                scratch_shapes=scratch,
            ),
            out_shape=shapes,
            input_output_aliases=aliases,
            compiler_params=SMALL,
            cost_estimate=pl.CostEstimate(
                flops=flops, bytes_accessed=moved, transcendentals=exps
            ),
            name=name,
        )(doc_lengths if lens is None else lens, place, *args)

    product = 2 * half * count * DH * DH
    array = half * count * DH * 2
    all_states = pltpu.VMEM((heads, DH, DH), BF16)
    block = owned
    single = grouped = whole
    buffer = pltpu.VMEM((chips, block, DH, DH), BF16)
    combining = (4 * half * DH * DH, 4 * half * DH * DH, 0)
    moves = 1

    def swap(state):
        return lax.ppermute(state, LAYER, [(i, i ^ 1) for i in range(members)])

    def exchange(states):
        pairs = [[(i, i ^ (2 * n)) for i in range(members)] for n in range(chips)]
        return [
            state if n == 0 else lax.ppermute(state, LAYER, pairs[n])
            for n, state in enumerate(states)
        ]

    def reach_out(merged, along, forward, name):
        came = exchange(merged)
        total, *along = run(
            functools.partial(total_kernel, forward, 2 * count, chips, len(along)),
            moves,
            [single] * chips + [untouched] * len(along),
            [single] + [untouched] * len(along),
            [owned_bf] + [jax.ShapeDtypeStruct(array.shape, array.dtype) for array in along],
            [buffer],
            [*came, *along],
            combining,
            name + "_total",
            aliases={2 + chips + j: 1 + j for j in range(len(along))},
        )
        others = []
        for s in reversed(reach):
            pairs = [(i, i + s) if forward else (i + s, i) for i in range(layers - s)]
            others.insert(0, lax.ppermute(total, "z", pairs))
        return came, others, total, along

    def spread(came, others, after, forward, name):
        sums = run(
            functools.partial(prefix_kernel, forward, 2 * count, chips, len(after)),
            moves,
            [single] * chips + [untouched] * len(after) + [single] * len(others),
            [single] * chips,
            [owned_bf] * chips,
            [buffer, buffer],
            [*came, *after, *others],
            combining,
            name + "_prefix",
        )
        return exchange(sums)

    narrow = (count, half * DH)
    lane = pl.BlockSpec((count, step_heads * DH), lambda i, *a: (0, i))
    pinned = [held_in_hbm(array) for array in (queries, keys, values, out_grad)]
    tail_work = (product, 3 * array, half * count * DH)
    copies = [
        jax.ShapeDtypeStruct((3, *narrow), BF16),
        jax.ShapeDtypeStruct(narrow, BF16),
    ]
    mate_tail, mate_three, mate_g = run(
        tail_kernel,
        steps,
        [tokens(1)] * 4,
        [halved, pl.BlockSpec((3, count, step_heads * DH), lambda i, *a: (0, 0, i)), lane],
        [half_bf, *copies],
        [],
        (pinned[1], pinned[2], pinned[0], pinned[3]),
        tail_work,
        "tail_mate",
        lens=held_in_hbm(doc_lengths),
    )
    (own_tail,) = run(
        tail_kernel,
        steps,
        [tokens(0)] * 2,
        [halved],
        [half_bf],
        [],
        pinned[1:3],
        tail_work,
        "tail_own",
        lens=held_in_hbm(doc_lengths),
    )
    mine = own_tail.reshape(chips, owned, DH, DH)
    other = swap(mate_tail).reshape(chips, owned, DH, DH)
    *merged, mate_three = run(
        functools.partial(merge_kernel, count),
        moves,
        [grouped] * 2 + [untouched],
        [single] * chips + [untouched],
        [owned_bf] * chips + copies[:1],
        [],
        (mine, other, mate_three),
        combining,
        "carried_chip",
        aliases={4: chips},
    )
    came, others, _, (mate_g, own_tail) = reach_out(merged, (mate_g, own_tail), True, "carried")
    mate_three, mate_g = swap(mate_three), swap(mate_g)
    few = 4 if half % 4 == 0 else 1
    parts = half // few

    def own_few(i, lens, place):
        return 0, (place[2] & 1) * parts + i

    own_tokens = pl.BlockSpec((count, few * DH), own_few)
    pair_tokens = pl.BlockSpec((2 * count, few * DH), lambda i, *a: (0, i))
    lane_few = pl.BlockSpec((count, few * DH), lambda i, *a: (0, i))
    turns = pl.BlockSpec((few, DH, 2 * count), lambda i, *a: (i, 0, 0))
    part, head_fq, turned = run(
        chip_kernel,
        parts,
        [own_tokens] * 3 + [pl.BlockSpec((3, count, few * DH), lambda i, *a: (0, 0, i))],
        [pair_tokens, pair_tokens, turns],
        [
            jax.ShapeDtypeStruct((2 * count, half * DH), F32),
            jax.ShapeDtypeStruct((2 * count, half * DH), BF16),
            jax.ShapeDtypeStruct((half, DH, 2 * count), BF16),
        ],
        [],
        (queries, keys, values, mate_three),
        (10 * product, 14 * array, 4 * half * count * DH),
        "within_chip",
    )
    late_tail = swap(own_tail)
    chip_in = spread(came, others, (part, late_tail), True, "carried")
    few_states = pl.BlockSpec((few, DH, DH), lambda i, *a: (i, 0, 0))
    one_owner = whole
    half_states = pltpu.VMEM((half, DH, DH), BF16)
    narrow_bf = jax.ShapeDtypeStruct(narrow, BF16)
    attn_half, mate_out, mine_ga, mate_ga, mine_in, mine_late, sent_in, sent_late, *merged = run(
        norm_kernel,
        parts,
        [pair_tokens, turns, own_tokens, lane_few, pair_tokens] + [one_owner] * chips,
        [own_tokens]
        + [lane_few] * 3
        + [whole, few_states, whole, few_states]
        + [one_owner] * chips,
        [token_bf] + [narrow_bf] * 3 + [half_bf] * 4 + [owned_bf] * chips,
        [half_states],
        (head_fq, turned, out_grad, mate_g, part, *chip_in),
        (8 * product, 16 * array, 2 * half * count * DH),
        "normed",
    )
    came, others, total, (mate_ga, sent_in) = reach_out(
        merged, (mate_ga, sent_in), False, "future"
    )
    other_ga, other_in = swap(mate_ga), swap(sent_in)
    other_ga = swap(mate_ga)
    def both(i, lens, place):
        return ((place[2] & 1) ^ (i // steps)) * steps + i % steps

    spans = pl.BlockSpec((count, step_heads * DH), lambda *a: (0, both(*a)))
    lanes = pl.BlockSpec((count, step_heads * DH), lambda i, *a: (0, i % steps))
    grad_queries, gk_part, gv_part, mate_out, sent_late = run(
        inner_kernel,
        2 * steps,
        [spans] * 3 + [lanes] * 2 + [whole] * 4 + [untouched] * 3,
        [spans] * 3 + [untouched] * 2,
        [token_bf, token_f32, token_f32, narrow_bf, half_bf],
        [all_states],
        (
            queries,
            keys,
            values,
            mine_ga,
            other_ga,
            mine_in,
            other_in,
            other.reshape(half, DH, DH),
            late_tail,
            total,
            mate_out,
            sent_late,
        ),
        (16 * product, 22 * array, 4 * half * count * DH),
        "grads_within",
        aliases={12: 3, 13: 4},
    )
    late = (mine_late, swap(sent_late))
    chip_out = spread(came, others, (gk_part,), False, "future")
    outgoing = (chip_out, [swap(state) for state in chip_out])
    def last(parity, extra_ins, extra_outs, shapes, args, aliases):
        return run(
            functools.partial(last_kernel, chips),
            steps,
            [tokens(parity)] * 4 + [whole] + [one_owner] * chips + extra_ins,
            extra_outs + [tokens(parity)] * 2,
            shapes,
            [half_states],
            (keys, values, gk_part, gv_part, late[parity], *outgoing[parity], *args),
            (2 * product, 9 * array, half * count * DH),
            f"grads_last_{parity}",
            aliases=aliases,
        )

    grad_keys, grad_values = last(0, [], [], [token_bf] * 2, (), {})
    attn_out, grad_keys, grad_values = last(
        1,
        [lane] + [untouched] * 3,
        [tokens(1)],
        [token_bf] * 3,
        (swap(mate_out), held_in_hbm(attn_half), grad_keys, grad_values),
        {8 + chips + j: j for j in range(3)},
    )
    return attn_out, grad_queries, grad_keys, grad_values


def solution(mesh):
    n_seq, n_head = mesh.shape["seq"], mesh.shape["head"]
    inner = 2 if n_seq % 2 == 0 else 1
    fine = Mesh(mesh.devices.reshape(n_seq // inner, inner, n_head), ("z", "x", "head"))
    rows = P(("z", "x", "head"), None)
    return jax.shard_map(
        local,
        mesh=fine,
        in_specs=(rows, rows, rows, rows, P()),
        out_specs=(rows, rows, rows, rows),
        check_vma=False,
    )
```

```python
import functools

import jax
import jax.numpy as jnp
from jax import lax
from jax.experimental import pallas as pl
from jax.experimental.pallas import tpu as pltpu
from jax.sharding import Mesh, PartitionSpec as P

DH = 128
F32 = jnp.float32
BF16 = jnp.bfloat16
NN = (((1,), (0,)), ((), ()))
NT = (((1,), (1,)), ((), ()))
LAYER = ("x", "head")


def mul(a, b, dims):
    return lax.dot_general(a, b, dims, preferred_element_type=F32)


def feature(wide):
    return jnp.where(wide > 0, wide + 1.0, jnp.exp(jnp.minimum(wide, 0.0)))


def slope(wide):
    return jnp.where(wide > 0, 1.0, jnp.exp(jnp.minimum(wide, 0.0)))


def doc_ends(lens):
    ends, total = [], 0
    for j in range(lens.shape[0]):
        total = total + lens[j]
        ends.append(total)
    return ends


def doc_at(ends, where):
    found = 0
    for end in ends:
        found = found + jnp.where(where >= end, 1, 0)
    return found


def rows_of(ends, first, count):
    at = first + lax.broadcasted_iota(jnp.int32, (count, 1), 0)
    return doc_at(ends, at)


def columns_of(ends, first, count):
    at = first + lax.broadcasted_iota(jnp.int32, (1, count), 1)
    return doc_at(ends, at)


def visible(ends, first, count):
    row = lax.broadcasted_iota(jnp.int32, (count, count), 0)
    column = lax.broadcasted_iota(jnp.int32, (count, count), 1)
    together = rows_of(ends, first, count) == columns_of(ends, first, count)
    return (row >= column) & together, (row <= column) & together


def identity(count):
    row = lax.broadcasted_iota(jnp.int32, (count, count), 0)
    column = lax.broadcasted_iota(jnp.int32, (count, count), 1)
    return jnp.where(row == column, 1.0, 0.0).astype(BF16)


def turn(array, eye):
    return mul(eye, array, NT).astype(BF16)


def head_mask(ends, first, count):
    return rows_of(ends, first, count) == doc_at(ends, first)


def tail_mask(ends, first, count):
    return rows_of(ends, first, count) == doc_at(ends, first + count - 1)


def cols(h):
    return slice(h * DH, (h + 1) * DH)


def bunches(heads, size=8):
    return [range(h, min(h + size, heads)) for h in range(0, heads, size)]


def halves(wide):
    high = wide.astype(BF16)
    return jnp.concatenate([high, (wide - high.astype(F32)).astype(BF16)], axis=1)


def tail_kernel(lens, place, k, v, *rest):
    if len(rest) > 1:
        q, g, out, three, last = rest
        three[0], three[1], three[2] = q[...], k[...], v[...]
        last[...] = g[...]
    else:
        (out,) = rest
    count = k.shape[0]
    tail = tail_mask(doc_ends(lens), place[0] * count, count)
    eye = identity(DH)
    for hs in bunches(out.shape[0]):
        fks = [
            jnp.where(tail, feature(k[:, cols(h)].astype(F32)), 0.0).astype(BF16) for h in hs
        ]
        turned = [turn(fk, eye) for fk in fks]
        sums = [mul(fk, v[:, cols(h)], NN).astype(BF16) for h, fk in zip(hs, turned)]
        for h, value in zip(hs, sums):
            out[h] = value


def pair_docs(lens, place, count):
    ends = doc_ends(lens)
    core = place[2] & 1
    own, mate = place[0] * count, (place[0] + 1 - 2 * core) * count

    def along(axis):
        shape = (2 * count, 1) if axis == 0 else (1, 2 * count)
        at = lax.broadcasted_iota(jnp.int32, shape, axis)
        return jnp.where(at < count, own + at, mate + at - count)

    rows, columns = along(0), along(1)
    row_docs, column_docs = doc_at(ends, rows), doc_at(ends, columns)
    seen = (rows >= columns) & (row_docs == column_docs)
    first = (place[0] - core) * count
    late = columns >= first + count
    return (
        seen,
        row_docs == doc_at(ends, first),
        column_docs == doc_at(ends, first),
        late & (column_docs == doc_at(ends, first + count)),
    )


def chip_kernel(lens, place, q, k, v, mate, part, head_fq, turned):
    count = q.shape[0]
    seen, head, chip_head, late_head = pair_docs(lens, place, count)
    eye = identity(DH)

    def both(mine, slot, h):
        return jnp.concatenate([mine[:, cols(h)], mate[slot, :, cols(h)]], axis=0)

    for hs in bunches(turned.shape[0], 4):
        wides = [feature(both(q, 0, h).astype(F32)) for h in hs]
        fks = [feature(both(k, 1, h).astype(F32)).astype(BF16) for h in hs]
        kept = [
            jnp.where(seen, mul(wide.astype(BF16), fk, NT), 0.0).astype(BF16)
            for wide, fk in zip(wides, fks)
        ]
        parts = [mul(s, both(v, 2, h), NN) for h, s in zip(hs, kept)]
        heads = [jnp.where(head, wide, 0.0).astype(BF16) for wide in wides]
        turns = [mul(eye, wide.astype(BF16), NT) for wide in wides]
        for h, p, f, t in zip(hs, parts, heads, turns):
            part[:, cols(h)] = p
            head_fq[:, cols(h)] = f
            turned[h, :DH] = jnp.where(chip_head, t, 0.0).astype(BF16)
            turned[h, DH:] = jnp.where(late_head, t, 0.0).astype(BF16)


def norm_kernel(lens, place, head_fq, turned, g, mate_g, part, *rest):
    kept = rest[-1]
    chips = (len(rest) - 9) // 2
    incoming, (out, mate_out, ga_out, mate_ga, came, lates, sent_in, sent_late) = (
        rest[:chips],
        rest[chips : chips + 8],
    )
    states = rest[chips + 8 : -1]
    count = g.shape[0]
    heads = turned.shape[0]
    step = pl.program_id(0)
    chip = place[2] >> 1

    @pl.when(step == 0)
    def _():
        for n, state in enumerate(incoming):
            owned = state.shape[0]
            came[pl.ds((chip ^ n) * owned, owned)] = state[...]
            sent_in[pl.ds((chip ^ n) * owned, owned)] = state[...]

    weights = jnp.full((2 * DH, DH), 1.0 / DH, BF16)
    for hs in bunches(heads, 4):
        atts = [
            part[:, cols(h)] + mul(head_fq[:, cols(h)], came[step * heads + h], NN) for h in hs
        ]
        gos = [
            jnp.concatenate([g[:, cols(h)], mate_g[:, cols(h)]], axis=0).astype(F32) for h in hs
        ]
        means = [
            mul(jnp.concatenate([halves(att * att), halves(go * att)], axis=0), weights, NN)
            for att, go in zip(atts, gos)
        ]
        invs = [lax.rsqrt(m[: 2 * count] + 1e-05) for m in means]
        norms = [att * inv for att, inv in zip(atts, invs)]
        gas = [
            ((go - normed * (m[2 * count :] * inv)) * inv).astype(BF16)
            for go, normed, m, inv in zip(gos, norms, means, invs)
        ]
        sums = [mul(turned[h], ga, NN).astype(BF16) for h, ga in zip(hs, gas)]
        for h, normed, ga, value in zip(hs, norms, gas, sums):
            normed = normed.astype(BF16)
            out[:, cols(h)], mate_out[:, cols(h)] = normed[:count], normed[count:]
            ga_out[:, cols(h)], mate_ga[:, cols(h)] = ga[:count], ga[count:]
            kept[step * heads + h] = value[:DH]
            lates[h] = value[DH:]
            sent_late[h] = value[DH:]

    @pl.when(step == pl.num_programs(0) - 1)
    def _():
        for n, state in enumerate(states):
            owned = state.shape[0]
            state[...] = kept[pl.ds((chip ^ n) * owned, owned)]


def inner_kernel(lens, place, q, k, v, mine_ga, other_ga, *rest):
    passed, earlier, (gq, gk, gv, _, _, came) = rest[:2], rest[2:4], rest[7:]
    count = q.shape[0]
    heads = q.shape[1] // DH
    step = pl.program_id(0)
    own = step < pl.num_programs(0) // 2

    @pl.when(step == 0)
    def _():
        half = came.shape[0] // 2
        core, (early_b, early_e, late_b, late_e) = chip_docs(lens, place, count)
        by_chip = jnp.where(core == 0, 1.0, same(late_b, early_b))
        by_mate = jnp.where(core == 0, 0.0, same(late_b, early_e))
        for j in range(2):
            came[pl.ds(j * half, half)] = (
                passed[j][...].astype(F32) * by_chip + earlier[j][...].astype(F32) * by_mate
            ).astype(BF16)

    ends = doc_ends(lens)
    first = place[0] * count
    seen, seeing = visible(ends, first, count)
    head = head_mask(ends, first, count)
    for hs in bunches(heads):
        wides = [q[:, cols(h)].astype(F32) for h in hs]
        fqs = [feature(wide).astype(BF16) for wide in wides]
        fks = [feature(k[:, cols(h)].astype(F32)).astype(BF16) for h in hs]
        gas = [jnp.where(own, mine_ga[:, cols(h)], other_ga[:, cols(h)]) for h in hs]
        gss = [
            jnp.where(seen, mul(ga, v[:, cols(h)], NT), 0.0).astype(BF16)
            for h, ga in zip(hs, gas)
        ]
        totals = [
            mul(gs, fk, NN) + jnp.where(head, mul(ga, came[step * heads + h], NT), 0.0)
            for h, gs, fk, ga in zip(hs, gss, fks, gas)
        ]
        flipped = [
            jnp.where(seeing, mul(v[:, cols(h)], ga, NT), 0.0).astype(BF16)
            for h, ga in zip(hs, gas)
        ]
        scores = [
            jnp.where(seeing, mul(fk, fq, NT), 0.0).astype(BF16) for fq, fk in zip(fqs, fks)
        ]
        gks = [mul(gs, fq, NN) for gs, fq in zip(flipped, fqs)]
        gvs = [mul(s, ga, NN) for s, ga in zip(scores, gas)]
        for h, total, wide, a, b in zip(hs, totals, wides, gks, gvs):
            gq[:, cols(h)] = (total * slope(wide)).astype(BF16)
            gk[:, cols(h)] = a
            gv[:, cols(h)] = b


def last_kernel(chips, lens, place, k, v, gk_part, gv_part, late, *rest):
    came = rest[-1]
    outgoing, gk, gv = rest[:chips], rest[-3], rest[-2]
    if len(rest) > chips + 3:
        rest[-4][...] = rest[chips][...]
        gk, gv = rest[-3], rest[-2]
    count = k.shape[0]
    heads = k.shape[1] // DH
    step = pl.program_id(0)

    @pl.when(step == 0)
    def _():
        core, (early_b, early_e, late_b, late_e) = chip_docs(lens, place, count)
        chip = place[2] >> 1
        by_far = jnp.where(core == 0, same(early_e, late_e), 1.0)
        by_late = jnp.where(core == 0, same(early_e, late_b), 0.0)
        for n, state in enumerate(outgoing):
            owned = state.shape[0]
            at = pl.ds((chip ^ n) * owned, owned)
            came[at] = (
                state[...].astype(F32) * by_far + late[at].astype(F32) * by_late
            ).astype(BF16)

    tail = tail_mask(doc_ends(lens), place[0] * count, count)
    for hs in bunches(heads):
        wides = [k[:, cols(h)].astype(F32) for h in hs]
        fks = [jnp.where(tail, feature(wide), 0.0).astype(BF16) for wide in wides]
        vts = [jnp.where(tail, v[:, cols(h)].astype(F32), 0.0).astype(BF16) for h in hs]
        states = [came[step * heads + h] for h in hs]
        gks = [gk_part[:, cols(h)] + mul(vt, o, NT) for h, vt, o in zip(hs, vts, states)]
        gvs = [gv_part[:, cols(h)] + mul(fk, o, NN) for h, fk, o in zip(hs, fks, states)]
        for h, a, wide, b in zip(hs, gks, wides, gvs):
            gk[:, cols(h)] = (a * slope(wide)).astype(BF16)
            gv[:, cols(h)] = b.astype(BF16)


def same(a, b):
    return jnp.where(a == b, 1.0, 0.0).astype(F32)


def chip_docs(lens, place, count):
    ends = doc_ends(lens)
    core = place[2] & 1
    start = (place[0] - core) * count
    marks = (start, start + count - 1, start + count, start + 2 * count - 1)
    return core, [doc_at(ends, mark) for mark in marks]


def merge_kernel(count, lens, place, mine, other, _, *outs):
    outs = outs[:-1]
    core, (early_b, early_e, late_b, late_e) = chip_docs(lens, place, count)
    far = same(early_e, late_e)
    mine_by = jnp.where(core == 0, far, 1.0)
    other_by = jnp.where(core == 0, 1.0, far)
    chip = place[2] >> 1
    for n, out in enumerate(outs):
        at = chip ^ n
        out[...] = (mine[at].astype(F32) * mine_by + other[at].astype(F32) * other_by).astype(
            BF16
        )


def total_kernel(forward, unit, members, passed, lens, place, *rest):
    states, total, held = rest[:members], rest[members + passed], rest[-1]
    chip = place[2] >> 1
    for n, state in enumerate(states):
        held[chip ^ n] = state[...]
    ends = doc_ends(lens)
    layer = place[1] * (members * unit)
    carry = None
    for step in range(members):
        i = step if forward else members - 1 - step
        mine = held[i].astype(F32)
        edge = layer + ((i + 1) * unit - 1 if forward else i * unit)
        here = doc_at(ends, edge)
        if carry is not None:
            mine = mine + carry * same(here, previous)
        carry, previous = mine, here
    total[...] = carry.astype(BF16)


def prefix_kernel(forward, unit, members, unread, lens, place, *rest):
    states, outs, (held, sums) = rest[:members], rest[-members - 2 : -2], rest[-2:]
    others = rest[members + unread : -members - 2]
    chip = place[2] >> 1
    for n, state in enumerate(states):
        held[chip ^ n] = state[...]
    span = members * unit
    ends = doc_ends(lens)
    layer = place[1] * span
    sign = -1 if forward else 1
    previous = doc_at(ends, layer - 1 if forward else layer + span)
    carry = None
    for s, other in enumerate(others):
        far = layer + sign * s * span
        there = doc_at(ends, far - 1 if forward else far + span)
        term = other[...].astype(F32) * same(there, previous)
        carry = term if carry is None else carry + term
    for step in range(members):
        i = step if forward else members - 1 - step
        near, far = layer + i * unit, layer + (i + 1) * unit - 1
        if not forward:
            near, far = far, near
        if carry is None:
            sums[i] = jnp.zeros(sums.shape[1:], BF16)
        else:
            sums[i] = (carry * same(doc_at(ends, near), previous)).astype(BF16)
        if step < members - 1:
            here = doc_at(ends, far)
            mine = held[i].astype(F32)
            if carry is not None:
                mine = mine + carry * same(here, previous)
            carry, previous = mine, here
    for n, out in enumerate(outs):
        out[...] = sums[chip ^ n]


SMALL = pltpu.CompilerParams(
    dimension_semantics=("arbitrary",), vmem_limit_bytes=16 * 1024 * 1024
)

def local(queries, keys, values, out_grad, doc_lengths):
    count, width = queries.shape
    heads = width // DH
    layers = lax.axis_size("z")
    members = lax.axis_size("x") * lax.axis_size("head")
    owned = heads // members
    half = heads // 2
    reach = range(1, min(layers - 1, -(-layers // 2)) + 1)
    place = jnp.stack(
        [lax.axis_index(("z", "x", "head")), lax.axis_index("z"), lax.axis_index(LAYER)]
    ).astype(jnp.int32)
    chips = members // 2
    step_heads = max(n for n in (8, 4, 2, 1) if half % n == 0)
    steps = half // step_heads

    def held_in_hbm(arg):
        return pltpu.with_memory_space_constraint(arg, pltpu.HBM)

    def at(parity):
        if parity is None:
            return lambda i, lens, place: i
        return lambda i, lens, place: ((place[2] & 1) ^ parity) * steps + i

    def tokens(parity):
        block = at(parity)
        return pl.BlockSpec((count, step_heads * DH), lambda *a: (0, block(*a)))

    whole = pl.BlockSpec(memory_space=pltpu.VMEM)
    halved = pl.BlockSpec((step_heads, DH, DH), lambda i, *a: (i, 0, 0))
    untouched = pl.BlockSpec(memory_space=pl.ANY)
    token_bf = pltpu.HBM((count, width), BF16)
    token_f32 = jax.ShapeDtypeStruct((count, width), F32)
    owned_bf = jax.ShapeDtypeStruct((owned, DH, DH), BF16)
    half_bf = jax.ShapeDtypeStruct((half, DH, DH), BF16)

    def run(kernel, grid, ins, outs, shapes, scratch, args, cost, name, aliases={}, lens=None):
        flops, moved, exps = cost
        return pl.pallas_call(
            kernel,
            grid_spec=pltpu.PrefetchScalarGridSpec(
                num_scalar_prefetch=2,
                grid=(grid,),
                in_specs=ins,
                out_specs=outs,
                scratch_shapes=scratch,
            ),
            out_shape=shapes,
            input_output_aliases=aliases,
            compiler_params=SMALL,
            cost_estimate=pl.CostEstimate(
                flops=flops, bytes_accessed=moved, transcendentals=exps
            ),
            name=name,
        )(doc_lengths if lens is None else lens, place, *args)

    product = 2 * half * count * DH * DH
    array = half * count * DH * 2
    all_states = pltpu.VMEM((heads, DH, DH), BF16)
    block = owned
    single = grouped = whole
    buffer = pltpu.VMEM((chips, block, DH, DH), BF16)
    combining = (4 * half * DH * DH, 4 * half * DH * DH, 0)
    moves = 1

    def swap(state):
        return lax.ppermute(state, LAYER, [(i, i ^ 1) for i in range(members)])

    def exchange(states):
        came = list(states)
        for n in reversed(range(1, chips)):
            pairs = [(i, i ^ (2 * n)) for i in range(members)]
            came[n] = lax.ppermute(states[n], LAYER, pairs)
        return came

    def reach_out(merged, along, forward, name):
        came = exchange(merged)
        total, *along = run(
            functools.partial(total_kernel, forward, 2 * count, chips, len(along)),
            moves,
            [single] * chips + [untouched] * len(along),
            [single] + [untouched] * len(along),
            [owned_bf] + [jax.ShapeDtypeStruct(array.shape, array.dtype) for array in along],
            [buffer],
            [*came, *along],
            combining,
            name + "_total",
            aliases={2 + chips + j: 1 + j for j in range(len(along))},
        )
        others = []
        for s in reversed(reach):
            pairs = [(i, i + s) if forward else (i + s, i) for i in range(layers - s)]
            others.insert(0, lax.ppermute(total, "z", pairs))
        return came, others, total, along

    def spread(came, others, after, forward, name):
        sums = run(
            functools.partial(prefix_kernel, forward, 2 * count, chips, len(after)),
            moves,
            [single] * chips + [untouched] * len(after) + [single] * len(others),
            [single] * chips,
            [owned_bf] * chips,
            [buffer, buffer],
            [*came, *after, *others],
            combining,
            name + "_prefix",
        )
        return exchange(sums)

    narrow = (count, half * DH)
    lane = pl.BlockSpec((count, step_heads * DH), lambda i, *a: (0, i))
    pinned = [held_in_hbm(array) for array in (queries, keys, values, out_grad)]
    tail_work = (product, 3 * array, half * count * DH)
    copies = [
        jax.ShapeDtypeStruct((3, *narrow), BF16),
        jax.ShapeDtypeStruct(narrow, BF16),
    ]
    mate_tail, mate_three, mate_g = run(
        tail_kernel,
        steps,
        [tokens(1)] * 4,
        [halved, pl.BlockSpec((3, count, step_heads * DH), lambda i, *a: (0, 0, i)), lane],
        [half_bf, *copies],
        [],
        (pinned[1], pinned[2], pinned[0], pinned[3]),
        tail_work,
        "tail_mate",
        lens=held_in_hbm(doc_lengths),
    )
    (own_tail,) = run(
        tail_kernel,
        steps,
        [tokens(0)] * 2,
        [halved],
        [half_bf],
        [],
        pinned[1:3],
        tail_work,
        "tail_own",
        lens=held_in_hbm(doc_lengths),
    )
    mine = own_tail.reshape(chips, owned, DH, DH)
    other = swap(mate_tail).reshape(chips, owned, DH, DH)
    *merged, mate_three = run(
        functools.partial(merge_kernel, count),
        moves,
        [grouped] * 2 + [untouched],
        [single] * chips + [untouched],
        [owned_bf] * chips + copies[:1],
        [],
        (mine, other, mate_three),
        combining,
        "carried_chip",
        aliases={4: chips},
    )
    came, others, _, (mate_g, own_tail) = reach_out(merged, (mate_g, own_tail), True, "carried")
    mate_three, mate_g = swap(mate_three), swap(mate_g)
    few = 4 if half % 4 == 0 else 1
    parts = half // few

    def own_few(i, lens, place):
        return 0, (place[2] & 1) * parts + i

    own_tokens = pl.BlockSpec((count, few * DH), own_few)
    pair_tokens = pl.BlockSpec((2 * count, few * DH), lambda i, *a: (0, i))
    lane_few = pl.BlockSpec((count, few * DH), lambda i, *a: (0, i))
    turns = pl.BlockSpec((few, 2 * DH, 2 * count), lambda i, *a: (i, 0, 0))
    part, head_fq, turned = run(
        chip_kernel,
        parts,
        [own_tokens] * 3 + [pl.BlockSpec((3, count, few * DH), lambda i, *a: (0, 0, i))],
        [pair_tokens, pair_tokens, turns],
        [
            jax.ShapeDtypeStruct((2 * count, half * DH), F32),
            jax.ShapeDtypeStruct((2 * count, half * DH), BF16),
            jax.ShapeDtypeStruct((half, 2 * DH, 2 * count), BF16),
        ],
        [],
        (queries, keys, values, mate_three),
        (10 * product, 14 * array, 4 * half * count * DH),
        "within_chip",
    )
    late_tail = swap(own_tail)
    chip_in = spread(came, others, (part, late_tail), True, "carried")
    few_states = pl.BlockSpec((few, DH, DH), lambda i, *a: (i, 0, 0))
    one_owner = whole
    half_states = pltpu.VMEM((half, DH, DH), BF16)
    narrow_bf = jax.ShapeDtypeStruct(narrow, BF16)
    attn_half, mate_out, mine_ga, mate_ga, mine_in, mine_late, sent_in, sent_late, *merged = run(
        norm_kernel,
        parts,
        [pair_tokens, turns, own_tokens, lane_few, pair_tokens] + [one_owner] * chips,
        [own_tokens]
        + [lane_few] * 3
        + [whole, few_states, whole, few_states]
        + [one_owner] * chips,
        [token_bf] + [narrow_bf] * 3 + [half_bf] * 4 + [owned_bf] * chips,
        [half_states],
        (head_fq, turned, out_grad, mate_g, part, *chip_in),
        (8 * product, 16 * array, 2 * half * count * DH),
        "normed",
    )
    came, others, total, (mate_ga, sent_in) = reach_out(
        merged, (mate_ga, sent_in), False, "future"
    )
    other_ga, other_in = swap(mate_ga), swap(sent_in)
    other_ga = swap(mate_ga)
    def both(i, lens, place):
        return ((place[2] & 1) ^ (i // steps)) * steps + i % steps

    spans = pl.BlockSpec((count, step_heads * DH), lambda *a: (0, both(*a)))
    lanes = pl.BlockSpec((count, step_heads * DH), lambda i, *a: (0, i % steps))
    grad_queries, gk_part, gv_part, mate_out, sent_late = run(
        inner_kernel,
        2 * steps,
        [spans] * 3 + [lanes] * 2 + [whole] * 4 + [untouched] * 3,
        [spans] * 3 + [untouched] * 2,
        [token_bf, token_f32, token_f32, narrow_bf, half_bf],
        [all_states],
        (
            queries,
            keys,
            values,
            mine_ga,
            other_ga,
            mine_in,
            other_in,
            other.reshape(half, DH, DH),
            late_tail,
            total,
            mate_out,
            sent_late,
        ),
        (16 * product, 22 * array, 4 * half * count * DH),
        "grads_within",
        aliases={12: 3, 13: 4},
    )
    late = (mine_late, swap(sent_late))
    chip_out = spread(came, others, (gk_part,), False, "future")
    outgoing = (chip_out, [swap(state) for state in chip_out])
    def last(parity, extra_ins, extra_outs, shapes, args, aliases):
        return run(
            functools.partial(last_kernel, chips),
            steps,
            [tokens(parity)] * 4 + [whole] + [one_owner] * chips + extra_ins,
            extra_outs + [tokens(parity)] * 2,
            shapes,
            [half_states],
            (keys, values, gk_part, gv_part, late[parity], *outgoing[parity], *args),
            (2 * product, 9 * array, half * count * DH),
            f"grads_last_{parity}",
            aliases=aliases,
        )

    grad_keys, grad_values = last(0, [], [], [token_bf] * 2, (), {})
    attn_out, grad_keys, grad_values = last(
        1,
        [lane] + [untouched] * 3,
        [tokens(1)],
        [token_bf] * 3,
        (swap(mate_out), held_in_hbm(attn_half), grad_keys, grad_values),
        {8 + chips + j: j for j in range(3)},
    )
    return attn_out, grad_queries, grad_keys, grad_values


def solution(mesh):
    n_seq, n_head = mesh.shape["seq"], mesh.shape["head"]
    inner = 2 if n_seq % 2 == 0 else 1
    fine = Mesh(mesh.devices.reshape(n_seq // inner, inner, n_head), ("z", "x", "head"))
    rows = P(("z", "x", "head"), None)
    return jax.shard_map(
        local,
        mesh=fine,
        in_specs=(rows, rows, rows, rows, P()),
        out_specs=(rows, rows, rows, rows),
        check_vma=False,
    )
```

```python
import functools

import jax
import jax.numpy as jnp
from jax import lax
from jax.experimental import pallas as pl
from jax.experimental.pallas import tpu as pltpu
from jax.sharding import Mesh, PartitionSpec as P

DH = 128
F32 = jnp.float32
BF16 = jnp.bfloat16
NN = (((1,), (0,)), ((), ()))
NT = (((1,), (1,)), ((), ()))
LAYER = ("x", "head")


def mul(a, b, dims):
    return lax.dot_general(a, b, dims, preferred_element_type=F32)


def feature(wide):
    return jnp.where(wide > 0, wide + 1.0, jnp.exp(jnp.minimum(wide, 0.0)))


def slope(wide):
    return jnp.where(wide > 0, 1.0, jnp.exp(jnp.minimum(wide, 0.0)))


def doc_ends(lens):
    ends, total = [], 0
    for j in range(lens.shape[0]):
        total = total + lens[j]
        ends.append(total)
    return ends


def doc_at(ends, where):
    found = 0
    for end in ends:
        found = found + jnp.where(where >= end, 1, 0)
    return found


def rows_of(ends, first, count):
    at = first + lax.broadcasted_iota(jnp.int32, (count, 1), 0)
    return doc_at(ends, at)


def columns_of(ends, first, count):
    at = first + lax.broadcasted_iota(jnp.int32, (1, count), 1)
    return doc_at(ends, at)


def visible(ends, first, count):
    row = lax.broadcasted_iota(jnp.int32, (count, count), 0)
    column = lax.broadcasted_iota(jnp.int32, (count, count), 1)
    together = rows_of(ends, first, count) == columns_of(ends, first, count)
    return (row >= column) & together, (row <= column) & together


def identity(count):
    row = lax.broadcasted_iota(jnp.int32, (count, count), 0)
    column = lax.broadcasted_iota(jnp.int32, (count, count), 1)
    return jnp.where(row == column, 1.0, 0.0).astype(BF16)


def turn(array, eye):
    return mul(eye, array, NT).astype(BF16)


def head_mask(ends, first, count):
    return rows_of(ends, first, count) == doc_at(ends, first)


def tail_mask(ends, first, count):
    return rows_of(ends, first, count) == doc_at(ends, first + count - 1)


def cols(h):
    return slice(h * DH, (h + 1) * DH)


def bunches(heads, size=8):
    return [range(h, min(h + size, heads)) for h in range(0, heads, size)]


def halves(wide):
    high = wide.astype(BF16)
    return jnp.concatenate([high, (wide - high.astype(F32)).astype(BF16)], axis=1)


def tail_kernel(lens, place, k, v, *rest):
    if len(rest) > 1:
        q, g, out, three, last = rest
        three[0], three[1], three[2] = q[...], k[...], v[...]
        last[...] = g[...]
    else:
        (out,) = rest
    count = k.shape[0]
    tail = tail_mask(doc_ends(lens), place[0] * count, count)
    eye = identity(DH)
    for hs in bunches(out.shape[0]):
        fks = [
            jnp.where(tail, feature(k[:, cols(h)].astype(F32)), 0.0).astype(BF16) for h in hs
        ]
        turned = [turn(fk, eye) for fk in fks]
        sums = [mul(fk, v[:, cols(h)], NN).astype(BF16) for h, fk in zip(hs, turned)]
        for h, value in zip(hs, sums):
            out[h] = value


def pair_docs(lens, place, count):
    ends = doc_ends(lens)
    core = place[2] & 1
    own, mate = place[0] * count, (place[0] + 1 - 2 * core) * count

    def along(axis):
        shape = (2 * count, 1) if axis == 0 else (1, 2 * count)
        at = lax.broadcasted_iota(jnp.int32, shape, axis)
        return jnp.where(at < count, own + at, mate + at - count)

    rows, columns = along(0), along(1)
    row_docs, column_docs = doc_at(ends, rows), doc_at(ends, columns)
    seen = (rows >= columns) & (row_docs == column_docs)
    first = (place[0] - core) * count
    late = columns >= first + count
    return (
        seen,
        row_docs == doc_at(ends, first),
        column_docs == doc_at(ends, first),
        late & (column_docs == doc_at(ends, first + count)),
    )


def chip_kernel(lens, place, q, k, v, mate, part, head_fq, turned):
    count = q.shape[0]
    seen, head, chip_head, late_head = pair_docs(lens, place, count)
    eye = identity(DH)

    def both(mine, slot, h):
        return jnp.concatenate([mine[:, cols(h)], mate[slot, :, cols(h)]], axis=0)

    for hs in bunches(turned.shape[0], 4):
        wides = [feature(both(q, 0, h).astype(F32)) for h in hs]
        fks = [feature(both(k, 1, h).astype(F32)).astype(BF16) for h in hs]
        kept = [
            jnp.where(seen, mul(wide.astype(BF16), fk, NT), 0.0).astype(BF16)
            for wide, fk in zip(wides, fks)
        ]
        parts = [mul(s, both(v, 2, h), NN) for h, s in zip(hs, kept)]
        heads = [jnp.where(head, wide, 0.0).astype(BF16) for wide in wides]
        turns = [mul(eye, wide.astype(BF16), NT) for wide in wides]
        for h, p, f, t in zip(hs, parts, heads, turns):
            part[:, cols(h)] = p
            head_fq[:, cols(h)] = f
            turned[h, :DH] = jnp.where(chip_head, t, 0.0).astype(BF16)
            turned[h, DH:] = jnp.where(late_head, t, 0.0).astype(BF16)


def norm_kernel(lens, place, head_fq, turned, g, mate_g, part, *rest):
    kept = rest[-1]
    chips = (len(rest) - 9) // 2
    incoming, (out, mate_out, ga_out, mate_ga, came, lates, sent_in, sent_late) = (
        rest[:chips],
        rest[chips : chips + 8],
    )
    states = rest[chips + 8 : -1]
    count = g.shape[0]
    heads = turned.shape[0]
    step = pl.program_id(0)
    chip = place[2] >> 1

    @pl.when(step == 0)
    def _():
        for n, state in enumerate(incoming[::-1]):
            owned = state.shape[0]
            came[pl.ds((chip ^ n) * owned, owned)] = state[...]
            sent_in[pl.ds((chip ^ n) * owned, owned)] = state[...]

    weights = jnp.full((2 * DH, DH), 1.0 / DH, BF16)
    for hs in bunches(heads, 4):
        atts = [
            part[:, cols(h)] + mul(head_fq[:, cols(h)], came[step * heads + h], NN) for h in hs
        ]
        gos = [
            jnp.concatenate([g[:, cols(h)], mate_g[:, cols(h)]], axis=0).astype(F32) for h in hs
        ]
        means = [
            mul(jnp.concatenate([halves(att * att), halves(go * att)], axis=0), weights, NN)
            for att, go in zip(atts, gos)
        ]
        invs = [lax.rsqrt(m[: 2 * count] + 1e-05) for m in means]
        norms = [att * inv for att, inv in zip(atts, invs)]
        gas = [
            ((go - normed * (m[2 * count :] * inv)) * inv).astype(BF16)
            for go, normed, m, inv in zip(gos, norms, means, invs)
        ]
        sums = [mul(turned[h], ga, NN).astype(BF16) for h, ga in zip(hs, gas)]
        for h, normed, ga, value in zip(hs, norms, gas, sums):
            normed = normed.astype(BF16)
            out[:, cols(h)], mate_out[:, cols(h)] = normed[:count], normed[count:]
            ga_out[:, cols(h)], mate_ga[:, cols(h)] = ga[:count], ga[count:]
            kept[step * heads + h] = value[:DH]
            lates[h] = value[DH:]
            sent_late[h] = value[DH:]

    @pl.when(step == pl.num_programs(0) - 1)
    def _():
        for n, state in enumerate(states):
            owned = state.shape[0]
            state[...] = kept[pl.ds((chip ^ n) * owned, owned)]


def inner_kernel(lens, place, q, k, v, mine_ga, other_ga, *rest):
    passed, earlier, (gq, gk, gv, _, _, came) = rest[:2], rest[2:4], rest[7:]
    count = q.shape[0]
    heads = q.shape[1] // DH
    step = pl.program_id(0)
    own = step < pl.num_programs(0) // 2

    @pl.when(step == 0)
    def _():
        half = came.shape[0] // 2
        core, (early_b, early_e, late_b, late_e) = chip_docs(lens, place, count)
        by_chip = jnp.where(core == 0, 1.0, same(late_b, early_b))
        by_mate = jnp.where(core == 0, 0.0, same(late_b, early_e))
        for j in range(2):
            came[pl.ds(j * half, half)] = (
                passed[j][...].astype(F32) * by_chip + earlier[j][...].astype(F32) * by_mate
            ).astype(BF16)

    ends = doc_ends(lens)
    first = place[0] * count
    seen, seeing = visible(ends, first, count)
    head = head_mask(ends, first, count)
    for hs in bunches(heads):
        wides = [q[:, cols(h)].astype(F32) for h in hs]
        fqs = [feature(wide).astype(BF16) for wide in wides]
        fks = [feature(k[:, cols(h)].astype(F32)).astype(BF16) for h in hs]
        gas = [jnp.where(own, mine_ga[:, cols(h)], other_ga[:, cols(h)]) for h in hs]
        gss = [
            jnp.where(seen, mul(ga, v[:, cols(h)], NT), 0.0).astype(BF16)
            for h, ga in zip(hs, gas)
        ]
        totals = [
            mul(gs, fk, NN) + jnp.where(head, mul(ga, came[step * heads + h], NT), 0.0)
            for h, gs, fk, ga in zip(hs, gss, fks, gas)
        ]
        flipped = [
            jnp.where(seeing, mul(v[:, cols(h)], ga, NT), 0.0).astype(BF16)
            for h, ga in zip(hs, gas)
        ]
        scores = [
            jnp.where(seeing, mul(fk, fq, NT), 0.0).astype(BF16) for fq, fk in zip(fqs, fks)
        ]
        gks = [mul(gs, fq, NN) for gs, fq in zip(flipped, fqs)]
        gvs = [mul(s, ga, NN) for s, ga in zip(scores, gas)]
        for h, total, wide, a, b in zip(hs, totals, wides, gks, gvs):
            gq[:, cols(h)] = (total * slope(wide)).astype(BF16)
            gk[:, cols(h)] = a
            gv[:, cols(h)] = b


def last_kernel(chips, lens, place, k, v, gk_part, gv_part, late, *rest):
    came = rest[-1]
    outgoing, gk, gv = rest[:chips], rest[-3], rest[-2]
    if len(rest) > chips + 3:
        rest[-4][...] = rest[chips][...]
        gk, gv = rest[-3], rest[-2]
    count = k.shape[0]
    heads = k.shape[1] // DH
    step = pl.program_id(0)

    @pl.when(step == 0)
    def _():
        core, (early_b, early_e, late_b, late_e) = chip_docs(lens, place, count)
        chip = place[2] >> 1
        by_far = jnp.where(core == 0, same(early_e, late_e), 1.0)
        by_late = jnp.where(core == 0, same(early_e, late_b), 0.0)
        for n, state in enumerate(outgoing[::-1]):
            owned = state.shape[0]
            at = pl.ds((chip ^ n) * owned, owned)
            came[at] = (
                state[...].astype(F32) * by_far + late[at].astype(F32) * by_late
            ).astype(BF16)

    tail = tail_mask(doc_ends(lens), place[0] * count, count)
    for hs in bunches(heads):
        wides = [k[:, cols(h)].astype(F32) for h in hs]
        fks = [jnp.where(tail, feature(wide), 0.0).astype(BF16) for wide in wides]
        vts = [jnp.where(tail, v[:, cols(h)].astype(F32), 0.0).astype(BF16) for h in hs]
        states = [came[step * heads + h] for h in hs]
        gks = [gk_part[:, cols(h)] + mul(vt, o, NT) for h, vt, o in zip(hs, vts, states)]
        gvs = [gv_part[:, cols(h)] + mul(fk, o, NN) for h, fk, o in zip(hs, fks, states)]
        for h, a, wide, b in zip(hs, gks, wides, gvs):
            gk[:, cols(h)] = (a * slope(wide)).astype(BF16)
            gv[:, cols(h)] = b.astype(BF16)


def same(a, b):
    return jnp.where(a == b, 1.0, 0.0).astype(F32)


def chip_docs(lens, place, count):
    ends = doc_ends(lens)
    core = place[2] & 1
    start = (place[0] - core) * count
    marks = (start, start + count - 1, start + count, start + 2 * count - 1)
    return core, [doc_at(ends, mark) for mark in marks]


def merge_kernel(count, lens, place, mine, other, _, *outs):
    outs = outs[:-1]
    core, (early_b, early_e, late_b, late_e) = chip_docs(lens, place, count)
    far = same(early_e, late_e)
    mine_by = jnp.where(core == 0, far, 1.0)
    other_by = jnp.where(core == 0, 1.0, far)
    chip = place[2] >> 1
    for n, out in enumerate(outs):
        at = chip ^ n
        out[...] = (mine[at].astype(F32) * mine_by + other[at].astype(F32) * other_by).astype(
            BF16
        )


def total_kernel(forward, unit, members, passed, lens, place, *rest):
    states, total, held = rest[:members][::-1], rest[members + passed], rest[-1]
    chip = place[2] >> 1
    for n, state in enumerate(states):
        held[chip ^ n] = state[...]
    ends = doc_ends(lens)
    layer = place[1] * (members * unit)
    carry = None
    for step in range(members):
        i = step if forward else members - 1 - step
        mine = held[i].astype(F32)
        edge = layer + ((i + 1) * unit - 1 if forward else i * unit)
        here = doc_at(ends, edge)
        if carry is not None:
            mine = mine + carry * same(here, previous)
        carry, previous = mine, here
    total[...] = carry.astype(BF16)


def prefix_kernel(forward, unit, members, unread, lens, place, *rest):
    states, outs, (held, sums) = rest[:members][::-1], rest[-members - 2 : -2], rest[-2:]
    others = rest[members + unread : -members - 2]
    chip = place[2] >> 1
    for n, state in enumerate(states):
        held[chip ^ n] = state[...]
    span = members * unit
    ends = doc_ends(lens)
    layer = place[1] * span
    sign = -1 if forward else 1
    previous = doc_at(ends, layer - 1 if forward else layer + span)
    carry = None
    for s, other in enumerate(others):
        far = layer + sign * s * span
        there = doc_at(ends, far - 1 if forward else far + span)
        term = other[...].astype(F32) * same(there, previous)
        carry = term if carry is None else carry + term
    for step in range(members):
        i = step if forward else members - 1 - step
        near, far = layer + i * unit, layer + (i + 1) * unit - 1
        if not forward:
            near, far = far, near
        if carry is None:
            sums[i] = jnp.zeros(sums.shape[1:], BF16)
        else:
            sums[i] = (carry * same(doc_at(ends, near), previous)).astype(BF16)
        if step < members - 1:
            here = doc_at(ends, far)
            mine = held[i].astype(F32)
            if carry is not None:
                mine = mine + carry * same(here, previous)
            carry, previous = mine, here
    for n, out in enumerate(outs):
        out[...] = sums[chip ^ n]


SMALL = pltpu.CompilerParams(
    dimension_semantics=("arbitrary",), vmem_limit_bytes=16 * 1024 * 1024
)

def local(queries, keys, values, out_grad, doc_lengths):
    count, width = queries.shape
    heads = width // DH
    layers = lax.axis_size("z")
    members = lax.axis_size("x") * lax.axis_size("head")
    owned = heads // members
    half = heads // 2
    reach = range(1, min(layers - 1, -(-layers // 2)) + 1)
    place = jnp.stack(
        [lax.axis_index(("z", "x", "head")), lax.axis_index("z"), lax.axis_index(LAYER)]
    ).astype(jnp.int32)
    chips = members // 2
    step_heads = max(n for n in (8, 4, 2, 1) if half % n == 0)
    steps = half // step_heads

    def held_in_hbm(arg):
        return pltpu.with_memory_space_constraint(arg, pltpu.HBM)

    def at(parity):
        if parity is None:
            return lambda i, lens, place: i
        return lambda i, lens, place: ((place[2] & 1) ^ parity) * steps + i

    def tokens(parity):
        block = at(parity)
        return pl.BlockSpec((count, step_heads * DH), lambda *a: (0, block(*a)))

    whole = pl.BlockSpec(memory_space=pltpu.VMEM)
    halved = pl.BlockSpec((step_heads, DH, DH), lambda i, *a: (i, 0, 0))
    untouched = pl.BlockSpec(memory_space=pl.ANY)
    token_bf = pltpu.HBM((count, width), BF16)
    token_f32 = jax.ShapeDtypeStruct((count, width), F32)
    owned_bf = jax.ShapeDtypeStruct((owned, DH, DH), BF16)
    half_bf = jax.ShapeDtypeStruct((half, DH, DH), BF16)

    def run(kernel, grid, ins, outs, shapes, scratch, args, cost, name, aliases={}, lens=None):
        flops, moved, exps = cost
        return pl.pallas_call(
            kernel,
            grid_spec=pltpu.PrefetchScalarGridSpec(
                num_scalar_prefetch=2,
                grid=(grid,),
                in_specs=ins,
                out_specs=outs,
                scratch_shapes=scratch,
            ),
            out_shape=shapes,
            input_output_aliases=aliases,
            compiler_params=SMALL,
            cost_estimate=pl.CostEstimate(
                flops=flops, bytes_accessed=moved, transcendentals=exps
            ),
            name=name,
        )(doc_lengths if lens is None else lens, place, *args)

    product = 2 * half * count * DH * DH
    array = half * count * DH * 2
    all_states = pltpu.VMEM((heads, DH, DH), BF16)
    block = owned
    single = grouped = whole
    buffer = pltpu.VMEM((chips, block, DH, DH), BF16)
    combining = (4 * half * DH * DH, 4 * half * DH * DH, 0)
    moves = 1

    def swap(state):
        return lax.ppermute(state, LAYER, [(i, i ^ 1) for i in range(members)])

    def exchange(states):
        came = list(states)
        for n in reversed(range(1, chips)):
            pairs = [(i, i ^ (2 * n)) for i in range(members)]
            came[n] = lax.ppermute(states[n], LAYER, pairs)
        return came

    def reach_out(merged, along, forward, name):
        came = exchange(merged)
        total, *along = run(
            functools.partial(total_kernel, forward, 2 * count, chips, len(along)),
            moves,
            [single] * chips + [untouched] * len(along),
            [single] + [untouched] * len(along),
            [owned_bf] + [jax.ShapeDtypeStruct(array.shape, array.dtype) for array in along],
            [buffer],
            [*came[::-1], *along],
            combining,
            name + "_total",
            aliases={2 + chips + j: 1 + j for j in range(len(along))},
        )
        others = []
        for s in reversed(reach):
            pairs = [(i, i + s) if forward else (i + s, i) for i in range(layers - s)]
            others.insert(0, lax.ppermute(total, "z", pairs))
        return came, others, total, along

    def spread(came, others, after, forward, name):
        sums = run(
            functools.partial(prefix_kernel, forward, 2 * count, chips, len(after)),
            moves,
            [single] * chips + [untouched] * len(after) + [single] * len(others),
            [single] * chips,
            [owned_bf] * chips,
            [buffer, buffer],
            [*came[::-1], *after, *others],
            combining,
            name + "_prefix",
        )
        return exchange(sums)

    narrow = (count, half * DH)
    lane = pl.BlockSpec((count, step_heads * DH), lambda i, *a: (0, i))
    pinned = [held_in_hbm(array) for array in (queries, keys, values, out_grad)]
    tail_work = (product, 3 * array, half * count * DH)
    copies = [
        jax.ShapeDtypeStruct((3, *narrow), BF16),
        jax.ShapeDtypeStruct(narrow, BF16),
    ]
    mate_tail, mate_three, mate_g = run(
        tail_kernel,
        steps,
        [tokens(1)] * 4,
        [halved, pl.BlockSpec((3, count, step_heads * DH), lambda i, *a: (0, 0, i)), lane],
        [half_bf, *copies],
        [],
        (pinned[1], pinned[2], pinned[0], pinned[3]),
        tail_work,
        "tail_mate",
        lens=held_in_hbm(doc_lengths),
    )
    (own_tail,) = run(
        tail_kernel,
        steps,
        [tokens(0)] * 2,
        [halved],
        [half_bf],
        [],
        pinned[1:3],
        tail_work,
        "tail_own",
        lens=held_in_hbm(doc_lengths),
    )
    mine = own_tail.reshape(chips, owned, DH, DH)
    other = swap(mate_tail).reshape(chips, owned, DH, DH)
    *merged, mate_three = run(
        functools.partial(merge_kernel, count),
        moves,
        [grouped] * 2 + [untouched],
        [single] * chips + [untouched],
        [owned_bf] * chips + copies[:1],
        [],
        (mine, other, mate_three),
        combining,
        "carried_chip",
        aliases={4: chips},
    )
    came, others, _, (mate_g, own_tail) = reach_out(merged, (mate_g, own_tail), True, "carried")
    mate_three, mate_g = swap(mate_three), swap(mate_g)
    few = 4 if half % 4 == 0 else 1
    parts = half // few

    def own_few(i, lens, place):
        return 0, (place[2] & 1) * parts + i

    own_tokens = pl.BlockSpec((count, few * DH), own_few)
    pair_tokens = pl.BlockSpec((2 * count, few * DH), lambda i, *a: (0, i))
    lane_few = pl.BlockSpec((count, few * DH), lambda i, *a: (0, i))
    turns = pl.BlockSpec((few, 2 * DH, 2 * count), lambda i, *a: (i, 0, 0))
    part, head_fq, turned = run(
        chip_kernel,
        parts,
        [own_tokens] * 3 + [pl.BlockSpec((3, count, few * DH), lambda i, *a: (0, 0, i))],
        [pair_tokens, pair_tokens, turns],
        [
            jax.ShapeDtypeStruct((2 * count, half * DH), F32),
            jax.ShapeDtypeStruct((2 * count, half * DH), BF16),
            jax.ShapeDtypeStruct((half, 2 * DH, 2 * count), BF16),
        ],
        [],
        (queries, keys, values, mate_three),
        (10 * product, 14 * array, 4 * half * count * DH),
        "within_chip",
    )
    late_tail = swap(own_tail)
    chip_in = spread(came, others, (part, late_tail), True, "carried")
    few_states = pl.BlockSpec((few, DH, DH), lambda i, *a: (i, 0, 0))
    one_owner = whole
    half_states = pltpu.VMEM((half, DH, DH), BF16)
    narrow_bf = jax.ShapeDtypeStruct(narrow, BF16)
    attn_half, mate_out, mine_ga, mate_ga, mine_in, mine_late, sent_in, sent_late, *merged = run(
        norm_kernel,
        parts,
        [pair_tokens, turns, own_tokens, lane_few, pair_tokens] + [one_owner] * chips,
        [own_tokens]
        + [lane_few] * 3
        + [whole, few_states, whole, few_states]
        + [one_owner] * chips,
        [token_bf] + [narrow_bf] * 3 + [half_bf] * 4 + [owned_bf] * chips,
        [half_states],
        (head_fq, turned, out_grad, mate_g, part, *chip_in[::-1]),
        (8 * product, 16 * array, 2 * half * count * DH),
        "normed",
    )
    came, others, total, (mate_ga, sent_in) = reach_out(
        merged, (mate_ga, sent_in), False, "future"
    )
    other_ga, other_in = swap(mate_ga), swap(sent_in)
    other_ga = swap(mate_ga)
    def both(i, lens, place):
        return ((place[2] & 1) ^ (i // steps)) * steps + i % steps

    spans = pl.BlockSpec((count, step_heads * DH), lambda *a: (0, both(*a)))
    lanes = pl.BlockSpec((count, step_heads * DH), lambda i, *a: (0, i % steps))
    grad_queries, gk_part, gv_part, mate_out, sent_late = run(
        inner_kernel,
        2 * steps,
        [spans] * 3 + [lanes] * 2 + [whole] * 4 + [untouched] * 3,
        [spans] * 3 + [untouched] * 2,
        [token_bf, token_f32, token_f32, narrow_bf, half_bf],
        [all_states],
        (
            queries,
            keys,
            values,
            mine_ga,
            other_ga,
            mine_in,
            other_in,
            other.reshape(half, DH, DH),
            late_tail,
            total,
            mate_out,
            sent_late,
        ),
        (16 * product, 22 * array, 4 * half * count * DH),
        "grads_within",
        aliases={12: 3, 13: 4},
    )
    late = (mine_late, swap(sent_late))
    chip_out = spread(came, others, (gk_part,), False, "future")
    outgoing = (chip_out, [swap(state) for state in chip_out])
    def last(parity, extra_ins, extra_outs, shapes, args, aliases):
        return run(
            functools.partial(last_kernel, chips),
            steps,
            [tokens(parity)] * 4 + [whole] + [one_owner] * chips + extra_ins,
            extra_outs + [tokens(parity)] * 2,
            shapes,
            [half_states],
            (keys, values, gk_part, gv_part, late[parity], *outgoing[parity][::-1], *args),
            (2 * product, 9 * array, half * count * DH),
            f"grads_last_{parity}",
            aliases=aliases,
        )

    grad_keys, grad_values = last(0, [], [], [token_bf] * 2, (), {})
    attn_out, grad_keys, grad_values = last(
        1,
        [lane] + [untouched] * 3,
        [tokens(1)],
        [token_bf] * 3,
        (swap(mate_out), held_in_hbm(attn_half), grad_keys, grad_values),
        {8 + chips + j: j for j in range(3)},
    )
    return attn_out, grad_queries, grad_keys, grad_values


def solution(mesh):
    n_seq, n_head = mesh.shape["seq"], mesh.shape["head"]
    inner = 2 if n_seq % 2 == 0 else 1
    fine = Mesh(mesh.devices.reshape(n_seq // inner, inner, n_head), ("z", "x", "head"))
    rows = P(("z", "x", "head"), None)
    return jax.shard_map(
        local,
        mesh=fine,
        in_specs=(rows, rows, rows, rows, P()),
        out_specs=(rows, rows, rows, rows),
        check_vma=False,
    )
```

```python
import functools

import jax
import jax.numpy as jnp
from jax import lax
from jax.experimental import pallas as pl
from jax.experimental.pallas import tpu as pltpu
from jax.sharding import Mesh, PartitionSpec as P

DH = 128
F32 = jnp.float32
BF16 = jnp.bfloat16
NN = (((1,), (0,)), ((), ()))
NT = (((1,), (1,)), ((), ()))
LAYER = ("x", "head")


def mul(a, b, dims):
    return lax.dot_general(a, b, dims, preferred_element_type=F32)


def feature(wide):
    return jnp.where(wide > 0, wide + 1.0, jnp.exp(jnp.minimum(wide, 0.0)))


def slope(wide):
    return jnp.where(wide > 0, 1.0, jnp.exp(jnp.minimum(wide, 0.0)))


def doc_ends(lens):
    ends, total = [], 0
    for j in range(lens.shape[0]):
        total = total + lens[j]
        ends.append(total)
    return ends


def doc_at(ends, where):
    found = 0
    for end in ends:
        found = found + jnp.where(where >= end, 1, 0)
    return found


def rows_of(ends, first, count):
    at = first + lax.broadcasted_iota(jnp.int32, (count, 1), 0)
    return doc_at(ends, at)


def columns_of(ends, first, count):
    at = first + lax.broadcasted_iota(jnp.int32, (1, count), 1)
    return doc_at(ends, at)


def visible(ends, first, count):
    row = lax.broadcasted_iota(jnp.int32, (count, count), 0)
    column = lax.broadcasted_iota(jnp.int32, (count, count), 1)
    together = rows_of(ends, first, count) == columns_of(ends, first, count)
    return (row >= column) & together, (row <= column) & together


def identity(count):
    row = lax.broadcasted_iota(jnp.int32, (count, count), 0)
    column = lax.broadcasted_iota(jnp.int32, (count, count), 1)
    return jnp.where(row == column, 1.0, 0.0).astype(BF16)


def turn(array, eye):
    return mul(eye, array, NT).astype(BF16)


def head_mask(ends, first, count):
    return rows_of(ends, first, count) == doc_at(ends, first)


def tail_mask(ends, first, count):
    return rows_of(ends, first, count) == doc_at(ends, first + count - 1)


def cols(h):
    return slice(h * DH, (h + 1) * DH)


def bunches(heads, size=8):
    return [range(h, min(h + size, heads)) for h in range(0, heads, size)]


def halves(wide):
    high = wide.astype(BF16)
    return jnp.concatenate([high, (wide - high.astype(F32)).astype(BF16)], axis=1)


def tail_kernel(lens, place, k, v, *rest):
    if len(rest) > 1:
        q, g, out, three, last = rest
        three[0], three[1], three[2] = q[...], k[...], v[...]
        last[...] = g[...]
    else:
        (out,) = rest
    count = k.shape[0]
    tail = tail_mask(doc_ends(lens), place[0] * count, count)
    eye = identity(DH)
    for hs in bunches(out.shape[0]):
        fks = [
            jnp.where(tail, feature(k[:, cols(h)].astype(F32)), 0.0).astype(BF16) for h in hs
        ]
        turned = [turn(fk, eye) for fk in fks]
        sums = [mul(fk, v[:, cols(h)], NN).astype(BF16) for h, fk in zip(hs, turned)]
        for h, value in zip(hs, sums):
            out[h] = value


def pair_docs(lens, place, count):
    ends = doc_ends(lens)
    core = place[2] & 1
    own, mate = place[0] * count, (place[0] + 1 - 2 * core) * count

    def along(axis):
        shape = (2 * count, 1) if axis == 0 else (1, 2 * count)
        at = lax.broadcasted_iota(jnp.int32, shape, axis)
        return jnp.where(at < count, own + at, mate + at - count)

    rows, columns = along(0), along(1)
    row_docs, column_docs = doc_at(ends, rows), doc_at(ends, columns)
    seen = (rows >= columns) & (row_docs == column_docs)
    first = (place[0] - core) * count
    late = columns >= first + count
    return (
        seen,
        row_docs == doc_at(ends, first),
        column_docs == doc_at(ends, first),
        late & (column_docs == doc_at(ends, first + count)),
    )


def chip_kernel(lens, place, q, k, v, mate, part, head_fq, turned):
    count = q.shape[0]
    seen, head, chip_head, late_head = pair_docs(lens, place, count)
    eye = identity(DH)

    def both(mine, slot, h):
        return jnp.concatenate([mine[:, cols(h)], mate[slot, :, cols(h)]], axis=0)

    for hs in bunches(turned.shape[0], 4):
        wides = [feature(both(q, 0, h).astype(F32)) for h in hs]
        fks = [feature(both(k, 1, h).astype(F32)).astype(BF16) for h in hs]
        kept = [
            jnp.where(seen, mul(wide.astype(BF16), fk, NT), 0.0).astype(BF16)
            for wide, fk in zip(wides, fks)
        ]
        parts = [mul(s, both(v, 2, h), NN) for h, s in zip(hs, kept)]
        heads = [jnp.where(head, wide, 0.0).astype(BF16) for wide in wides]
        turns = [mul(eye, wide.astype(BF16), NT) for wide in wides]
        for h, p, f, t in zip(hs, parts, heads, turns):
            part[:, cols(h)] = p
            head_fq[:, cols(h)] = f
            turned[h, :DH] = jnp.where(chip_head, t, 0.0).astype(BF16)
            turned[h, DH:] = jnp.where(late_head, t, 0.0).astype(BF16)


def norm_kernel(lens, place, head_fq, turned, g, mate_g, part, *rest):
    kept = rest[-1]
    chips = (len(rest) - 9) // 2
    incoming, (out, mate_out, ga_out, mate_ga, came, lates, sent_in, sent_late) = (
        rest[:chips],
        rest[chips : chips + 8],
    )
    states = rest[chips + 8 : -1]
    count = g.shape[0]
    heads = turned.shape[0]
    step = pl.program_id(0)
    chip = place[2] >> 1

    @pl.when(step == 0)
    def _():
        for n, state in enumerate(incoming[::-1]):
            owned = state.shape[0]
            came[pl.ds((chip ^ n) * owned, owned)] = state[...]
            sent_in[pl.ds((chip ^ n) * owned, owned)] = state[...]

    weights = jnp.full((2 * DH, DH), 1.0 / DH, BF16)
    for hs in bunches(heads, 4):
        atts = [
            part[:, cols(h)] + mul(head_fq[:, cols(h)], came[step * heads + h], NN) for h in hs
        ]
        gos = [
            jnp.concatenate([g[:, cols(h)], mate_g[:, cols(h)]], axis=0).astype(F32) for h in hs
        ]
        means = [
            mul(jnp.concatenate([halves(att * att), halves(go * att)], axis=0), weights, NN)
            for att, go in zip(atts, gos)
        ]
        invs = [lax.rsqrt(m[: 2 * count] + 1e-05) for m in means]
        norms = [att * inv for att, inv in zip(atts, invs)]
        gas = [
            ((go - normed * (m[2 * count :] * inv)) * inv).astype(BF16)
            for go, normed, m, inv in zip(gos, norms, means, invs)
        ]
        sums = [mul(turned[h], ga, NN).astype(BF16) for h, ga in zip(hs, gas)]
        for h, normed, ga, value in zip(hs, norms, gas, sums):
            normed = normed.astype(BF16)
            out[:, cols(h)], mate_out[:, cols(h)] = normed[:count], normed[count:]
            ga_out[:, cols(h)], mate_ga[:, cols(h)] = ga[:count], ga[count:]
            kept[step * heads + h] = value[:DH]
            lates[h] = value[DH:]
            sent_late[h] = value[DH:]

    @pl.when(step == pl.num_programs(0) - 1)
    def _():
        for n, state in enumerate(states):
            owned = state.shape[0]
            state[...] = kept[pl.ds((chip ^ n) * owned, owned)]


def inner_kernel(along, lens, place, q, k, v, grad_att, passed, earlier, *rest):
    (gq, gk, gv), came = rest[-4 - along : -1 - along], rest[-1]
    count = q.shape[0]
    heads = q.shape[1] // DH
    step = pl.program_id(0)

    @pl.when(step == 0)
    def _():
        core, (early_b, early_e, late_b, late_e) = chip_docs(lens, place, count)
        by_chip = jnp.where(core == 0, 1.0, same(late_b, early_b))
        by_mate = jnp.where(core == 0, 0.0, same(late_b, early_e))
        came[...] = (
            passed[...].astype(F32) * by_chip + earlier[...].astype(F32) * by_mate
        ).astype(BF16)

    ends = doc_ends(lens)
    first = place[0] * count
    seen, seeing = visible(ends, first, count)
    head = head_mask(ends, first, count)
    for hs in bunches(heads):
        wides = [q[:, cols(h)].astype(F32) for h in hs]
        fqs = [feature(wide).astype(BF16) for wide in wides]
        fks = [feature(k[:, cols(h)].astype(F32)).astype(BF16) for h in hs]
        gas = [grad_att[:, cols(h)] for h in hs]
        gss = [
            jnp.where(seen, mul(ga, v[:, cols(h)], NT), 0.0).astype(BF16)
            for h, ga in zip(hs, gas)
        ]
        totals = [
            mul(gs, fk, NN) + jnp.where(head, mul(ga, came[step * heads + h], NT), 0.0)
            for h, gs, fk, ga in zip(hs, gss, fks, gas)
        ]
        flipped = [
            jnp.where(seeing, mul(v[:, cols(h)], ga, NT), 0.0).astype(BF16)
            for h, ga in zip(hs, gas)
        ]
        scores = [
            jnp.where(seeing, mul(fk, fq, NT), 0.0).astype(BF16) for fq, fk in zip(fqs, fks)
        ]
        gks = [mul(gs, fq, NN) for gs, fq in zip(flipped, fqs)]
        gvs = [mul(s, ga, NN) for s, ga in zip(scores, gas)]
        for h, total, wide, a, b in zip(hs, totals, wides, gks, gvs):
            gq[:, cols(h)] = (total * slope(wide)).astype(BF16)
            gk[:, cols(h)] = a
            gv[:, cols(h)] = b


def last_kernel(chips, lens, place, k, v, gk_part, gv_part, late, *rest):
    came = rest[-1]
    outgoing, gk, gv = rest[:chips], rest[-3], rest[-2]
    if len(rest) > chips + 3:
        rest[-4][...] = rest[chips][...]
        gk, gv = rest[-3], rest[-2]
    count = k.shape[0]
    heads = k.shape[1] // DH
    step = pl.program_id(0)

    @pl.when(step == 0)
    def _():
        core, (early_b, early_e, late_b, late_e) = chip_docs(lens, place, count)
        chip = place[2] >> 1
        by_far = jnp.where(core == 0, same(early_e, late_e), 1.0)
        by_late = jnp.where(core == 0, same(early_e, late_b), 0.0)
        for n, state in enumerate(outgoing[::-1]):
            owned = state.shape[0]
            at = pl.ds((chip ^ n) * owned, owned)
            came[at] = (
                state[...].astype(F32) * by_far + late[at].astype(F32) * by_late
            ).astype(BF16)

    tail = tail_mask(doc_ends(lens), place[0] * count, count)
    for hs in bunches(heads):
        wides = [k[:, cols(h)].astype(F32) for h in hs]
        fks = [jnp.where(tail, feature(wide), 0.0).astype(BF16) for wide in wides]
        vts = [jnp.where(tail, v[:, cols(h)].astype(F32), 0.0).astype(BF16) for h in hs]
        states = [came[step * heads + h] for h in hs]
        gks = [gk_part[:, cols(h)] + mul(vt, o, NT) for h, vt, o in zip(hs, vts, states)]
        gvs = [gv_part[:, cols(h)] + mul(fk, o, NN) for h, fk, o in zip(hs, fks, states)]
        for h, a, wide, b in zip(hs, gks, wides, gvs):
            gk[:, cols(h)] = (a * slope(wide)).astype(BF16)
            gv[:, cols(h)] = b.astype(BF16)


def same(a, b):
    return jnp.where(a == b, 1.0, 0.0).astype(F32)


def chip_docs(lens, place, count):
    ends = doc_ends(lens)
    core = place[2] & 1
    start = (place[0] - core) * count
    marks = (start, start + count - 1, start + count, start + 2 * count - 1)
    return core, [doc_at(ends, mark) for mark in marks]


def merge_kernel(count, lens, place, mine, other, _, *outs):
    outs = outs[:-1]
    core, (early_b, early_e, late_b, late_e) = chip_docs(lens, place, count)
    far = same(early_e, late_e)
    mine_by = jnp.where(core == 0, far, 1.0)
    other_by = jnp.where(core == 0, 1.0, far)
    chip = place[2] >> 1
    for n, out in enumerate(outs):
        at = chip ^ n
        out[...] = (mine[at].astype(F32) * mine_by + other[at].astype(F32) * other_by).astype(
            BF16
        )


def total_kernel(forward, unit, members, passed, lens, place, *rest):
    states, total, held = rest[:members][::-1], rest[members + passed], rest[-1]
    chip = place[2] >> 1
    for n, state in enumerate(states):
        held[chip ^ n] = state[...]
    ends = doc_ends(lens)
    layer = place[1] * (members * unit)
    carry = None
    for step in range(members):
        i = step if forward else members - 1 - step
        mine = held[i].astype(F32)
        edge = layer + ((i + 1) * unit - 1 if forward else i * unit)
        here = doc_at(ends, edge)
        if carry is not None:
            mine = mine + carry * same(here, previous)
        carry, previous = mine, here
    total[...] = carry.astype(BF16)


def prefix_kernel(forward, unit, members, unread, lens, place, *rest):
    states, outs, (held, sums) = rest[:members][::-1], rest[-members - 2 : -2], rest[-2:]
    others = rest[members + unread : -members - 2]
    chip = place[2] >> 1
    for n, state in enumerate(states):
        held[chip ^ n] = state[...]
    span = members * unit
    ends = doc_ends(lens)
    layer = place[1] * span
    sign = -1 if forward else 1
    previous = doc_at(ends, layer - 1 if forward else layer + span)
    carry = None
    for s, other in enumerate(others):
        far = layer + sign * s * span
        there = doc_at(ends, far - 1 if forward else far + span)
        term = other[...].astype(F32) * same(there, previous)
        carry = term if carry is None else carry + term
    for step in range(members):
        i = step if forward else members - 1 - step
        near, far = layer + i * unit, layer + (i + 1) * unit - 1
        if not forward:
            near, far = far, near
        if carry is None:
            sums[i] = jnp.zeros(sums.shape[1:], BF16)
        else:
            sums[i] = (carry * same(doc_at(ends, near), previous)).astype(BF16)
        if step < members - 1:
            here = doc_at(ends, far)
            mine = held[i].astype(F32)
            if carry is not None:
                mine = mine + carry * same(here, previous)
            carry, previous = mine, here
    for n, out in enumerate(outs):
        out[...] = sums[chip ^ n]


SMALL = pltpu.CompilerParams(
    dimension_semantics=("arbitrary",), vmem_limit_bytes=16 * 1024 * 1024
)

def local(queries, keys, values, out_grad, doc_lengths):
    count, width = queries.shape
    heads = width // DH
    layers = lax.axis_size("z")
    members = lax.axis_size("x") * lax.axis_size("head")
    owned = heads // members
    half = heads // 2
    reach = range(1, min(layers - 1, -(-layers // 2)) + 1)
    place = jnp.stack(
        [lax.axis_index(("z", "x", "head")), lax.axis_index("z"), lax.axis_index(LAYER)]
    ).astype(jnp.int32)
    chips = members // 2
    step_heads = max(n for n in (8, 4, 2, 1) if half % n == 0)
    steps = half // step_heads

    def held_in_hbm(arg):
        return pltpu.with_memory_space_constraint(arg, pltpu.HBM)

    def at(parity):
        if parity is None:
            return lambda i, lens, place: i
        return lambda i, lens, place: ((place[2] & 1) ^ parity) * steps + i

    def tokens(parity):
        block = at(parity)
        return pl.BlockSpec((count, step_heads * DH), lambda *a: (0, block(*a)))

    whole = pl.BlockSpec(memory_space=pltpu.VMEM)
    halved = pl.BlockSpec((step_heads, DH, DH), lambda i, *a: (i, 0, 0))
    untouched = pl.BlockSpec(memory_space=pl.ANY)
    token_bf = pltpu.HBM((count, width), BF16)
    token_f32 = jax.ShapeDtypeStruct((count, width), F32)
    owned_bf = jax.ShapeDtypeStruct((owned, DH, DH), BF16)
    half_bf = jax.ShapeDtypeStruct((half, DH, DH), BF16)

    def run(kernel, grid, ins, outs, shapes, scratch, args, cost, name, aliases={}, lens=None):
        flops, moved, exps = cost
        return pl.pallas_call(
            kernel,
            grid_spec=pltpu.PrefetchScalarGridSpec(
                num_scalar_prefetch=2,
                grid=(grid,),
                in_specs=ins,
                out_specs=outs,
                scratch_shapes=scratch,
            ),
            out_shape=shapes,
            input_output_aliases=aliases,
            compiler_params=SMALL,
            cost_estimate=pl.CostEstimate(
                flops=flops, bytes_accessed=moved, transcendentals=exps
            ),
            name=name,
        )(doc_lengths if lens is None else lens, place, *args)

    product = 2 * half * count * DH * DH
    array = half * count * DH * 2
    all_states = pltpu.VMEM((heads, DH, DH), BF16)
    block = owned
    single = grouped = whole
    buffer = pltpu.VMEM((chips, block, DH, DH), BF16)
    combining = (4 * half * DH * DH, 4 * half * DH * DH, 0)
    moves = 1

    def swap(state):
        return lax.ppermute(state, LAYER, [(i, i ^ 1) for i in range(members)])

    def exchange(states):
        came = list(states)
        for n in reversed(range(1, chips)):
            pairs = [(i, i ^ (2 * n)) for i in range(members)]
            came[n] = lax.ppermute(states[n], LAYER, pairs)
        return came

    def reach_out(merged, along, forward, name):
        came = exchange(merged)
        total, *along = run(
            functools.partial(total_kernel, forward, 2 * count, chips, len(along)),
            moves,
            [single] * chips + [untouched] * len(along),
            [single] + [untouched] * len(along),
            [owned_bf] + [jax.ShapeDtypeStruct(array.shape, array.dtype) for array in along],
            [buffer],
            [*came[::-1], *along],
            combining,
            name + "_total",
            aliases={2 + chips + j: 1 + j for j in range(len(along))},
        )
        others = []
        for s in reversed(reach):
            pairs = [(i, i + s) if forward else (i + s, i) for i in range(layers - s)]
            others.insert(0, lax.ppermute(total, "z", pairs))
        return came, others, total, along

    def spread(came, others, after, forward, name):
        sums = run(
            functools.partial(prefix_kernel, forward, 2 * count, chips, len(after)),
            moves,
            [single] * chips + [untouched] * len(after) + [single] * len(others),
            [single] * chips,
            [owned_bf] * chips,
            [buffer, buffer],
            [*came[::-1], *after, *others],
            combining,
            name + "_prefix",
        )
        return exchange(sums)

    narrow = (count, half * DH)
    lane = pl.BlockSpec((count, step_heads * DH), lambda i, *a: (0, i))
    pinned = [held_in_hbm(array) for array in (queries, keys, values, out_grad)]
    tail_work = (product, 3 * array, half * count * DH)
    copies = [
        jax.ShapeDtypeStruct((3, *narrow), BF16),
        jax.ShapeDtypeStruct(narrow, BF16),
    ]
    mate_tail, mate_three, mate_g = run(
        tail_kernel,
        steps,
        [tokens(1)] * 4,
        [halved, pl.BlockSpec((3, count, step_heads * DH), lambda i, *a: (0, 0, i)), lane],
        [half_bf, *copies],
        [],
        (pinned[1], pinned[2], pinned[0], pinned[3]),
        tail_work,
        "tail_mate",
        lens=held_in_hbm(doc_lengths),
    )
    (own_tail,) = run(
        tail_kernel,
        steps,
        [tokens(0)] * 2,
        [halved],
        [half_bf],
        [],
        pinned[1:3],
        tail_work,
        "tail_own",
        lens=held_in_hbm(doc_lengths),
    )
    mine = own_tail.reshape(chips, owned, DH, DH)
    other = swap(mate_tail).reshape(chips, owned, DH, DH)
    *merged, mate_three = run(
        functools.partial(merge_kernel, count),
        moves,
        [grouped] * 2 + [untouched],
        [single] * chips + [untouched],
        [owned_bf] * chips + copies[:1],
        [],
        (mine, other, mate_three),
        combining,
        "carried_chip",
        aliases={4: chips},
    )
    came, others, _, (mate_g, own_tail) = reach_out(merged, (mate_g, own_tail), True, "carried")
    mate_three, mate_g = swap(mate_three), swap(mate_g)
    few = 4 if half % 4 == 0 else 1
    parts = half // few

    def own_few(i, lens, place):
        return 0, (place[2] & 1) * parts + i

    own_tokens = pl.BlockSpec((count, few * DH), own_few)
    pair_tokens = pl.BlockSpec((2 * count, few * DH), lambda i, *a: (0, i))
    lane_few = pl.BlockSpec((count, few * DH), lambda i, *a: (0, i))
    turns = pl.BlockSpec((few, 2 * DH, 2 * count), lambda i, *a: (i, 0, 0))
    part, head_fq, turned = run(
        chip_kernel,
        parts,
        [own_tokens] * 3 + [pl.BlockSpec((3, count, few * DH), lambda i, *a: (0, 0, i))],
        [pair_tokens, pair_tokens, turns],
        [
            jax.ShapeDtypeStruct((2 * count, half * DH), F32),
            jax.ShapeDtypeStruct((2 * count, half * DH), BF16),
            jax.ShapeDtypeStruct((half, 2 * DH, 2 * count), BF16),
        ],
        [],
        (queries, keys, values, mate_three),
        (10 * product, 14 * array, 4 * half * count * DH),
        "within_chip",
    )
    late_tail = swap(own_tail)
    chip_in = spread(came, others, (part, late_tail), True, "carried")
    few_states = pl.BlockSpec((few, DH, DH), lambda i, *a: (i, 0, 0))
    one_owner = whole
    half_states = pltpu.VMEM((half, DH, DH), BF16)
    narrow_bf = jax.ShapeDtypeStruct(narrow, BF16)
    attn_half, mate_out, mine_ga, mate_ga, mine_in, mine_late, sent_in, sent_late, *merged = run(
        norm_kernel,
        parts,
        [pair_tokens, turns, own_tokens, lane_few, pair_tokens] + [one_owner] * chips,
        [own_tokens]
        + [lane_few] * 3
        + [whole, few_states, whole, few_states]
        + [one_owner] * chips,
        [token_bf] + [narrow_bf] * 3 + [half_bf] * 4 + [owned_bf] * chips,
        [half_states],
        (head_fq, turned, out_grad, mate_g, part, *chip_in[::-1]),
        (8 * product, 16 * array, 2 * half * count * DH),
        "normed",
    )
    def inner(parity, grad_att, passed, earlier, after, made, along):
        return run(
            functools.partial(inner_kernel, len(along)),
            steps,
            [tokens(parity)] * 3
            + [lane]
            + [whole] * 2
            + [untouched] * (len(after) + len(made) + len(along)),
            [tokens(parity)] * 3 + [untouched] * len(along),
            [token_bf, token_f32, token_f32]
            + [jax.ShapeDtypeStruct(array.shape, array.dtype) for array in along],
            [half_states],
            (queries, keys, values, grad_att, passed, earlier, *after, *made, *along),
            (7 * product, 11 * array, 2 * half * count * DH),
            f"grads_within_{parity}",
            aliases={8 + len(after) + j: j for j in range(len(made) + len(along))},
        )

    made = inner(0, mine_ga, mine_in, other.reshape(half, DH, DH), (), (), ())
    came, others, total, (mate_ga, sent_in, gk_half) = reach_out(
        merged, (mate_ga, sent_in, made[1]), False, "future"
    )
    made = (held_in_hbm(made[0]), gk_half, made[2])
    grad_queries, gk_part, gv_part, mate_out, sent_late = inner(
        1, swap(mate_ga), swap(sent_in), late_tail, (total,), made, (mate_out, sent_late)
    )
    late = (mine_late, swap(sent_late))
    chip_out = spread(came, others, (gk_part,), False, "future")
    outgoing = (chip_out, [swap(state) for state in chip_out])
    def last(parity, extra_ins, extra_outs, shapes, args, aliases):
        return run(
            functools.partial(last_kernel, chips),
            steps,
            [tokens(parity)] * 4 + [whole] + [one_owner] * chips + extra_ins,
            extra_outs + [tokens(parity)] * 2,
            shapes,
            [half_states],
            (keys, values, gk_part, gv_part, late[parity], *outgoing[parity][::-1], *args),
            (2 * product, 9 * array, half * count * DH),
            f"grads_last_{parity}",
            aliases=aliases,
        )

    grad_keys, grad_values = last(0, [], [], [token_bf] * 2, (), {})
    attn_out, grad_keys, grad_values = last(
        1,
        [lane] + [untouched] * 3,
        [tokens(1)],
        [token_bf] * 3,
        (swap(mate_out), held_in_hbm(attn_half), grad_keys, grad_values),
        {8 + chips + j: j for j in range(3)},
    )
    return attn_out, grad_queries, grad_keys, grad_values


def solution(mesh):
    n_seq, n_head = mesh.shape["seq"], mesh.shape["head"]
    inner = 2 if n_seq % 2 == 0 else 1
    fine = Mesh(mesh.devices.reshape(n_seq // inner, inner, n_head), ("z", "x", "head"))
    rows = P(("z", "x", "head"), None)
    return jax.shard_map(
        local,
        mesh=fine,
        in_specs=(rows, rows, rows, rows, P()),
        out_specs=(rows, rows, rows, rows),
        check_vma=False,
    )
```

```python
import functools

import jax
import jax.numpy as jnp
from jax import lax
from jax.experimental import pallas as pl
from jax.experimental.pallas import tpu as pltpu
from jax.sharding import Mesh, PartitionSpec as P

DH = 128
F32 = jnp.float32
BF16 = jnp.bfloat16
NN = (((1,), (0,)), ((), ()))
NT = (((1,), (1,)), ((), ()))
LAYER = ("x", "head")


def mul(a, b, dims):
    return lax.dot_general(a, b, dims, preferred_element_type=F32)


def feature(wide):
    return jnp.where(wide > 0, wide + 1.0, jnp.exp(jnp.minimum(wide, 0.0)))


def slope(wide):
    return jnp.where(wide > 0, 1.0, jnp.exp(jnp.minimum(wide, 0.0)))


def doc_ends(lens):
    ends, total = [], 0
    for j in range(lens.shape[0]):
        total = total + lens[j]
        ends.append(total)
    return ends


def doc_at(ends, where):
    found = 0
    for end in ends:
        found = found + jnp.where(where >= end, 1, 0)
    return found


def rows_of(ends, first, count):
    at = first + lax.broadcasted_iota(jnp.int32, (count, 1), 0)
    return doc_at(ends, at)


def columns_of(ends, first, count):
    at = first + lax.broadcasted_iota(jnp.int32, (1, count), 1)
    return doc_at(ends, at)


def visible(ends, first, count):
    row = lax.broadcasted_iota(jnp.int32, (count, count), 0)
    column = lax.broadcasted_iota(jnp.int32, (count, count), 1)
    together = rows_of(ends, first, count) == columns_of(ends, first, count)
    return (row >= column) & together, (row <= column) & together


def identity(count):
    row = lax.broadcasted_iota(jnp.int32, (count, count), 0)
    column = lax.broadcasted_iota(jnp.int32, (count, count), 1)
    return jnp.where(row == column, 1.0, 0.0).astype(BF16)


def turn(array, eye):
    return mul(eye, array, NT).astype(BF16)


def head_mask(ends, first, count):
    return rows_of(ends, first, count) == doc_at(ends, first)


def tail_mask(ends, first, count):
    return rows_of(ends, first, count) == doc_at(ends, first + count - 1)


def cols(h):
    return slice(h * DH, (h + 1) * DH)


def bunches(heads, size=8):
    return [range(h, min(h + size, heads)) for h in range(0, heads, size)]


def halves(wide):
    high = wide.astype(BF16)
    return jnp.concatenate([high, (wide - high.astype(F32)).astype(BF16)], axis=1)


def tail_kernel(lens, place, k, v, *rest):
    if len(rest) > 1:
        q, g, out, three, last = rest
        three[0], three[1], three[2] = q[...], k[...], v[...]
        last[...] = g[...]
    else:
        (out,) = rest
    count = k.shape[0]
    tail = tail_mask(doc_ends(lens), place[0] * count, count)
    eye = identity(DH)
    for hs in bunches(out.shape[0]):
        fks = [
            jnp.where(tail, feature(k[:, cols(h)].astype(F32)), 0.0).astype(BF16) for h in hs
        ]
        turned = [turn(fk, eye) for fk in fks]
        sums = [mul(fk, v[:, cols(h)], NN).astype(BF16) for h, fk in zip(hs, turned)]
        for h, value in zip(hs, sums):
            out[h] = value


def pair_docs(lens, place, count):
    ends = doc_ends(lens)
    core = place[2] & 1
    own, mate = place[0] * count, (place[0] + 1 - 2 * core) * count

    def along(axis):
        shape = (2 * count, 1) if axis == 0 else (1, 2 * count)
        at = lax.broadcasted_iota(jnp.int32, shape, axis)
        return jnp.where(at < count, own + at, mate + at - count)

    rows, columns = along(0), along(1)
    row_docs, column_docs = doc_at(ends, rows), doc_at(ends, columns)
    seen = (rows >= columns) & (row_docs == column_docs)
    first = (place[0] - core) * count
    late = columns >= first + count
    return (
        seen,
        row_docs == doc_at(ends, first),
        column_docs == doc_at(ends, first),
        late & (column_docs == doc_at(ends, first + count)),
    )


def chip_kernel(lens, place, q, k, v, mate, part, head_fq, turned):
    count = q.shape[0]
    seen, head, chip_head, late_head = pair_docs(lens, place, count)
    eye = identity(DH)

    def both(mine, slot, h):
        return jnp.concatenate([mine[:, cols(h)], mate[slot, :, cols(h)]], axis=0)

    for hs in bunches(turned.shape[0], 4):
        wides = [feature(both(q, 0, h).astype(F32)) for h in hs]
        fks = [feature(both(k, 1, h).astype(F32)).astype(BF16) for h in hs]
        kept = [
            jnp.where(seen, mul(wide.astype(BF16), fk, NT), 0.0).astype(BF16)
            for wide, fk in zip(wides, fks)
        ]
        parts = [mul(s, both(v, 2, h), NN) for h, s in zip(hs, kept)]
        heads = [jnp.where(head, wide, 0.0).astype(BF16) for wide in wides]
        turns = [mul(eye, wide.astype(BF16), NT) for wide in wides]
        for h, p, f, t in zip(hs, parts, heads, turns):
            part[:, cols(h)] = p
            head_fq[:, cols(h)] = f
            turned[h, :DH] = jnp.where(chip_head, t, 0.0).astype(BF16)
            turned[h, DH:] = jnp.where(late_head, t, 0.0).astype(BF16)


def norm_order(chips):
    order = list(reversed(range(chips)))
    return order[1:2] + order[:1] + order[2:]


def norm_kernel(lens, place, head_fq, turned, g, mate_g, part, *rest):
    kept = rest[-1]
    chips = (len(rest) - 9) // 2
    incoming, (out, mate_out, ga_out, mate_ga, came, lates, sent_in, sent_late) = (
        rest[:chips],
        rest[chips : chips + 8],
    )
    states = rest[chips + 8 : -1]
    count = g.shape[0]
    heads = turned.shape[0]
    step = pl.program_id(0)
    chip = place[2] >> 1

    @pl.when(step == 0)
    def _():
        for n, state in zip(norm_order(chips), incoming):
            owned = state.shape[0]
            came[pl.ds((chip ^ n) * owned, owned)] = state[...]
            sent_in[pl.ds((chip ^ n) * owned, owned)] = state[...]

    weights = jnp.full((2 * DH, DH), 1.0 / DH, BF16)
    for hs in bunches(heads, 4):
        atts = [
            part[:, cols(h)] + mul(head_fq[:, cols(h)], came[step * heads + h], NN) for h in hs
        ]
        gos = [
            jnp.concatenate([g[:, cols(h)], mate_g[:, cols(h)]], axis=0).astype(F32) for h in hs
        ]
        means = [
            mul(jnp.concatenate([halves(att * att), halves(go * att)], axis=0), weights, NN)
            for att, go in zip(atts, gos)
        ]
        invs = [lax.rsqrt(m[: 2 * count] + 1e-05) for m in means]
        norms = [att * inv for att, inv in zip(atts, invs)]
        gas = [
            ((go - normed * (m[2 * count :] * inv)) * inv).astype(BF16)
            for go, normed, m, inv in zip(gos, norms, means, invs)
        ]
        sums = [mul(turned[h], ga, NN).astype(BF16) for h, ga in zip(hs, gas)]
        for h, normed, ga, value in zip(hs, norms, gas, sums):
            normed = normed.astype(BF16)
            out[:, cols(h)], mate_out[:, cols(h)] = normed[:count], normed[count:]
            ga_out[:, cols(h)], mate_ga[:, cols(h)] = ga[:count], ga[count:]
            kept[step * heads + h] = value[:DH]
            lates[h] = value[DH:]
            sent_late[h] = value[DH:]

    @pl.when(step == pl.num_programs(0) - 1)
    def _():
        for n, state in enumerate(states):
            owned = state.shape[0]
            state[...] = kept[pl.ds((chip ^ n) * owned, owned)]


def inner_kernel(along, lens, place, q, k, v, grad_att, passed, earlier, *rest):
    (gq, gk, gv), came = rest[-4 - along : -1 - along], rest[-1]
    count = q.shape[0]
    heads = q.shape[1] // DH
    step = pl.program_id(0)

    @pl.when(step == 0)
    def _():
        core, (early_b, early_e, late_b, late_e) = chip_docs(lens, place, count)
        by_chip = jnp.where(core == 0, 1.0, same(late_b, early_b))
        by_mate = jnp.where(core == 0, 0.0, same(late_b, early_e))
        came[...] = (
            passed[...].astype(F32) * by_chip + earlier[...].astype(F32) * by_mate
        ).astype(BF16)

    ends = doc_ends(lens)
    first = place[0] * count
    seen, seeing = visible(ends, first, count)
    head = head_mask(ends, first, count)
    for hs in bunches(heads):
        wides = [q[:, cols(h)].astype(F32) for h in hs]
        fqs = [feature(wide).astype(BF16) for wide in wides]
        fks = [feature(k[:, cols(h)].astype(F32)).astype(BF16) for h in hs]
        gas = [grad_att[:, cols(h)] for h in hs]
        gss = [
            jnp.where(seen, mul(ga, v[:, cols(h)], NT), 0.0).astype(BF16)
            for h, ga in zip(hs, gas)
        ]
        totals = [
            mul(gs, fk, NN) + jnp.where(head, mul(ga, came[step * heads + h], NT), 0.0)
            for h, gs, fk, ga in zip(hs, gss, fks, gas)
        ]
        flipped = [
            jnp.where(seeing, mul(v[:, cols(h)], ga, NT), 0.0).astype(BF16)
            for h, ga in zip(hs, gas)
        ]
        scores = [
            jnp.where(seeing, mul(fk, fq, NT), 0.0).astype(BF16) for fq, fk in zip(fqs, fks)
        ]
        gks = [mul(gs, fq, NN) for gs, fq in zip(flipped, fqs)]
        gvs = [mul(s, ga, NN) for s, ga in zip(scores, gas)]
        for h, total, wide, a, b in zip(hs, totals, wides, gks, gvs):
            gq[:, cols(h)] = (total * slope(wide)).astype(BF16)
            gk[:, cols(h)] = a
            gv[:, cols(h)] = b


def last_kernel(chips, lens, place, k, v, gk_part, gv_part, late, *rest):
    came = rest[-1]
    outgoing, gk, gv = rest[:chips], rest[-3], rest[-2]
    if len(rest) > chips + 3:
        rest[-4][...] = rest[chips][...]
        gk, gv = rest[-3], rest[-2]
    count = k.shape[0]
    heads = k.shape[1] // DH
    step = pl.program_id(0)

    @pl.when(step == 0)
    def _():
        core, (early_b, early_e, late_b, late_e) = chip_docs(lens, place, count)
        chip = place[2] >> 1
        by_far = jnp.where(core == 0, same(early_e, late_e), 1.0)
        by_late = jnp.where(core == 0, same(early_e, late_b), 0.0)
        for n, state in enumerate(outgoing[::-1]):
            owned = state.shape[0]
            at = pl.ds((chip ^ n) * owned, owned)
            came[at] = (
                state[...].astype(F32) * by_far + late[at].astype(F32) * by_late
            ).astype(BF16)

    tail = tail_mask(doc_ends(lens), place[0] * count, count)
    for hs in bunches(heads):
        wides = [k[:, cols(h)].astype(F32) for h in hs]
        fks = [jnp.where(tail, feature(wide), 0.0).astype(BF16) for wide in wides]
        vts = [jnp.where(tail, v[:, cols(h)].astype(F32), 0.0).astype(BF16) for h in hs]
        states = [came[step * heads + h] for h in hs]
        gks = [gk_part[:, cols(h)] + mul(vt, o, NT) for h, vt, o in zip(hs, vts, states)]
        gvs = [gv_part[:, cols(h)] + mul(fk, o, NN) for h, fk, o in zip(hs, fks, states)]
        for h, a, wide, b in zip(hs, gks, wides, gvs):
            gk[:, cols(h)] = (a * slope(wide)).astype(BF16)
            gv[:, cols(h)] = b.astype(BF16)


def same(a, b):
    return jnp.where(a == b, 1.0, 0.0).astype(F32)


def chip_docs(lens, place, count):
    ends = doc_ends(lens)
    core = place[2] & 1
    start = (place[0] - core) * count
    marks = (start, start + count - 1, start + count, start + 2 * count - 1)
    return core, [doc_at(ends, mark) for mark in marks]


def merge_kernel(count, lens, place, mine, other, _, *outs):
    outs = outs[:-1]
    core, (early_b, early_e, late_b, late_e) = chip_docs(lens, place, count)
    far = same(early_e, late_e)
    mine_by = jnp.where(core == 0, far, 1.0)
    other_by = jnp.where(core == 0, 1.0, far)
    chip = place[2] >> 1
    for n, out in enumerate(outs):
        at = chip ^ n
        out[...] = (mine[at].astype(F32) * mine_by + other[at].astype(F32) * other_by).astype(
            BF16
        )


def total_kernel(forward, unit, members, passed, lens, place, *rest):
    states, total, held = rest[:members][::-1], rest[members + passed], rest[-1]
    chip = place[2] >> 1
    for n, state in enumerate(states):
        held[chip ^ n] = state[...]
    ends = doc_ends(lens)
    layer = place[1] * (members * unit)
    carry = None
    for step in range(members):
        i = step if forward else members - 1 - step
        mine = held[i].astype(F32)
        edge = layer + ((i + 1) * unit - 1 if forward else i * unit)
        here = doc_at(ends, edge)
        if carry is not None:
            mine = mine + carry * same(here, previous)
        carry, previous = mine, here
    total[...] = carry.astype(BF16)


def prefix_kernel(forward, unit, members, unread, lens, place, *rest):
    states, outs, (held, sums) = rest[:members][::-1], rest[-members - 2 : -2], rest[-2:]
    others = rest[members + unread : -members - 2]
    chip = place[2] >> 1
    for n, state in enumerate(states):
        held[chip ^ n] = state[...]
    span = members * unit
    ends = doc_ends(lens)
    layer = place[1] * span
    sign = -1 if forward else 1
    previous = doc_at(ends, layer - 1 if forward else layer + span)
    carry = None
    for s, other in enumerate(others):
        far = layer + sign * s * span
        there = doc_at(ends, far - 1 if forward else far + span)
        term = other[...].astype(F32) * same(there, previous)
        carry = term if carry is None else carry + term
    for step in range(members):
        i = step if forward else members - 1 - step
        near, far = layer + i * unit, layer + (i + 1) * unit - 1
        if not forward:
            near, far = far, near
        if carry is None:
            sums[i] = jnp.zeros(sums.shape[1:], BF16)
        else:
            sums[i] = (carry * same(doc_at(ends, near), previous)).astype(BF16)
        if step < members - 1:
            here = doc_at(ends, far)
            mine = held[i].astype(F32)
            if carry is not None:
                mine = mine + carry * same(here, previous)
            carry, previous = mine, here
    for n, out in enumerate(outs):
        out[...] = sums[chip ^ n]


SMALL = pltpu.CompilerParams(
    dimension_semantics=("arbitrary",), vmem_limit_bytes=16 * 1024 * 1024
)

def local(queries, keys, values, out_grad, doc_lengths):
    count, width = queries.shape
    heads = width // DH
    layers = lax.axis_size("z")
    members = lax.axis_size("x") * lax.axis_size("head")
    owned = heads // members
    half = heads // 2
    reach = range(1, min(layers - 1, -(-layers // 2)) + 1)
    place = jnp.stack(
        [lax.axis_index(("z", "x", "head")), lax.axis_index("z"), lax.axis_index(LAYER)]
    ).astype(jnp.int32)
    chips = members // 2
    step_heads = max(n for n in (8, 4, 2, 1) if half % n == 0)
    steps = half // step_heads

    def held_in_hbm(arg):
        return pltpu.with_memory_space_constraint(arg, pltpu.HBM)

    def at(parity):
        if parity is None:
            return lambda i, lens, place: i
        return lambda i, lens, place: ((place[2] & 1) ^ parity) * steps + i

    def tokens(parity):
        block = at(parity)
        return pl.BlockSpec((count, step_heads * DH), lambda *a: (0, block(*a)))

    whole = pl.BlockSpec(memory_space=pltpu.VMEM)
    halved = pl.BlockSpec((step_heads, DH, DH), lambda i, *a: (i, 0, 0))
    untouched = pl.BlockSpec(memory_space=pl.ANY)
    token_bf = pltpu.HBM((count, width), BF16)
    token_f32 = jax.ShapeDtypeStruct((count, width), F32)
    owned_bf = jax.ShapeDtypeStruct((owned, DH, DH), BF16)
    half_bf = jax.ShapeDtypeStruct((half, DH, DH), BF16)

    def run(kernel, grid, ins, outs, shapes, scratch, args, cost, name, aliases={}, lens=None):
        flops, moved, exps = cost
        return pl.pallas_call(
            kernel,
            grid_spec=pltpu.PrefetchScalarGridSpec(
                num_scalar_prefetch=2,
                grid=(grid,),
                in_specs=ins,
                out_specs=outs,
                scratch_shapes=scratch,
            ),
            out_shape=shapes,
            input_output_aliases=aliases,
            compiler_params=SMALL,
            cost_estimate=pl.CostEstimate(
                flops=flops, bytes_accessed=moved, transcendentals=exps
            ),
            name=name,
        )(doc_lengths if lens is None else lens, place, *args)

    product = 2 * half * count * DH * DH
    array = half * count * DH * 2
    all_states = pltpu.VMEM((heads, DH, DH), BF16)
    block = owned
    single = grouped = whole
    buffer = pltpu.VMEM((chips, block, DH, DH), BF16)
    combining = (4 * half * DH * DH, 4 * half * DH * DH, 0)
    moves = 1

    def swap(state):
        return lax.ppermute(state, LAYER, [(i, i ^ 1) for i in range(members)])

    def exchange(states):
        came = list(states)
        for n in reversed(range(1, chips)):
            pairs = [(i, i ^ (2 * n)) for i in range(members)]
            came[n] = lax.ppermute(states[n], LAYER, pairs)
        return came

    def reach_out(merged, along, forward, name):
        came = exchange(merged)
        total, *along = run(
            functools.partial(total_kernel, forward, 2 * count, chips, len(along)),
            moves,
            [single] * chips + [untouched] * len(along),
            [single] + [untouched] * len(along),
            [owned_bf] + [jax.ShapeDtypeStruct(array.shape, array.dtype) for array in along],
            [buffer],
            [*came[::-1], *along],
            combining,
            name + "_total",
            aliases={2 + chips + j: 1 + j for j in range(len(along))},
        )
        others = []
        for s in reversed(reach):
            pairs = [(i, i + s) if forward else (i + s, i) for i in range(layers - s)]
            others.insert(0, lax.ppermute(total, "z", pairs))
        return came, others, total, along

    def spread(came, others, after, forward, name):
        sums = run(
            functools.partial(prefix_kernel, forward, 2 * count, chips, len(after)),
            moves,
            [single] * chips + [untouched] * len(after) + [single] * len(others),
            [single] * chips,
            [owned_bf] * chips,
            [buffer, buffer],
            [*came[::-1], *after, *others],
            combining,
            name + "_prefix",
        )
        return exchange(sums)

    narrow = (count, half * DH)
    lane = pl.BlockSpec((count, step_heads * DH), lambda i, *a: (0, i))
    pinned = [held_in_hbm(array) for array in (queries, keys, values, out_grad)]
    tail_work = (product, 3 * array, half * count * DH)
    copies = [
        jax.ShapeDtypeStruct((3, *narrow), BF16),
        jax.ShapeDtypeStruct(narrow, BF16),
    ]
    mate_tail, mate_three, mate_g = run(
        tail_kernel,
        steps,
        [tokens(1)] * 4,
        [halved, pl.BlockSpec((3, count, step_heads * DH), lambda i, *a: (0, 0, i)), lane],
        [half_bf, *copies],
        [],
        (pinned[1], pinned[2], pinned[0], pinned[3]),
        tail_work,
        "tail_mate",
        lens=held_in_hbm(doc_lengths),
    )
    (own_tail,) = run(
        tail_kernel,
        steps,
        [tokens(0)] * 2,
        [halved],
        [half_bf],
        [],
        pinned[1:3],
        tail_work,
        "tail_own",
        lens=held_in_hbm(doc_lengths),
    )
    mine = own_tail.reshape(chips, owned, DH, DH)
    other = swap(mate_tail).reshape(chips, owned, DH, DH)
    *merged, mate_three = run(
        functools.partial(merge_kernel, count),
        moves,
        [grouped] * 2 + [untouched],
        [single] * chips + [untouched],
        [owned_bf] * chips + copies[:1],
        [],
        (mine, other, mate_three),
        combining,
        "carried_chip",
        aliases={4: chips},
    )
    came, others, _, (mate_g, own_tail) = reach_out(merged, (mate_g, own_tail), True, "carried")
    mate_three, mate_g = swap(mate_three), swap(mate_g)
    few = 4 if half % 4 == 0 else 1
    parts = half // few

    def own_few(i, lens, place):
        return 0, (place[2] & 1) * parts + i

    own_tokens = pl.BlockSpec((count, few * DH), own_few)
    pair_tokens = pl.BlockSpec((2 * count, few * DH), lambda i, *a: (0, i))
    lane_few = pl.BlockSpec((count, few * DH), lambda i, *a: (0, i))
    turns = pl.BlockSpec((few, 2 * DH, 2 * count), lambda i, *a: (i, 0, 0))
    part, head_fq, turned = run(
        chip_kernel,
        parts,
        [own_tokens] * 3 + [pl.BlockSpec((3, count, few * DH), lambda i, *a: (0, 0, i))],
        [pair_tokens, pair_tokens, turns],
        [
            jax.ShapeDtypeStruct((2 * count, half * DH), F32),
            jax.ShapeDtypeStruct((2 * count, half * DH), BF16),
            jax.ShapeDtypeStruct((half, 2 * DH, 2 * count), BF16),
        ],
        [],
        (queries, keys, values, mate_three),
        (10 * product, 14 * array, 4 * half * count * DH),
        "within_chip",
    )
    late_tail = swap(own_tail)
    chip_in = spread(came, others, (part, late_tail), True, "carried")
    few_states = pl.BlockSpec((few, DH, DH), lambda i, *a: (i, 0, 0))
    one_owner = whole
    half_states = pltpu.VMEM((half, DH, DH), BF16)
    narrow_bf = jax.ShapeDtypeStruct(narrow, BF16)
    attn_half, mate_out, mine_ga, mate_ga, mine_in, mine_late, sent_in, sent_late, *merged = run(
        norm_kernel,
        parts,
        [pair_tokens, turns, own_tokens, lane_few, pair_tokens] + [one_owner] * chips,
        [own_tokens]
        + [lane_few] * 3
        + [whole, few_states, whole, few_states]
        + [one_owner] * chips,
        [token_bf] + [narrow_bf] * 3 + [half_bf] * 4 + [owned_bf] * chips,
        [half_states],
        (head_fq, turned, out_grad, mate_g, part, *[chip_in[n] for n in norm_order(chips)]),
        (8 * product, 16 * array, 2 * half * count * DH),
        "normed",
    )
    def inner(parity, grad_att, passed, earlier, after, made, along):
        return run(
            functools.partial(inner_kernel, len(along)),
            steps,
            [tokens(parity)] * 3
            + [lane]
            + [whole] * 2
            + [untouched] * (len(after) + len(made) + len(along)),
            [tokens(parity)] * 3 + [untouched] * len(along),
            [token_bf, token_f32, token_f32]
            + [jax.ShapeDtypeStruct(array.shape, array.dtype) for array in along],
            [half_states],
            (queries, keys, values, grad_att, passed, earlier, *after, *made, *along),
            (7 * product, 11 * array, 2 * half * count * DH),
            f"grads_within_{parity}",
            aliases={8 + len(after) + j: j for j in range(len(made) + len(along))},
        )

    made = inner(0, mine_ga, mine_in, other.reshape(half, DH, DH), (), (), ())
    came, others, total, (mate_ga, sent_in, gk_half) = reach_out(
        merged, (mate_ga, sent_in, made[1]), False, "future"
    )
    made = (held_in_hbm(made[0]), gk_half, made[2])
    grad_queries, gk_part, gv_part, mate_out, sent_late = inner(
        1, swap(mate_ga), swap(sent_in), late_tail, (total,), made, (mate_out, sent_late)
    )
    late = (mine_late, swap(sent_late))
    chip_out = spread(came, others, (gk_part,), False, "future")
    outgoing = (chip_out, [swap(state) for state in chip_out])
    def last(parity, extra_ins, extra_outs, shapes, args, aliases):
        return run(
            functools.partial(last_kernel, chips),
            steps,
            [tokens(parity)] * 4 + [whole] + [one_owner] * chips + extra_ins,
            extra_outs + [tokens(parity)] * 2,
            shapes,
            [half_states],
            (keys, values, gk_part, gv_part, late[parity], *outgoing[parity][::-1], *args),
            (2 * product, 9 * array, half * count * DH),
            f"grads_last_{parity}",
            aliases=aliases,
        )

    grad_keys, grad_values = last(0, [], [], [token_bf] * 2, (), {})
    attn_out, grad_keys, grad_values = last(
        1,
        [lane] + [untouched] * 3,
        [tokens(1)],
        [token_bf] * 3,
        (swap(mate_out), held_in_hbm(attn_half), grad_keys, grad_values),
        {8 + chips + j: j for j in range(3)},
    )
    return attn_out, grad_queries, grad_keys, grad_values


def solution(mesh):
    n_seq, n_head = mesh.shape["seq"], mesh.shape["head"]
    inner = 2 if n_seq % 2 == 0 else 1
    fine = Mesh(mesh.devices.reshape(n_seq // inner, inner, n_head), ("z", "x", "head"))
    rows = P(("z", "x", "head"), None)
    return jax.shard_map(
        local,
        mesh=fine,
        in_specs=(rows, rows, rows, rows, P()),
        out_specs=(rows, rows, rows, rows),
        check_vma=False,
    )
```

```python
import functools

import jax
import jax.numpy as jnp
from jax import lax
from jax.experimental import pallas as pl
from jax.experimental.pallas import tpu as pltpu
from jax.sharding import Mesh, PartitionSpec as P

DH = 128
F32 = jnp.float32
BF16 = jnp.bfloat16
NN = (((1,), (0,)), ((), ()))
NT = (((1,), (1,)), ((), ()))
LAYER = ("x", "head")


def mul(a, b, dims):
    return lax.dot_general(a, b, dims, preferred_element_type=F32)


def feature(wide):
    return jnp.where(wide > 0, wide + 1.0, jnp.exp(jnp.minimum(wide, 0.0)))


def slope(wide):
    return jnp.where(wide > 0, 1.0, jnp.exp(jnp.minimum(wide, 0.0)))


def doc_ends(lens):
    ends, total = [], 0
    for j in range(lens.shape[0]):
        total = total + lens[j]
        ends.append(total)
    return ends


def doc_at(ends, where):
    found = 0
    for end in ends:
        found = found + jnp.where(where >= end, 1, 0)
    return found


def rows_of(ends, first, count):
    at = first + lax.broadcasted_iota(jnp.int32, (count, 1), 0)
    return doc_at(ends, at)


def columns_of(ends, first, count):
    at = first + lax.broadcasted_iota(jnp.int32, (1, count), 1)
    return doc_at(ends, at)


def visible(ends, first, count):
    row = lax.broadcasted_iota(jnp.int32, (count, count), 0)
    column = lax.broadcasted_iota(jnp.int32, (count, count), 1)
    together = rows_of(ends, first, count) == columns_of(ends, first, count)
    return (row >= column) & together, (row <= column) & together


def identity(count):
    row = lax.broadcasted_iota(jnp.int32, (count, count), 0)
    column = lax.broadcasted_iota(jnp.int32, (count, count), 1)
    return jnp.where(row == column, 1.0, 0.0).astype(BF16)


def turn(array, eye):
    return mul(eye, array, NT).astype(BF16)


def head_mask(ends, first, count):
    return rows_of(ends, first, count) == doc_at(ends, first)


def tail_mask(ends, first, count):
    return rows_of(ends, first, count) == doc_at(ends, first + count - 1)


def cols(h):
    return slice(h * DH, (h + 1) * DH)


def bunches(heads, size=8):
    return [range(h, min(h + size, heads)) for h in range(0, heads, size)]


def halves(wide):
    high = wide.astype(BF16)
    return jnp.concatenate([high, (wide - high.astype(F32)).astype(BF16)], axis=1)


def tail_kernel(lens, place, k, v, *rest):
    if len(rest) > 1:
        q, g, out, three, last = rest
        three[0], three[1], three[2] = q[...], k[...], v[...]
        last[...] = g[...]
    else:
        (out,) = rest
    count = k.shape[0]
    tail = tail_mask(doc_ends(lens), place[0] * count, count)
    eye = identity(DH)
    for hs in bunches(out.shape[0]):
        fks = [
            jnp.where(tail, feature(k[:, cols(h)].astype(F32)), 0.0).astype(BF16) for h in hs
        ]
        turned = [turn(fk, eye) for fk in fks]
        sums = [mul(fk, v[:, cols(h)], NN).astype(BF16) for h, fk in zip(hs, turned)]
        for h, value in zip(hs, sums):
            out[h] = value


def pair_docs(lens, place, count):
    ends = doc_ends(lens)
    core = place[2] & 1
    own, mate = place[0] * count, (place[0] + 1 - 2 * core) * count

    def along(axis):
        shape = (2 * count, 1) if axis == 0 else (1, 2 * count)
        at = lax.broadcasted_iota(jnp.int32, shape, axis)
        return jnp.where(at < count, own + at, mate + at - count)

    rows, columns = along(0), along(1)
    row_docs, column_docs = doc_at(ends, rows), doc_at(ends, columns)
    seen = (rows >= columns) & (row_docs == column_docs)
    first = (place[0] - core) * count
    late = columns >= first + count
    return (
        seen,
        row_docs == doc_at(ends, first),
        column_docs == doc_at(ends, first),
        late & (column_docs == doc_at(ends, first + count)),
    )


def chip_kernel(lens, place, q, k, v, mate, part, head_fq, turned):
    count = q.shape[0]
    seen, head, chip_head, late_head = pair_docs(lens, place, count)
    eye = identity(DH)

    def both(mine, slot, h):
        return jnp.concatenate([mine[:, cols(h)], mate[slot, :, cols(h)]], axis=0)

    for hs in bunches(turned.shape[0], 4):
        wides = [feature(both(q, 0, h).astype(F32)) for h in hs]
        fks = [feature(both(k, 1, h).astype(F32)).astype(BF16) for h in hs]
        kept = [
            jnp.where(seen, mul(wide.astype(BF16), fk, NT), 0.0).astype(BF16)
            for wide, fk in zip(wides, fks)
        ]
        parts = [mul(s, both(v, 2, h), NN) for h, s in zip(hs, kept)]
        heads = [jnp.where(head, wide, 0.0).astype(BF16) for wide in wides]
        turns = [mul(eye, wide.astype(BF16), NT) for wide in wides]
        for h, p, f, t in zip(hs, parts, heads, turns):
            part[:, cols(h)] = p
            head_fq[:, cols(h)] = f
            turned[h, :DH] = jnp.where(chip_head, t, 0.0).astype(BF16)
            turned[h, DH:] = jnp.where(late_head, t, 0.0).astype(BF16)


def norm_kernel(lens, place, head_fq, turned, g, mate_g, part, *rest):
    kept = rest[-1]
    chips = (len(rest) - 9) // 2
    incoming, (out, mate_out, ga_out, mate_ga, came, lates, sent_in, sent_late) = (
        rest[:chips],
        rest[chips : chips + 8],
    )
    states = rest[chips + 8 : -1]
    count = g.shape[0]
    heads = turned.shape[0]
    step = pl.program_id(0)
    chip = place[2] >> 1

    @pl.when(step == 0)
    def _():
        for n, state in enumerate(incoming[::-1]):
            owned = state.shape[0]
            came[pl.ds((chip ^ n) * owned, owned)] = state[...]
            sent_in[pl.ds((chip ^ n) * owned, owned)] = state[...]

    weights = jnp.full((2 * DH, DH), 1.0 / DH, BF16)
    for hs in bunches(heads, 4):
        atts = [
            part[:, cols(h)] + mul(head_fq[:, cols(h)], came[step * heads + h], NN) for h in hs
        ]
        gos = [
            jnp.concatenate([g[:, cols(h)], mate_g[:, cols(h)]], axis=0).astype(F32) for h in hs
        ]
        means = [
            mul(jnp.concatenate([halves(att * att), halves(go * att)], axis=0), weights, NN)
            for att, go in zip(atts, gos)
        ]
        invs = [lax.rsqrt(m[: 2 * count] + 1e-05) for m in means]
        norms = [att * inv for att, inv in zip(atts, invs)]
        gas = [
            ((go - normed * (m[2 * count :] * inv)) * inv).astype(BF16)
            for go, normed, m, inv in zip(gos, norms, means, invs)
        ]
        sums = [mul(turned[h], ga, NN).astype(BF16) for h, ga in zip(hs, gas)]
        for h, normed, ga, value in zip(hs, norms, gas, sums):
            normed = normed.astype(BF16)
            out[:, cols(h)], mate_out[:, cols(h)] = normed[:count], normed[count:]
            ga_out[:, cols(h)], mate_ga[:, cols(h)] = ga[:count], ga[count:]
            kept[step * heads + h] = value[:DH]
            lates[h] = value[DH:]
            sent_late[h] = value[DH:]

    @pl.when(step == pl.num_programs(0) - 1)
    def _():
        for n, state in enumerate(states):
            owned = state.shape[0]
            state[...] = kept[pl.ds((chip ^ n) * owned, owned)]


def inner_kernel(along, lens, place, q, k, v, grad_att, passed, earlier, *rest):
    (gq, gk, gv), came = rest[-4 - along : -1 - along], rest[-1]
    count = q.shape[0]
    heads = q.shape[1] // DH
    step = pl.program_id(0)

    @pl.when(step == 0)
    def _():
        core, (early_b, early_e, late_b, late_e) = chip_docs(lens, place, count)
        by_chip = jnp.where(core == 0, 1.0, same(late_b, early_b))
        by_mate = jnp.where(core == 0, 0.0, same(late_b, early_e))
        came[...] = (
            passed[...].astype(F32) * by_chip + earlier[...].astype(F32) * by_mate
        ).astype(BF16)

    ends = doc_ends(lens)
    first = place[0] * count
    seen, seeing = visible(ends, first, count)
    head = head_mask(ends, first, count)
    for hs in bunches(heads):
        wides = [q[:, cols(h)].astype(F32) for h in hs]
        fqs = [feature(wide).astype(BF16) for wide in wides]
        fks = [feature(k[:, cols(h)].astype(F32)).astype(BF16) for h in hs]
        gas = [grad_att[:, cols(h)] for h in hs]
        gss = [
            jnp.where(seen, mul(ga, v[:, cols(h)], NT), 0.0).astype(BF16)
            for h, ga in zip(hs, gas)
        ]
        totals = [
            mul(gs, fk, NN) + jnp.where(head, mul(ga, came[step * heads + h], NT), 0.0)
            for h, gs, fk, ga in zip(hs, gss, fks, gas)
        ]
        flipped = [
            jnp.where(seeing, mul(v[:, cols(h)], ga, NT), 0.0).astype(BF16)
            for h, ga in zip(hs, gas)
        ]
        scores = [
            jnp.where(seeing, mul(fk, fq, NT), 0.0).astype(BF16) for fq, fk in zip(fqs, fks)
        ]
        gks = [mul(gs, fq, NN) for gs, fq in zip(flipped, fqs)]
        gvs = [mul(s, ga, NN) for s, ga in zip(scores, gas)]
        for h, total, wide, a, b in zip(hs, totals, wides, gks, gvs):
            gq[:, cols(h)] = (total * slope(wide)).astype(BF16)
            gk[:, cols(h)] = a
            gv[:, cols(h)] = b


def last_kernel(chips, lens, place, k, v, gk_part, gv_part, late, *rest):
    came = rest[-1]
    outgoing, gk, gv = rest[:chips], rest[-3], rest[-2]
    if len(rest) > chips + 3:
        rest[-4][...] = rest[chips][...]
        gk, gv = rest[-3], rest[-2]
    count = k.shape[0]
    heads = k.shape[1] // DH
    step = pl.program_id(0)

    @pl.when(step == 0)
    def _():
        core, (early_b, early_e, late_b, late_e) = chip_docs(lens, place, count)
        chip = place[2] >> 1
        by_far = jnp.where(core == 0, same(early_e, late_e), 1.0)
        by_late = jnp.where(core == 0, same(early_e, late_b), 0.0)
        for n, state in enumerate(outgoing[::-1]):
            owned = state.shape[0]
            at = pl.ds((chip ^ n) * owned, owned)
            came[at] = (
                state[...].astype(F32) * by_far + late[at].astype(F32) * by_late
            ).astype(BF16)

    tail = tail_mask(doc_ends(lens), place[0] * count, count)
    for hs in bunches(heads):
        wides = [k[:, cols(h)].astype(F32) for h in hs]
        fks = [jnp.where(tail, feature(wide), 0.0).astype(BF16) for wide in wides]
        vts = [jnp.where(tail, v[:, cols(h)].astype(F32), 0.0).astype(BF16) for h in hs]
        states = [came[step * heads + h] for h in hs]
        gks = [gk_part[:, cols(h)] + mul(vt, o, NT) for h, vt, o in zip(hs, vts, states)]
        gvs = [gv_part[:, cols(h)] + mul(fk, o, NN) for h, fk, o in zip(hs, fks, states)]
        for h, a, wide, b in zip(hs, gks, wides, gvs):
            gk[:, cols(h)] = (a * slope(wide)).astype(BF16)
            gv[:, cols(h)] = b.astype(BF16)


def same(a, b):
    return jnp.where(a == b, 1.0, 0.0).astype(F32)


def chip_docs(lens, place, count):
    ends = doc_ends(lens)
    core = place[2] & 1
    start = (place[0] - core) * count
    marks = (start, start + count - 1, start + count, start + 2 * count - 1)
    return core, [doc_at(ends, mark) for mark in marks]


def merge_kernel(count, lens, place, mine, other, _, *outs):
    outs = outs[:-1]
    core, (early_b, early_e, late_b, late_e) = chip_docs(lens, place, count)
    far = same(early_e, late_e)
    mine_by = jnp.where(core == 0, far, 1.0)
    other_by = jnp.where(core == 0, 1.0, far)
    chip = place[2] >> 1
    for n, out in enumerate(outs):
        at = chip ^ n
        out[...] = (mine[at].astype(F32) * mine_by + other[at].astype(F32) * other_by).astype(
            BF16
        )


def total_kernel(forward, unit, members, passed, lens, place, *rest):
    states, total, held = rest[:members][::-1], rest[members + passed], rest[-1]
    chip = place[2] >> 1
    for n, state in enumerate(states):
        held[chip ^ n] = state[...]
    ends = doc_ends(lens)
    layer = place[1] * (members * unit)
    carry = None
    for step in range(members):
        i = step if forward else members - 1 - step
        mine = held[i].astype(F32)
        edge = layer + ((i + 1) * unit - 1 if forward else i * unit)
        here = doc_at(ends, edge)
        if carry is not None:
            mine = mine + carry * same(here, previous)
        carry, previous = mine, here
    total[...] = carry.astype(BF16)


def prefix_kernel(forward, unit, members, unread, lens, place, *rest):
    states, outs, (held, sums) = rest[:members][::-1], rest[-members - 2 : -2], rest[-2:]
    others = rest[members + unread : -members - 2]
    chip = place[2] >> 1
    for n, state in enumerate(states):
        held[chip ^ n] = state[...]
    span = members * unit
    ends = doc_ends(lens)
    layer = place[1] * span
    sign = -1 if forward else 1
    previous = doc_at(ends, layer - 1 if forward else layer + span)
    carry = None
    for s, other in enumerate(others):
        far = layer + sign * s * span
        there = doc_at(ends, far - 1 if forward else far + span)
        term = other[...].astype(F32) * same(there, previous)
        carry = term if carry is None else carry + term
    for step in range(members):
        i = step if forward else members - 1 - step
        near, far = layer + i * unit, layer + (i + 1) * unit - 1
        if not forward:
            near, far = far, near
        if carry is None:
            sums[i] = jnp.zeros(sums.shape[1:], BF16)
        else:
            sums[i] = (carry * same(doc_at(ends, near), previous)).astype(BF16)
        if step < members - 1:
            here = doc_at(ends, far)
            mine = held[i].astype(F32)
            if carry is not None:
                mine = mine + carry * same(here, previous)
            carry, previous = mine, here
    for n, out in enumerate(outs):
        out[...] = sums[chip ^ n]


SMALL = pltpu.CompilerParams(
    dimension_semantics=("arbitrary",), vmem_limit_bytes=16 * 1024 * 1024
)

def local(queries, keys, values, out_grad, doc_lengths):
    count, width = queries.shape
    heads = width // DH
    layers = lax.axis_size("z")
    members = lax.axis_size("x") * lax.axis_size("head")
    owned = heads // members
    half = heads // 2
    reach = range(1, min(layers - 1, -(-layers // 2)) + 1)
    place = jnp.stack(
        [lax.axis_index(("z", "x", "head")), lax.axis_index("z"), lax.axis_index(LAYER)]
    ).astype(jnp.int32)
    chips = members // 2
    step_heads = max(n for n in (8, 4, 2, 1) if half % n == 0)
    steps = half // step_heads

    def held_in_hbm(arg):
        return pltpu.with_memory_space_constraint(arg, pltpu.HBM)

    def at(parity):
        if parity is None:
            return lambda i, lens, place: i
        return lambda i, lens, place: ((place[2] & 1) ^ parity) * steps + i

    def tokens(parity):
        block = at(parity)
        return pl.BlockSpec((count, step_heads * DH), lambda *a: (0, block(*a)))

    whole = pl.BlockSpec(memory_space=pltpu.VMEM)
    halved = pl.BlockSpec((step_heads, DH, DH), lambda i, *a: (i, 0, 0))
    untouched = pl.BlockSpec(memory_space=pl.ANY)
    token_bf = pltpu.HBM((count, width), BF16)
    token_f32 = jax.ShapeDtypeStruct((count, width), F32)
    owned_bf = jax.ShapeDtypeStruct((owned, DH, DH), BF16)
    half_bf = jax.ShapeDtypeStruct((half, DH, DH), BF16)

    def run(kernel, grid, ins, outs, shapes, scratch, args, cost, name, aliases={}, lens=None):
        flops, moved, exps = cost
        return pl.pallas_call(
            kernel,
            grid_spec=pltpu.PrefetchScalarGridSpec(
                num_scalar_prefetch=2,
                grid=(grid,),
                in_specs=ins,
                out_specs=outs,
                scratch_shapes=scratch,
            ),
            out_shape=shapes,
            input_output_aliases=aliases,
            compiler_params=SMALL,
            cost_estimate=pl.CostEstimate(
                flops=flops, bytes_accessed=moved, transcendentals=exps
            ),
            name=name,
        )(doc_lengths if lens is None else lens, place, *args)

    product = 2 * half * count * DH * DH
    array = half * count * DH * 2
    all_states = pltpu.VMEM((heads, DH, DH), BF16)
    block = owned
    single = grouped = whole
    buffer = pltpu.VMEM((chips, block, DH, DH), BF16)
    combining = (4 * half * DH * DH, 4 * half * DH * DH, 0)
    moves = 1

    def swap(state):
        return lax.ppermute(state, LAYER, [(i, i ^ 1) for i in range(members)])

    def exchange(states):
        came = list(states)
        for n in reversed(range(1, chips)):
            pairs = [(i, i ^ (2 * n)) for i in range(members)]
            came[n] = lax.ppermute(states[n], LAYER, pairs)
        return came

    def reach_out(merged, along, forward, name):
        came = exchange(merged)
        total, *along = run(
            functools.partial(total_kernel, forward, 2 * count, chips, len(along)),
            moves,
            [single] * chips + [untouched] * len(along),
            [single] + [untouched] * len(along),
            [owned_bf] + [jax.ShapeDtypeStruct(array.shape, array.dtype) for array in along],
            [buffer],
            [*came[::-1], *along],
            combining,
            name + "_total",
            aliases={2 + chips + j: 1 + j for j in range(len(along))},
        )
        others = []
        for s in reversed(reach):
            pairs = [(i, i + s) if forward else (i + s, i) for i in range(layers - s)]
            others.insert(0, lax.ppermute(total, "z", pairs))
        return came, others, total, along

    def spread(came, others, after, forward, name):
        sums = run(
            functools.partial(prefix_kernel, forward, 2 * count, chips, len(after)),
            moves,
            [single] * chips + [untouched] * len(after) + [single] * len(others),
            [single] * chips,
            [owned_bf] * chips,
            [buffer, buffer],
            [*came[::-1], *after, *others],
            combining,
            name + "_prefix",
        )
        return exchange(sums)

    narrow = (count, half * DH)
    lane = pl.BlockSpec((count, step_heads * DH), lambda i, *a: (0, i))
    pinned = [held_in_hbm(array) for array in (queries, keys, values, out_grad)]
    tail_work = (product, 3 * array, half * count * DH)
    copies = [
        jax.ShapeDtypeStruct((3, *narrow), BF16),
        jax.ShapeDtypeStruct(narrow, BF16),
    ]
    mate_tail, mate_three, mate_g = run(
        tail_kernel,
        steps,
        [tokens(1)] * 4,
        [halved, pl.BlockSpec((3, count, step_heads * DH), lambda i, *a: (0, 0, i)), lane],
        [half_bf, *copies],
        [],
        (pinned[1], pinned[2], pinned[0], pinned[3]),
        tail_work,
        "tail_mate",
        lens=held_in_hbm(doc_lengths),
    )
    (own_tail,) = run(
        tail_kernel,
        steps,
        [tokens(0)] * 2,
        [halved],
        [half_bf],
        [],
        pinned[1:3],
        tail_work,
        "tail_own",
        lens=held_in_hbm(doc_lengths),
    )
    mine = own_tail.reshape(chips, owned, DH, DH)
    other = swap(mate_tail).reshape(chips, owned, DH, DH)
    *merged, mate_three = run(
        functools.partial(merge_kernel, count),
        moves,
        [grouped] * 2 + [untouched],
        [single] * chips + [untouched],
        [owned_bf] * chips + copies[:1],
        [],
        (mine, other, mate_three),
        combining,
        "carried_chip",
        aliases={4: chips},
    )
    came, others, _, (mate_g, own_tail) = reach_out(merged, (mate_g, own_tail), True, "carried")
    mate_three, mate_g = swap(mate_three), swap(mate_g)
    few = max(n for n in (8, 4, 2, 1) if half % n == 0)
    parts = half // few

    def own_few(i, lens, place):
        return 0, (place[2] & 1) * parts + i

    own_tokens = pl.BlockSpec((count, few * DH), own_few)
    pair_tokens = pl.BlockSpec((2 * count, few * DH), lambda i, *a: (0, i))
    lane_few = pl.BlockSpec((count, few * DH), lambda i, *a: (0, i))
    turns = pl.BlockSpec((few, 2 * DH, 2 * count), lambda i, *a: (i, 0, 0))
    part, head_fq, turned = run(
        chip_kernel,
        parts,
        [own_tokens] * 3 + [pl.BlockSpec((3, count, few * DH), lambda i, *a: (0, 0, i))],
        [pair_tokens, pair_tokens, turns],
        [
            jax.ShapeDtypeStruct((2 * count, half * DH), F32),
            jax.ShapeDtypeStruct((2 * count, half * DH), BF16),
            jax.ShapeDtypeStruct((half, 2 * DH, 2 * count), BF16),
        ],
        [],
        (queries, keys, values, mate_three),
        (10 * product, 14 * array, 4 * half * count * DH),
        "within_chip",
    )
    late_tail = swap(own_tail)
    chip_in = spread(came, others, (part, late_tail), True, "carried")
    few_states = pl.BlockSpec((few, DH, DH), lambda i, *a: (i, 0, 0))
    one_owner = whole
    half_states = pltpu.VMEM((half, DH, DH), BF16)
    narrow_bf = jax.ShapeDtypeStruct(narrow, BF16)
    attn_half, mate_out, mine_ga, mate_ga, mine_in, mine_late, sent_in, sent_late, *merged = run(
        norm_kernel,
        parts,
        [pair_tokens, turns, own_tokens, lane_few, pair_tokens] + [one_owner] * chips,
        [own_tokens]
        + [lane_few] * 3
        + [whole, few_states, whole, few_states]
        + [one_owner] * chips,
        [token_bf] + [narrow_bf] * 3 + [half_bf] * 4 + [owned_bf] * chips,
        [half_states],
        (head_fq, turned, out_grad, mate_g, part, *chip_in[::-1]),
        (8 * product, 16 * array, 2 * half * count * DH),
        "normed",
    )
    def inner(parity, grad_att, passed, earlier, after, made, along):
        return run(
            functools.partial(inner_kernel, len(along)),
            steps,
            [tokens(parity)] * 3
            + [lane]
            + [whole] * 2
            + [untouched] * (len(after) + len(made) + len(along)),
            [tokens(parity)] * 3 + [untouched] * len(along),
            [token_bf, token_f32, token_f32]
            + [jax.ShapeDtypeStruct(array.shape, array.dtype) for array in along],
            [half_states],
            (queries, keys, values, grad_att, passed, earlier, *after, *made, *along),
            (7 * product, 11 * array, 2 * half * count * DH),
            f"grads_within_{parity}",
            aliases={8 + len(after) + j: j for j in range(len(made) + len(along))},
        )

    made = inner(0, mine_ga, mine_in, other.reshape(half, DH, DH), (), (), ())
    came, others, total, (mate_ga, sent_in, gk_half) = reach_out(
        merged, (mate_ga, sent_in, made[1]), False, "future"
    )
    made = (held_in_hbm(made[0]), gk_half, made[2])
    grad_queries, gk_part, gv_part, mate_out, sent_late = inner(
        1, swap(mate_ga), swap(sent_in), late_tail, (total,), made, (mate_out, sent_late)
    )
    late = (mine_late, swap(sent_late))
    chip_out = spread(came, others, (gk_part,), False, "future")
    outgoing = (chip_out, [swap(state) for state in chip_out])
    def last(parity, extra_ins, extra_outs, shapes, args, aliases):
        return run(
            functools.partial(last_kernel, chips),
            steps,
            [tokens(parity)] * 4 + [whole] + [one_owner] * chips + extra_ins,
            extra_outs + [tokens(parity)] * 2,
            shapes,
            [half_states],
            (keys, values, gk_part, gv_part, late[parity], *outgoing[parity][::-1], *args),
            (2 * product, 9 * array, half * count * DH),
            f"grads_last_{parity}",
            aliases=aliases,
        )

    grad_keys, grad_values = last(0, [], [], [token_bf] * 2, (), {})
    attn_out, grad_keys, grad_values = last(
        1,
        [lane] + [untouched] * 3,
        [tokens(1)],
        [token_bf] * 3,
        (swap(mate_out), held_in_hbm(attn_half), grad_keys, grad_values),
        {8 + chips + j: j for j in range(3)},
    )
    return attn_out, grad_queries, grad_keys, grad_values


def solution(mesh):
    n_seq, n_head = mesh.shape["seq"], mesh.shape["head"]
    inner = 2 if n_seq % 2 == 0 else 1
    fine = Mesh(mesh.devices.reshape(n_seq // inner, inner, n_head), ("z", "x", "head"))
    rows = P(("z", "x", "head"), None)
    return jax.shard_map(
        local,
        mesh=fine,
        in_specs=(rows, rows, rows, rows, P()),
        out_specs=(rows, rows, rows, rows),
        check_vma=False,
    )
```

```python
import functools

import jax
import jax.numpy as jnp
from jax import lax
from jax.experimental import pallas as pl
from jax.experimental.pallas import tpu as pltpu
from jax.sharding import Mesh, PartitionSpec as P

DH = 128
F32 = jnp.float32
BF16 = jnp.bfloat16
NN = (((1,), (0,)), ((), ()))
NT = (((1,), (1,)), ((), ()))
LAYER = ("x", "head")


def mul(a, b, dims):
    return lax.dot_general(a, b, dims, preferred_element_type=F32)


def feature(wide):
    return jnp.where(wide > 0, wide + 1.0, jnp.exp(jnp.minimum(wide, 0.0)))


def slope(wide):
    return jnp.where(wide > 0, 1.0, jnp.exp(jnp.minimum(wide, 0.0)))


def doc_ends(lens):
    ends, total = [], 0
    for j in range(lens.shape[0]):
        total = total + lens[j]
        ends.append(total)
    return ends


def doc_at(ends, where):
    found = 0
    for end in ends:
        found = found + jnp.where(where >= end, 1, 0)
    return found


def rows_of(ends, first, count):
    at = first + lax.broadcasted_iota(jnp.int32, (count, 1), 0)
    return doc_at(ends, at)


def columns_of(ends, first, count):
    at = first + lax.broadcasted_iota(jnp.int32, (1, count), 1)
    return doc_at(ends, at)


def visible(ends, first, count):
    row = lax.broadcasted_iota(jnp.int32, (count, count), 0)
    column = lax.broadcasted_iota(jnp.int32, (count, count), 1)
    together = rows_of(ends, first, count) == columns_of(ends, first, count)
    return (row >= column) & together, (row <= column) & together


def identity(count):
    row = lax.broadcasted_iota(jnp.int32, (count, count), 0)
    column = lax.broadcasted_iota(jnp.int32, (count, count), 1)
    return jnp.where(row == column, 1.0, 0.0).astype(BF16)


def turn(array, eye):
    return mul(eye, array, NT).astype(BF16)


def head_mask(ends, first, count):
    return rows_of(ends, first, count) == doc_at(ends, first)


def tail_mask(ends, first, count):
    return rows_of(ends, first, count) == doc_at(ends, first + count - 1)


def cols(h):
    return slice(h * DH, (h + 1) * DH)


def bunches(heads, size=8):
    return [range(h, min(h + size, heads)) for h in range(0, heads, size)]


def halves(wide):
    high = wide.astype(BF16)
    return jnp.concatenate([high, (wide - high.astype(F32)).astype(BF16)], axis=1)


def tail_kernel(lens, place, k, v, *rest):
    if len(rest) > 1:
        q, g, out, three, last = rest
        three[0], three[1], three[2] = q[...], k[...], v[...]
        last[...] = g[...]
    else:
        (out,) = rest
    count = k.shape[0]
    tail = tail_mask(doc_ends(lens), place[0] * count, count)
    eye = identity(DH)
    for hs in bunches(out.shape[0]):
        fks = [
            jnp.where(tail, feature(k[:, cols(h)].astype(F32)), 0.0).astype(BF16) for h in hs
        ]
        turned = [turn(fk, eye) for fk in fks]
        sums = [mul(fk, v[:, cols(h)], NN).astype(BF16) for h, fk in zip(hs, turned)]
        for h, value in zip(hs, sums):
            out[h] = value


def pair_docs(lens, place, count):
    ends = doc_ends(lens)
    core = place[2] & 1
    own, mate = place[0] * count, (place[0] + 1 - 2 * core) * count

    def along(axis):
        shape = (2 * count, 1) if axis == 0 else (1, 2 * count)
        at = lax.broadcasted_iota(jnp.int32, shape, axis)
        return jnp.where(at < count, own + at, mate + at - count)

    rows, columns = along(0), along(1)
    row_docs, column_docs = doc_at(ends, rows), doc_at(ends, columns)
    seen = (rows >= columns) & (row_docs == column_docs)
    first = (place[0] - core) * count
    late = columns >= first + count
    return (
        seen,
        row_docs == doc_at(ends, first),
        column_docs == doc_at(ends, first),
        late & (column_docs == doc_at(ends, first + count)),
    )


def chip_kernel(lens, place, q, k, v, mate, part, head_fq, turned):
    count = q.shape[0]
    seen, head, chip_head, late_head = pair_docs(lens, place, count)
    eye = identity(DH)

    def both(mine, slot, h):
        return jnp.concatenate([mine[:, cols(h)], mate[slot, :, cols(h)]], axis=0)

    for hs in bunches(turned.shape[0], 4):
        wides = [feature(both(q, 0, h).astype(F32)) for h in hs]
        fks = [feature(both(k, 1, h).astype(F32)).astype(BF16) for h in hs]
        kept = [
            jnp.where(seen, mul(wide.astype(BF16), fk, NT), 0.0).astype(BF16)
            for wide, fk in zip(wides, fks)
        ]
        parts = [mul(s, both(v, 2, h), NN) for h, s in zip(hs, kept)]
        heads = [jnp.where(head, wide, 0.0).astype(BF16) for wide in wides]
        turns = [mul(eye, wide.astype(BF16), NT) for wide in wides]
        for h, p, f, t in zip(hs, parts, heads, turns):
            part[:, cols(h)] = p
            head_fq[:, cols(h)] = f
            turned[h, :DH] = jnp.where(chip_head, t, 0.0).astype(BF16)
            turned[h, DH:] = jnp.where(late_head, t, 0.0).astype(BF16)


def norm_kernel(lens, place, head_fq, turned, g, mate_g, part, *rest):
    kept = rest[-1]
    chips = (len(rest) - 9) // 2
    incoming, (out, mate_out, ga_out, mate_ga, came, lates, sent_in, sent_late) = (
        rest[:chips],
        rest[chips : chips + 8],
    )
    states = rest[chips + 8 : -1]
    count = g.shape[0]
    heads = turned.shape[0]
    step = pl.program_id(0)
    chip = place[2] >> 1

    @pl.when(step == 0)
    def _():
        for n, state in enumerate(incoming[::-1]):
            owned = state.shape[0]
            came[pl.ds((chip ^ n) * owned, owned)] = state[...]
            sent_in[pl.ds((chip ^ n) * owned, owned)] = state[...]

    weights = jnp.full((2 * DH, DH), 1.0 / DH, BF16)
    for hs in bunches(heads, 8):
        atts = [
            part[:, cols(h)] + mul(head_fq[:, cols(h)], came[step * heads + h], NN) for h in hs
        ]
        gos = [
            jnp.concatenate([g[:, cols(h)], mate_g[:, cols(h)]], axis=0).astype(F32) for h in hs
        ]
        means = [
            mul(jnp.concatenate([halves(att * att), halves(go * att)], axis=0), weights, NN)
            for att, go in zip(atts, gos)
        ]
        invs = [lax.rsqrt(m[: 2 * count] + 1e-05) for m in means]
        norms = [att * inv for att, inv in zip(atts, invs)]
        gas = [
            ((go - normed * (m[2 * count :] * inv)) * inv).astype(BF16)
            for go, normed, m, inv in zip(gos, norms, means, invs)
        ]
        sums = [mul(turned[h], ga, NN).astype(BF16) for h, ga in zip(hs, gas)]
        for h, normed, ga, value in zip(hs, norms, gas, sums):
            normed = normed.astype(BF16)
            out[:, cols(h)], mate_out[:, cols(h)] = normed[:count], normed[count:]
            ga_out[:, cols(h)], mate_ga[:, cols(h)] = ga[:count], ga[count:]
            kept[step * heads + h] = value[:DH]
            lates[h] = value[DH:]
            sent_late[h] = value[DH:]

    @pl.when(step == pl.num_programs(0) - 1)
    def _():
        for n, state in enumerate(states):
            owned = state.shape[0]
            state[...] = kept[pl.ds((chip ^ n) * owned, owned)]


def inner_kernel(along, lens, place, q, k, v, grad_att, passed, earlier, *rest):
    (gq, gk, gv), came = rest[-4 - along : -1 - along], rest[-1]
    count = q.shape[0]
    heads = q.shape[1] // DH
    step = pl.program_id(0)

    @pl.when(step == 0)
    def _():
        core, (early_b, early_e, late_b, late_e) = chip_docs(lens, place, count)
        by_chip = jnp.where(core == 0, 1.0, same(late_b, early_b))
        by_mate = jnp.where(core == 0, 0.0, same(late_b, early_e))
        came[...] = (
            passed[...].astype(F32) * by_chip + earlier[...].astype(F32) * by_mate
        ).astype(BF16)

    ends = doc_ends(lens)
    first = place[0] * count
    seen, seeing = visible(ends, first, count)
    head = head_mask(ends, first, count)
    for hs in bunches(heads):
        wides = [q[:, cols(h)].astype(F32) for h in hs]
        fqs = [feature(wide).astype(BF16) for wide in wides]
        fks = [feature(k[:, cols(h)].astype(F32)).astype(BF16) for h in hs]
        gas = [grad_att[:, cols(h)] for h in hs]
        gss = [
            jnp.where(seen, mul(ga, v[:, cols(h)], NT), 0.0).astype(BF16)
            for h, ga in zip(hs, gas)
        ]
        totals = [
            mul(gs, fk, NN) + jnp.where(head, mul(ga, came[step * heads + h], NT), 0.0)
            for h, gs, fk, ga in zip(hs, gss, fks, gas)
        ]
        flipped = [
            jnp.where(seeing, mul(v[:, cols(h)], ga, NT), 0.0).astype(BF16)
            for h, ga in zip(hs, gas)
        ]
        scores = [
            jnp.where(seeing, mul(fk, fq, NT), 0.0).astype(BF16) for fq, fk in zip(fqs, fks)
        ]
        gks = [mul(gs, fq, NN) for gs, fq in zip(flipped, fqs)]
        gvs = [mul(s, ga, NN) for s, ga in zip(scores, gas)]
        for h, total, wide, a, b in zip(hs, totals, wides, gks, gvs):
            gq[:, cols(h)] = (total * slope(wide)).astype(BF16)
            gk[:, cols(h)] = a
            gv[:, cols(h)] = b


def last_kernel(chips, lens, place, k, v, gk_part, gv_part, late, *rest):
    came = rest[-1]
    outgoing, gk, gv = rest[:chips], rest[-3], rest[-2]
    if len(rest) > chips + 3:
        rest[-4][...] = rest[chips][...]
        gk, gv = rest[-3], rest[-2]
    count = k.shape[0]
    heads = k.shape[1] // DH
    step = pl.program_id(0)

    @pl.when(step == 0)
    def _():
        core, (early_b, early_e, late_b, late_e) = chip_docs(lens, place, count)
        chip = place[2] >> 1
        by_far = jnp.where(core == 0, same(early_e, late_e), 1.0)
        by_late = jnp.where(core == 0, same(early_e, late_b), 0.0)
        for n, state in enumerate(outgoing[::-1]):
            owned = state.shape[0]
            at = pl.ds((chip ^ n) * owned, owned)
            came[at] = (
                state[...].astype(F32) * by_far + late[at].astype(F32) * by_late
            ).astype(BF16)

    tail = tail_mask(doc_ends(lens), place[0] * count, count)
    for hs in bunches(heads):
        wides = [k[:, cols(h)].astype(F32) for h in hs]
        fks = [jnp.where(tail, feature(wide), 0.0).astype(BF16) for wide in wides]
        vts = [jnp.where(tail, v[:, cols(h)].astype(F32), 0.0).astype(BF16) for h in hs]
        states = [came[step * heads + h] for h in hs]
        gks = [gk_part[:, cols(h)] + mul(vt, o, NT) for h, vt, o in zip(hs, vts, states)]
        gvs = [gv_part[:, cols(h)] + mul(fk, o, NN) for h, fk, o in zip(hs, fks, states)]
        for h, a, wide, b in zip(hs, gks, wides, gvs):
            gk[:, cols(h)] = (a * slope(wide)).astype(BF16)
            gv[:, cols(h)] = b.astype(BF16)


def same(a, b):
    return jnp.where(a == b, 1.0, 0.0).astype(F32)


def chip_docs(lens, place, count):
    ends = doc_ends(lens)
    core = place[2] & 1
    start = (place[0] - core) * count
    marks = (start, start + count - 1, start + count, start + 2 * count - 1)
    return core, [doc_at(ends, mark) for mark in marks]


def merge_kernel(count, lens, place, mine, other, _, *outs):
    outs = outs[:-1]
    core, (early_b, early_e, late_b, late_e) = chip_docs(lens, place, count)
    far = same(early_e, late_e)
    mine_by = jnp.where(core == 0, far, 1.0)
    other_by = jnp.where(core == 0, 1.0, far)
    chip = place[2] >> 1
    for n, out in enumerate(outs):
        at = chip ^ n
        out[...] = (mine[at].astype(F32) * mine_by + other[at].astype(F32) * other_by).astype(
            BF16
        )


def total_kernel(forward, unit, members, passed, lens, place, *rest):
    states, total, held = rest[:members][::-1], rest[members + passed], rest[-1]
    chip = place[2] >> 1
    for n, state in enumerate(states):
        held[chip ^ n] = state[...]
    ends = doc_ends(lens)
    layer = place[1] * (members * unit)
    carry = None
    for step in range(members):
        i = step if forward else members - 1 - step
        mine = held[i].astype(F32)
        edge = layer + ((i + 1) * unit - 1 if forward else i * unit)
        here = doc_at(ends, edge)
        if carry is not None:
            mine = mine + carry * same(here, previous)
        carry, previous = mine, here
    total[...] = carry.astype(BF16)


def prefix_kernel(forward, unit, members, unread, lens, place, *rest):
    states, outs, (held, sums) = rest[:members][::-1], rest[-members - 2 : -2], rest[-2:]
    others = rest[members + unread : -members - 2]
    chip = place[2] >> 1
    for n, state in enumerate(states):
        held[chip ^ n] = state[...]
    span = members * unit
    ends = doc_ends(lens)
    layer = place[1] * span
    sign = -1 if forward else 1
    previous = doc_at(ends, layer - 1 if forward else layer + span)
    carry = None
    for s, other in enumerate(others):
        far = layer + sign * s * span
        there = doc_at(ends, far - 1 if forward else far + span)
        term = other[...].astype(F32) * same(there, previous)
        carry = term if carry is None else carry + term
    for step in range(members):
        i = step if forward else members - 1 - step
        near, far = layer + i * unit, layer + (i + 1) * unit - 1
        if not forward:
            near, far = far, near
        if carry is None:
            sums[i] = jnp.zeros(sums.shape[1:], BF16)
        else:
            sums[i] = (carry * same(doc_at(ends, near), previous)).astype(BF16)
        if step < members - 1:
            here = doc_at(ends, far)
            mine = held[i].astype(F32)
            if carry is not None:
                mine = mine + carry * same(here, previous)
            carry, previous = mine, here
    for n, out in enumerate(outs):
        out[...] = sums[chip ^ n]


SMALL = pltpu.CompilerParams(
    dimension_semantics=("arbitrary",), vmem_limit_bytes=16 * 1024 * 1024
)

def local(queries, keys, values, out_grad, doc_lengths):
    count, width = queries.shape
    heads = width // DH
    layers = lax.axis_size("z")
    members = lax.axis_size("x") * lax.axis_size("head")
    owned = heads // members
    half = heads // 2
    reach = range(1, min(layers - 1, -(-layers // 2)) + 1)
    place = jnp.stack(
        [lax.axis_index(("z", "x", "head")), lax.axis_index("z"), lax.axis_index(LAYER)]
    ).astype(jnp.int32)
    chips = members // 2
    step_heads = max(n for n in (8, 4, 2, 1) if half % n == 0)
    steps = half // step_heads

    def held_in_hbm(arg):
        return pltpu.with_memory_space_constraint(arg, pltpu.HBM)

    def at(parity):
        if parity is None:
            return lambda i, lens, place: i
        return lambda i, lens, place: ((place[2] & 1) ^ parity) * steps + i

    def tokens(parity):
        block = at(parity)
        return pl.BlockSpec((count, step_heads * DH), lambda *a: (0, block(*a)))

    whole = pl.BlockSpec(memory_space=pltpu.VMEM)
    halved = pl.BlockSpec((step_heads, DH, DH), lambda i, *a: (i, 0, 0))
    untouched = pl.BlockSpec(memory_space=pl.ANY)
    token_bf = pltpu.HBM((count, width), BF16)
    token_f32 = jax.ShapeDtypeStruct((count, width), F32)
    owned_bf = jax.ShapeDtypeStruct((owned, DH, DH), BF16)
    half_bf = jax.ShapeDtypeStruct((half, DH, DH), BF16)

    def run(kernel, grid, ins, outs, shapes, scratch, args, cost, name, aliases={}, lens=None):
        flops, moved, exps = cost
        return pl.pallas_call(
            kernel,
            grid_spec=pltpu.PrefetchScalarGridSpec(
                num_scalar_prefetch=2,
                grid=(grid,),
                in_specs=ins,
                out_specs=outs,
                scratch_shapes=scratch,
            ),
            out_shape=shapes,
            input_output_aliases=aliases,
            compiler_params=SMALL,
            cost_estimate=pl.CostEstimate(
                flops=flops, bytes_accessed=moved, transcendentals=exps
            ),
            name=name,
        )(doc_lengths if lens is None else lens, place, *args)

    product = 2 * half * count * DH * DH
    array = half * count * DH * 2
    all_states = pltpu.VMEM((heads, DH, DH), BF16)
    block = owned
    single = grouped = whole
    buffer = pltpu.VMEM((chips, block, DH, DH), BF16)
    combining = (4 * half * DH * DH, 4 * half * DH * DH, 0)
    moves = 1

    def swap(state):
        return lax.ppermute(state, LAYER, [(i, i ^ 1) for i in range(members)])

    def exchange(states):
        came = list(states)
        for n in reversed(range(1, chips)):
            pairs = [(i, i ^ (2 * n)) for i in range(members)]
            came[n] = lax.ppermute(states[n], LAYER, pairs)
        return came

    def reach_out(merged, along, forward, name):
        came = exchange(merged)
        total, *along = run(
            functools.partial(total_kernel, forward, 2 * count, chips, len(along)),
            moves,
            [single] * chips + [untouched] * len(along),
            [single] + [untouched] * len(along),
            [owned_bf] + [jax.ShapeDtypeStruct(array.shape, array.dtype) for array in along],
            [buffer],
            [*came[::-1], *along],
            combining,
            name + "_total",
            aliases={2 + chips + j: 1 + j for j in range(len(along))},
        )
        others = []
        for s in reversed(reach):
            pairs = [(i, i + s) if forward else (i + s, i) for i in range(layers - s)]
            others.insert(0, lax.ppermute(total, "z", pairs))
        return came, others, total, along

    def spread(came, others, after, forward, name):
        sums = run(
            functools.partial(prefix_kernel, forward, 2 * count, chips, len(after)),
            moves,
            [single] * chips + [untouched] * len(after) + [single] * len(others),
            [single] * chips,
            [owned_bf] * chips,
            [buffer, buffer],
            [*came[::-1], *after, *others],
            combining,
            name + "_prefix",
        )
        return exchange(sums)

    narrow = (count, half * DH)
    lane = pl.BlockSpec((count, step_heads * DH), lambda i, *a: (0, i))
    pinned = [held_in_hbm(array) for array in (queries, keys, values, out_grad)]
    tail_work = (product, 3 * array, half * count * DH)
    copies = [
        jax.ShapeDtypeStruct((3, *narrow), BF16),
        jax.ShapeDtypeStruct(narrow, BF16),
    ]
    mate_tail, mate_three, mate_g = run(
        tail_kernel,
        steps,
        [tokens(1)] * 4,
        [halved, pl.BlockSpec((3, count, step_heads * DH), lambda i, *a: (0, 0, i)), lane],
        [half_bf, *copies],
        [],
        (pinned[1], pinned[2], pinned[0], pinned[3]),
        tail_work,
        "tail_mate",
        lens=held_in_hbm(doc_lengths),
    )
    (own_tail,) = run(
        tail_kernel,
        steps,
        [tokens(0)] * 2,
        [halved],
        [half_bf],
        [],
        pinned[1:3],
        tail_work,
        "tail_own",
        lens=held_in_hbm(doc_lengths),
    )
    mine = own_tail.reshape(chips, owned, DH, DH)
    other = swap(mate_tail).reshape(chips, owned, DH, DH)
    *merged, mate_three = run(
        functools.partial(merge_kernel, count),
        moves,
        [grouped] * 2 + [untouched],
        [single] * chips + [untouched],
        [owned_bf] * chips + copies[:1],
        [],
        (mine, other, mate_three),
        combining,
        "carried_chip",
        aliases={4: chips},
    )
    came, others, _, (mate_g, own_tail) = reach_out(merged, (mate_g, own_tail), True, "carried")
    mate_three, mate_g = swap(mate_three), swap(mate_g)
    few = max(n for n in (8, 4, 2, 1) if half % n == 0)
    parts = half // few

    def own_few(i, lens, place):
        return 0, (place[2] & 1) * parts + i

    own_tokens = pl.BlockSpec((count, few * DH), own_few)
    pair_tokens = pl.BlockSpec((2 * count, few * DH), lambda i, *a: (0, i))
    lane_few = pl.BlockSpec((count, few * DH), lambda i, *a: (0, i))
    turns = pl.BlockSpec((few, 2 * DH, 2 * count), lambda i, *a: (i, 0, 0))
    part, head_fq, turned = run(
        chip_kernel,
        parts,
        [own_tokens] * 3 + [pl.BlockSpec((3, count, few * DH), lambda i, *a: (0, 0, i))],
        [pair_tokens, pair_tokens, turns],
        [
            jax.ShapeDtypeStruct((2 * count, half * DH), F32),
            jax.ShapeDtypeStruct((2 * count, half * DH), BF16),
            jax.ShapeDtypeStruct((half, 2 * DH, 2 * count), BF16),
        ],
        [],
        (queries, keys, values, mate_three),
        (10 * product, 14 * array, 4 * half * count * DH),
        "within_chip",
    )
    late_tail = swap(own_tail)
    chip_in = spread(came, others, (part, late_tail), True, "carried")
    few_states = pl.BlockSpec((few, DH, DH), lambda i, *a: (i, 0, 0))
    one_owner = whole
    half_states = pltpu.VMEM((half, DH, DH), BF16)
    narrow_bf = jax.ShapeDtypeStruct(narrow, BF16)
    attn_half, mate_out, mine_ga, mate_ga, mine_in, mine_late, sent_in, sent_late, *merged = run(
        norm_kernel,
        parts,
        [pair_tokens, turns, own_tokens, lane_few, pair_tokens] + [one_owner] * chips,
        [own_tokens]
        + [lane_few] * 3
        + [whole, few_states, whole, few_states]
        + [one_owner] * chips,
        [token_bf] + [narrow_bf] * 3 + [half_bf] * 4 + [owned_bf] * chips,
        [half_states],
        (head_fq, turned, out_grad, mate_g, part, *chip_in[::-1]),
        (8 * product, 16 * array, 2 * half * count * DH),
        "normed",
    )
    def inner(parity, grad_att, passed, earlier, after, made, along):
        return run(
            functools.partial(inner_kernel, len(along)),
            steps,
            [tokens(parity)] * 3
            + [lane]
            + [whole] * 2
            + [untouched] * (len(after) + len(made) + len(along)),
            [tokens(parity)] * 3 + [untouched] * len(along),
            [token_bf, token_f32, token_f32]
            + [jax.ShapeDtypeStruct(array.shape, array.dtype) for array in along],
            [half_states],
            (queries, keys, values, grad_att, passed, earlier, *after, *made, *along),
            (7 * product, 11 * array, 2 * half * count * DH),
            f"grads_within_{parity}",
            aliases={8 + len(after) + j: j for j in range(len(made) + len(along))},
        )

    made = inner(0, mine_ga, mine_in, other.reshape(half, DH, DH), (), (), ())
    came, others, total, (mate_ga, sent_in, gk_half) = reach_out(
        merged, (mate_ga, sent_in, made[1]), False, "future"
    )
    made = (held_in_hbm(made[0]), gk_half, made[2])
    grad_queries, gk_part, gv_part, mate_out, sent_late = inner(
        1, swap(mate_ga), swap(sent_in), late_tail, (total,), made, (mate_out, sent_late)
    )
    late = (mine_late, swap(sent_late))
    chip_out = spread(came, others, (gk_part,), False, "future")
    outgoing = (chip_out, [swap(state) for state in chip_out])
    def last(parity, extra_ins, extra_outs, shapes, args, aliases):
        return run(
            functools.partial(last_kernel, chips),
            steps,
            [tokens(parity)] * 4 + [whole] + [one_owner] * chips + extra_ins,
            extra_outs + [tokens(parity)] * 2,
            shapes,
            [half_states],
            (keys, values, gk_part, gv_part, late[parity], *outgoing[parity][::-1], *args),
            (2 * product, 9 * array, half * count * DH),
            f"grads_last_{parity}",
            aliases=aliases,
        )

    grad_keys, grad_values = last(0, [], [], [token_bf] * 2, (), {})
    attn_out, grad_keys, grad_values = last(
        1,
        [lane] + [untouched] * 3,
        [tokens(1)],
        [token_bf] * 3,
        (swap(mate_out), held_in_hbm(attn_half), grad_keys, grad_values),
        {8 + chips + j: j for j in range(3)},
    )
    return attn_out, grad_queries, grad_keys, grad_values


def solution(mesh):
    n_seq, n_head = mesh.shape["seq"], mesh.shape["head"]
    inner = 2 if n_seq % 2 == 0 else 1
    fine = Mesh(mesh.devices.reshape(n_seq // inner, inner, n_head), ("z", "x", "head"))
    rows = P(("z", "x", "head"), None)
    return jax.shard_map(
        local,
        mesh=fine,
        in_specs=(rows, rows, rows, rows, P()),
        out_specs=(rows, rows, rows, rows),
        check_vma=False,
    )
```
